32 devices in a mesh: grp: 2 (over y), tp: 8 (over z, x), rep: 2 (over core).
Axes of the slice: x: 2, y: 2, z: 4, core: 2. Of those that a mesh axis runs over, the one named last changes fastest.
Arguments:
- stretch: bfloat16 [192, 12, 16384], P(None, ('grp', 'rep'), 'tp'), parts along dimension 1, may hold values from -512 to 512
- norm_gain: float32 [16384], P('tp'), may hold values from 0.1 to 1.9
- kv_codes: int32 [16384, 2048], P('tp'), may hold values from 0 to 15
- scale_codes: int32 [256, 2048], P('tp'), may hold values from 0 to 255
- outer_scales: float32 [256, 8], P('tp'), may hold values from 0.01 to 0.09
- prompt_lengths: int32 [12], P('grp'), parts along dimension 0, may hold values from 194 to 2240, as said below
- target_rows: int32 [12], P('grp'), parts along dimension 0, may hold values from 0 to 7, as said below
- cache_lengths: int32 [16], P(('grp', 'tp')), parts along dimension 0, may hold values from 2 to 2048, as said below
- kv_cache: bfloat16 [16, 2048, 2048], P(('grp', 'tp'), 'rep'), parts along dimension 0, may hold values from -6 to 6
- queries: bfloat16 [16, 2, 16384], P(('grp', 'tp')), parts along dimension 0, may hold values from -96 to 96
- new_kv: bfloat16 [16, 2, 2048], P(('grp', 'tp')), parts along dimension 0, may hold values from -6 to 6
Outputs:
- attended: bfloat16 [16, 2, 16384], P(('grp', 'tp')), parts along dimension 0
The draws below stay inside these ranges and needn't reach their ends.
There are 2 independent parts, one for each index of `grp`. The reference program is written for one: setup_inputs(seed, part) draws one part's arguments, and reference() takes and returns one part's arrays. A program takes and returns all parts, laid end to end along the dimension named above; an argument that names none is the same for every part. Nothing has to cross between parts.
Inputs may be any that keep to these rules, and one draw needn't show every extreme that they name: `target_rows`: distinct rows; the 3 prompts of one index of rep go to distinct owners, the owner of row g being g. `prompt_lengths`: both ends are reached. `cache_lengths`: both ends are reached.
All inputs are finite; a program needn't handle non-finite values.
Results may differ from the reference program's by a relative error of at most 0.013.
Values may be sent and summed in bfloat16 or wider, within the bound.
No kernel may reach another device: no remote copies, remote signals or barrier semaphores. Data moves between devices by JAX's collectives and lax.ppermute only.
A program may use at most 128 MiB of HBM per device.

```python
import math
import jax
import jax.numpy as jnp
from jax import lax

D = 16384
HEADS = 128
KV_HEADS = 8
HEAD_DIM = 128
KV_WIDTH = 2048
STRETCH = 192
QBLOCK = 64
QGROUP = 256
PER_REP = 3
PROMPTS = 6
SLOTS = 1
ROWS = 8
CACHE = 2048
STEPS = 2


def draw_stretch(key, part):
    key = jax.random.fold_in(key, 13)
    row_key, column_key, noise_key = jax.random.split(key, 3)
    row_scale = jnp.exp(math.log(10.0) * jax.random.uniform(row_key, (STRETCH, PROMPTS, 1), jnp.float32))
    trend = jnp.arange(D, dtype=jnp.float32) / D
    column_scale = jnp.exp(math.log(10.0) * (0.5 * trend + 0.5 * jax.random.uniform(column_key, (D,), jnp.float32)))
    noise = jnp.clip(jax.random.normal(noise_key, (STRETCH, PROMPTS, D), jnp.float32), -5.0, 5.0)
    return jnp.clip(noise * row_scale * column_scale, -512.0, 512.0).astype(jnp.bfloat16)


def draw_target_rows(key, part):
    key = jax.random.fold_in(key, 14)
    order_key, base_key = jax.random.split(key)
    owner_count = ROWS // SLOTS
    order = jax.random.permutation(order_key, owner_count)
    first_owners = order[:PER_REP]
    second_owners = order[PER_REP:2 * PER_REP]
    base_slot = jax.random.randint(base_key, (owner_count,), 0, SLOTS)
    first_rows = first_owners * SLOTS + base_slot[first_owners]
    second_rows = second_owners * SLOTS + base_slot[second_owners]
    return jnp.concatenate([first_rows, second_rows]).astype(jnp.int32)


def draw_prompt_lengths(key, part):
    key = jax.random.fold_in(key, 15)
    value_key, pick_key = jax.random.split(key)
    values = jax.random.randint(value_key, (PROMPTS,), STRETCH + 2, CACHE + STRETCH + 1)
    picks = jax.random.permutation(pick_key, PROMPTS)
    values = values.at[picks[0]].set(CACHE + STRETCH).at[picks[1]].set(STRETCH + 2)
    return values.astype(jnp.int32)


def draw_cache_lengths(key, part):
    key = jax.random.fold_in(key, 16)
    first_key, second_key, pick_key = jax.random.split(key, 3)
    values = jnp.minimum(jax.random.randint(first_key, (ROWS,), 2, CACHE + 1), jax.random.randint(second_key, (ROWS,), 2, CACHE + 1))
    picks = jax.random.permutation(pick_key, ROWS)
    values = values.at[picks[0]].set(CACHE).at[picks[1]].set(2)
    return values.astype(jnp.int32)


def draw_kv_cache(key, part):
    key = jax.random.fold_in(key, 17)
    values = jax.random.normal(key, (ROWS, CACHE, KV_WIDTH), jnp.float32)
    return jnp.clip(values, -6.0, 6.0).astype(jnp.bfloat16)


def draw_queries(key, part):
    key = jax.random.fold_in(key, 18)
    values = jnp.clip(2.0 * jax.random.normal(key, (ROWS, STEPS, HEADS * HEAD_DIM), jnp.float32), -12.0, 12.0)
    return values.astype(jnp.bfloat16)


def touch_ends(drawn, rng, low, largest):
    index_at = [jax.random.randint(jax.random.fold_in(rng, axis), (), 0, length) for axis, length in enumerate(drawn.shape)]
    longest = drawn.shape.index(max(drawn.shape))
    neighbour = index_at[:longest] + [(index_at[longest] + 1) % drawn.shape[longest]] + index_at[longest + 1:]
    return drawn.at[tuple(index_at)].set(low).at[tuple(neighbour)].set(largest)


def shard_levels(key, extent, cuts, least, largest):
    factor_of, own = 1.0, jax.random.fold_in(key, 6)
    for dim, shards_of in cuts:
        draws = jnp.exp(jax.random.uniform(jax.random.fold_in(own, dim), (shards_of,), jnp.float32, least / len(cuts), largest / len(cuts)))
        factor_of = factor_of * jnp.repeat(draws, extent[dim] // shards_of).reshape([-1 if axis == dim else 1 for axis in range(len(extent))])
    return factor_of


def normal_values(key, dims, spread, limit, shards=(), held_as=jnp.bfloat16):
    values = jax.random.normal(key, dims, jnp.float32) * spread
    if len(shards) > 0:
        values = shard_levels(key, dims, shards, -0.22, 0.18) * values
    return jnp.clip(values, min=-limit, max=limit).astype(held_as)


def setup_inputs(seed: int = 0, part: int = 0) -> dict:
    streams_of = jax.random.split(jax.random.key(seed), 12)
    part_splits = jax.random.split(jax.random.fold_in(streams_of[11], part), 12)
    return {
        "stretch": draw_stretch(jax.random.fold_in(jax.random.fold_in(streams_of[11], part), 71), part),
        "norm_gain": jnp.clip(1.0 + 0.18 * jax.random.normal(streams_of[1], (D,), jnp.float32), 0.1, 1.9),
        "kv_codes": touch_ends(jax.random.randint(streams_of[2], (D, KV_WIDTH), 0, 16), jax.random.fold_in(streams_of[2], 1), 0, 15).astype(jnp.int32),
        "scale_codes": touch_ends(jax.random.randint(streams_of[3], (D // QBLOCK, KV_WIDTH), 0, 256), jax.random.fold_in(streams_of[3], 1), 0, 255).astype(jnp.int32),
        "outer_scales": jnp.clip(jnp.exp(math.log(0.09) - 2.1972246 * jax.random.uniform(streams_of[4], (D // QBLOCK, KV_WIDTH // QGROUP), jnp.float32) ** shard_levels(streams_of[4], (D // QBLOCK, KV_WIDTH // QGROUP), ((0, 8),), -0.2, 0.2)), 0.01, 0.09),
        "prompt_lengths": draw_prompt_lengths(jax.random.fold_in(jax.random.fold_in(streams_of[11], part), 71), part),
        "target_rows": draw_target_rows(jax.random.fold_in(jax.random.fold_in(streams_of[11], part), 71), part),
        "cache_lengths": draw_cache_lengths(jax.random.fold_in(jax.random.fold_in(streams_of[11], part), 71), part),
        "kv_cache": draw_kv_cache(jax.random.fold_in(jax.random.fold_in(streams_of[11], part), 71), part),
        "queries": draw_queries(jax.random.fold_in(jax.random.fold_in(streams_of[11], part), 71), part),
        "new_kv": normal_values(part_splits[10], (ROWS, STEPS, KV_WIDTH), 1.5, 6.0, ((0, 8),)),
    }


NORMAL_FLOAT_LEVELS = [-1.0, -0.6961928009986877, -0.5250730514526367, -0.39491748809814453, -0.28444138169288635, -0.18477343022823334, -0.09105003625154495, 0.0, 0.07958029955625534, 0.16093020141124725, 0.24611230194568634, 0.33791524171829224, 0.44070982933044434, 0.5626170039176941, 0.7229568362236023, 1.0]
ROTARY_BASE = 500000.0
EPSILON = 1e-05
NEGATIVE = -1e+30

def dequantize(weight_codes, block_codes, group_scales):
    table = jnp.array(NORMAL_FLOAT_LEVELS, jnp.float32)
    levels = jnp.take(table, weight_codes, axis=0)
    inner = (block_codes.astype(jnp.float32) + 1.0) / 256.0
    columns_per = weight_codes.shape[1] // group_scales.shape[1]
    block_scale = inner * jnp.repeat(group_scales, columns_per, axis=1)
    rows_per = weight_codes.shape[0] // block_codes.shape[0]
    return (levels * jnp.repeat(block_scale, rows_per, axis=0)).astype(jnp.bfloat16)

def rotate_keys(keys, positions):
    half_dim = HEAD_DIM // 2
    frequency = ROTARY_BASE ** (-jnp.arange(half_dim, dtype=jnp.float32) / half_dim)
    angles = positions[..., None] * frequency
    cosine = jnp.cos(angles)[..., None, :]
    sine_part = jnp.sin(angles)[..., None, :]
    heads = keys.reshape(keys.shape[:-1] + (KV_HEADS, HEAD_DIM))
    lower = heads[..., :half_dim]
    upper = heads[..., half_dim:]
    turned = jnp.concatenate([lower * cosine - upper * sine_part, upper * cosine + lower * sine_part], axis=-1)
    return turned.reshape(keys.shape)

def reference(stretch, norm_gain, kv_codes, scale_codes, outer_scales, prompt_lengths, target_rows, cache_lengths, kv_cache, queries, new_kv):
    key_width = KV_HEADS * HEAD_DIM
    group_size = HEADS // KV_HEADS
    widened = stretch.astype(jnp.float32)
    inverse = lax.rsqrt(lax.optimization_barrier(jnp.sum(widened * widened, axis=2)) / D + EPSILON)
    normed = (widened * inverse[..., None] * norm_gain).astype(jnp.bfloat16)
    weight = dequantize(kv_codes, scale_codes, outer_scales)
    projected = jnp.dot(normed.reshape(STRETCH * PROMPTS, D), weight, preferred_element_type=jnp.float32)
    projected = projected.astype(jnp.bfloat16).reshape(STRETCH, PROMPTS, KV_WIDTH)
    offsets = jnp.arange(STRETCH, dtype=jnp.int32)[:, None]
    positions = (prompt_lengths[None, :] - STRETCH + offsets).astype(jnp.float32)
    rotated = rotate_keys(projected[..., :key_width].astype(jnp.float32), positions).astype(jnp.bfloat16)
    handed = jnp.concatenate([rotated, projected[..., key_width:]], axis=2)
    places = jnp.arange(CACHE + STRETCH + STEPS, dtype=jnp.int32)
    fresh_offset = places - CACHE - STRETCH
    step_index = jnp.arange(STEPS, dtype=jnp.int32)
    scaling = HEAD_DIM ** (-0.5)

    def one_row(row_items):
        row_index, cache_rows, query_rows, fresh_rows, stored_length = row_items
        matches = target_rows == row_index
        received = jnp.any(matches)
        chosen = jnp.einsum('p,cpn->cn', matches.astype(jnp.float32), handed.astype(jnp.float32)).astype(jnp.bfloat16)
        row_span = jnp.where(received, jnp.sum(jnp.where(matches, prompt_lengths - STRETCH, 0)), stored_length)
        every_row = jnp.concatenate([cache_rows, chosen, fresh_rows], axis=0)
        keys = every_row[:, :key_width].astype(jnp.float32).reshape(-1, KV_HEADS, HEAD_DIM)
        values = every_row[:, key_width:].astype(jnp.float32).reshape(-1, KV_HEADS, HEAD_DIM)
        grouped = query_rows.astype(jnp.float32).reshape(STEPS, KV_HEADS, group_size, HEAD_DIM)
        scores = jnp.einsum('tkgd,jkd->tkgj', grouped, keys) * scaling
        earlier = jnp.where(places < CACHE, places < row_span, jnp.where(places < CACHE + STRETCH, received, False))
        allowed = earlier[None, :] | (fresh_offset[None, :] >= 0) & (fresh_offset[None, :] <= step_index[:, None])
        masking = allowed[:, None, None, :]
        highest = lax.optimization_barrier(jnp.max(jnp.where(masking, scores, NEGATIVE), axis=-1, keepdims=True))
        weights = jnp.where(masking, jnp.exp(scores - highest), 0.0)
        totals = lax.optimization_barrier(jnp.sum(weights, axis=-1))
        rounded = lax.optimization_barrier(weights.astype(jnp.bfloat16)).astype(jnp.float32)
        combined = jnp.einsum('tkgj,jkd->tkgd', rounded, values)
        return (combined / totals[..., None]).astype(jnp.bfloat16).reshape(STEPS, HEADS * HEAD_DIM)
    row_numbers = jnp.arange(ROWS, dtype=jnp.int32)
    return lax.map(one_row, (row_numbers, kv_cache, queries, new_kv, cache_lengths))
```

```python
import functools
import math

import jax
import jax.numpy as jnp
from jax import lax
from jax.experimental import pallas as pl
from jax.experimental.pallas import tpu as pltpu
from jax.sharding import PartitionSpec as P

D = 16384
HEADS = 128
KV_HEADS = 8
HEAD_DIM = 128
STRETCH = 192
STEPS = 2
QBLOCK = 64
GROUP = HEADS // KV_HEADS
ROWS = STEPS * GROUP
TAIL = 16
PART = ROWS + TAIL
NORMAL_FLOAT_LEVELS = [
    -1.0,
    -0.6961928009986877,
    -0.5250730514526367,
    -0.39491748809814453,
    -0.28444138169288635,
    -0.18477343022823334,
    -0.09105003625154495,
    0.0,
    0.07958029955625534,
    0.16093020141124725,
    0.24611230194568634,
    0.33791524171829224,
    0.44070982933044434,
    0.5626170039176941,
    0.7229568362236023,
    1.0,
]
ROTARY_BASE = 500000.0
EPSILON = 1e-05
NEGATIVE = -1e30
BF16 = jnp.bfloat16
F32 = jnp.float32


def ring_device(place, count):
    half = count // 2
    if isinstance(place, int):
        return 2 * place if place < half else 2 * (count - 1 - place) + 1
    return jnp.where(place < half, 2 * place, 2 * (count - 1 - place) + 1)


def project_kernel(
    heads, groups, x, key_codes, value_codes, key_scales, value_scales, outer, gain, levels,
    out, table,
):
    item, block = pl.program_id(0), pl.program_id(1)
    depth = key_codes.shape[0]

    @pl.when((item == 0) & (block == 0))
    def _():
        rows = lax.broadcasted_iota(jnp.int32, (128, 128), 0)
        lanes = lax.broadcasted_iota(jnp.int32, (128, 128), 1)
        for at in range(gain.shape[0]):
            column = jnp.sum(
                jnp.where(rows == lanes, gain[at : at + 1, :], 0.0), axis=1, keepdims=True
            )
            table[at * 128 : (at + 1) * 128, :] = column * levels[...]

    begin = pl.multiple_of(block * depth, depth)
    source = table[pl.ds(begin, depth), :]
    scale_rows = depth // QBLOCK
    if scale_rows == key_scales.shape[0]:
        scale_at = slice(None)
    else:
        scale_at = pl.ds(pl.multiple_of(block * scale_rows, scale_rows), scale_rows)
    head = heads[item]
    outer_here = outer[scale_at, :]
    lane = lax.broadcasted_iota(jnp.int32, outer_here.shape, 1)

    def weight(codes, scales, column):
        second = jnp.sum(jnp.where(lane == column, outer_here, 0.0), axis=1, keepdims=True)
        scale = (scales[scale_at, :].astype(F32) + 1.0) / 256.0 * second
        level = jnp.take_along_axis(source, codes[...], axis=1)
        level = level.reshape(scale_rows, QBLOCK, HEAD_DIM) * scale[:, None, :]
        return level.reshape(depth, HEAD_DIM).astype(BF16)

    heads_per = KV_HEADS // (outer.shape[1] // 2)
    both = jnp.concatenate(
        [
            weight(key_codes, key_scales, head // heads_per),
            weight(value_codes, value_scales, outer.shape[1] // 2 + head // heads_per),
        ],
        axis=1,
    )
    product = jnp.dot(x[0, :, pl.ds(begin, depth)], both, preferred_element_type=F32)

    if x.shape[2] == depth:
        out[0, 0] = product[:, :HEAD_DIM].astype(out.dtype)
        out[0, 1] = product[:, HEAD_DIM:].astype(out.dtype)
    else:

        @pl.when(block == 0)
        def _():
            out[0, 0] = product[:, :HEAD_DIM]
            out[0, 1] = product[:, HEAD_DIM:]

        @pl.when(block != 0)
        def _():
            out[0, 0] += product[:, :HEAD_DIM]
            out[0, 1] += product[:, HEAD_DIM:]


def project(owners, x, codes, scales, outer, gain, levels):
    count = owners.shape[0]
    tokens, features = x.shape[1:]
    depth = min(1024, features)
    blocks = features // depth
    heads = owners % KV_HEADS
    groups = owners // KV_HEADS
    return pl.pallas_call(
        project_kernel,
        grid_spec=pltpu.PrefetchScalarGridSpec(
            num_scalar_prefetch=2,
            grid=(count, blocks),
            in_specs=[
                pl.BlockSpec((1, tokens, features), lambda i, k, h, g: (g[i], 0, 0)),
                pl.BlockSpec((depth, HEAD_DIM), lambda i, k, h, g: (k, h[i])),
                pl.BlockSpec((depth, HEAD_DIM), lambda i, k, h, g: (k, KV_HEADS + h[i])),
                pl.BlockSpec((scales.shape[0], HEAD_DIM), lambda i, k, h, g: (0, h[i])),
                pl.BlockSpec((scales.shape[0], HEAD_DIM), lambda i, k, h, g: (0, KV_HEADS + h[i])),
                pl.BlockSpec(outer.shape, lambda i, k, h, g: (0, 0)),
                pl.BlockSpec(gain.shape, lambda i, k, h, g: (0, 0)),
                pl.BlockSpec(levels.shape, lambda i, k, h, g: (0, 0)),
            ],
            out_specs=pl.BlockSpec((1, 2, tokens, HEAD_DIM), lambda i, k, h, g: (i, 0, 0, 0)),
            scratch_shapes=[pltpu.VMEM((features, 128), F32)],
        ),
        out_shape=jax.ShapeDtypeStruct((count, 2, tokens, HEAD_DIM), F32),
        compiler_params=pltpu.CompilerParams(vmem_limit_bytes=24 * 1024 * 1024),
        cost_estimate=pl.CostEstimate(
            flops=count * 4 * tokens * features * HEAD_DIM,
            bytes_accessed=count * features * 2 * HEAD_DIM * 4 + x.shape[1] * features * 2,
            transcendentals=0,
        ),
        name="project",
    )(heads, groups, x, codes, codes, scales, scales, outer, gain, levels)


def pieces_tail(logs):
    rows = lax.broadcasted_iota(jnp.int32, (ROWS, 128), 0)
    lanes = lax.broadcasted_iota(jnp.int32, (ROWS, 128), 1)
    row = jnp.sum(jnp.where(rows == lanes, logs, 0.0), axis=0, keepdims=True)
    high = row.astype(BF16).astype(F32)
    middle = (row - high).astype(BF16).astype(F32)
    low = row - high - middle
    at = lax.broadcasted_iota(jnp.int32, (TAIL, 128), 0)
    tail = jnp.where(at == 0, high, jnp.where(at == 1, middle, jnp.where(at == 2, low, 0.0)))
    return tail.astype(BF16)


def tail_pieces(tail):
    tail = tail.astype(F32)
    row = tail[0:1, :] + tail[1:2, :] + tail[2:3, :]
    rows = lax.broadcasted_iota(jnp.int32, (ROWS, 128), 0)
    lanes = lax.broadcasted_iota(jnp.int32, (ROWS, 128), 1)
    return jnp.sum(jnp.where(rows == lanes, row, 0.0), axis=1, keepdims=True)


def cache_kernel(info, q, keys, values, fresh_keys, fresh_values, out):
    scaling = HEAD_DIM ** (-0.5)
    dims = (((1,), (1,)), ((), ()))
    length = keys.shape[1]
    query = q[0]
    scores = lax.dot_general(query, keys[0], dims, preferred_element_type=F32) * scaling
    fresh = lax.dot_general(query, fresh_keys[...], dims, preferred_element_type=F32) * scaling
    place = lax.broadcasted_iota(jnp.int32, scores.shape, 1) + info[1] * length
    allowed = place < info[0]
    slot = lax.broadcasted_iota(jnp.int32, fresh.shape, 1)
    step = lax.broadcasted_iota(jnp.int32, fresh.shape, 0) // GROUP
    fresh_allowed = (slot <= step) & (slot < STEPS) & (info[1] == 0)
    highest = jnp.maximum(
        jnp.max(jnp.where(allowed, scores, NEGATIVE), axis=1, keepdims=True),
        jnp.max(jnp.where(fresh_allowed, fresh, NEGATIVE), axis=1, keepdims=True),
    )
    weights = jnp.where(allowed, jnp.exp(scores - highest), 0.0)
    fresh_weights = jnp.where(fresh_allowed, jnp.exp(fresh - highest), 0.0)
    totals = jnp.sum(weights, axis=1, keepdims=True) + jnp.sum(
        fresh_weights, axis=1, keepdims=True
    )
    sums = jnp.dot(weights.astype(BF16), values[0], preferred_element_type=F32)
    sums += jnp.dot(fresh_weights.astype(BF16), fresh_values[...], preferred_element_type=F32)
    some = totals > 0.0
    out[0, :ROWS] = jnp.where(some, sums / jnp.where(some, totals, 1.0), 0.0).astype(BF16)
    logs = jnp.where(some, highest + jnp.log(jnp.where(some, totals, 1.0)), NEGATIVE)
    out[0, ROWS:] = pieces_tail(logs)


def cache_attention(info, grouped, kv_cache, fresh):
    length = kv_cache.shape[1]
    return pl.pallas_call(
        cache_kernel,
        grid_spec=pltpu.PrefetchScalarGridSpec(
            num_scalar_prefetch=1,
            grid=(KV_HEADS,),
            in_specs=[
                pl.BlockSpec((1, ROWS, HEAD_DIM), lambda h, s: (h, 0, 0)),
                pl.BlockSpec((1, length, HEAD_DIM), lambda h, s: (0, 0, h)),
                pl.BlockSpec((1, length, HEAD_DIM), lambda h, s: (0, 0, KV_HEADS + h)),
                pl.BlockSpec((fresh.shape[0], HEAD_DIM), lambda h, s: (0, h)),
                pl.BlockSpec((fresh.shape[0], HEAD_DIM), lambda h, s: (0, KV_HEADS + h)),
            ],
            out_specs=pl.BlockSpec((1, PART, HEAD_DIM), lambda h, s: (h, 0, 0)),
        ),
        out_shape=jax.ShapeDtypeStruct((KV_HEADS, PART, HEAD_DIM), BF16),
        compiler_params=pltpu.CompilerParams(vmem_limit_bytes=16 * 1024 * 1024),
        cost_estimate=pl.CostEstimate(
            flops=4 * HEADS * STEPS * length * HEAD_DIM,
            bytes_accessed=length * 2 * KV_HEADS * HEAD_DIM * 2,
            transcendentals=HEADS * STEPS * length,
        ),
        name="cache_attention",
    )(info, grouped, kv_cache, kv_cache, fresh, fresh)


def stretch_kernel(targets, own, right, left, inverse, cosine, sine, q, out):
    scaling = HEAD_DIM ** (-0.5)
    dims = (((1,), (1,)), ((), ()))
    empty = jnp.zeros((ROWS, HEAD_DIM), BF16)
    empty_tail = pieces_tail(jnp.full((ROWS, 1), NEGATIVE, F32))
    for owner in range(out.shape[0]):
        for core in range(2):
            out[owner, core, :ROWS] = empty
            out[owner, core, ROWS:] = empty_tail
    for prompt in range(own.shape[2] // STRETCH):
        at = slice(prompt * STRETCH, (prompt + 1) * STRETCH)
        scale = inverse[at, :]
        keys = own[0, 0, at] + right[0, at].astype(F32) + left[0, at].astype(F32)
        values = own[0, 1, at] + right[1, at].astype(F32) + left[1, at].astype(F32)
        keys = (keys * scale).astype(BF16).astype(F32)
        values = (values * scale).astype(BF16)
        keys = keys * cosine[at, :] + pltpu.roll(keys, HEAD_DIM // 2, 1) * sine[at, :]
        target = targets[prompt]
        query = q[target, :ROWS]
        scores = lax.dot_general(query, keys.astype(BF16), dims, preferred_element_type=F32)
        scores = scores * scaling
        highest = jnp.max(scores, axis=1, keepdims=True)
        weights = jnp.exp(scores - highest)
        totals = jnp.sum(weights, axis=1, keepdims=True)
        sums = jnp.dot(weights.astype(BF16), values, preferred_element_type=F32)
        result = (sums / totals).astype(BF16)
        tail = pieces_tail(highest + jnp.log(totals))
        for core in range(2):
            out[target, core, :ROWS] = result
            out[target, core, ROWS:] = tail


def stretch_attention(targets, own, right, left, inverse, cosine, sine, q):
    vmem = pl.BlockSpec(memory_space=pltpu.VMEM)
    return pl.pallas_call(
        stretch_kernel,
        in_specs=[pl.BlockSpec(memory_space=pltpu.SMEM)] + [vmem] * 7,
        out_specs=vmem,
        out_shape=jax.ShapeDtypeStruct((q.shape[0], 2, PART, HEAD_DIM), BF16),
        compiler_params=pltpu.CompilerParams(vmem_limit_bytes=16 * 1024 * 1024),
        name="stretch_attention",
    )(targets, own, right, left, inverse, cosine, sine, q)


def combine_kernel(cached, handed, out):
    groups = handed.shape[0]
    for head in range(KV_HEADS):
        parts = [cached[0, head], cached[1, head]]
        for group in range(groups):
            parts += [handed[group, head, 0], handed[group, head, 1]]
        logs = [tail_pieces(part[ROWS:]) for part in parts]
        highest = functools.reduce(jnp.maximum, logs)
        shares = [jnp.exp(log - highest) for log in logs]
        total = functools.reduce(jnp.add, shares)
        sums = functools.reduce(
            jnp.add, [share * part[:ROWS].astype(F32) for share, part in zip(shares, parts)]
        )
        result = (sums / total).astype(BF16)
        for step in range(STEPS):
            out[step, head * GROUP : (head + 1) * GROUP] = result[
                step * GROUP : (step + 1) * GROUP
            ]


def combine(cached, handed):
    vmem = pl.BlockSpec(memory_space=pltpu.VMEM)
    return pl.pallas_call(
        combine_kernel,
        in_specs=[vmem] * 2,
        out_specs=vmem,
        out_shape=jax.ShapeDtypeStruct((STEPS, HEADS, HEAD_DIM), BF16),
        compiler_params=pltpu.CompilerParams(vmem_limit_bytes=16 * 1024 * 1024),
        name="combine",
    )(cached, handed)


def split_pieces(value):
    high = lax.reduce_precision(value, 8, 7)
    middle = lax.reduce_precision(value - high, 8, 7)
    low = lax.reduce_precision(value - high - middle, 8, 7)
    return jnp.stack([high, middle, low], axis=1).astype(BF16)


def per_device(
    stretch,
    norm_gain,
    kv_codes,
    scale_codes,
    outer_scales,
    prompt_lengths,
    target_rows,
    cache_lengths,
    kv_cache,
    queries,
    new_kv,
):
    count = lax.axis_size("tp")
    here = lax.axis_index("tp")
    rep_here = lax.axis_index("rep")
    per_rep = stretch.shape[1]
    features = stretch.shape[2]
    groups = count // KV_HEADS
    per_group = per_rep // groups
    tokens = per_group * STRETCH
    group_here = here // KV_HEADS
    place = jnp.where(here % 2 == 0, here // 2, count - 1 - here // 2)

    x = stretch.transpose(1, 0, 2).reshape(groups, tokens, features)
    gain = norm_gain.reshape(features // 128, 128)
    levels = jnp.pad(jnp.array(NORMAL_FLOAT_LEVELS, F32), (0, 128 - 16)).reshape(1, 128)

    def owners_at(distances):
        places = (place + jnp.array(distances, jnp.int32)) % count
        return ring_device(places, count).astype(jnp.int32)

    def project_at(distances):
        return project(
            owners_at(distances), x, kv_codes, scale_codes, outer_scales, gain, levels
        )

    ring = [ring_device(at, count) for at in range(count)]
    to_right = [(ring[at], ring[(at + 1) % count]) for at in range(count)]
    to_left = [(ring[at], ring[at - 1]) for at in range(count)]

    half = count // 2
    far = project_at([half])[0].astype(BF16)
    right = lax.ppermute(far[0], "tp", to_right)
    left = lax.ppermute(far[1], "tp", to_left)

    grouped = queries.reshape(STEPS, KV_HEADS, GROUP, HEAD_DIM).transpose(1, 0, 2, 3)
    grouped = grouped.reshape(KV_HEADS, ROWS, HEAD_DIM)
    squares = jnp.sum(jnp.square(x.astype(F32)), axis=2)
    width = -(-tokens // 128) * 128
    squares = split_pieces(jnp.pad(squares, ((0, 0), (0, width - tokens))))
    squares = squares.reshape(groups, 3 * width // 128, 128)
    squares = jnp.pad(squares, ((0, 0), (0, TAIL - squares.shape[1]), (0, 0)))
    outgoing = jnp.concatenate(
        [
            jnp.broadcast_to(grouped[None], (groups, KV_HEADS, ROWS, HEAD_DIM)),
            jnp.broadcast_to(squares[:, None], (groups, KV_HEADS, TAIL, HEAD_DIM)),
        ],
        axis=2,
    ).reshape(count, PART, HEAD_DIM)
    incoming = lax.all_to_all(outgoing, "tp", split_axis=0, concat_axis=0, tiled=True)
    squares = jnp.sum(incoming[:, ROWS : ROWS + 3 * width // 128].astype(F32), axis=0)
    squares = jnp.sum(squares.reshape(3, width), axis=0)[:tokens]
    inverse = lax.rsqrt(squares / D + EPSILON)[:, None]

    first = rep_here * per_rep + group_here * per_group
    targets = lax.dynamic_slice_in_dim(target_rows, first, per_group)
    lengths = lax.dynamic_slice_in_dim(prompt_lengths, first, per_group)
    half_dim = HEAD_DIM // 2
    frequency = ROTARY_BASE ** (-jnp.arange(half_dim, dtype=F32) / half_dim)
    positions = (lengths[:, None] - STRETCH + jnp.arange(STRETCH, dtype=jnp.int32)[None, :])
    angles = positions.astype(F32).reshape(tokens, 1) * frequency
    cosine, sine = jnp.cos(angles), jnp.sin(angles)
    cosine = jnp.concatenate([cosine, cosine], axis=1)
    sine = jnp.concatenate([-sine, sine], axis=1)

    matches = target_rows == here
    span = jnp.where(
        jnp.any(matches),
        jnp.sum(jnp.where(matches, prompt_lengths - STRETCH, 0)),
        cache_lengths[0],
    )
    info = jnp.stack([span, rep_here]).astype(jnp.int32)
    fresh = jnp.pad(new_kv[0], ((0, 16 - STEPS), (0, 0)))
    cached = cache_attention(info, grouped, kv_cache, fresh)
    cached = lax.all_gather(cached, "rep")

    distances = list(range(half - 1, 0, -1))
    size = max(1, -(-len(distances) // 3))
    own = None
    for begin in range(0, len(distances), size):
        here_distances = distances[begin : begin + size]
        wanted = [sign * d for d in here_distances for sign in (1, -1)]
        if begin + size >= len(distances):
            wanted = wanted + [0]
        terms = project_at(wanted)
        for at, distance in enumerate(here_distances):
            if distance == half - 1:
                right = jnp.stack([terms[2 * at, 0] + right.astype(F32), terms[2 * at, 1]])
                left = jnp.stack([terms[2 * at + 1, 0], terms[2 * at + 1, 1] + left.astype(F32)])
            else:
                right = terms[2 * at] + right.astype(F32)
                left = terms[2 * at + 1] + left.astype(F32)
            right = lax.ppermute(right.astype(BF16), "tp", to_right)
            left = lax.ppermute(left.astype(BF16), "tp", to_left)
        own = terms[-1:]

    handed = stretch_attention(targets, own, right, left, inverse, cosine, sine, incoming)
    handed = handed.reshape(2 * count, PART, HEAD_DIM)
    handed = lax.all_to_all(handed, ("tp", "rep"), split_axis=0, concat_axis=0, tiled=True)
    handed = handed.reshape(groups, KV_HEADS, 2, PART, HEAD_DIM)
    return combine(cached, handed).reshape(1, STEPS, HEADS * HEAD_DIM)


def solution(mesh):
    in_specs = (
        P(None, ("grp", "rep"), "tp"),
        P("tp"),
        P("tp", None),
        P("tp", None),
        P("tp", None),
        P("grp"),
        P("grp"),
        P(("grp", "tp")),
        P(("grp", "tp"), "rep", None),
        P(("grp", "tp"), None, None),
        P(("grp", "tp"), None, None),
    )
    out_specs = P(("grp", "tp"), None, None)
    return jax.shard_map(
        per_device, mesh=mesh, in_specs=in_specs, out_specs=out_specs, check_vma=False
    )
```

```python
import functools
import math

import jax
import jax.numpy as jnp
from jax import lax
from jax.experimental import pallas as pl
from jax.experimental.pallas import tpu as pltpu
from jax.sharding import PartitionSpec as P

D = 16384
HEADS = 128
KV_HEADS = 8
HEAD_DIM = 128
STRETCH = 192
STEPS = 2
QBLOCK = 64
GROUP = HEADS // KV_HEADS
ROWS = STEPS * GROUP
TAIL = 16
PART = ROWS + TAIL
NORMAL_FLOAT_LEVELS = [
    -1.0,
    -0.6961928009986877,
    -0.5250730514526367,
    -0.39491748809814453,
    -0.28444138169288635,
    -0.18477343022823334,
    -0.09105003625154495,
    0.0,
    0.07958029955625534,
    0.16093020141124725,
    0.24611230194568634,
    0.33791524171829224,
    0.44070982933044434,
    0.5626170039176941,
    0.7229568362236023,
    1.0,
]
ROTARY_BASE = 500000.0
EPSILON = 1e-05
NEGATIVE = -1e30
BF16 = jnp.bfloat16
F32 = jnp.float32


def ring_device(place, count):
    half = count // 2
    if isinstance(place, int):
        return 2 * place if place < half else 2 * (count - 1 - place) + 1
    return jnp.where(place < half, 2 * place, 2 * (count - 1 - place) + 1)


def in_hbm(*arrays):
    return [pltpu.with_memory_space_constraint(array, pltpu.HBM) for array in arrays]


def weights(codes, scales, outer, column, block):
    depth = codes.shape[0]
    count = depth // QBLOCK
    line = lax.broadcasted_iota(jnp.int32, outer.shape, 0)
    line = jnp.sum(jnp.where(line == column, outer, 0.0), axis=0, keepdims=True)
    rows = lax.broadcasted_iota(jnp.int32, (count, outer.shape[1]), 0) + block * count
    lanes = lax.broadcasted_iota(jnp.int32, (count, outer.shape[1]), 1)
    second = jnp.sum(jnp.where(rows == lanes, line, 0.0), axis=1, keepdims=True)
    scale = (scales.astype(F32) + 1.0) / 256.0 * second
    lane = lax.broadcasted_iota(jnp.int32, (8, 128), 1)
    table = jnp.zeros((8, 128), F32)
    for code, level in enumerate(NORMAL_FLOAT_LEVELS):
        table = jnp.where(lane == code, level, table)
    table = jnp.broadcast_to(table[None], (depth // 8, 8, 128)).reshape(depth, 128)
    level = jnp.take_along_axis(table, codes, axis=1, mode="promise_in_bounds")
    level = level.reshape(depth // QBLOCK, QBLOCK, HEAD_DIM) * scale[:, None, :]
    return level.reshape(depth, HEAD_DIM).astype(BF16)


def both_weights(key_codes, value_codes, key_scales, value_scales, outer, head, block):
    half = outer.shape[0] // 2
    column = head // (KV_HEADS // half)
    count = key_codes.shape[0] // QBLOCK
    rows = slice(None)
    if count < outer.shape[1]:
        rows = pl.ds(pl.multiple_of(block * count, count), count)
    return jnp.concatenate(
        [
            weights(key_codes[...], key_scales[rows, :], outer[...], column, block),
            weights(value_codes[...], value_scales[rows, :], outer[...], half + column, block),
        ],
        axis=1,
    )


def first_kernel(
    owners, x, key_codes, value_codes, key_scales, value_scales, outer, gain,
    key_out, value_out, scaled, total,
):
    block = pl.program_id(0)
    groups, tokens, depth = x.shape
    owner = owners[0]
    both = both_weights(
        key_codes, value_codes, key_scales, value_scales, outer, owner % KV_HEADS, block
    )
    for group in range(groups):
        scaled[group] = (x[group].astype(F32) * gain[...]).astype(BF16)
    product = jnp.dot(scaled[owner // KV_HEADS], both, preferred_element_type=F32)

    @pl.when(block == 0)
    def _():
        total[...] = product

    @pl.when(block != 0)
    def _():
        total[...] += product

    @pl.when(block == pl.num_programs(0) - 1)
    def _():
        key_out[...] = total[:, :HEAD_DIM].astype(BF16)
        value_out[...] = total[:, HEAD_DIM:].astype(BF16)


def project_first(owners, x, codes, scales, outer, gain):
    groups, tokens, features = x.shape
    depth = min(512, features)
    whole = lambda k, o: (0, 0)
    x, codes, scales, outer, gain = in_hbm(x, codes, scales, outer, gain.reshape(1, features))
    half_out = jax.ShapeDtypeStruct((tokens, HEAD_DIM), BF16)
    return pl.pallas_call(
        first_kernel,
        grid_spec=pltpu.PrefetchScalarGridSpec(
            num_scalar_prefetch=1,
            grid=(features // depth,),
            in_specs=[
                pl.BlockSpec((groups, tokens, depth), lambda k, o: (0, 0, k)),
                pl.BlockSpec((depth, HEAD_DIM), lambda k, o: (k, o[0] % KV_HEADS)),
                pl.BlockSpec((depth, HEAD_DIM), lambda k, o: (k, KV_HEADS + o[0] % KV_HEADS)),
                pl.BlockSpec((scales.shape[0], HEAD_DIM), lambda k, o: (0, o[0] % KV_HEADS)),
                pl.BlockSpec(
                    (scales.shape[0], HEAD_DIM), lambda k, o: (0, KV_HEADS + o[0] % KV_HEADS)
                ),
                pl.BlockSpec(outer.shape, whole),
                pl.BlockSpec((1, depth), lambda k, o: (0, k)),
            ],
            out_specs=[
                pl.BlockSpec((tokens, HEAD_DIM), whole),
                pl.BlockSpec((tokens, HEAD_DIM), whole),
                pl.BlockSpec((groups, tokens, depth), lambda k, o: (0, 0, k)),
            ],
            scratch_shapes=[pltpu.VMEM((tokens, 2 * HEAD_DIM), F32)],
        ),
        out_shape=[half_out, half_out, jax.ShapeDtypeStruct(x.shape, BF16)],
        compiler_params=pltpu.CompilerParams(vmem_limit_bytes=24 * 1024 * 1024),
        cost_estimate=pl.CostEstimate(
            flops=4 * tokens * features * HEAD_DIM,
            bytes_accessed=features * 2 * HEAD_DIM * 4 + 2 * x.size * 2,
            transcendentals=0,
        ),
        name="project_first",
    )(owners, x, codes, codes, scales, scales, outer, gain)


def project_kernel(
    owners, x, key_codes, value_codes, key_scales, value_scales, outer, out
):
    item, block = pl.program_id(0), pl.program_id(1)
    depth = key_codes.shape[0]
    owner = owners[item]
    both = both_weights(
        key_codes, value_codes, key_scales, value_scales, outer, owner % KV_HEADS, block
    )
    begin = pl.multiple_of(block * depth, depth)
    lines = x[owner // KV_HEADS, :, pl.ds(begin, depth)]
    product = jnp.dot(lines, both, preferred_element_type=F32)

    if x.shape[2] == depth:
        out[0, 0] = product[:, :HEAD_DIM]
        out[0, 1] = product[:, HEAD_DIM:]
    else:

        @pl.when(block == 0)
        def _():
            out[0, 0] = product[:, :HEAD_DIM]
            out[0, 1] = product[:, HEAD_DIM:]

        @pl.when(block != 0)
        def _():
            out[0, 0] += product[:, :HEAD_DIM]
            out[0, 1] += product[:, HEAD_DIM:]


def project(owners, x, codes, scales, outer):
    count = owners.shape[0]
    tokens, features = x.shape[1:]
    depth = min(1024, features)
    whole = lambda i, k, o: (0, 0)
    codes, scales, outer = in_hbm(codes, scales, outer)
    return pl.pallas_call(
        project_kernel,
        grid_spec=pltpu.PrefetchScalarGridSpec(
            num_scalar_prefetch=1,
            grid=(count, features // depth),
            in_specs=[
                pl.BlockSpec(memory_space=pltpu.VMEM),
                pl.BlockSpec((depth, HEAD_DIM), lambda i, k, o: (k, o[i] % KV_HEADS)),
                pl.BlockSpec((depth, HEAD_DIM), lambda i, k, o: (k, KV_HEADS + o[i] % KV_HEADS)),
                pl.BlockSpec((scales.shape[0], HEAD_DIM), lambda i, k, o: (0, o[i] % KV_HEADS)),
                pl.BlockSpec(
                    (scales.shape[0], HEAD_DIM), lambda i, k, o: (0, KV_HEADS + o[i] % KV_HEADS)
                ),
                pl.BlockSpec(outer.shape, whole),
            ],
            out_specs=pl.BlockSpec((1, 2, tokens, HEAD_DIM), lambda i, k, o: (i, 0, 0, 0)),
        ),
        out_shape=jax.ShapeDtypeStruct((count, 2, tokens, HEAD_DIM), F32),
        compiler_params=pltpu.CompilerParams(vmem_limit_bytes=24 * 1024 * 1024),
        cost_estimate=pl.CostEstimate(
            flops=count * 4 * tokens * features * HEAD_DIM,
            bytes_accessed=count * features * 2 * HEAD_DIM * 4 + x.shape[1] * features * 2,
            transcendentals=0,
        ),
        name="project",
    )(owners, x, codes, codes, scales, scales, outer)


def merge_kernel(terms, right, left, to_right, to_left):
    to_right[0] = (terms[0, 0] + right[...].astype(F32)).astype(BF16)
    to_right[1] = terms[0, 1].astype(BF16)
    to_left[0] = terms[1, 0].astype(BF16)
    to_left[1] = (terms[1, 1] + left[...].astype(F32)).astype(BF16)


def merge(terms, right, left):
    vmem = pl.BlockSpec(memory_space=pltpu.VMEM)
    shape = jax.ShapeDtypeStruct(terms.shape[1:], BF16)
    return pl.pallas_call(
        merge_kernel,
        in_specs=[vmem] * 3,
        out_specs=[vmem] * 2,
        out_shape=[shape, shape],
        compiler_params=pltpu.CompilerParams(vmem_limit_bytes=16 * 1024 * 1024),
        name="merge",
    )(terms, right, left)


def pieces_tail(logs):
    rows = lax.broadcasted_iota(jnp.int32, (ROWS, 128), 0)
    lanes = lax.broadcasted_iota(jnp.int32, (ROWS, 128), 1)
    row = jnp.sum(jnp.where(rows == lanes, logs, 0.0), axis=0, keepdims=True)
    high = row.astype(BF16).astype(F32)
    middle = (row - high).astype(BF16).astype(F32)
    low = row - high - middle
    at = lax.broadcasted_iota(jnp.int32, (TAIL, 128), 0)
    tail = jnp.where(at == 0, high, jnp.where(at == 1, middle, jnp.where(at == 2, low, 0.0)))
    return tail.astype(BF16)


def tail_pieces(tail):
    tail = tail.astype(F32)
    row = tail[0:1, :] + tail[1:2, :] + tail[2:3, :]
    rows = lax.broadcasted_iota(jnp.int32, (ROWS, 128), 0)
    lanes = lax.broadcasted_iota(jnp.int32, (ROWS, 128), 1)
    return jnp.sum(jnp.where(rows == lanes, row, 0.0), axis=1, keepdims=True)


def cache_kernel(info, q, keys, values, fresh_keys, fresh_values, out):
    scaling = HEAD_DIM ** (-0.5)
    dims = (((1,), (1,)), ((), ()))
    length = keys.shape[1]
    query = q[0]
    scores = lax.dot_general(query, keys[0], dims, preferred_element_type=F32) * scaling
    fresh = lax.dot_general(query, fresh_keys[...], dims, preferred_element_type=F32) * scaling
    place = lax.broadcasted_iota(jnp.int32, scores.shape, 1) + info[1] * length
    allowed = place < info[0]
    slot = lax.broadcasted_iota(jnp.int32, fresh.shape, 1)
    step = lax.broadcasted_iota(jnp.int32, fresh.shape, 0) // GROUP
    fresh_allowed = (slot <= step) & (slot < STEPS) & (info[1] == 0)
    highest = jnp.maximum(
        jnp.max(jnp.where(allowed, scores, NEGATIVE), axis=1, keepdims=True),
        jnp.max(jnp.where(fresh_allowed, fresh, NEGATIVE), axis=1, keepdims=True),
    )
    weights = jnp.where(allowed, jnp.exp(scores - highest), 0.0)
    fresh_weights = jnp.where(fresh_allowed, jnp.exp(fresh - highest), 0.0)
    totals = jnp.sum(weights, axis=1, keepdims=True) + jnp.sum(
        fresh_weights, axis=1, keepdims=True
    )
    sums = jnp.dot(weights.astype(BF16), values[0], preferred_element_type=F32)
    sums += jnp.dot(fresh_weights.astype(BF16), fresh_values[...], preferred_element_type=F32)
    some = totals > 0.0
    out[0, :ROWS] = jnp.where(some, sums / jnp.where(some, totals, 1.0), 0.0).astype(BF16)
    logs = jnp.where(some, highest + jnp.log(jnp.where(some, totals, 1.0)), NEGATIVE)
    out[0, ROWS:] = pieces_tail(logs)


def cache_attention(info, grouped, kv_cache, fresh):
    length = kv_cache.shape[1]
    (kv_cache,) = in_hbm(kv_cache)
    return pl.pallas_call(
        cache_kernel,
        grid_spec=pltpu.PrefetchScalarGridSpec(
            num_scalar_prefetch=1,
            grid=(KV_HEADS,),
            in_specs=[
                pl.BlockSpec((1, ROWS, HEAD_DIM), lambda h, s: (h, 0, 0)),
                pl.BlockSpec((1, length, HEAD_DIM), lambda h, s: (0, 0, h)),
                pl.BlockSpec((1, length, HEAD_DIM), lambda h, s: (0, 0, KV_HEADS + h)),
                pl.BlockSpec((fresh.shape[0], HEAD_DIM), lambda h, s: (0, h)),
                pl.BlockSpec((fresh.shape[0], HEAD_DIM), lambda h, s: (0, KV_HEADS + h)),
            ],
            out_specs=pl.BlockSpec((1, PART, HEAD_DIM), lambda h, s: (h, 0, 0)),
        ),
        out_shape=jax.ShapeDtypeStruct((KV_HEADS, PART, HEAD_DIM), BF16),
        compiler_params=pltpu.CompilerParams(vmem_limit_bytes=16 * 1024 * 1024),
        cost_estimate=pl.CostEstimate(
            flops=4 * HEADS * STEPS * length * HEAD_DIM,
            bytes_accessed=length * 2 * KV_HEADS * HEAD_DIM * 2,
            transcendentals=HEADS * STEPS * length,
        ),
        name="cache_attention",
    )(info, grouped, kv_cache, kv_cache, fresh, fresh)


def stretch_kernel(targets, own, right, left, inverse, cosine, sine, q, out):
    scaling = HEAD_DIM ** (-0.5)
    dims = (((1,), (1,)), ((), ()))
    empty = jnp.zeros((ROWS, HEAD_DIM), BF16)
    empty_tail = pieces_tail(jnp.full((ROWS, 1), NEGATIVE, F32))
    for owner in range(out.shape[0]):
        for core in range(2):
            out[owner, core, :ROWS] = empty
            out[owner, core, ROWS:] = empty_tail
    mine = own.shape[0] - 1
    for prompt in range(own.shape[2] // STRETCH):
        at = slice(prompt * STRETCH, (prompt + 1) * STRETCH)
        scale = inverse[at, :]
        keys = own[mine, 0, at] + right[0, at].astype(F32) + left[0, at].astype(F32)
        values = own[mine, 1, at] + right[1, at].astype(F32) + left[1, at].astype(F32)
        keys = (keys * scale).astype(BF16).astype(F32)
        values = (values * scale).astype(BF16)
        keys = keys * cosine[at, :] + pltpu.roll(keys, HEAD_DIM // 2, 1) * sine[at, :]
        target = targets[prompt]
        query = q[target, :ROWS]
        scores = lax.dot_general(query, keys.astype(BF16), dims, preferred_element_type=F32)
        scores = scores * scaling
        highest = jnp.max(scores, axis=1, keepdims=True)
        weights = jnp.exp(scores - highest)
        totals = jnp.sum(weights, axis=1, keepdims=True)
        sums = jnp.dot(weights.astype(BF16), values, preferred_element_type=F32)
        result = (sums / totals).astype(BF16)
        tail = pieces_tail(highest + jnp.log(totals))
        for core in range(2):
            out[target, core, :ROWS] = result
            out[target, core, ROWS:] = tail


def stretch_attention(targets, own, right, left, inverse, cosine, sine, q):
    vmem = pl.BlockSpec(memory_space=pltpu.VMEM)
    return pl.pallas_call(
        stretch_kernel,
        in_specs=[pl.BlockSpec(memory_space=pltpu.SMEM)] + [vmem] * 7,
        out_specs=vmem,
        out_shape=jax.ShapeDtypeStruct((q.shape[0], 2, PART, HEAD_DIM), BF16),
        compiler_params=pltpu.CompilerParams(vmem_limit_bytes=16 * 1024 * 1024),
        name="stretch_attention",
    )(targets, own, right, left, inverse, cosine, sine, q)


def combine_kernel(cached, handed, out):
    groups = handed.shape[0]
    for head in range(KV_HEADS):
        parts = [cached[0, head], cached[1, head]]
        for group in range(groups):
            parts += [handed[group, head, 0], handed[group, head, 1]]
        logs = [tail_pieces(part[ROWS:]) for part in parts]
        highest = functools.reduce(jnp.maximum, logs)
        shares = [jnp.exp(log - highest) for log in logs]
        total = functools.reduce(jnp.add, shares)
        sums = functools.reduce(
            jnp.add, [share * part[:ROWS].astype(F32) for share, part in zip(shares, parts)]
        )
        result = (sums / total).astype(BF16)
        for step in range(STEPS):
            out[step, head * GROUP : (head + 1) * GROUP] = result[
                step * GROUP : (step + 1) * GROUP
            ]


def combine(cached, handed):
    vmem = pl.BlockSpec(memory_space=pltpu.VMEM)
    return pl.pallas_call(
        combine_kernel,
        in_specs=[vmem] * 2,
        out_specs=vmem,
        out_shape=jax.ShapeDtypeStruct((STEPS, HEADS, HEAD_DIM), BF16),
        compiler_params=pltpu.CompilerParams(vmem_limit_bytes=16 * 1024 * 1024),
        name="combine",
    )(cached, handed)


def split_pieces(value):
    high = lax.reduce_precision(value, 8, 7)
    middle = lax.reduce_precision(value - high, 8, 7)
    low = lax.reduce_precision(value - high - middle, 8, 7)
    return jnp.stack([high, middle, low], axis=1).astype(BF16)


def per_device(
    stretch,
    norm_gain,
    kv_codes,
    scale_codes,
    outer_scales,
    prompt_lengths,
    target_rows,
    cache_lengths,
    kv_cache,
    queries,
    new_kv,
):
    count = lax.axis_size("tp")
    here = lax.axis_index("tp")
    rep_here = lax.axis_index("rep")
    per_rep = stretch.shape[1]
    features = stretch.shape[2]
    groups = count // KV_HEADS
    per_group = per_rep // groups
    tokens = per_group * STRETCH
    group_here = here // KV_HEADS
    place = jnp.where(here % 2 == 0, here // 2, count - 1 - here // 2)

    x = stretch.transpose(1, 0, 2).reshape(groups, tokens, features)
    outer = outer_scales.T

    def owners_at(distances):
        places = (place + jnp.array(distances, jnp.int32)) % count
        return ring_device(places, count).astype(jnp.int32)

    ring = [ring_device(at, count) for at in range(count)]
    to_right = [(ring[at], ring[(at + 1) % count]) for at in range(count)]
    to_left = [(ring[at], ring[at - 1]) for at in range(count)]

    grouped = queries.reshape(STEPS, KV_HEADS, GROUP, HEAD_DIM).transpose(1, 0, 2, 3)
    grouped = grouped.reshape(KV_HEADS, ROWS, HEAD_DIM)
    squares = jnp.sum(jnp.square(x.astype(F32)), axis=2)
    width = -(-tokens // 128) * 128
    squares = split_pieces(jnp.pad(squares, ((0, 0), (0, width - tokens))))
    squares = squares.reshape(groups, 3 * width // 128, 128)
    squares = jnp.pad(squares, ((0, 0), (0, TAIL - squares.shape[1]), (0, 0)))
    outgoing = jnp.concatenate(
        [
            jnp.broadcast_to(grouped[None], (groups, KV_HEADS, ROWS, HEAD_DIM)),
            jnp.broadcast_to(squares[:, None], (groups, KV_HEADS, TAIL, HEAD_DIM)),
        ],
        axis=2,
    ).reshape(count, PART, HEAD_DIM)
    first = rep_here * per_rep + group_here * per_group
    targets = lax.dynamic_slice_in_dim(target_rows, first, per_group)
    lengths = lax.dynamic_slice_in_dim(prompt_lengths, first, per_group)
    half_dim = HEAD_DIM // 2
    frequency = ROTARY_BASE ** (-jnp.arange(half_dim, dtype=F32) / half_dim)
    positions = (lengths[:, None] - STRETCH + jnp.arange(STRETCH, dtype=jnp.int32)[None, :])
    angles = positions.astype(F32).reshape(tokens, 1) * frequency
    cosine, sine = jnp.cos(angles), jnp.sin(angles)
    cosine = jnp.concatenate([cosine, cosine], axis=1)
    sine = jnp.concatenate([-sine, sine], axis=1)

    matches = target_rows == here
    span = jnp.where(
        jnp.any(matches),
        jnp.sum(jnp.where(matches, prompt_lengths - STRETCH, 0)),
        cache_lengths[0],
    )
    info = jnp.stack([span, rep_here]).astype(jnp.int32)
    fresh = jnp.pad(new_kv[0], ((0, 16 - STEPS), (0, 0)))
    half = count // 2
    far_keys, far_values, x_scaled = project_first(
        owners_at([half]), x, kv_codes, scale_codes, outer, norm_gain
    )
    right_in = lax.ppermute(far_keys, "tp", to_right)
    left_in = lax.ppermute(far_values, "tp", to_left)

    distances = list(range(half - 1, 0, -1))
    size = max(1, -(-len(distances) // 3))
    for begin in range(0, len(distances), size):
        here_distances = distances[begin : begin + size]
        wanted = [sign * d for d in here_distances for sign in (1, -1)]
        if begin + size >= len(distances):
            wanted = wanted + [0]
        owners = owners_at(wanted)
        if begin > 0:
            owners, right, left = lax.optimization_barrier((owners, right, left))
        terms = project(owners, x_scaled, kv_codes, scale_codes, outer)
        for at, distance in enumerate(here_distances):
            if distance == half - 1:
                right, left = merge(terms, right_in, left_in)
            else:
                right = (terms[2 * at] + right_in.astype(F32)).astype(BF16)
                left = (terms[2 * at + 1] + left_in.astype(F32)).astype(BF16)
            if distance == half - 1:
                outgoing, right, left = lax.optimization_barrier((outgoing, right, left))
                incoming = lax.all_to_all(
                    outgoing, "tp", split_axis=0, concat_axis=0, tiled=True
                )
            if distance == 1:
                info, right, left = lax.optimization_barrier((info, right, left))
            right_in = lax.ppermute(right, "tp", to_right)
            left_in = lax.ppermute(left, "tp", to_left)

    cached = lax.all_gather(cache_attention(info, grouped, kv_cache, fresh), "rep")
    squares = jnp.sum(incoming[:, ROWS : ROWS + 3 * width // 128].astype(F32), axis=0)
    squares = jnp.sum(squares.reshape(3, width), axis=0)[:tokens]
    inverse = lax.rsqrt(squares / D + EPSILON)[:, None]
    inverse, cached = lax.optimization_barrier((inverse, cached))

    handed = stretch_attention(targets, terms, right_in, left_in, inverse, cosine, sine, incoming)
    handed = handed.reshape(2 * count, PART, HEAD_DIM)
    handed = lax.all_to_all(handed, ("tp", "rep"), split_axis=0, concat_axis=0, tiled=True)
    handed = handed.reshape(groups, KV_HEADS, 2, PART, HEAD_DIM)
    return combine(cached, handed).reshape(1, STEPS, HEADS * HEAD_DIM)


def solution(mesh):
    in_specs = (
        P(None, ("grp", "rep"), "tp"),
        P("tp"),
        P("tp", None),
        P("tp", None),
        P("tp", None),
        P("grp"),
        P("grp"),
        P(("grp", "tp")),
        P(("grp", "tp"), "rep", None),
        P(("grp", "tp"), None, None),
        P(("grp", "tp"), None, None),
    )
    out_specs = P(("grp", "tp"), None, None)
    return jax.shard_map(
        per_device, mesh=mesh, in_specs=in_specs, out_specs=out_specs, check_vma=False
    )
```

```python
import functools
import math

import jax
import jax.numpy as jnp
import numpy as np
from jax import lax
from jax.experimental import pallas as pl
from jax.experimental.pallas import tpu as pltpu
from jax.sharding import PartitionSpec as P

D = 16384
HEADS = 128
KV_HEADS = 8
HEAD_DIM = 128
STRETCH = 192
STEPS = 2
QBLOCK = 64
GROUP = HEADS // KV_HEADS
ROWS = GROUP * STEPS
TAIL = 16
PART = ROWS + TAIL
NORMAL_FLOAT_LEVELS = [
    -1.0,
    -0.6961928009986877,
    -0.5250730514526367,
    -0.39491748809814453,
    -0.28444138169288635,
    -0.18477343022823334,
    -0.09105003625154495,
    0.0,
    0.07958029955625534,
    0.16093020141124725,
    0.24611230194568634,
    0.33791524171829224,
    0.44070982933044434,
    0.5626170039176941,
    0.7229568362236023,
    1.0,
]
ROTARY_BASE = 500000.0
EPSILON = 1e-05
NEGATIVE = -1e30
BF16 = jnp.bfloat16
F32 = jnp.float32
MIB = 1024 * 1024
VMEM = pl.BlockSpec(memory_space=pltpu.VMEM)
SMEM = pl.BlockSpec(memory_space=pltpu.SMEM)


def in_hbm(*arrays):
    return [pltpu.with_memory_space_constraint(array, pltpu.HBM) for array in arrays]


def ring_device(place, count):
    half = count // 2
    if isinstance(place, int):
        return 2 * place if place < half else 2 * (count - 1 - place) + 1
    return jnp.where(place < half, 2 * place, 2 * (count - 1 - place) + 1)


def owner_at(distance):
    count = lax.axis_size("tp")
    here = lax.axis_index("tp")
    place = jnp.where(here % 2 == 0, here // 2, count - 1 - here // 2)
    return ring_device((place + distance + count) % count, count)


def gathered_levels(codes):
    lane = lax.broadcasted_iota(jnp.int32, (8, 128), 1)
    table = jnp.zeros((8, 128), F32)
    for code, level in enumerate(NORMAL_FLOAT_LEVELS):
        table = jnp.where(lane == code, level, table)
    depth = codes.shape[0]
    table = jnp.broadcast_to(table[None], (depth // 8, 8, 128)).reshape(depth, 128)
    return jnp.take_along_axis(table, codes, axis=1, mode="promise_in_bounds")


def selected_levels(codes):
    values = [jnp.float32(level) for level in NORMAL_FLOAT_LEVELS]
    for bit in (1, 2, 4, 8):
        mask = (codes & bit) != 0 if bit < 8 else codes >= 8
        values = [
            jnp.where(mask, values[at + 1], values[at]) for at in range(0, len(values), 2)
        ]
    return values[0]


def weights(levels, scales, outer, column, block):
    depth = levels.shape[0]
    count = depth // QBLOCK
    line = lax.broadcasted_iota(jnp.int32, outer.shape, 0)
    line = jnp.sum(jnp.where(line == column, outer, 0.0), axis=0, keepdims=True)
    rows = lax.broadcasted_iota(jnp.int32, (count, outer.shape[1]), 0) + block * count
    lanes = lax.broadcasted_iota(jnp.int32, (count, outer.shape[1]), 1)
    second = jnp.sum(jnp.where(rows == lanes, line, 0.0), axis=1, keepdims=True)
    scale = (scales.astype(F32) + 1.0) / 256.0 * second
    levels = levels.reshape(count, QBLOCK, HEAD_DIM) * scale[:, None, :]
    return levels.reshape(depth, HEAD_DIM).astype(BF16)


def both_weights(key_codes, value_codes, key_scales, value_scales, outer, head, block):
    half = outer.shape[0] // 2
    column = head // (KV_HEADS // half)
    count = key_codes.shape[0] // QBLOCK
    rows = slice(None)
    if count < outer.shape[1]:
        rows = pl.ds(pl.multiple_of(block * count, count), count)
    keys = gathered_levels(key_codes[...])
    values = selected_levels(value_codes[...])
    return jnp.concatenate(
        [
            weights(keys, key_scales[rows, :], outer[...], column, block),
            weights(values, value_scales[rows, :], outer[...], half + column, block),
        ],
        axis=1,
    )


def first_kernel(
    x, key_codes, value_codes, key_scales, value_scales, outer, gain,
    key_out, value_out, scaled, total,
):
    block = pl.program_id(0)
    owner = owner_at(lax.axis_size("tp") // 2)
    both = both_weights(
        key_codes, value_codes, key_scales, value_scales, outer, owner % KV_HEADS, block
    )
    for group in range(x.shape[0]):
        scaled[group] = (x[group].astype(F32) * gain[...]).astype(BF16)
    product = jnp.dot(scaled[owner // KV_HEADS], both, preferred_element_type=F32)

    @pl.when(block == 0)
    def _():
        total[...] = product

    @pl.when(block != 0)
    def _():
        total[...] += product

    @pl.when(block == pl.num_programs(0) - 1)
    def _():
        key_out[...] = total[:, :HEAD_DIM].astype(BF16)
        value_out[...] = total[:, HEAD_DIM:].astype(BF16)


def project_first(x, codes, scales, outer, gain):
    groups, tokens, features = x.shape
    depth = min(512, features)
    head = lambda: owner_at(lax.axis_size("tp") // 2) % KV_HEADS
    whole = lambda k: (0, 0)
    scale_block = (scales.shape[0], HEAD_DIM)
    x, codes, scales, outer, gain = in_hbm(x, codes, scales, outer, gain.reshape(1, features))
    half_out = jax.ShapeDtypeStruct((tokens, HEAD_DIM), BF16)
    return pl.pallas_call(
        first_kernel,
        grid=(features // depth,),
        in_specs=[
            pl.BlockSpec((groups, tokens, depth), lambda k: (0, 0, k)),
            pl.BlockSpec((depth, HEAD_DIM), lambda k: (k, head())),
            pl.BlockSpec((depth, HEAD_DIM), lambda k: (k, KV_HEADS + head())),
            pl.BlockSpec(scale_block, lambda k: (0, head())),
            pl.BlockSpec(scale_block, lambda k: (0, KV_HEADS + head())),
            pl.BlockSpec(outer.shape, whole),
            pl.BlockSpec((1, depth), lambda k: (0, k)),
        ],
        out_specs=[
            pl.BlockSpec((tokens, HEAD_DIM), whole),
            pl.BlockSpec((tokens, HEAD_DIM), whole),
            pl.BlockSpec((groups, tokens, depth), lambda k: (0, 0, k)),
        ],
        scratch_shapes=[pltpu.VMEM((tokens, 2 * HEAD_DIM), F32)],
        out_shape=[half_out, half_out, jax.ShapeDtypeStruct(x.shape, BF16)],
        compiler_params=pltpu.CompilerParams(vmem_limit_bytes=24 * MIB),
        cost_estimate=pl.CostEstimate(
            flops=4 * tokens * features * HEAD_DIM,
            bytes_accessed=features * 2 * HEAD_DIM * 4 + 2 * x.size * 2,
            transcendentals=0,
        ),
        name="project_first",
    )(x, codes, codes, scales, scales, outer, gain)


def distance_at(farthest, item):
    return (farthest - item // 2) * (1 - 2 * (item % 2))


def project_kernel(
    farthest, x, key_codes, value_codes, key_scales, value_scales, outer, out
):
    item, block = pl.program_id(0), pl.program_id(1)
    depth = key_codes.shape[0]
    owner = owner_at(distance_at(farthest, item))
    both = both_weights(
        key_codes, value_codes, key_scales, value_scales, outer, owner % KV_HEADS, block
    )
    begin = pl.multiple_of(block * depth, depth)
    lines = x[owner // KV_HEADS, :, pl.ds(begin, depth)]
    product = jnp.dot(lines, both, preferred_element_type=F32)

    @pl.when(block == 0)
    def _():
        out[item, 0] = product[:, :HEAD_DIM]
        out[item, 1] = product[:, HEAD_DIM:]

    @pl.when(block != 0)
    def _():
        out[item, 0] += product[:, :HEAD_DIM]
        out[item, 1] += product[:, HEAD_DIM:]


def project(farthest, count, x, codes, scales, outer):
    tokens, features = x.shape[1:]
    depth = min(1024, features)
    head = lambda i: owner_at(distance_at(farthest, i)) % KV_HEADS
    scale_block = (scales.shape[0], HEAD_DIM)
    codes, scales, outer = in_hbm(codes, scales, outer)
    return pl.pallas_call(
        functools.partial(project_kernel, farthest),
        grid=(count, features // depth),
        in_specs=[
            VMEM,
            pl.BlockSpec((depth, HEAD_DIM), lambda i, k: (k, head(i))),
            pl.BlockSpec((depth, HEAD_DIM), lambda i, k: (k, KV_HEADS + head(i))),
            pl.BlockSpec(scale_block, lambda i, k: (0, head(i))),
            pl.BlockSpec(scale_block, lambda i, k: (0, KV_HEADS + head(i))),
            pl.BlockSpec(outer.shape, lambda i, k: (0, 0)),
        ],
        out_specs=VMEM,
        out_shape=jax.ShapeDtypeStruct((count, 2, tokens, HEAD_DIM), F32),
        compiler_params=pltpu.CompilerParams(vmem_limit_bytes=40 * MIB),
        cost_estimate=pl.CostEstimate(
            flops=count * 4 * tokens * features * HEAD_DIM,
            bytes_accessed=count * features * 2 * HEAD_DIM * 4 + x.shape[1] * features * 2,
            transcendentals=0,
        ),
        name="project",
    )(x, codes, codes, scales, scales, outer)


def send_kernel(item, halves, terms, right, left, to_right, to_left):
    if halves:
        to_right[0] = (terms[item, 0] + right[...].astype(F32)).astype(BF16)
        to_right[1] = terms[item, 1].astype(BF16)
        to_left[0] = terms[item + 1, 0].astype(BF16)
        to_left[1] = (terms[item + 1, 1] + left[...].astype(F32)).astype(BF16)
    else:
        to_right[...] = (terms[item] + right[...].astype(F32)).astype(BF16)
        to_left[...] = (terms[item + 1] + left[...].astype(F32)).astype(BF16)


def sends(item, halves, terms, right, left):
    shape = jax.ShapeDtypeStruct(terms.shape[1:], BF16)
    return pl.pallas_call(
        functools.partial(send_kernel, item, halves),
        in_specs=[VMEM] * 3,
        out_specs=[VMEM] * 2,
        out_shape=[shape, shape],
        compiler_params=pltpu.CompilerParams(vmem_limit_bytes=16 * MIB),
        name="sends",
    )(terms, right, left)


def direct(count):
    return count <= 8


def part_shapes(count, copies):
    if direct(count):
        return [jax.ShapeDtypeStruct((PART, HEAD_DIM), BF16)] * count
    return [jax.ShapeDtypeStruct((count, copies, PART, HEAD_DIM), BF16)]


def exchange(parts):
    count = lax.axis_size("tp")
    if not direct(count):
        swapped = lax.all_to_all(parts[0], "tp", split_axis=0, concat_axis=0, tiled=True)
        return [swapped]
    turn = lambda by: [(at, (at + by) % count) for at in range(count)]
    return [parts[0]] + [lax.ppermute(parts[by], "tp", turn(by)) for by in range(1, count)]


def exchange_to_both(parts):
    count = lax.axis_size("tp")
    if not direct(count):
        flat = parts[0].reshape(2 * count, PART, HEAD_DIM)
        flat = lax.all_to_all(flat, ("tp", "rep"), split_axis=0, concat_axis=0, tiled=True)
        return [flat.reshape(count, 2, PART, HEAD_DIM)]
    cross = lambda by: [
        (2 * at + rep, 2 * ((at + by) % count) + 1 - rep) for at in range(count) for rep in range(2)
    ]
    other = [lax.ppermute(parts[by], ("tp", "rep"), cross(by)) for by in range(count)]
    return exchange(parts) + other


def pack_kernel(queries, squares, grouped, *outs):
    count = lax.axis_size("tp")
    here = lax.axis_index("tp")
    per_group = squares.shape[0] // (count // KV_HEADS)
    for head in range(KV_HEADS):
        for member in range(GROUP):
            lanes = slice((head * GROUP + member) * HEAD_DIM, (head * GROUP + member + 1) * HEAD_DIM)
            grouped[head, member * STEPS : (member + 1) * STEPS] = queries[0, :, lanes]
    at = lax.broadcasted_iota(jnp.int32, (TAIL, 128), 0)
    tails = []
    for group in range(count // KV_HEADS):
        tail = jnp.zeros((TAIL, 128), F32)
        for prompt in range(per_group):
            line = squares[group * per_group + prompt : group * per_group + prompt + 1, :]
            ends = jnp.concatenate(
                [line[:, 128:], jnp.zeros((1, 256 - STRETCH), F32)], axis=1
            )
            for half, piece in enumerate((line[:, :128], ends)):
                high = piece.astype(BF16).astype(F32)
                tail = jnp.where(at == 2 * prompt + half, high, tail)
                tail = jnp.where(at == TAIL // 2 + 2 * prompt + half, piece - high, tail)
        tails.append(tail.astype(BF16))
    if direct(count):
        for by in range(count):
            outs[by][:ROWS] = grouped[(here + by) % KV_HEADS]
            outs[by][ROWS:] = tails[0]
    else:
        for owner in range(count):
            outs[0][owner, 0, :ROWS] = grouped[owner % KV_HEADS]
            outs[0][owner, 0, ROWS:] = tails[owner // KV_HEADS]


def pack(queries, squares, count):
    return pl.pallas_call(
        pack_kernel,
        in_specs=[VMEM] * 2,
        out_specs=[VMEM] * (1 + len(part_shapes(count, 1))),
        out_shape=[jax.ShapeDtypeStruct((KV_HEADS, ROWS, HEAD_DIM), BF16)] + part_shapes(count, 1),
        compiler_params=pltpu.CompilerParams(vmem_limit_bytes=16 * MIB),
        name="pack",
    )(queries, squares)


def turned(column):
    rows = lax.broadcasted_iota(jnp.int32, (column.shape[0], 128), 0)
    lanes = lax.broadcasted_iota(jnp.int32, (column.shape[0], 128), 1)
    return jnp.sum(jnp.where(rows == lanes, column, 0.0), axis=0, keepdims=True)


def stood(row, count):
    rows = lax.broadcasted_iota(jnp.int32, (count, 128), 0)
    lanes = lax.broadcasted_iota(jnp.int32, (count, 128), 1)
    return jnp.sum(jnp.where(rows == lanes, row, 0.0), axis=1, keepdims=True)


def pieces_tail(logs):
    row = turned(logs)
    high = row.astype(BF16).astype(F32)
    middle = (row - high).astype(BF16).astype(F32)
    low = row - high - middle
    at = lax.broadcasted_iota(jnp.int32, (TAIL, 128), 0)
    tail = jnp.where(at == 0, high, jnp.where(at == 1, middle, jnp.where(at == 2, low, 0.0)))
    return tail.astype(BF16)


def tail_pieces(tail):
    tail = tail.astype(F32)
    return stood(tail[0:1, :] + tail[1:2, :] + tail[2:3, :], ROWS)


CACHE_HEADS = 4


def cache_kernel(targets, lengths, stored, q, keys, values, fresh_keys, fresh_values, out):
    scaling = HEAD_DIM ** (-0.5)
    dims = (((1,), (1,)), ((), ()))
    here = lax.axis_index("tp")
    rep = lax.axis_index("rep")
    length = keys.shape[1]
    span = stored[0]
    for prompt in range(targets.shape[0]):
        span = jnp.where(targets[prompt] == here, lengths[prompt] - STRETCH, span)
    place = lax.broadcasted_iota(jnp.int32, (ROWS, length), 1)
    allowed = place < span - rep * length
    second_step = lax.broadcasted_iota(jnp.int32, (ROWS, 1), 0) % STEPS == 1
    for at in range(CACHE_HEADS):
        lanes = slice(at * HEAD_DIM, (at + 1) * HEAD_DIM)
        query = q[at]
        wide = query.astype(F32)
        scores = lax.dot_general(query, keys[0, :, lanes], dims, preferred_element_type=F32)
        scores = jnp.where(allowed, scores * scaling, NEGATIVE)
        highest = jnp.max(scores, axis=1, keepdims=True)
        fresh = []
        for step in range(STEPS):
            key = fresh_keys[0, step : step + 1, lanes].astype(F32)
            score = jnp.sum(wide * key, axis=1, keepdims=True) * scaling
            shown = rep == 0 if step == 0 else second_step & (rep == 0)
            score = jnp.where(shown, score, NEGATIVE)
            highest = jnp.maximum(highest, score)
            fresh.append(score)
        some = highest > 0.5 * NEGATIVE
        highest = jnp.where(some, highest, 0.0)
        weight = jnp.exp(scores - highest)
        totals = jnp.sum(weight, axis=1, keepdims=True)
        sums = jnp.dot(weight.astype(BF16), values[0, :, lanes], preferred_element_type=F32)
        for step in range(STEPS):
            share = jnp.exp(fresh[step] - highest)
            totals += share
            value = fresh_values[0, step : step + 1, lanes].astype(F32)
            sums += share.astype(BF16).astype(F32) * value
        totals = jnp.where(some, totals, 1.0)
        out[at, :ROWS] = (sums / totals).astype(BF16)
        out[at, ROWS:] = pieces_tail(jnp.where(some, highest + jnp.log(totals), NEGATIVE))


def cache_attention(targets, lengths, stored, grouped, kv_cache, new_kv):
    length = kv_cache.shape[1]
    (kv_cache,) = in_hbm(kv_cache)
    width = CACHE_HEADS * HEAD_DIM
    blocks = KV_HEADS // CACHE_HEADS
    return pl.pallas_call(
        cache_kernel,
        grid=(blocks,),
        in_specs=[
            SMEM,
            SMEM,
            SMEM,
            pl.BlockSpec((CACHE_HEADS, ROWS, HEAD_DIM), lambda h: (h, 0, 0)),
            pl.BlockSpec((1, length, width), lambda h: (0, 0, h)),
            pl.BlockSpec((1, length, width), lambda h: (0, 0, blocks + h)),
            pl.BlockSpec((1, STEPS, width), lambda h: (0, 0, h)),
            pl.BlockSpec((1, STEPS, width), lambda h: (0, 0, blocks + h)),
        ],
        out_specs=pl.BlockSpec((CACHE_HEADS, PART, HEAD_DIM), lambda h: (h, 0, 0)),
        out_shape=jax.ShapeDtypeStruct((KV_HEADS, PART, HEAD_DIM), BF16),
        compiler_params=pltpu.CompilerParams(vmem_limit_bytes=24 * MIB),
        cost_estimate=pl.CostEstimate(
            flops=4 * HEADS * STEPS * length * HEAD_DIM,
            bytes_accessed=length * 2 * KV_HEADS * HEAD_DIM * 2,
            transcendentals=HEADS * STEPS * length,
        ),
        name="cache_attention",
    )(targets, lengths, stored, grouped, kv_cache, kv_cache, new_kv, new_kv)


def stretch_kernel(
    target_rows, starts, turns, own, right, left, *refs
):
    count = lax.axis_size("tp")
    here = lax.axis_index("tp")
    received = refs[: len(part_shapes(count, 1))]
    outs = refs[len(received) : -1]
    rows = refs[-1]
    groups = count // KV_HEADS
    per_group = own.shape[2] // STRETCH
    first = (lax.axis_index("rep") * groups + here // KV_HEADS) * per_group
    scaling = HEAD_DIM ** (-0.5)
    dims = (((1,), (1,)), ((), ()))
    mine = own.shape[0] - 1

    squares = jnp.zeros((TAIL, 128), F32)
    for by in range(count):
        if direct(count):
            rows[(here - by + count) % count] = received[by][:ROWS]
            squares += received[by][ROWS:].astype(F32)
        else:
            rows[by] = received[0][by, 0, :ROWS]
            squares += received[0][by, 0, ROWS:].astype(F32)
    inverse = lax.rsqrt((squares[: TAIL // 2] + squares[TAIL // 2 :]) / D + EPSILON)

    results = []
    for prompt in range(per_group):
        at = slice(prompt * STRETCH, (prompt + 1) * STRETCH)
        scale = jnp.concatenate(
            [
                stood(inverse[2 * prompt : 2 * prompt + 1], 128),
                stood(inverse[2 * prompt + 1 : 2 * prompt + 2], STRETCH - 128),
            ],
            axis=0,
        )
        keys = own[mine, 0, at] + right[0, at].astype(F32) + left[0, at].astype(F32)
        values = own[mine, 1, at] + right[1, at].astype(F32) + left[1, at].astype(F32)
        keys = (keys * scale).astype(BF16).astype(F32)
        values = (values * scale).astype(BF16)
        start_cosine = starts[0, pl.ds(first + prompt, 1), :]
        start_sine = starts[1, pl.ds(first + prompt, 1), :]
        cosine = turns[0] * start_cosine - turns[1] * start_sine
        sine = turns[1] * start_cosine + turns[0] * start_sine
        lane = lax.broadcasted_iota(jnp.int32, sine.shape, 1)
        sine = jnp.where(lane < HEAD_DIM // 2, -sine, sine)
        keys = keys * cosine + pltpu.roll(keys, HEAD_DIM // 2, 1) * sine
        target = target_rows[first + prompt]
        scores = lax.dot_general(rows[target], keys.astype(BF16), dims, preferred_element_type=F32)
        scores = scores * scaling
        highest = jnp.max(scores, axis=1, keepdims=True)
        weight = jnp.exp(scores - highest)
        totals = jnp.sum(weight, axis=1, keepdims=True)
        sums = jnp.dot(weight.astype(BF16), values, preferred_element_type=F32)
        tail = pieces_tail(highest + jnp.log(totals))
        results.append((target, sums / totals, tail))

    empty_tail = pieces_tail(jnp.full((ROWS, 1), NEGATIVE, F32))
    for by in range(count):
        owner = (here + by) % count if direct(count) else by
        part = jnp.zeros((ROWS, HEAD_DIM), F32)
        tail = empty_tail.astype(F32)
        for target, result, result_tail in results:
            part = jnp.where(target == owner, result, part)
            tail = jnp.where(target == owner, result_tail.astype(F32), tail)
        if direct(count):
            outs[by][:ROWS] = part.astype(BF16)
            outs[by][ROWS:] = tail.astype(BF16)
        else:
            for core in range(2):
                outs[0][by, core, :ROWS] = part.astype(BF16)
                outs[0][by, core, ROWS:] = tail.astype(BF16)


def stretch_attention(target_rows, starts, turns, own, right, left, received):
    count = lax.axis_size("tp")
    shapes = part_shapes(count, 2)
    return pl.pallas_call(
        stretch_kernel,
        in_specs=[SMEM] + [VMEM] * (5 + len(received)),
        out_specs=[VMEM] * len(shapes),
        out_shape=shapes,
        scratch_shapes=[pltpu.VMEM((count, ROWS, HEAD_DIM), BF16)],
        compiler_params=pltpu.CompilerParams(vmem_limit_bytes=16 * MIB),
        name="stretch_attention",
    )(target_rows, starts, turns, own, right, left, *received)


def combine_kernel(cached, *refs):
    count = lax.axis_size("tp")
    here = lax.axis_index("tp")
    out = refs[-1]
    for at in range(KV_HEADS):
        if direct(count):
            head = (here - at + count) % count
            handed = [refs[at][...], refs[count + at][...]]
        else:
            head = at
            handed = [
                refs[0][owner, core] for owner in range(at, count, KV_HEADS) for core in range(2)
            ]
        parts = [cached[0, head], cached[1, head]] + handed
        logs = [tail_pieces(part[ROWS:]) for part in parts]
        highest = functools.reduce(jnp.maximum, logs)
        shares = [jnp.exp(log - highest) for log in logs]
        total = functools.reduce(jnp.add, shares)
        sums = functools.reduce(
            jnp.add, [share * part[:ROWS].astype(F32) for share, part in zip(shares, parts)]
        )
        result = (sums / total).astype(BF16)
        for member in range(GROUP):
            begin = pl.multiple_of((head * GROUP + member) * HEAD_DIM, HEAD_DIM)
            out[:, pl.ds(begin, HEAD_DIM)] = result[member * STEPS : (member + 1) * STEPS]


def combine(cached, handed):
    return pl.pallas_call(
        combine_kernel,
        in_specs=[VMEM] * (1 + len(handed)),
        out_specs=VMEM,
        out_shape=jax.ShapeDtypeStruct((STEPS, HEADS * HEAD_DIM), BF16),
        compiler_params=pltpu.CompilerParams(vmem_limit_bytes=16 * MIB),
        name="combine",
    )(cached, *handed)


def rotary_turns():
    half = np.arange(HEAD_DIM // 2, dtype=np.float64) / (HEAD_DIM // 2)
    frequency = ROTARY_BASE ** (-np.concatenate([half, half]))
    angles = np.arange(STRETCH, dtype=np.float64)[:, None] * frequency
    return frequency.astype(np.float32), np.stack([np.cos(angles), np.sin(angles)]).astype(np.float32)


def per_device(
    stretch,
    norm_gain,
    kv_codes,
    scale_codes,
    outer_scales,
    prompt_lengths,
    target_rows,
    cache_lengths,
    kv_cache,
    queries,
    new_kv,
):
    count = lax.axis_size("tp")
    per_rep, features = stretch.shape[1:]
    groups = count // KV_HEADS
    lines = stretch.transpose(1, 0, 2)
    x = lines.reshape(groups, per_rep // groups * STRETCH, features)
    outer = outer_scales.T

    ring = [ring_device(at, count) for at in range(count)]
    to_right = [(ring[at], ring[(at + 1) % count]) for at in range(count)]
    to_left = [(ring[at], ring[at - 1]) for at in range(count)]

    half = count // 2
    far_keys, far_values, x_scaled = project_first(x, kv_codes, scale_codes, outer, norm_gain)
    right_in = lax.ppermute(far_keys, "tp", to_right)
    left_in = lax.ppermute(far_values, "tp", to_left)

    squares = jnp.sum(jnp.square(lines.astype(F32)), axis=2)
    grouped, *parts = pack(queries, squares, count)
    frequency, turns = rotary_turns()
    start = (prompt_lengths - STRETCH).astype(F32)[:, None] * jnp.asarray(frequency)
    starts = jnp.stack([jnp.cos(start), jnp.sin(start)])

    calls = [(half - 1, 2), (half - 2, 2 * (half - 2) + 1)]
    terms, item = None, 0
    for distance in range(half - 1, 0, -1):
        for farthest, items in calls:
            if farthest == distance:
                if distance < half - 1:
                    outer, right, left = lax.optimization_barrier((outer, right, left))
                terms = project(farthest, items, x_scaled, kv_codes, scale_codes, outer)
                item = 0
        right, left = sends(item, distance == half - 1, terms, right_in, left_in)
        item += 2
        if distance == half - 1:
            right, left, *parts = lax.optimization_barrier((right, left, *parts))
            received = exchange(parts)
        if distance == max(1, half - 2):
            right, left, grouped = lax.optimization_barrier((right, left, grouped))
        right_in = lax.ppermute(right, "tp", to_right)
        left_in = lax.ppermute(left, "tp", to_left)

    cached = cache_attention(
        target_rows, prompt_lengths, cache_lengths, grouped, kv_cache, new_kv
    )
    cached = lax.all_gather(cached, "rep")
    starts, cached = lax.optimization_barrier((starts, cached))
    handed = stretch_attention(
        target_rows, starts, jnp.asarray(turns), terms, right_in, left_in, received
    )
    out = combine(cached, exchange_to_both(handed))
    return out.reshape(1, STEPS, HEADS * HEAD_DIM)


def solution(mesh):
    in_specs = (
        P(None, ("grp", "rep"), "tp"),
        P("tp"),
        P("tp", None),
        P("tp", None),
        P("tp", None),
        P("grp"),
        P("grp"),
        P(("grp", "tp")),
        P(("grp", "tp"), "rep", None),
        P(("grp", "tp"), None, None),
        P(("grp", "tp"), None, None),
    )
    out_specs = P(("grp", "tp"), None, None)
    return jax.shard_map(
        per_device, mesh=mesh, in_specs=in_specs, out_specs=out_specs, check_vma=False
    )
```

```python
import functools
import math

import jax
import jax.numpy as jnp
import numpy as np
from jax import lax
from jax.experimental import pallas as pl
from jax.experimental.pallas import tpu as pltpu
from jax.sharding import PartitionSpec as P

D = 16384
HEADS = 128
KV_HEADS = 8
HEAD_DIM = 128
STRETCH = 192
STEPS = 2
QBLOCK = 64
GROUP = HEADS // KV_HEADS
ROWS = GROUP * STEPS
TAIL = 16
PART = ROWS + TAIL
CORE_HEADS = KV_HEADS // 2
NORMAL_FLOAT_LEVELS = [
    -1.0,
    -0.6961928009986877,
    -0.5250730514526367,
    -0.39491748809814453,
    -0.28444138169288635,
    -0.18477343022823334,
    -0.09105003625154495,
    0.0,
    0.07958029955625534,
    0.16093020141124725,
    0.24611230194568634,
    0.33791524171829224,
    0.44070982933044434,
    0.5626170039176941,
    0.7229568362236023,
    1.0,
]
ROTARY_BASE = 500000.0
EPSILON = 1e-05
NEGATIVE = -1e30
BF16 = jnp.bfloat16
F32 = jnp.float32
MIB = 1024 * 1024
VMEM = pl.BlockSpec(memory_space=pltpu.VMEM)
SMEM = pl.BlockSpec(memory_space=pltpu.SMEM)


def in_hbm(*arrays):
    return [pltpu.with_memory_space_constraint(array, pltpu.HBM) for array in arrays]


def ring_device(place, count):
    half = count // 2
    if isinstance(place, int):
        return 2 * place if place < half else 2 * (count - 1 - place) + 1
    return jnp.where(place < half, 2 * place, 2 * (count - 1 - place) + 1)


def owner_at(distance):
    count = lax.axis_size("tp")
    here = lax.axis_index("tp")
    place = jnp.where(here % 2 == 0, here // 2, count - 1 - here // 2)
    return ring_device((place + distance + count) % count, count)


def turned(column):
    rows = lax.broadcasted_iota(jnp.int32, (column.shape[0], 128), 0)
    lanes = lax.broadcasted_iota(jnp.int32, (column.shape[0], 128), 1)
    return jnp.sum(jnp.where(rows == lanes, column, 0.0), axis=0, keepdims=True)


def stood(row, count):
    rows = lax.broadcasted_iota(jnp.int32, (count, 128), 0)
    lanes = lax.broadcasted_iota(jnp.int32, (count, 128), 1)
    return jnp.sum(jnp.where(rows == lanes, row, 0.0), axis=1, keepdims=True)


def token_rows(column):
    at = lax.broadcasted_iota(jnp.int32, (8, 128), 0)
    ends = turned(column[128:])
    return jnp.where(at == 0, turned(column[:128]), jnp.where(at == 1, ends, 0.0))


def token_column(rows):
    return jnp.concatenate([stood(rows[0:1], 128), stood(rows[1:2], STRETCH - 128)], axis=0)


def two_pieces(rows):
    high = rows.astype(BF16).astype(F32)
    return jnp.concatenate([high, rows - high], axis=0).astype(BF16)


def one_piece(rows):
    rows = rows.astype(F32)
    return rows[:8] + rows[8:]


def pieces_tail(logs):
    row = turned(logs)
    high = row.astype(BF16).astype(F32)
    middle = (row - high).astype(BF16).astype(F32)
    low = row - high - middle
    at = lax.broadcasted_iota(jnp.int32, (TAIL, 128), 0)
    tail = jnp.where(at == 0, high, jnp.where(at == 1, middle, jnp.where(at == 2, low, 0.0)))
    return tail.astype(BF16)


def tail_pieces(tail):
    tail = tail.astype(F32)
    return stood(tail[0:1, :] + tail[1:2, :] + tail[2:3, :], ROWS)


def gathered_levels(table, codes):
    table = jnp.broadcast_to(table[None], (codes.shape[0] // 8, 8, 128)).reshape(codes.shape)
    return jnp.take_along_axis(table, codes, axis=1, mode="promise_in_bounds")


def selected_levels(codes):
    values = [jnp.float32(level) for level in NORMAL_FLOAT_LEVELS]
    for bit in (1, 2, 4, 8):
        mask = (codes & bit) != 0 if bit < 8 else codes >= 8
        values = [
            jnp.where(mask, values[at + 1], values[at]) for at in range(0, len(values), 2)
        ]
    return values[0]


def block_scales(scales, outer, column):
    count = scales.shape[0]
    line = lax.broadcasted_iota(jnp.int32, outer.shape, 0)
    line = jnp.sum(jnp.where(line == column, outer, 0.0), axis=0, keepdims=True)
    rows = lax.broadcasted_iota(jnp.int32, (count, count), 0)
    lanes = lax.broadcasted_iota(jnp.int32, (count, count), 1)
    second = jnp.sum(jnp.where(rows == lanes, line, 0.0), axis=1, keepdims=True)
    return (scales.astype(F32) + 1.0) / 256.0 * second


def scaled_block(x, gain, begin, out, squares):
    width = x.shape[2]
    for prompt in range(x.shape[0]):
        wide = x[prompt].astype(F32)
        out[prompt, :, pl.ds(begin, width)] = (wide * gain[...]).astype(BF16)
        squares[prompt] += token_rows(jnp.sum(wide * wide, axis=1, keepdims=True))


def weights_kernel(
    x, key_codes, value_codes, key_scales, value_scales, outer, gain,
    out, scaled, squares, scales,
):
    item = pl.program_id(0)
    features = key_codes.shape[0]
    head = lax.axis_index("rep") * CORE_HEADS + item
    half = outer.shape[0] // 2
    column = head // (KV_HEADS // half)
    scales[0] = block_scales(key_scales[...], outer[...], column)
    scales[1] = block_scales(value_scales[...], outer[...], half + column)
    lane = lax.broadcasted_iota(jnp.int32, (8, 128), 1)
    table = jnp.zeros((8, 128), F32)
    for code, level in enumerate(NORMAL_FLOAT_LEVELS):
        table = jnp.where(lane == code, level, table)

    def body(block, _):
        rows = pl.ds(pl.multiple_of(block * QBLOCK, QBLOCK), QBLOCK)
        keys = gathered_levels(table, key_codes[rows, :])
        values = selected_levels(value_codes[rows, :])
        keys *= scales[0, pl.ds(block, 1), :]
        values *= scales[1, pl.ds(block, 1), :]
        out[item, rows, :HEAD_DIM] = keys.astype(BF16)
        out[item, rows, HEAD_DIM:] = values.astype(BF16)
        return 0

    lax.fori_loop(0, features // QBLOCK, body, 0, unroll=4)

    @pl.when(item == 0)
    def _():
        squares[...] = jnp.zeros(squares.shape, F32)

    @pl.when(item < features // x.shape[2])
    def _():
        scaled_block(x, gain, pl.multiple_of(item * x.shape[2], 128), scaled, squares)


def feature_width(features):
    return max(128, features // CORE_HEADS)


def feature_shapes(x):
    return [
        jax.ShapeDtypeStruct(x.shape, BF16),
        jax.ShapeDtypeStruct((x.shape[0], 8, 128), F32),
    ]


def dequantize(x, codes, scales, outer, gain):
    per_rep, _, features = x.shape
    width = feature_width(features)
    head = lambda i: lax.axis_index("rep") * CORE_HEADS + i
    block = lambda i: jnp.minimum(i, features // width - 1)
    x, codes, scales, outer, gain = in_hbm(x, codes, scales, outer, gain)
    return pl.pallas_call(
        weights_kernel,
        grid=(CORE_HEADS,),
        in_specs=[
            pl.BlockSpec((per_rep, STRETCH, width), lambda i: (0, 0, block(i))),
            pl.BlockSpec((features, HEAD_DIM), lambda i: (0, head(i))),
            pl.BlockSpec((features, HEAD_DIM), lambda i: (0, KV_HEADS + head(i))),
            pl.BlockSpec((scales.shape[0], HEAD_DIM), lambda i: (0, head(i))),
            pl.BlockSpec((scales.shape[0], HEAD_DIM), lambda i: (0, KV_HEADS + head(i))),
            pl.BlockSpec(outer.shape, lambda i: (0, 0)),
            pl.BlockSpec((1, width), lambda i: (0, block(i))),
        ],
        out_specs=[VMEM] * 3,
        out_shape=[
            jax.ShapeDtypeStruct((CORE_HEADS, features, 2 * HEAD_DIM), BF16)
        ] + feature_shapes(x),
        scratch_shapes=[pltpu.VMEM((2, scales.shape[0], HEAD_DIM), F32)],
        compiler_params=pltpu.CompilerParams(vmem_limit_bytes=32 * MIB),
        cost_estimate=pl.CostEstimate(
            flops=64 * codes.size // 2, bytes_accessed=codes.size * 2, transcendentals=0
        ),
        name="dequantize",
    )(x, codes, codes, scales, scales, outer, gain)


def scale_kernel(x, gain, scaled, squares):
    item = pl.program_id(0)

    @pl.when(item == 0)
    def _():
        squares[...] = jnp.zeros(squares.shape, F32)

    scaled_block(x, gain, pl.multiple_of(item * x.shape[2], 128), scaled, squares)


def scale_features(x, gain):
    per_rep, _, features = x.shape
    width = feature_width(features)
    return pl.pallas_call(
        scale_kernel,
        grid=(features // width,),
        in_specs=[
            pl.BlockSpec((per_rep, STRETCH, width), lambda i: (0, 0, i)),
            pl.BlockSpec((1, width), lambda i: (0, i)),
        ],
        out_specs=[VMEM] * 2,
        out_shape=feature_shapes(x),
        compiler_params=pltpu.CompilerParams(vmem_limit_bytes=24 * MIB),
        name="scale_features",
    )(x, gain)


def prompt_of(targets, owner):
    prompt = jnp.int32(-1)
    for at in range(targets.shape[0]):
        prompt = jnp.where(targets[at] == owner, at, prompt)
    return prompt


def first_kernel(targets, own, squares, other, gain, weight, *refs):
    outs, (line, total) = refs[:4], refs[4:]
    per_rep = own.shape[0]
    prompt = prompt_of(targets, owner_at(lax.axis_size("tp") // 2))
    at = lax.rem(jnp.maximum(prompt, 0), per_rep)
    is_own = prompt // per_rep == lax.axis_index("rep")

    @pl.when((prompt >= 0) & is_own)
    def _():
        line[...] = own[at]
        total[...] = squares[at]

    @pl.when((prompt >= 0) & jnp.logical_not(is_own))
    def _():
        wide = other[at].astype(F32)
        line[...] = (wide * gain[...]).astype(BF16)
        total[...] = token_rows(jnp.sum(wide * wide, axis=1, keepdims=True))

    @pl.when(prompt < 0)
    def _():
        line[...] = jnp.zeros(line.shape, BF16)
        total[...] = jnp.zeros(total.shape, F32)

    for head in range(CORE_HEADS):
        right, left = outs[2 * (head // 2)], outs[2 * (head // 2) + 1]
        rows = slice(head % 2 * STRETCH, (head % 2 + 1) * STRETCH)
        product = jnp.dot(line[...], weight[head], preferred_element_type=F32)
        right[rows] = product[:, :HEAD_DIM].astype(BF16)
        left[rows] = product[:, HEAD_DIM:].astype(BF16)
    outs[0][2 * STRETCH :] = two_pieces(total[...])


def project_first(targets, own, squares, other, gain, weight):
    rows = 2 * STRETCH
    shapes = [
        jax.ShapeDtypeStruct((size, HEAD_DIM), BF16) for size in (rows + TAIL, rows, rows, rows)
    ]
    return pl.pallas_call(
        first_kernel,
        in_specs=[SMEM] + [VMEM] * 5,
        out_specs=[VMEM] * 4,
        out_shape=shapes,
        scratch_shapes=[pltpu.VMEM(own.shape[1:], BF16), pltpu.VMEM((8, 128), F32)],
        compiler_params=pltpu.CompilerParams(vmem_limit_bytes=24 * MIB),
        cost_estimate=pl.CostEstimate(
            flops=STRETCH * weight.size * 2, bytes_accessed=weight.size, transcendentals=0
        ),
        name="project_first",
    )(targets, own, squares, other, gain, weight)


def distance_at(farthest, item):
    return (farthest - item // 2) * (1 - 2 * (item % 2))


def project_kernel(farthest, targets, own, squares, other, other_squares, weight, out):
    item = pl.program_id(0)
    per_rep = own.shape[0]
    prompt = prompt_of(targets, owner_at(distance_at(farthest, item)))
    at = lax.rem(jnp.maximum(prompt, 0), per_rep)
    is_own = prompt // per_rep == lax.axis_index("rep")

    def products(lines, sums):
        for head in range(CORE_HEADS):
            product = jnp.dot(lines[at], weight[head], preferred_element_type=F32)
            begin = head % 2 * STRETCH
            out[item, head // 2, begin : begin + STRETCH] = product[:, :HEAD_DIM]
            begin += 2 * STRETCH
            out[item, head // 2, begin : begin + STRETCH] = product[:, HEAD_DIM:]
        for half in range(2):
            out[item, half, 4 * STRETCH :] = sums[at]

    @pl.when((prompt >= 0) & is_own)
    def _():
        products(own, squares)

    @pl.when((prompt >= 0) & jnp.logical_not(is_own))
    def _():
        products(other, other_squares)

    @pl.when(prompt < 0)
    def _():
        out[item] = jnp.zeros(out.shape[1:], F32)


def project(farthest, items, targets, own, squares, other, other_squares, weight):
    return pl.pallas_call(
        functools.partial(project_kernel, farthest),
        grid=(items,),
        in_specs=[SMEM] + [VMEM] * 5,
        out_specs=VMEM,
        out_shape=jax.ShapeDtypeStruct((items, 2, 4 * STRETCH + 8, HEAD_DIM), F32),
        compiler_params=pltpu.CompilerParams(vmem_limit_bytes=24 * MIB),
        cost_estimate=pl.CostEstimate(
            flops=items * STRETCH * weight.size * 2, bytes_accessed=weight.size, transcendentals=0
        ),
        name="project",
    )(targets, own, squares, other, other_squares, weight)


def send_kernel(half, first, terms, right, left, to_right, to_left):
    rows = 4 * STRETCH
    middle = 2 * STRETCH
    if first:
        to_right[:middle] = (terms[0, half, :middle] + right[:middle].astype(F32)).astype(BF16)
        to_right[middle:rows] = terms[0, half, middle:rows].astype(BF16)
        to_left[:middle] = terms[1, half, :middle].astype(BF16)
        to_left[middle:rows] = (terms[1, half, middle:rows] + left[...].astype(F32)).astype(BF16)
    else:
        to_right[:rows] = (terms[0, half, :rows] + right[:rows].astype(F32)).astype(BF16)
        to_left[:rows] = (terms[1, half, :rows] + left[:rows].astype(F32)).astype(BF16)
    if half == 0:
        right_sum, left_sum = terms[0, 0, rows:], terms[1, 0, rows:]
        right_sum += one_piece(right[middle if first else rows :])
        if not first:
            left_sum += one_piece(left[rows:])
        to_right[rows:] = two_pieces(right_sum)
        to_left[rows:] = two_pieces(left_sum)


def sends(half, first, terms, right, left):
    rows = 4 * STRETCH + (TAIL if half == 0 else 0)
    shape = jax.ShapeDtypeStruct((rows, HEAD_DIM), BF16)
    return pl.pallas_call(
        functools.partial(send_kernel, half, first),
        in_specs=[VMEM] * 3,
        out_specs=[VMEM] * 2,
        out_shape=[shape, shape],
        compiler_params=pltpu.CompilerParams(vmem_limit_bytes=16 * MIB),
        name="sends",
    )(terms, right, left)


def regroup_kernel(queries, grouped):
    for head in range(KV_HEADS):
        for member in range(GROUP):
            begin = (head * GROUP + member) * HEAD_DIM
            rows = slice(member * STEPS, (member + 1) * STEPS)
            grouped[head, rows] = queries[0, :, begin : begin + HEAD_DIM]


def regroup(queries):
    return pl.pallas_call(
        regroup_kernel,
        in_specs=[VMEM],
        out_specs=VMEM,
        out_shape=jax.ShapeDtypeStruct((KV_HEADS, ROWS, HEAD_DIM), BF16),
        name="regroup",
    )(queries)


CACHE_HEADS = 4


def cache_kernel(targets, lengths, stored, q, keys, values, fresh_keys, fresh_values, out):
    scaling = HEAD_DIM ** (-0.5)
    dims = (((1,), (1,)), ((), ()))
    here = lax.axis_index("tp")
    rep = lax.axis_index("rep")
    length = keys.shape[1]
    span = stored[0]
    for prompt in range(targets.shape[0]):
        span = jnp.where(targets[prompt] == here, lengths[prompt] - STRETCH, span)
    place = lax.broadcasted_iota(jnp.int32, (ROWS, length), 1)
    allowed = place < span - rep * length
    second_step = lax.broadcasted_iota(jnp.int32, (ROWS, 1), 0) % STEPS == 1
    for at in range(CACHE_HEADS):
        lanes = slice(at * HEAD_DIM, (at + 1) * HEAD_DIM)
        query = q[at]
        wide = query.astype(F32)
        scores = lax.dot_general(query, keys[0, :, lanes], dims, preferred_element_type=F32)
        scores = jnp.where(allowed, scores * scaling, NEGATIVE)
        highest = jnp.max(scores, axis=1, keepdims=True)
        fresh = []
        for step in range(STEPS):
            key = fresh_keys[0, step : step + 1, lanes].astype(F32)
            score = jnp.sum(wide * key, axis=1, keepdims=True) * scaling
            shown = rep == 0 if step == 0 else second_step & (rep == 0)
            score = jnp.where(shown, score, NEGATIVE)
            highest = jnp.maximum(highest, score)
            fresh.append(score)
        some = highest > 0.5 * NEGATIVE
        highest = jnp.where(some, highest, 0.0)
        weight = jnp.exp(scores - highest)
        totals = jnp.sum(weight, axis=1, keepdims=True)
        sums = jnp.dot(weight.astype(BF16), values[0, :, lanes], preferred_element_type=F32)
        for step in range(STEPS):
            share = jnp.exp(fresh[step] - highest)
            totals += share
            value = fresh_values[0, step : step + 1, lanes].astype(F32)
            sums += share.astype(BF16).astype(F32) * value
        totals = jnp.where(some, totals, 1.0)
        out[at, :ROWS] = (sums / totals).astype(BF16)
        out[at, ROWS:] = pieces_tail(jnp.where(some, highest + jnp.log(totals), NEGATIVE))


def cache_attention(part, targets, lengths, stored, grouped, kv_cache, new_kv):
    length = kv_cache.shape[1]
    (kv_cache,) = in_hbm(kv_cache)
    width = CACHE_HEADS * HEAD_DIM
    blocks = KV_HEADS // CACHE_HEADS
    return pl.pallas_call(
        cache_kernel,
        grid=(1,),
        in_specs=[
            SMEM,
            SMEM,
            SMEM,
            pl.BlockSpec((CACHE_HEADS, ROWS, HEAD_DIM), lambda h: (part, 0, 0)),
            pl.BlockSpec((1, length, width), lambda h: (0, 0, part)),
            pl.BlockSpec((1, length, width), lambda h: (0, 0, blocks + part)),
            pl.BlockSpec((1, STEPS, width), lambda h: (0, 0, part)),
            pl.BlockSpec((1, STEPS, width), lambda h: (0, 0, blocks + part)),
        ],
        out_specs=pl.BlockSpec((CACHE_HEADS, PART, HEAD_DIM), lambda h: (0, 0, 0)),
        out_shape=jax.ShapeDtypeStruct((CACHE_HEADS, PART, HEAD_DIM), BF16),
        compiler_params=pltpu.CompilerParams(vmem_limit_bytes=24 * MIB),
        cost_estimate=pl.CostEstimate(
            flops=4 * CACHE_HEADS * ROWS * length * HEAD_DIM,
            bytes_accessed=length * 2 * width * 2,
            transcendentals=CACHE_HEADS * ROWS * length,
        ),
        name="cache_attention",
    )(targets, lengths, stored, grouped, kv_cache, kv_cache, new_kv, new_kv)


def final_kernel(
    targets, starts, turns, own, right_a, left_a, right_b, left_b, grouped, cached, out
):
    scaling = HEAD_DIM ** (-0.5)
    dims = (((1,), (1,)), ((), ()))
    mine = own.shape[0] - 1
    first = lax.axis_index("rep") * CORE_HEADS
    prompt = prompt_of(targets, lax.axis_index("tp"))
    row = pl.ds(jnp.maximum(prompt, 0), 1)
    start_cosine, start_sine = starts[0, row, :], starts[1, row, :]
    cosine = turns[0] * start_cosine - turns[1] * start_sine
    sine = turns[1] * start_cosine + turns[0] * start_sine
    lane = lax.broadcasted_iota(jnp.int32, sine.shape, 1)
    sine = jnp.where(lane < HEAD_DIM // 2, -sine, sine)
    rows = 4 * STRETCH
    squares = own[mine, 0, rows:] + one_piece(right_a[rows:]) + one_piece(left_a[rows:])
    scale = token_column(lax.rsqrt(squares / D + EPSILON))
    for head in range(CORE_HEADS):
        right, left = ((right_a, left_a), (right_b, left_b))[head // 2]
        at = slice(head % 2 * STRETCH, (head % 2 + 1) * STRETCH)
        keys = own[mine, head // 2, at] + right[at].astype(F32) + left[at].astype(F32)
        at = slice((2 + head % 2) * STRETCH, (3 + head % 2) * STRETCH)
        values = own[mine, head // 2, at] + right[at].astype(F32) + left[at].astype(F32)
        keys = (keys * scale).astype(BF16).astype(F32)
        values = (values * scale).astype(BF16)
        keys = keys * cosine + pltpu.roll(keys, HEAD_DIM // 2, 1) * sine
        scores = lax.dot_general(
            grouped[first + head], keys.astype(BF16), dims, preferred_element_type=F32
        )
        scores = scores * scaling
        highest = jnp.max(scores, axis=1, keepdims=True)
        weight = jnp.exp(scores - highest)
        totals = jnp.sum(weight, axis=1, keepdims=True)
        sums = jnp.dot(weight.astype(BF16), values, preferred_element_type=F32) / totals
        logs = jnp.where(prompt >= 0, highest + jnp.log(totals), NEGATIVE)
        parts = [cached[0, first + head], cached[1, first + head]]
        logs = [tail_pieces(part[ROWS:]) for part in parts] + [logs]
        sums = [part[:ROWS].astype(F32) for part in parts] + [sums]
        highest = functools.reduce(jnp.maximum, logs)
        shares = [jnp.exp(log - highest) for log in logs]
        total = functools.reduce(jnp.add, shares)
        joined = functools.reduce(jnp.add, [share * part for share, part in zip(shares, sums)])
        result = (joined / total).astype(BF16)
        for member in range(GROUP):
            begin = (head * GROUP + member) * HEAD_DIM
            out[:, begin : begin + HEAD_DIM] = result[member * STEPS : (member + 1) * STEPS]


def finish(targets, starts, turns, own, arrived, grouped, cached):
    width = CORE_HEADS * GROUP * HEAD_DIM
    return pl.pallas_call(
        final_kernel,
        in_specs=[SMEM] + [VMEM] * 9,
        out_specs=VMEM,
        out_shape=jax.ShapeDtypeStruct((STEPS, width), BF16),
        compiler_params=pltpu.CompilerParams(vmem_limit_bytes=16 * MIB),
        name="finish",
    )(targets, starts, turns, own, *arrived, grouped, cached)


def rotary_turns():
    half = np.arange(HEAD_DIM // 2, dtype=np.float64) / (HEAD_DIM // 2)
    frequency = ROTARY_BASE ** (-np.concatenate([half, half]))
    angles = np.arange(STRETCH, dtype=np.float64)[:, None] * frequency
    return frequency.astype(np.float32), np.stack([np.cos(angles), np.sin(angles)]).astype(np.float32)


def per_device(
    stretch,
    norm_gain,
    kv_codes,
    scale_codes,
    outer_scales,
    prompt_lengths,
    target_rows,
    cache_lengths,
    kv_cache,
    queries,
    new_kv,
):
    count = lax.axis_size("tp")
    half = count // 2
    lines = stretch.transpose(1, 0, 2)
    gain = norm_gain.reshape(1, -1)
    ring = [ring_device(at, count) for at in range(count)]
    to_right = [(ring[at], ring[(at + 1) % count]) for at in range(count)]
    to_left = [(ring[at], ring[at - 1]) for at in range(count)]

    def pass_on(right, left):
        return lax.ppermute(right, "tp", to_right), lax.ppermute(left, "tp", to_left)

    other_lines = lax.ppermute(lines, "rep", [(0, 1), (1, 0)])
    weight, own, squares = dequantize(lines, kv_codes, scale_codes, outer_scales.T, gain)
    firsts = project_first(target_rows, own, squares, other_lines, gain, weight)
    arrived = [pass_on(*firsts[:2]), pass_on(*firsts[2:])]

    gain, queries, _ = lax.optimization_barrier((gain, queries, firsts[3]))
    other, other_squares = scale_features(other_lines, gain)
    grouped = regroup(queries)
    frequency, turns = rotary_turns()
    start = (prompt_lengths - STRETCH).astype(F32)[:, None] * jnp.asarray(frequency)
    starts = jnp.stack([jnp.cos(start), jnp.sin(start)])

    targets = target_rows
    cached = []
    for distance in range(half - 1, 0, -1):
        items = 3 if distance == 1 else 2
        terms = project(distance, items, targets, own, squares, other, other_squares, weight)
        for part in range(2):
            right, left = sends(part, distance == half - 1, terms, *arrived[part])
            targets, _ = lax.optimization_barrier((target_rows, right))
            arrived[part] = pass_on(right, left)
            if distance == 1:
                cached.append(
                    cache_attention(
                        part, targets, prompt_lengths, cache_lengths, grouped, kv_cache, new_kv
                    )
                )

    cached = lax.all_gather(jnp.concatenate(cached), "rep")
    out = finish(
        target_rows, starts, jnp.asarray(turns), terms, [*arrived[0], *arrived[1]], grouped, cached
    )
    return lax.all_gather(out, "rep", axis=1, tiled=True).reshape(1, STEPS, HEADS * HEAD_DIM)


def solution(mesh):
    in_specs = (
        P(None, ("grp", "rep"), "tp"),
        P("tp"),
        P("tp", None),
        P("tp", None),
        P("tp", None),
        P("grp"),
        P("grp"),
        P(("grp", "tp")),
        P(("grp", "tp"), "rep", None),
        P(("grp", "tp"), None, None),
        P(("grp", "tp"), None, None),
    )
    out_specs = P(("grp", "tp"), None, None)
    return jax.shard_map(
        per_device, mesh=mesh, in_specs=in_specs, out_specs=out_specs, check_vma=False
    )
```

```python
import functools
import math

import jax
import jax.numpy as jnp
import numpy as np
from jax import lax
from jax.experimental import pallas as pl
from jax.experimental.pallas import tpu as pltpu
from jax.sharding import PartitionSpec as P

D = 16384
HEADS = 128
KV_HEADS = 8
HEAD_DIM = 128
STRETCH = 192
STEPS = 2
QBLOCK = 64
GROUP = HEADS // KV_HEADS
ROWS = GROUP * STEPS
TAIL = 16
PART = ROWS + TAIL
CORE_HEADS = KV_HEADS // 2
NORMAL_FLOAT_LEVELS = [
    -1.0,
    -0.6961928009986877,
    -0.5250730514526367,
    -0.39491748809814453,
    -0.28444138169288635,
    -0.18477343022823334,
    -0.09105003625154495,
    0.0,
    0.07958029955625534,
    0.16093020141124725,
    0.24611230194568634,
    0.33791524171829224,
    0.44070982933044434,
    0.5626170039176941,
    0.7229568362236023,
    1.0,
]
ROTARY_BASE = 500000.0
EPSILON = 1e-05
NEGATIVE = -1e30
BF16 = jnp.bfloat16
F32 = jnp.float32
MIB = 1024 * 1024
VMEM = pl.BlockSpec(memory_space=pltpu.VMEM)
SMEM = pl.BlockSpec(memory_space=pltpu.SMEM)


def in_hbm(*arrays):
    return [pltpu.with_memory_space_constraint(array, pltpu.HBM) for array in arrays]


def ring_device(place, count):
    half = count // 2
    if isinstance(place, int):
        return 2 * place if place < half else 2 * (count - 1 - place) + 1
    return jnp.where(place < half, 2 * place, 2 * (count - 1 - place) + 1)


def owner_at(distance):
    count = lax.axis_size("tp")
    here = lax.axis_index("tp")
    place = jnp.where(here % 2 == 0, here // 2, count - 1 - here // 2)
    return ring_device((place + distance + count) % count, count)


def turned(column):
    rows = lax.broadcasted_iota(jnp.int32, (column.shape[0], 128), 0)
    lanes = lax.broadcasted_iota(jnp.int32, (column.shape[0], 128), 1)
    return jnp.sum(jnp.where(rows == lanes, column, 0.0), axis=0, keepdims=True)


def stood(row, count):
    rows = lax.broadcasted_iota(jnp.int32, (count, 128), 0)
    lanes = lax.broadcasted_iota(jnp.int32, (count, 128), 1)
    return jnp.sum(jnp.where(rows == lanes, row, 0.0), axis=1, keepdims=True)


def token_rows(column):
    at = lax.broadcasted_iota(jnp.int32, (8, 128), 0)
    ends = turned(column[128:])
    return jnp.where(at == 0, turned(column[:128]), jnp.where(at == 1, ends, 0.0))


def token_column(rows):
    return jnp.concatenate([stood(rows[0:1], 128), stood(rows[1:2], STRETCH - 128)], axis=0)


def two_pieces(rows):
    high = rows.astype(BF16).astype(F32)
    return jnp.concatenate([high, rows - high], axis=0).astype(BF16)


def one_piece(rows):
    rows = rows.astype(F32)
    return rows[:8] + rows[8:]


def pieces_tail(logs):
    row = turned(logs)
    high = row.astype(BF16).astype(F32)
    middle = (row - high).astype(BF16).astype(F32)
    low = row - high - middle
    at = lax.broadcasted_iota(jnp.int32, (TAIL, 128), 0)
    tail = jnp.where(at == 0, high, jnp.where(at == 1, middle, jnp.where(at == 2, low, 0.0)))
    return tail.astype(BF16)


def tail_pieces(tail):
    tail = tail.astype(F32)
    return stood(tail[0:1, :] + tail[1:2, :] + tail[2:3, :], ROWS)


def gathered_levels(table, codes):
    table = jnp.broadcast_to(table[None], (codes.shape[0] // 8, 8, 128)).reshape(codes.shape)
    return jnp.take_along_axis(table, codes, axis=1, mode="promise_in_bounds")


def selected_levels(codes):
    values = [jnp.float32(level) for level in NORMAL_FLOAT_LEVELS]
    for bit in (1, 2, 4, 8):
        mask = (codes & bit) != 0 if bit < 8 else codes >= 8
        values = [
            jnp.where(mask, values[at + 1], values[at]) for at in range(0, len(values), 2)
        ]
    return values[0]


def block_scales(scales, outer, column):
    count = scales.shape[0]
    line = lax.broadcasted_iota(jnp.int32, outer.shape, 0)
    line = jnp.sum(jnp.where(line == column, outer, 0.0), axis=0, keepdims=True)
    rows = lax.broadcasted_iota(jnp.int32, (count, count), 0)
    lanes = lax.broadcasted_iota(jnp.int32, (count, count), 1)
    second = jnp.sum(jnp.where(rows == lanes, line, 0.0), axis=1, keepdims=True)
    return (scales.astype(F32) + 1.0) / 256.0 * second


def weights_kernel(
    half, key_codes, value_codes, key_scales, value_scales, outer, *refs
):
    if half == 0:
        x, gain, out, scaled, squares, scales = refs
    else:
        out, scales = refs
    item, block = pl.program_id(0), pl.program_id(1)
    depth = key_codes.shape[0]
    head = lax.axis_index("rep") * CORE_HEADS + 2 * half + item
    columns = outer.shape[0] // 2
    column = head // (KV_HEADS // columns)

    @pl.when(block == 0)
    def _():
        scales[0] = block_scales(key_scales[...], outer[...], column)
        scales[1] = block_scales(value_scales[...], outer[...], columns + column)

    lane = lax.broadcasted_iota(jnp.int32, (8, 128), 1)
    table = jnp.zeros((8, 128), F32)
    for code, level in enumerate(NORMAL_FLOAT_LEVELS):
        table = jnp.where(lane == code, level, table)
    together = 4

    def body(step, _):
        begins = [
            pl.multiple_of((step * together + at) * QBLOCK, QBLOCK) for at in range(together)
        ]
        codes = [
            (key_codes[pl.ds(begin, QBLOCK), :], value_codes[pl.ds(begin, QBLOCK), :])
            for begin in begins
        ]
        results = []
        for at, (key, value) in enumerate(codes):
            row = pl.ds(block * (depth // QBLOCK) + step * together + at, 1)
            results.append(
                (
                    (gathered_levels(table, key) * scales[0, row, :]).astype(BF16),
                    (selected_levels(value) * scales[1, row, :]).astype(BF16),
                )
            )
        for begin, (key, value) in zip(begins, results):
            rows = pl.ds(pl.multiple_of(block * depth + begin, QBLOCK), QBLOCK)
            out[item, rows, :HEAD_DIM] = key
            out[item, rows, HEAD_DIM:] = value
        return 0

    lax.fori_loop(0, depth // (QBLOCK * together), body, 0)

    if half == 0:
        at = item * pl.num_programs(1) + block

        @pl.when(at == 0)
        def _():
            squares[...] = jnp.zeros(squares.shape, F32)

        width = x.shape[2]
        begin = pl.multiple_of(at * width, 128)
        for prompt in range(x.shape[0]):
            wide = x[prompt].astype(F32)
            scaled[prompt, :, pl.ds(begin, width)] = (wide * gain[...]).astype(BF16)
            squares[prompt] += token_rows(jnp.sum(wide * wide, axis=1, keepdims=True))


def dequantize(half, x, codes, scales, outer, gain):
    per_rep, _, features = x.shape
    depth = min(1024, features)
    blocks = features // depth
    width = features // (2 * blocks)
    head = lambda i: lax.axis_index("rep") * CORE_HEADS + 2 * half + i
    x, codes, scales, outer, gain = in_hbm(x, codes, scales, outer, gain)
    in_specs = [
        pl.BlockSpec((depth, HEAD_DIM), lambda i, k: (k, head(i))),
        pl.BlockSpec((depth, HEAD_DIM), lambda i, k: (k, KV_HEADS + head(i))),
        pl.BlockSpec((scales.shape[0], HEAD_DIM), lambda i, k: (0, head(i))),
        pl.BlockSpec((scales.shape[0], HEAD_DIM), lambda i, k: (0, KV_HEADS + head(i))),
        pl.BlockSpec(outer.shape, lambda i, k: (0, 0)),
    ]
    operands = [codes, codes, scales, scales, outer]
    shapes = [jax.ShapeDtypeStruct((2, features, 2 * HEAD_DIM), BF16)]
    if half == 0:
        in_specs += [
            pl.BlockSpec((per_rep, STRETCH, width), lambda i, k: (0, 0, i * blocks + k)),
            pl.BlockSpec((1, width), lambda i, k: (0, i * blocks + k)),
        ]
        operands += [x, gain]
        shapes += [
            jax.ShapeDtypeStruct(x.shape, BF16),
            jax.ShapeDtypeStruct((per_rep, 8, 128), F32),
        ]
    return pl.pallas_call(
        functools.partial(weights_kernel, half),
        grid=(2, blocks),
        in_specs=in_specs,
        out_specs=[VMEM] * len(shapes),
        out_shape=shapes,
        scratch_shapes=[pltpu.VMEM((2, scales.shape[0], HEAD_DIM), F32)],
        compiler_params=pltpu.CompilerParams(vmem_limit_bytes=32 * MIB),
        cost_estimate=pl.CostEstimate(
            flops=16 * codes.size, bytes_accessed=codes.size, transcendentals=0
        ),
        name="dequantize",
    )(*operands)


def prompt_of(targets, owner):
    prompt = jnp.int32(-1)
    for at in range(targets.shape[0]):
        prompt = jnp.where(targets[at] == owner, at, prompt)
    return prompt


def lines_of(targets, distance, own, squares, other, gain, line, total):
    per_rep = own.shape[0]
    prompt = prompt_of(targets, owner_at(distance))
    at = lax.rem(jnp.maximum(prompt, 0), per_rep)
    is_own = prompt // per_rep == lax.axis_index("rep")

    @pl.when((prompt >= 0) & is_own)
    def _():
        line[...] = own[at]
        total[...] = squares[at]

    @pl.when((prompt >= 0) & jnp.logical_not(is_own))
    def _():
        wide = other[at].astype(F32)
        line[...] = (wide * gain[...]).astype(BF16)
        total[...] = token_rows(jnp.sum(wide * wide, axis=1, keepdims=True))

    @pl.when(prompt < 0)
    def _():
        line[...] = jnp.zeros(line.shape, BF16)
        total[...] = jnp.zeros(total.shape, F32)


def line_specs(distances, x):
    return [
        jax.ShapeDtypeStruct((len(distances) * STRETCH, x.shape[2]), BF16),
        jax.ShapeDtypeStruct((len(distances), 8, 128), F32),
    ]


def first_kernel(distances, targets, own, squares, other, gain, weight, *refs):
    right, left, terms, lines, totals = refs
    for item, distance in enumerate(distances):
        line = lines.at[item * STRETCH : (item + 1) * STRETCH]
        lines_of(targets, distance, own, squares, other, gain, line, totals.at[item])
    products(distances, lines, totals, weight, right, left, terms)


def second_kernel(distances, lines, totals, weight, *refs):
    products(distances, lines, totals, weight, *refs)


def products(distances, lines, totals, weight, right, left, terms):
    for head in range(2):
        product = jnp.dot(lines[...], weight[head], preferred_element_type=F32)
        rows = slice(head * STRETCH, (head + 1) * STRETCH)
        right[rows] = product[:STRETCH, :HEAD_DIM].astype(BF16)
        left[rows] = product[:STRETCH, HEAD_DIM:].astype(BF16)
        for item in range(1, len(distances)):
            part = product[item * STRETCH : (item + 1) * STRETCH]
            begin = head * STRETCH
            terms[item - 1, begin : begin + STRETCH] = part[:, :HEAD_DIM]
            begin += 2 * STRETCH
            terms[item - 1, begin : begin + STRETCH] = part[:, HEAD_DIM:]
    for item in range(1, len(distances)):
        terms[item - 1, 4 * STRETCH :] = totals[item]
    right[2 * STRETCH :] = two_pieces(totals[0])


def first_shapes(distances):
    rows = 2 * STRETCH
    return [
        jax.ShapeDtypeStruct((rows + TAIL, HEAD_DIM), BF16),
        jax.ShapeDtypeStruct((rows, HEAD_DIM), BF16),
        jax.ShapeDtypeStruct((len(distances) - 1, 2 * rows + 8, HEAD_DIM), F32),
    ]


def project_cost(distances, weight):
    return pl.CostEstimate(
        flops=len(distances) * STRETCH * weight.size * 2,
        bytes_accessed=weight.size,
        transcendentals=0,
    )


def project_first(distances, targets, own, squares, other, gain, weight):
    return pl.pallas_call(
        functools.partial(first_kernel, distances),
        in_specs=[SMEM] + [VMEM] * 5,
        out_specs=[VMEM] * 5,
        out_shape=first_shapes(distances) + line_specs(distances, own),
        compiler_params=pltpu.CompilerParams(vmem_limit_bytes=24 * MIB),
        cost_estimate=project_cost(distances, weight),
        name="project_first",
    )(targets, own, squares, other, gain, weight)


def project_second(distances, lines, totals, weight):
    return pl.pallas_call(
        functools.partial(second_kernel, distances),
        in_specs=[VMEM] * 3,
        out_specs=[VMEM] * 3,
        out_shape=first_shapes(distances),
        compiler_params=pltpu.CompilerParams(vmem_limit_bytes=24 * MIB),
        cost_estimate=project_cost(distances, weight),
        name="project_second",
    )(lines, totals, weight)


def project_kernel(
    distances, targets, own, squares, other, gain, weight_a, weight_b, out_a, out_b, lines, totals
):
    for item, distance in enumerate(distances):
        line = lines.at[item * STRETCH : (item + 1) * STRETCH]
        lines_of(targets, distance, own, squares, other, gain, line, totals.at[item])
    for weight, out in ((weight_a, out_a), (weight_b, out_b)):
        for head in range(2):
            product = jnp.dot(lines[...], weight[head], preferred_element_type=F32)
            for item in range(len(distances)):
                part = product[item * STRETCH : (item + 1) * STRETCH]
                begin = head * STRETCH
                out[item, begin : begin + STRETCH] = part[:, :HEAD_DIM]
                begin += 2 * STRETCH
                out[item, begin : begin + STRETCH] = part[:, HEAD_DIM:]
        for item in range(len(distances)):
            out[item, 4 * STRETCH :] = totals[item]


def project(distances, targets, own, squares, other, gain, weights):
    shape = jax.ShapeDtypeStruct((len(distances), 4 * STRETCH + 8, HEAD_DIM), F32)
    line, total = line_specs(distances, own)
    return pl.pallas_call(
        functools.partial(project_kernel, distances),
        in_specs=[SMEM] + [VMEM] * 6,
        out_specs=[VMEM] * 2,
        out_shape=[shape, shape],
        scratch_shapes=[pltpu.VMEM(line.shape, BF16), pltpu.VMEM(total.shape, F32)],
        compiler_params=pltpu.CompilerParams(vmem_limit_bytes=24 * MIB),
        cost_estimate=project_cost(distances, weights[0]),
        name="project",
    )(targets, own, squares, other, gain, *weights)


def send_kernel(half, first, terms, right, left, to_right, to_left):
    rows = 4 * STRETCH
    middle = 2 * STRETCH
    if first:
        to_right[:middle] = (terms[0, :middle] + right[:middle].astype(F32)).astype(BF16)
        to_right[middle:rows] = terms[0, middle:rows].astype(BF16)
        to_left[:middle] = terms[1, :middle].astype(BF16)
        to_left[middle:rows] = (terms[1, middle:rows] + left[...].astype(F32)).astype(BF16)
    else:
        to_right[:rows] = (terms[0, :rows] + right[:rows].astype(F32)).astype(BF16)
        to_left[:rows] = (terms[1, :rows] + left[:rows].astype(F32)).astype(BF16)
    if half == 0:
        right_sum, left_sum = terms[0, rows:], terms[1, rows:]
        right_sum += one_piece(right[middle if first else rows :])
        if not first:
            left_sum += one_piece(left[rows:])
        to_right[rows:] = two_pieces(right_sum)
        to_left[rows:] = two_pieces(left_sum)


def sends(half, first, terms, right, left):
    rows = 4 * STRETCH + (TAIL if half == 0 else 0)
    shape = jax.ShapeDtypeStruct((rows, HEAD_DIM), BF16)
    return pl.pallas_call(
        functools.partial(send_kernel, half, first),
        in_specs=[VMEM] * 3,
        out_specs=[VMEM] * 2,
        out_shape=[shape, shape],
        compiler_params=pltpu.CompilerParams(vmem_limit_bytes=16 * MIB),
        name="sends",
    )(terms, right, left)


def prepare_kernel(targets, queries, starts, turns, grouped, rotary):
    for head in range(KV_HEADS):
        for member in range(GROUP):
            begin = (head * GROUP + member) * HEAD_DIM
            rows = slice(member * STEPS, (member + 1) * STEPS)
            grouped[head, rows] = queries[0, :, begin : begin + HEAD_DIM]
    row = pl.ds(jnp.maximum(prompt_of(targets, lax.axis_index("tp")), 0), 1)
    cosine, sine = starts[0, row, :], starts[1, row, :]
    lane = lax.broadcasted_iota(jnp.int32, turns.shape[1:], 1)
    rotary[0] = turns[0] * cosine - turns[1] * sine
    sine = turns[1] * cosine + turns[0] * sine
    rotary[1] = jnp.where(lane < HEAD_DIM // 2, -sine, sine)


def prepare(targets, queries, starts, turns):
    return pl.pallas_call(
        prepare_kernel,
        in_specs=[SMEM] + [VMEM] * 3,
        out_specs=[VMEM] * 2,
        out_shape=[
            jax.ShapeDtypeStruct((KV_HEADS, ROWS, HEAD_DIM), BF16),
            jax.ShapeDtypeStruct(turns.shape, F32),
        ],
        compiler_params=pltpu.CompilerParams(vmem_limit_bytes=16 * MIB),
        name="prepare",
    )(targets, queries, starts, turns)


CACHE_HEADS = 2


def cache_kernel(targets, lengths, stored, q, keys, values, fresh_keys, fresh_values, out):
    scaling = HEAD_DIM ** (-0.5)
    dims = (((1,), (1,)), ((), ()))
    here = lax.axis_index("tp")
    rep = lax.axis_index("rep")
    length = keys.shape[1]
    span = stored[0]
    for prompt in range(targets.shape[0]):
        span = jnp.where(targets[prompt] == here, lengths[prompt] - STRETCH, span)
    place = lax.broadcasted_iota(jnp.int32, (ROWS, length), 1)
    allowed = place < span - rep * length
    second_step = lax.broadcasted_iota(jnp.int32, (ROWS, 1), 0) % STEPS == 1
    for at in range(CACHE_HEADS):
        lanes = slice(at * HEAD_DIM, (at + 1) * HEAD_DIM)
        query = q[at]
        wide = query.astype(F32)
        scores = lax.dot_general(query, keys[0, :, lanes], dims, preferred_element_type=F32)
        scores = jnp.where(allowed, scores * scaling, NEGATIVE)
        highest = jnp.max(scores, axis=1, keepdims=True)
        fresh = []
        for step in range(STEPS):
            key = fresh_keys[0, step : step + 1, lanes].astype(F32)
            score = jnp.sum(wide * key, axis=1, keepdims=True) * scaling
            shown = rep == 0 if step == 0 else second_step & (rep == 0)
            score = jnp.where(shown, score, NEGATIVE)
            highest = jnp.maximum(highest, score)
            fresh.append(score)
        some = highest > 0.5 * NEGATIVE
        highest = jnp.where(some, highest, 0.0)
        weight = jnp.exp(scores - highest)
        totals = jnp.sum(weight, axis=1, keepdims=True)
        sums = jnp.dot(weight.astype(BF16), values[0, :, lanes], preferred_element_type=F32)
        for step in range(STEPS):
            share = jnp.exp(fresh[step] - highest)
            totals += share
            value = fresh_values[0, step : step + 1, lanes].astype(F32)
            sums += share.astype(BF16).astype(F32) * value
        totals = jnp.where(some, totals, 1.0)
        out[at, :ROWS] = (sums / totals).astype(BF16)
        out[at, ROWS:] = pieces_tail(jnp.where(some, highest + jnp.log(totals), NEGATIVE))


def cache_attention(part, targets, lengths, stored, grouped, kv_cache, new_kv):
    length = kv_cache.shape[1]
    (kv_cache,) = in_hbm(kv_cache)
    width = CACHE_HEADS * HEAD_DIM
    blocks = KV_HEADS // CACHE_HEADS
    return pl.pallas_call(
        cache_kernel,
        grid=(2,),
        in_specs=[
            SMEM,
            SMEM,
            SMEM,
            pl.BlockSpec((CACHE_HEADS, ROWS, HEAD_DIM), lambda h: (2 * part + h, 0, 0)),
            pl.BlockSpec((1, length, width), lambda h: (0, 0, 2 * part + h)),
            pl.BlockSpec((1, length, width), lambda h: (0, 0, blocks + 2 * part + h)),
            pl.BlockSpec((1, STEPS, width), lambda h: (0, 0, 2 * part + h)),
            pl.BlockSpec((1, STEPS, width), lambda h: (0, 0, blocks + 2 * part + h)),
        ],
        out_specs=pl.BlockSpec((CACHE_HEADS, PART, HEAD_DIM), lambda h: (h, 0, 0)),
        out_shape=jax.ShapeDtypeStruct((2 * CACHE_HEADS, PART, HEAD_DIM), BF16),
        compiler_params=pltpu.CompilerParams(vmem_limit_bytes=24 * MIB),
        cost_estimate=pl.CostEstimate(
            flops=8 * CACHE_HEADS * ROWS * length * HEAD_DIM,
            bytes_accessed=2 * length * 2 * width * 2,
            transcendentals=2 * CACHE_HEADS * ROWS * length,
        ),
        name="cache_attention",
    )(targets, lengths, stored, grouped, kv_cache, kv_cache, new_kv, new_kv)


def final_kernel(
    targets, rotary, own_a, own_b, right_a, left_a, right_b, left_b, grouped, *refs
):
    cached, out = refs
    scaling = HEAD_DIM ** (-0.5)
    dims = (((1,), (1,)), ((), ()))
    mine = own_a.shape[0] - 1
    rep = lax.axis_index("rep")
    first = rep * CORE_HEADS
    prompt = prompt_of(targets, lax.axis_index("tp"))
    cosine, sine = rotary[0], rotary[1]
    rows = 4 * STRETCH
    squares = own_a[mine, rows:] + one_piece(right_a[rows:]) + one_piece(left_a[rows:])
    scale = token_column(lax.rsqrt(squares / D + EPSILON))
    for head in range(CORE_HEADS):
        own, right, left = ((own_a, right_a, left_a), (own_b, right_b, left_b))[head // 2]
        at = slice(head % 2 * STRETCH, (head % 2 + 1) * STRETCH)
        keys = own[mine, at] + right[at].astype(F32) + left[at].astype(F32)
        at = slice((2 + head % 2) * STRETCH, (3 + head % 2) * STRETCH)
        values = own[mine, at] + right[at].astype(F32) + left[at].astype(F32)
        keys = (keys * scale).astype(BF16).astype(F32)
        values = (values * scale).astype(BF16)
        keys = keys * cosine + pltpu.roll(keys, HEAD_DIM // 2, 1) * sine
        scores = lax.dot_general(
            grouped[first + head], keys.astype(BF16), dims, preferred_element_type=F32
        )
        scores = scores * scaling
        highest = jnp.max(scores, axis=1, keepdims=True)
        weight = jnp.exp(scores - highest)
        totals = jnp.sum(weight, axis=1, keepdims=True)
        sums = jnp.dot(weight.astype(BF16), values, preferred_element_type=F32) / totals
        logs = jnp.where(prompt >= 0, highest + jnp.log(totals), NEGATIVE)
        parts = [cached[0, first + head], cached[1, first + head]]
        logs = [tail_pieces(part[ROWS:]) for part in parts] + [logs]
        sums = [part[:ROWS].astype(F32) for part in parts] + [sums]
        highest = functools.reduce(jnp.maximum, logs)
        shares = [jnp.exp(log - highest) for log in logs]
        total = functools.reduce(jnp.add, shares)
        joined = functools.reduce(jnp.add, [share * part for share, part in zip(shares, sums)])
        result = (joined / total).astype(BF16)
        for member in range(GROUP):
            begin = (head * GROUP + member) * HEAD_DIM
            out[0, :, begin : begin + HEAD_DIM] = result[member * STEPS : (member + 1) * STEPS]


def finish(targets, rotary, own, arrived, grouped, cached):
    width = CORE_HEADS * GROUP * HEAD_DIM
    return pl.pallas_call(
        final_kernel,
        in_specs=[SMEM] + [VMEM] * 9,
        out_specs=VMEM,
        out_shape=jax.ShapeDtypeStruct((1, STEPS, width), BF16),
        compiler_params=pltpu.CompilerParams(vmem_limit_bytes=16 * MIB),
        name="finish",
    )(targets, rotary, *own, *arrived, grouped, cached)


def rotary_turns():
    half = np.arange(HEAD_DIM // 2, dtype=np.float64) / (HEAD_DIM // 2)
    frequency = ROTARY_BASE ** (-np.concatenate([half, half]))
    angles = np.arange(STRETCH, dtype=np.float64)[:, None] * frequency
    return frequency.astype(np.float32), np.stack([np.cos(angles), np.sin(angles)]).astype(np.float32)


def per_device(
    stretch,
    norm_gain,
    kv_codes,
    scale_codes,
    outer_scales,
    prompt_lengths,
    target_rows,
    cache_lengths,
    kv_cache,
    queries,
    new_kv,
):
    count = lax.axis_size("tp")
    half = count // 2
    lines = stretch.transpose(1, 0, 2)
    gain = norm_gain.reshape(1, -1)
    ring = [ring_device(at, count) for at in range(count)]
    to_right = [(ring[at], ring[(at + 1) % count]) for at in range(count)]
    to_left = [(ring[at], ring[at - 1]) for at in range(count)]

    def pass_on(right, left):
        return lax.ppermute(right, "tp", to_right), lax.ppermute(left, "tp", to_left)

    other = lax.ppermute(lines, "rep", [(0, 1), (1, 0)])
    first_half, own, squares = dequantize(0, lines, kv_codes, scale_codes, outer_scales.T, gain)
    (second_half,) = dequantize(1, lines, kv_codes, scale_codes, outer_scales.T, gain)
    frequency, turns = rotary_turns()
    start = (prompt_lengths - STRETCH).astype(F32)[:, None] * jnp.asarray(frequency)
    starts = jnp.stack([jnp.cos(start), jnp.sin(start)])
    targets, second_half = lax.optimization_barrier((target_rows, second_half))
    grouped, rotary = prepare(targets, queries, starts, jnp.asarray(turns))

    gain, second_half, grouped, rotary = lax.optimization_barrier(
        (gain, second_half, grouped, rotary)
    )
    distances = [half, half - 1, 1 - half]
    right, left, terms_a, lines_here, totals = project_first(
        distances, target_rows, own, squares, other, gain, first_half
    )
    arrived = [pass_on(right, left), None]
    right, left, terms_b = project_second(distances, lines_here, totals, second_half)
    arrived[1] = pass_on(right, left)
    terms = [terms_a, terms_b]

    targets = target_rows
    cached = []
    for distance in range(half - 1, 0, -1):
        if distance < half - 1:
            distances = [distance, -distance] + ([0] if distance == 1 else [])
            terms = list(
                project(distances, targets, own, squares, other, gain, [first_half, second_half])
            )
        for part in range(2):
            right, left = sends(part, distance == half - 1, terms[part], *arrived[part])
            if part == 0:
                right, cached, terms[1] = lax.optimization_barrier((right, cached, terms[1]))
            targets, _ = lax.optimization_barrier((target_rows, right))
            arrived[part] = pass_on(right, left)
        if distance in (2, 3):
            cached.append(
                cache_attention(
                    3 - distance, targets, prompt_lengths, cache_lengths, grouped, kv_cache, new_kv
                )
            )

    cached, _ = lax.optimization_barrier((cached, right))
    cached = lax.all_gather(jnp.concatenate(cached), "rep")
    out = finish(target_rows, rotary, terms, [*arrived[0], *arrived[1]], grouped, cached)
    return lax.all_gather(out, "rep", axis=2, tiled=True)


def solution(mesh):
    in_specs = (
        P(None, ("grp", "rep"), "tp"),
        P("tp"),
        P("tp", None),
        P("tp", None),
        P("tp", None),
        P("grp"),
        P("grp"),
        P(("grp", "tp")),
        P(("grp", "tp"), "rep", None),
        P(("grp", "tp"), None, None),
        P(("grp", "tp"), None, None),
    )
    out_specs = P(("grp", "tp"), None, None)
    return jax.shard_map(
        per_device, mesh=mesh, in_specs=in_specs, out_specs=out_specs, check_vma=False
    )
```

```python
import functools
import math

import jax
import jax.numpy as jnp
import numpy as np
from jax import lax
from jax.experimental import pallas as pl
from jax.experimental.pallas import tpu as pltpu
from jax.sharding import PartitionSpec as P

D = 16384
HEADS = 128
KV_HEADS = 8
HEAD_DIM = 128
STRETCH = 192
STEPS = 2
QBLOCK = 64
GROUP = HEADS // KV_HEADS
ROWS = GROUP * STEPS
TAIL = 16
PART = ROWS + TAIL
CORE_HEADS = KV_HEADS // 2
NORMAL_FLOAT_LEVELS = [
    -1.0,
    -0.6961928009986877,
    -0.5250730514526367,
    -0.39491748809814453,
    -0.28444138169288635,
    -0.18477343022823334,
    -0.09105003625154495,
    0.0,
    0.07958029955625534,
    0.16093020141124725,
    0.24611230194568634,
    0.33791524171829224,
    0.44070982933044434,
    0.5626170039176941,
    0.7229568362236023,
    1.0,
]
ROTARY_BASE = 500000.0
EPSILON = 1e-05
NEGATIVE = -1e30
BF16 = jnp.bfloat16
F32 = jnp.float32
MIB = 1024 * 1024
VMEM = pl.BlockSpec(memory_space=pltpu.VMEM)
SMEM = pl.BlockSpec(memory_space=pltpu.SMEM)


def in_hbm(*arrays):
    return [pltpu.with_memory_space_constraint(array, pltpu.HBM) for array in arrays]


def ring_device(place, count):
    half = count // 2
    if isinstance(place, int):
        return 2 * place if place < half else 2 * (count - 1 - place) + 1
    return jnp.where(place < half, 2 * place, 2 * (count - 1 - place) + 1)


def owner_at(distance):
    count = lax.axis_size("tp")
    here = lax.axis_index("tp")
    place = jnp.where(here % 2 == 0, here // 2, count - 1 - here // 2)
    return ring_device((place + distance + count) % count, count)


def turned(column):
    rows = lax.broadcasted_iota(jnp.int32, (column.shape[0], 128), 0)
    lanes = lax.broadcasted_iota(jnp.int32, (column.shape[0], 128), 1)
    return jnp.sum(jnp.where(rows == lanes, column, 0.0), axis=0, keepdims=True)


def stood(row, count):
    rows = lax.broadcasted_iota(jnp.int32, (count, 128), 0)
    lanes = lax.broadcasted_iota(jnp.int32, (count, 128), 1)
    return jnp.sum(jnp.where(rows == lanes, row, 0.0), axis=1, keepdims=True)


def token_rows(column):
    at = lax.broadcasted_iota(jnp.int32, (8, 128), 0)
    ends = turned(column[128:])
    return jnp.where(at == 0, turned(column[:128]), jnp.where(at == 1, ends, 0.0))


def token_column(rows):
    return jnp.concatenate([stood(rows[0:1], 128), stood(rows[1:2], STRETCH - 128)], axis=0)


def two_pieces(rows):
    high = rows.astype(BF16).astype(F32)
    return jnp.concatenate([high, rows - high], axis=0).astype(BF16)


def one_piece(rows):
    rows = rows.astype(F32)
    return rows[:8] + rows[8:]


def pieces_tail(logs):
    row = turned(logs)
    high = row.astype(BF16).astype(F32)
    middle = (row - high).astype(BF16).astype(F32)
    low = row - high - middle
    at = lax.broadcasted_iota(jnp.int32, (TAIL, 128), 0)
    tail = jnp.where(at == 0, high, jnp.where(at == 1, middle, jnp.where(at == 2, low, 0.0)))
    return tail.astype(BF16)


def tail_pieces(tail):
    tail = tail.astype(F32)
    return stood(tail[0:1, :] + tail[1:2, :] + tail[2:3, :], ROWS)


def gathered_levels(table, codes):
    table = jnp.broadcast_to(table[None], (codes.shape[0] // 8, 8, 128)).reshape(codes.shape)
    return jnp.take_along_axis(table, codes, axis=1, mode="promise_in_bounds")


def selected_levels(codes):
    values = [jnp.float32(level) for level in NORMAL_FLOAT_LEVELS]
    for bit in (1, 2, 4, 8):
        mask = (codes & bit) != 0 if bit < 8 else codes >= 8
        values = [
            jnp.where(mask, values[at + 1], values[at]) for at in range(0, len(values), 2)
        ]
    return values[0]


def block_scales(scales, outer, column):
    count = scales.shape[0]
    line = lax.broadcasted_iota(jnp.int32, outer.shape, 0)
    line = jnp.sum(jnp.where(line == column, outer, 0.0), axis=0, keepdims=True)
    rows = lax.broadcasted_iota(jnp.int32, (count, count), 0)
    lanes = lax.broadcasted_iota(jnp.int32, (count, count), 1)
    second = jnp.sum(jnp.where(rows == lanes, line, 0.0), axis=1, keepdims=True)
    return (scales.astype(F32) + 1.0) / 256.0 * second


def weights_kernel(
    x, key_codes, value_codes, key_scales, value_scales, outer, gain,
    out_a, out_b, scaled, squares, scales,
):
    block = pl.program_id(0)
    depth = key_codes.shape[0]
    columns = outer.shape[0] // 2

    @pl.when(block == 0)
    def _():
        squares[...] = jnp.zeros(squares.shape, F32)
        for at in range(CORE_HEADS):
            head = lax.axis_index("rep") * CORE_HEADS + at
            column = head // (KV_HEADS // columns)
            lanes = slice(at * HEAD_DIM, (at + 1) * HEAD_DIM)
            scales[2 * at] = block_scales(key_scales[:, lanes], outer[...], column)
            scales[2 * at + 1] = block_scales(value_scales[:, lanes], outer[...], columns + column)

    lane = lax.broadcasted_iota(jnp.int32, (8, 128), 1)
    table = jnp.zeros((8, 128), F32)
    for code, level in enumerate(NORMAL_FLOAT_LEVELS):
        table = jnp.where(lane == code, level, table)

    def body(step, _):
        begin = pl.multiple_of(step * QBLOCK, QBLOCK)
        codes = []
        for at in range(CORE_HEADS):
            lanes = slice(at * HEAD_DIM, (at + 1) * HEAD_DIM)
            rows = pl.ds(begin, QBLOCK)
            codes.append((key_codes[rows, lanes], value_codes[rows, lanes]))
        row = pl.ds(block * (depth // QBLOCK) + step, 1)
        results = []
        for at, (key, value) in enumerate(codes):
            results.append(
                (
                    (gathered_levels(table, key) * scales[2 * at, row, :]).astype(BF16),
                    (selected_levels(value) * scales[2 * at + 1, row, :]).astype(BF16),
                )
            )
        rows = pl.ds(pl.multiple_of(block * depth + begin, QBLOCK), QBLOCK)
        for at, (key, value) in enumerate(results):
            out = (out_a, out_b)[at // 2]
            out[at % 2, rows, :HEAD_DIM] = key
            out[at % 2, rows, HEAD_DIM:] = value
        return 0

    lax.fori_loop(0, depth // QBLOCK, body, 0)

    width = x.shape[2]
    begin = pl.multiple_of(block * width, 128)
    for prompt in range(x.shape[0]):
        wide = x[prompt].astype(F32)
        scaled[prompt, :, pl.ds(begin, width)] = (wide * gain[...]).astype(BF16)
        squares[prompt] += token_rows(jnp.sum(wide * wide, axis=1, keepdims=True))


def dequantize(x, codes, scales, outer, gain):
    per_rep, _, features = x.shape
    depth = min(256, features)
    width = CORE_HEADS * HEAD_DIM
    rep = lambda: lax.axis_index("rep")
    x, codes, scales, outer, gain = in_hbm(x, codes, scales, outer, gain)
    weight = jax.ShapeDtypeStruct((2, features, 2 * HEAD_DIM), BF16)
    return pl.pallas_call(
        weights_kernel,
        grid=(features // depth,),
        in_specs=[
            pl.BlockSpec((per_rep, STRETCH, depth), lambda k: (0, 0, k)),
            pl.BlockSpec((depth, width), lambda k: (k, rep())),
            pl.BlockSpec((depth, width), lambda k: (k, 2 + rep())),
            pl.BlockSpec((scales.shape[0], width), lambda k: (0, rep())),
            pl.BlockSpec((scales.shape[0], width), lambda k: (0, 2 + rep())),
            pl.BlockSpec(outer.shape, lambda k: (0, 0)),
            pl.BlockSpec((1, depth), lambda k: (0, k)),
        ],
        out_specs=[VMEM] * 4,
        out_shape=[
            weight,
            weight,
            jax.ShapeDtypeStruct(x.shape, BF16),
            jax.ShapeDtypeStruct((per_rep, 8, 128), F32),
        ],
        scratch_shapes=[pltpu.VMEM((2 * CORE_HEADS, scales.shape[0], HEAD_DIM), F32)],
        compiler_params=pltpu.CompilerParams(vmem_limit_bytes=32 * MIB),
        cost_estimate=pl.CostEstimate(
            flops=32 * codes.size, bytes_accessed=codes.size * 2, transcendentals=0
        ),
        name="dequantize",
    )(x, codes, codes, scales, scales, outer, gain)


def prompt_of(targets, owner):
    prompt = jnp.int32(-1)
    for at in range(targets.shape[0]):
        prompt = jnp.where(targets[at] == owner, at, prompt)
    return prompt


def lines_of(targets, distance, own, squares, other, gain, line, total):
    per_rep = own.shape[0]
    prompt = prompt_of(targets, owner_at(distance))
    at = lax.rem(jnp.maximum(prompt, 0), per_rep)
    is_own = prompt // per_rep == lax.axis_index("rep")

    @pl.when((prompt >= 0) & is_own)
    def _():
        line[...] = own[at]
        total[...] = squares[at]

    @pl.when((prompt >= 0) & jnp.logical_not(is_own))
    def _():
        wide = other[at].astype(F32)
        line[...] = (wide * gain[...]).astype(BF16)
        total[...] = token_rows(jnp.sum(wide * wide, axis=1, keepdims=True))

    @pl.when(prompt < 0)
    def _():
        line[...] = jnp.zeros(line.shape, BF16)
        total[...] = jnp.zeros(total.shape, F32)


def line_specs(distances, x):
    return [
        jax.ShapeDtypeStruct((len(distances) * STRETCH, x.shape[2]), BF16),
        jax.ShapeDtypeStruct((len(distances), 8, 128), F32),
    ]


def first_kernel(distances, targets, own, squares, other, gain, weight, *refs):
    right, left, terms, lines, totals = refs
    for item, distance in enumerate(distances):
        line = lines.at[item * STRETCH : (item + 1) * STRETCH]
        lines_of(targets, distance, own, squares, other, gain, line, totals.at[item])
    products(distances, lines, totals, weight, right, left, terms)


def second_kernel(distances, lines, totals, weight, *refs):
    products(distances, lines, totals, weight, *refs)


def products(distances, lines, totals, weight, right, left, terms):
    for head in range(2):
        product = jnp.dot(lines[...], weight[head], preferred_element_type=F32)
        rows = slice(head * STRETCH, (head + 1) * STRETCH)
        right[rows] = product[:STRETCH, :HEAD_DIM].astype(BF16)
        left[rows] = product[:STRETCH, HEAD_DIM:].astype(BF16)
        for item in range(1, len(distances)):
            part = product[item * STRETCH : (item + 1) * STRETCH]
            begin = head * STRETCH
            terms[item - 1, begin : begin + STRETCH] = part[:, :HEAD_DIM]
            begin += 2 * STRETCH
            terms[item - 1, begin : begin + STRETCH] = part[:, HEAD_DIM:]
    for item in range(1, len(distances)):
        terms[item - 1, 4 * STRETCH :] = totals[item]
    right[2 * STRETCH :] = two_pieces(totals[0])


def first_shapes(distances):
    rows = 2 * STRETCH
    return [
        jax.ShapeDtypeStruct((rows + TAIL, HEAD_DIM), BF16),
        jax.ShapeDtypeStruct((rows, HEAD_DIM), BF16),
        jax.ShapeDtypeStruct((len(distances) - 1, 2 * rows + 8, HEAD_DIM), F32),
    ]


def project_cost(distances, weight):
    return pl.CostEstimate(
        flops=len(distances) * STRETCH * weight.size * 2,
        bytes_accessed=weight.size,
        transcendentals=0,
    )


def project_first(distances, targets, own, squares, other, gain, weight):
    return pl.pallas_call(
        functools.partial(first_kernel, distances),
        in_specs=[SMEM] + [VMEM] * 5,
        out_specs=[VMEM] * 5,
        out_shape=first_shapes(distances) + line_specs(distances, own),
        compiler_params=pltpu.CompilerParams(vmem_limit_bytes=24 * MIB),
        cost_estimate=project_cost(distances, weight),
        name="project_first",
    )(targets, own, squares, other, gain, weight)


def project_second(distances, lines, totals, weight):
    return pl.pallas_call(
        functools.partial(second_kernel, distances),
        in_specs=[VMEM] * 3,
        out_specs=[VMEM] * 3,
        out_shape=first_shapes(distances),
        compiler_params=pltpu.CompilerParams(vmem_limit_bytes=24 * MIB),
        cost_estimate=project_cost(distances, weight),
        name="project_second",
    )(lines, totals, weight)


def project_kernel(
    distances, targets, own, squares, other, gain, weight_a, weight_b, out_a, out_b, lines, totals
):
    for item, distance in enumerate(distances):
        line = lines.at[item * STRETCH : (item + 1) * STRETCH]
        lines_of(targets, distance, own, squares, other, gain, line, totals.at[item])
    for weight, out in ((weight_a, out_a), (weight_b, out_b)):
        for head in range(2):
            product = jnp.dot(lines[...], weight[head], preferred_element_type=F32)
            for item in range(len(distances)):
                part = product[item * STRETCH : (item + 1) * STRETCH]
                begin = head * STRETCH
                out[item, begin : begin + STRETCH] = part[:, :HEAD_DIM]
                begin += 2 * STRETCH
                out[item, begin : begin + STRETCH] = part[:, HEAD_DIM:]
        for item in range(len(distances)):
            out[item, 4 * STRETCH :] = totals[item]


def project(distances, targets, own, squares, other, gain, weights):
    shape = jax.ShapeDtypeStruct((len(distances), 4 * STRETCH + 8, HEAD_DIM), F32)
    line, total = line_specs(distances, own)
    return pl.pallas_call(
        functools.partial(project_kernel, distances),
        in_specs=[SMEM] + [VMEM] * 6,
        out_specs=[VMEM] * 2,
        out_shape=[shape, shape],
        scratch_shapes=[pltpu.VMEM(line.shape, BF16), pltpu.VMEM(total.shape, F32)],
        compiler_params=pltpu.CompilerParams(vmem_limit_bytes=24 * MIB),
        cost_estimate=project_cost(distances, weights[0]),
        name="project",
    )(targets, own, squares, other, gain, *weights)


def send_kernel(half, first, terms, right, left, to_right, to_left):
    rows = 4 * STRETCH
    middle = 2 * STRETCH
    if first:
        to_right[:middle] = (terms[0, :middle] + right[:middle].astype(F32)).astype(BF16)
        to_right[middle:rows] = terms[0, middle:rows].astype(BF16)
        to_left[:middle] = terms[1, :middle].astype(BF16)
        to_left[middle:rows] = (terms[1, middle:rows] + left[...].astype(F32)).astype(BF16)
    else:
        to_right[:rows] = (terms[0, :rows] + right[:rows].astype(F32)).astype(BF16)
        to_left[:rows] = (terms[1, :rows] + left[:rows].astype(F32)).astype(BF16)
    if half == 0:
        right_sum, left_sum = terms[0, rows:], terms[1, rows:]
        right_sum += one_piece(right[middle if first else rows :])
        if not first:
            left_sum += one_piece(left[rows:])
        to_right[rows:] = two_pieces(right_sum)
        to_left[rows:] = two_pieces(left_sum)


def sends(half, first, terms, right, left):
    rows = 4 * STRETCH + (TAIL if half == 0 else 0)
    shape = jax.ShapeDtypeStruct((rows, HEAD_DIM), BF16)
    return pl.pallas_call(
        functools.partial(send_kernel, half, first),
        in_specs=[VMEM] * 3,
        out_specs=[VMEM] * 2,
        out_shape=[shape, shape],
        compiler_params=pltpu.CompilerParams(vmem_limit_bytes=16 * MIB),
        name="sends",
    )(terms, right, left)


def prepare_kernel(targets, queries, starts, turns, grouped, rotary):
    for head in range(KV_HEADS):
        for member in range(GROUP):
            begin = (head * GROUP + member) * HEAD_DIM
            rows = slice(member * STEPS, (member + 1) * STEPS)
            grouped[head, rows] = queries[0, :, begin : begin + HEAD_DIM]
    row = pl.ds(jnp.maximum(prompt_of(targets, lax.axis_index("tp")), 0), 1)
    cosine, sine = starts[0, row, :], starts[1, row, :]
    lane = lax.broadcasted_iota(jnp.int32, turns.shape[1:], 1)
    rotary[0] = turns[0] * cosine - turns[1] * sine
    sine = turns[1] * cosine + turns[0] * sine
    rotary[1] = jnp.where(lane < HEAD_DIM // 2, -sine, sine)


def prepare(targets, queries, starts, turns):
    return pl.pallas_call(
        prepare_kernel,
        in_specs=[SMEM] + [VMEM] * 3,
        out_specs=[VMEM] * 2,
        out_shape=[
            jax.ShapeDtypeStruct((KV_HEADS, ROWS, HEAD_DIM), BF16),
            jax.ShapeDtypeStruct(turns.shape, F32),
        ],
        compiler_params=pltpu.CompilerParams(vmem_limit_bytes=16 * MIB),
        name="prepare",
    )(targets, queries, starts, turns)


def cache_kernel(part, targets, lengths, stored, q, cache, new, out):
    scaling = HEAD_DIM ** (-0.5)
    dims = (((1,), (1,)), ((), ()))
    here = lax.axis_index("tp")
    rep = lax.axis_index("rep")
    length = cache.shape[1]
    prompt = prompt_of(targets, here)
    handed = lengths[jnp.maximum(prompt, 0)] - STRETCH
    span = jnp.where(prompt >= 0, handed, stored[0]) - rep * length
    allowed = lax.broadcasted_iota(jnp.int32, (ROWS, length), 1) < span
    second_step = lax.broadcasted_iota(jnp.int32, (ROWS, 1), 0) % STEPS == 1
    for at in range(CORE_HEADS):
        head = part * CORE_HEADS + at
        key_lanes = slice(head * HEAD_DIM, (head + 1) * HEAD_DIM)
        value_lanes = slice((KV_HEADS + head) * HEAD_DIM, (KV_HEADS + head + 1) * HEAD_DIM)
        query = q[head]
        wide = query.astype(F32)
        scores = lax.dot_general(query, cache[0, :, key_lanes], dims, preferred_element_type=F32)
        scores = jnp.where(allowed, scores * scaling, NEGATIVE)
        highest = jnp.max(scores, axis=1, keepdims=True)
        fresh = []
        for step in range(STEPS):
            key = new[0, step : step + 1, key_lanes].astype(F32)
            score = jnp.sum(wide * key, axis=1, keepdims=True) * scaling
            shown = rep == 0 if step == 0 else second_step & (rep == 0)
            score = jnp.where(shown, score, NEGATIVE)
            highest = jnp.maximum(highest, score)
            fresh.append(score)
        some = highest > 0.5 * NEGATIVE
        highest = jnp.where(some, highest, 0.0)
        weight = jnp.exp(scores - highest)
        totals = jnp.sum(weight, axis=1, keepdims=True)
        sums = jnp.dot(weight.astype(BF16), cache[0, :, value_lanes], preferred_element_type=F32)
        for step in range(STEPS):
            share = jnp.exp(fresh[step] - highest)
            totals += share
            value = new[0, step : step + 1, value_lanes].astype(F32)
            sums += share.astype(BF16).astype(F32) * value
        totals = jnp.where(some, totals, 1.0)
        out[at, :ROWS] = (sums / totals).astype(BF16)
        out[at, ROWS:] = pieces_tail(jnp.where(some, highest + jnp.log(totals), NEGATIVE))


def cache_attention(part, targets, lengths, stored, grouped, kv_cache, new_kv):
    return pl.pallas_call(
        functools.partial(cache_kernel, part),
        in_specs=[SMEM] * 3 + [VMEM] * 3,
        out_specs=VMEM,
        out_shape=jax.ShapeDtypeStruct((CORE_HEADS, PART, HEAD_DIM), BF16),
        compiler_params=pltpu.CompilerParams(vmem_limit_bytes=16 * MIB),
        cost_estimate=pl.CostEstimate(
            flops=2 * grouped.size * kv_cache.shape[1],
            bytes_accessed=kv_cache.size,
            transcendentals=CORE_HEADS * ROWS * kv_cache.shape[1],
        ),
        name="cache_attention",
    )(targets, lengths, stored, grouped, kv_cache, new_kv)


def final_kernel(
    targets, rotary, own_a, own_b, right_a, left_a, right_b, left_b, grouped, *refs
):
    cached, out = refs
    scaling = HEAD_DIM ** (-0.5)
    dims = (((1,), (1,)), ((), ()))
    mine = own_a.shape[0] - 1
    rep = lax.axis_index("rep")
    first = rep * CORE_HEADS
    prompt = prompt_of(targets, lax.axis_index("tp"))
    cosine, sine = rotary[0], rotary[1]
    rows = 4 * STRETCH
    squares = own_a[mine, rows:] + one_piece(right_a[rows:]) + one_piece(left_a[rows:])
    scale = token_column(lax.rsqrt(squares / D + EPSILON))
    for head in range(CORE_HEADS):
        own, right, left = ((own_a, right_a, left_a), (own_b, right_b, left_b))[head // 2]
        at = slice(head % 2 * STRETCH, (head % 2 + 1) * STRETCH)
        keys = own[mine, at] + right[at].astype(F32) + left[at].astype(F32)
        at = slice((2 + head % 2) * STRETCH, (3 + head % 2) * STRETCH)
        values = own[mine, at] + right[at].astype(F32) + left[at].astype(F32)
        keys = (keys * scale).astype(BF16).astype(F32)
        values = (values * scale).astype(BF16)
        keys = keys * cosine + pltpu.roll(keys, HEAD_DIM // 2, 1) * sine
        scores = lax.dot_general(
            grouped[first + head], keys.astype(BF16), dims, preferred_element_type=F32
        )
        scores = scores * scaling
        highest = jnp.max(scores, axis=1, keepdims=True)
        weight = jnp.exp(scores - highest)
        totals = jnp.sum(weight, axis=1, keepdims=True)
        sums = jnp.dot(weight.astype(BF16), values, preferred_element_type=F32) / totals
        logs = jnp.where(prompt >= 0, highest + jnp.log(totals), NEGATIVE)
        parts = [cached[0, first + head], cached[1, first + head]]
        logs = [tail_pieces(part[ROWS:]) for part in parts] + [logs]
        sums = [part[:ROWS].astype(F32) for part in parts] + [sums]
        highest = functools.reduce(jnp.maximum, logs)
        shares = [jnp.exp(log - highest) for log in logs]
        total = functools.reduce(jnp.add, shares)
        joined = functools.reduce(jnp.add, [share * part for share, part in zip(shares, sums)])
        result = (joined / total).astype(BF16)
        for member in range(GROUP):
            begin = (head * GROUP + member) * HEAD_DIM
            out[0, :, begin : begin + HEAD_DIM] = result[member * STEPS : (member + 1) * STEPS]


def finish(targets, rotary, own, arrived, grouped, cached):
    width = CORE_HEADS * GROUP * HEAD_DIM
    return pl.pallas_call(
        final_kernel,
        in_specs=[SMEM] + [VMEM] * 9,
        out_specs=VMEM,
        out_shape=jax.ShapeDtypeStruct((1, STEPS, width), BF16),
        compiler_params=pltpu.CompilerParams(vmem_limit_bytes=16 * MIB),
        name="finish",
    )(targets, rotary, *own, *arrived, grouped, cached)


def rotary_turns():
    half = np.arange(HEAD_DIM // 2, dtype=np.float64) / (HEAD_DIM // 2)
    frequency = ROTARY_BASE ** (-np.concatenate([half, half]))
    angles = np.arange(STRETCH, dtype=np.float64)[:, None] * frequency
    return frequency.astype(np.float32), np.stack([np.cos(angles), np.sin(angles)]).astype(np.float32)


def per_device(
    stretch,
    norm_gain,
    kv_codes,
    scale_codes,
    outer_scales,
    prompt_lengths,
    target_rows,
    cache_lengths,
    kv_cache,
    queries,
    new_kv,
):
    count = lax.axis_size("tp")
    half = count // 2
    lines = stretch.transpose(1, 0, 2)
    gain = norm_gain.reshape(1, -1)
    ring = [ring_device(at, count) for at in range(count)]
    to_right = [(ring[at], ring[(at + 1) % count]) for at in range(count)]
    to_left = [(ring[at], ring[at - 1]) for at in range(count)]

    def pass_on(right, left):
        return lax.ppermute(right, "tp", to_right), lax.ppermute(left, "tp", to_left)

    other = lax.ppermute(lines, "rep", [(0, 1), (1, 0)])
    first_half, second_half, own, squares = dequantize(
        lines, kv_codes, scale_codes, outer_scales.T, gain
    )
    frequency, turns = rotary_turns()
    start = (prompt_lengths - STRETCH).astype(F32)[:, None] * jnp.asarray(frequency)
    starts = jnp.stack([jnp.cos(start), jnp.sin(start)])
    targets, second_half = lax.optimization_barrier((target_rows, second_half))
    grouped, rotary = prepare(targets, queries, starts, jnp.asarray(turns))

    gain, second_half, grouped, rotary = lax.optimization_barrier(
        (gain, second_half, grouped, rotary)
    )
    distances = [half, half - 1, 1 - half]
    right, left, terms_a, lines_here, totals = project_first(
        distances, target_rows, own, squares, other, gain, first_half
    )
    arrived = [pass_on(right, left), None]
    right, left, terms_b = project_second(distances, lines_here, totals, second_half)
    arrived[1] = pass_on(right, left)
    terms = [terms_a, terms_b]

    targets = target_rows
    cached = []
    for distance in range(half - 1, 0, -1):
        if distance < half - 1:
            distances = [distance, -distance] + ([0] if distance == 1 else [])
            terms = list(
                project(distances, targets, own, squares, other, gain, [first_half, second_half])
            )
        for part in range(2):
            right, left = sends(part, distance == half - 1, terms[part], *arrived[part])
            if part == 0:
                right, cached, terms[1] = lax.optimization_barrier((right, cached, terms[1]))
            targets, _ = lax.optimization_barrier((target_rows, right))
            arrived[part] = pass_on(right, left)
        if distance in (2, 3):
            cached.append(
                cache_attention(
                    3 - distance, targets, prompt_lengths, cache_lengths, grouped, kv_cache, new_kv
                )
            )

    cached, _ = lax.optimization_barrier((cached, right))
    cached = lax.all_gather(jnp.concatenate(cached), "rep")
    out = finish(target_rows, rotary, terms, [*arrived[0], *arrived[1]], grouped, cached)
    return lax.all_gather(out, "rep", axis=2, tiled=True)


def solution(mesh):
    in_specs = (
        P(None, ("grp", "rep"), "tp"),
        P("tp"),
        P("tp", None),
        P("tp", None),
        P("tp", None),
        P("grp"),
        P("grp"),
        P(("grp", "tp")),
        P(("grp", "tp"), "rep", None),
        P(("grp", "tp"), None, None),
        P(("grp", "tp"), None, None),
    )
    out_specs = P(("grp", "tp"), None, None)
    return jax.shard_map(
        per_device, mesh=mesh, in_specs=in_specs, out_specs=out_specs, check_vma=False
    )
```

```python
import functools
import math

import jax
import jax.numpy as jnp
import numpy as np
from jax import lax
from jax.experimental import pallas as pl
from jax.experimental.pallas import tpu as pltpu
from jax.sharding import PartitionSpec as P

D = 16384
HEADS = 128
KV_HEADS = 8
HEAD_DIM = 128
STRETCH = 192
STEPS = 2
QBLOCK = 64
GROUP = HEADS // KV_HEADS
ROWS = GROUP * STEPS
TAIL = 16
PART = ROWS + TAIL
CORE_HEADS = KV_HEADS // 2
NORMAL_FLOAT_LEVELS = [
    -1.0,
    -0.6961928009986877,
    -0.5250730514526367,
    -0.39491748809814453,
    -0.28444138169288635,
    -0.18477343022823334,
    -0.09105003625154495,
    0.0,
    0.07958029955625534,
    0.16093020141124725,
    0.24611230194568634,
    0.33791524171829224,
    0.44070982933044434,
    0.5626170039176941,
    0.7229568362236023,
    1.0,
]
ROTARY_BASE = 500000.0
EPSILON = 1e-05
NEGATIVE = -1e30
BF16 = jnp.bfloat16
F32 = jnp.float32
MIB = 1024 * 1024
VMEM = pl.BlockSpec(memory_space=pltpu.VMEM)
SMEM = pl.BlockSpec(memory_space=pltpu.SMEM)


def in_hbm(*arrays):
    return [pltpu.with_memory_space_constraint(array, pltpu.HBM) for array in arrays]


def ring_device(place, count):
    half = count // 2
    if isinstance(place, int):
        return 2 * place if place < half else 2 * (count - 1 - place) + 1
    return jnp.where(place < half, 2 * place, 2 * (count - 1 - place) + 1)


def owner_at(distance):
    count = lax.axis_size("tp")
    here = lax.axis_index("tp")
    place = jnp.where(here % 2 == 0, here // 2, count - 1 - here // 2)
    return ring_device((place + distance + count) % count, count)


def turned(column):
    rows = lax.broadcasted_iota(jnp.int32, (column.shape[0], 128), 0)
    lanes = lax.broadcasted_iota(jnp.int32, (column.shape[0], 128), 1)
    return jnp.sum(jnp.where(rows == lanes, column, 0.0), axis=0, keepdims=True)


def stood(row, count):
    rows = lax.broadcasted_iota(jnp.int32, (count, 128), 0)
    lanes = lax.broadcasted_iota(jnp.int32, (count, 128), 1)
    return jnp.sum(jnp.where(rows == lanes, row, 0.0), axis=1, keepdims=True)


def token_rows(column):
    at = lax.broadcasted_iota(jnp.int32, (8, 128), 0)
    ends = turned(column[128:])
    return jnp.where(at == 0, turned(column[:128]), jnp.where(at == 1, ends, 0.0))


def token_column(rows):
    return jnp.concatenate([stood(rows[0:1], 128), stood(rows[1:2], STRETCH - 128)], axis=0)


def two_pieces(rows):
    high = rows.astype(BF16).astype(F32)
    return jnp.concatenate([high, rows - high], axis=0).astype(BF16)


def one_piece(rows):
    rows = rows.astype(F32)
    return rows[:8] + rows[8:]


def pieces_tail(logs):
    row = turned(logs)
    high = row.astype(BF16).astype(F32)
    middle = (row - high).astype(BF16).astype(F32)
    low = row - high - middle
    at = lax.broadcasted_iota(jnp.int32, (TAIL, 128), 0)
    tail = jnp.where(at == 0, high, jnp.where(at == 1, middle, jnp.where(at == 2, low, 0.0)))
    return tail.astype(BF16)


def tail_pieces(tail):
    tail = tail.astype(F32)
    return stood(tail[0:1, :] + tail[1:2, :] + tail[2:3, :], ROWS)


def gathered_levels(table, codes):
    numbers = lax.GatherDimensionNumbers(
        offset_dims=(),
        collapsed_slice_dims=(1,),
        start_index_map=(1,),
        operand_batching_dims=(0,),
        start_indices_batching_dims=(0,),
    )
    return lax.gather(
        table, codes[..., None], numbers, (1, 1), mode=lax.GatherScatterMode.PROMISE_IN_BOUNDS
    )


def selected_levels(codes):
    masks = [(codes & 1) != 0, (codes & 2) != 0, (codes & 4) != 0, codes >= 8]

    def node(bit, base):
        if bit < 0:
            return jnp.float32(NORMAL_FLOAT_LEVELS[base])
        low = node(bit - 1, base)
        return jnp.where(masks[bit], node(bit - 1, base + (1 << bit)), low)

    return node(3, 0)


def block_scales(scales, outer, column):
    count = scales.shape[0]
    line = lax.broadcasted_iota(jnp.int32, outer.shape, 0)
    line = jnp.sum(jnp.where(line == column, outer, 0.0), axis=0, keepdims=True)
    rows = lax.broadcasted_iota(jnp.int32, (count, count), 0)
    lanes = lax.broadcasted_iota(jnp.int32, (count, count), 1)
    second = jnp.sum(jnp.where(rows == lanes, line, 0.0), axis=1, keepdims=True)
    return (scales.astype(F32) + 1.0) / 256.0 * second


def weights_kernel(
    x, key_codes, value_codes, key_scales, value_scales, outer, gain,
    out_a, out_b, scaled, squares, scales,
):
    block = pl.program_id(0)
    depth = key_codes.shape[0]
    columns = outer.shape[0] // 2

    @pl.when(block == 0)
    def _():
        squares[...] = jnp.zeros(squares.shape, F32)
        for at in range(CORE_HEADS):
            head = lax.axis_index("rep") * CORE_HEADS + at
            column = head // (KV_HEADS // columns)
            lanes = slice(at * HEAD_DIM, (at + 1) * HEAD_DIM)
            scales[2 * at] = block_scales(key_scales[:, lanes], outer[...], column)
            scales[2 * at + 1] = block_scales(value_scales[:, lanes], outer[...], columns + column)

    lane = lax.broadcasted_iota(jnp.int32, (8, 128), 1)
    table = jnp.zeros((8, 128), F32)
    for code, level in enumerate(NORMAL_FLOAT_LEVELS):
        table = jnp.where(lane == code, level, table)

    def body(step, _):
        begin = pl.multiple_of(step * QBLOCK, QBLOCK)
        row = pl.ds(block * (depth // QBLOCK) + step, 1)
        for at in range(CORE_HEADS):
            lanes = slice(at * HEAD_DIM, (at + 1) * HEAD_DIM)
            out = (out_a, out_b)[at // 2]
            key_scale, value_scale = scales[2 * at, row, :], scales[2 * at + 1, row, :]
            for tile in range(QBLOCK // 16):
                rows = pl.ds(pl.multiple_of(begin + 16 * tile, 16), 16)
                key, value = key_codes[rows, lanes], value_codes[rows, lanes]
                keys = [gathered_levels(table, key[half : half + 8]) for half in (0, 8)]
                values = [selected_levels(value[half : half + 8]) for half in (0, 8)]
                rows = pl.ds(pl.multiple_of(block * depth + begin + 16 * tile, 16), 16)
                keys = jnp.concatenate([level * key_scale for level in keys], axis=0)
                values = jnp.concatenate([level * value_scale for level in values], axis=0)
                out[at % 2, rows, :HEAD_DIM] = keys.astype(BF16)
                out[at % 2, rows, HEAD_DIM:] = values.astype(BF16)
        return 0

    lax.fori_loop(0, depth // QBLOCK, body, 0)

    width = x.shape[2]
    begin = pl.multiple_of(block * width, 128)
    for prompt in range(x.shape[0]):
        wide = x[prompt].astype(F32)
        scaled[prompt, :, pl.ds(begin, width)] = (wide * gain[...]).astype(BF16)
        squares[prompt] += token_rows(jnp.sum(wide * wide, axis=1, keepdims=True))


def dequantize(x, codes, scales, outer, gain):
    per_rep, _, features = x.shape
    depth = min(256, features)
    width = CORE_HEADS * HEAD_DIM
    rep = lambda: lax.axis_index("rep")
    x, codes, scales, outer, gain = in_hbm(x, codes, scales, outer, gain)
    weight = jax.ShapeDtypeStruct((2, features, 2 * HEAD_DIM), BF16)
    return pl.pallas_call(
        weights_kernel,
        grid=(features // depth,),
        in_specs=[
            pl.BlockSpec((per_rep, STRETCH, depth), lambda k: (0, 0, k)),
            pl.BlockSpec((depth, width), lambda k: (k, rep())),
            pl.BlockSpec((depth, width), lambda k: (k, 2 + rep())),
            pl.BlockSpec((scales.shape[0], width), lambda k: (0, rep())),
            pl.BlockSpec((scales.shape[0], width), lambda k: (0, 2 + rep())),
            pl.BlockSpec(outer.shape, lambda k: (0, 0)),
            pl.BlockSpec((1, depth), lambda k: (0, k)),
        ],
        out_specs=[VMEM] * 4,
        out_shape=[
            weight,
            weight,
            jax.ShapeDtypeStruct(x.shape, BF16),
            jax.ShapeDtypeStruct((per_rep, 8, 128), F32),
        ],
        scratch_shapes=[pltpu.VMEM((2 * CORE_HEADS, scales.shape[0], HEAD_DIM), F32)],
        compiler_params=pltpu.CompilerParams(vmem_limit_bytes=32 * MIB),
        cost_estimate=pl.CostEstimate(
            flops=32 * codes.size, bytes_accessed=codes.size * 2, transcendentals=0
        ),
        name="dequantize",
    )(x, codes, codes, scales, scales, outer, gain)


def prompt_of(targets, owner):
    prompt = jnp.int32(-1)
    for at in range(targets.shape[0]):
        prompt = jnp.where(targets[at] == owner, at, prompt)
    return prompt


def lines_of(targets, distance, own, squares, other, gain, line, total):
    per_rep = own.shape[0]
    prompt = prompt_of(targets, owner_at(distance))
    at = lax.rem(jnp.maximum(prompt, 0), per_rep)
    is_own = prompt // per_rep == lax.axis_index("rep")

    @pl.when((prompt >= 0) & is_own)
    def _():
        line[...] = own[at]
        total[...] = squares[at]

    @pl.when((prompt >= 0) & jnp.logical_not(is_own))
    def _():
        wide = other[at].astype(F32)
        line[...] = (wide * gain[...]).astype(BF16)
        total[...] = token_rows(jnp.sum(wide * wide, axis=1, keepdims=True))

    @pl.when(prompt < 0)
    def _():
        line[...] = jnp.zeros(line.shape, BF16)
        total[...] = jnp.zeros(total.shape, F32)


def line_specs(distances, x):
    return [
        jax.ShapeDtypeStruct((len(distances) * STRETCH, x.shape[2]), BF16),
        jax.ShapeDtypeStruct((len(distances), 8, 128), F32),
    ]


def first_kernel(distances, targets, own, squares, other, gain, weight, *refs):
    right, left, terms, lines, totals = refs
    for item, distance in enumerate(distances):
        line = lines.at[item * STRETCH : (item + 1) * STRETCH]
        lines_of(targets, distance, own, squares, other, gain, line, totals.at[item])
    products(distances, lines, totals, weight, right, left, terms)


def second_kernel(distances, lines, totals, weight, *refs):
    products(distances, lines, totals, weight, *refs)


def products(distances, lines, totals, weight, right, left, terms):
    for head in range(2):
        product = jnp.dot(lines[...], weight[head], preferred_element_type=F32)
        rows = slice(head * STRETCH, (head + 1) * STRETCH)
        right[rows] = product[:STRETCH, :HEAD_DIM].astype(BF16)
        left[rows] = product[:STRETCH, HEAD_DIM:].astype(BF16)
        for item in range(1, len(distances)):
            part = product[item * STRETCH : (item + 1) * STRETCH]
            begin = head * STRETCH
            terms[item - 1, begin : begin + STRETCH] = part[:, :HEAD_DIM]
            begin += 2 * STRETCH
            terms[item - 1, begin : begin + STRETCH] = part[:, HEAD_DIM:]
    for item in range(1, len(distances)):
        terms[item - 1, 4 * STRETCH :] = totals[item]
    right[2 * STRETCH :] = two_pieces(totals[0])


def first_shapes(distances):
    rows = 2 * STRETCH
    return [
        jax.ShapeDtypeStruct((rows + TAIL, HEAD_DIM), BF16),
        jax.ShapeDtypeStruct((rows, HEAD_DIM), BF16),
        jax.ShapeDtypeStruct((len(distances) - 1, 2 * rows + 8, HEAD_DIM), F32),
    ]


def project_cost(distances, weight):
    return pl.CostEstimate(
        flops=len(distances) * STRETCH * weight.size * 2,
        bytes_accessed=weight.size,
        transcendentals=0,
    )


def project_first(distances, targets, own, squares, other, gain, weight):
    return pl.pallas_call(
        functools.partial(first_kernel, distances),
        in_specs=[SMEM] + [VMEM] * 5,
        out_specs=[VMEM] * 5,
        out_shape=first_shapes(distances) + line_specs(distances, own),
        compiler_params=pltpu.CompilerParams(vmem_limit_bytes=24 * MIB),
        cost_estimate=project_cost(distances, weight),
        name="project_first",
    )(targets, own, squares, other, gain, weight)


def project_second(distances, lines, totals, weight):
    return pl.pallas_call(
        functools.partial(second_kernel, distances),
        in_specs=[VMEM] * 3,
        out_specs=[VMEM] * 3,
        out_shape=first_shapes(distances),
        compiler_params=pltpu.CompilerParams(vmem_limit_bytes=24 * MIB),
        cost_estimate=project_cost(distances, weight),
        name="project_second",
    )(lines, totals, weight)


def project_kernel(
    distances, targets, own, squares, other, gain, weight_a, weight_b, out_a, out_b, lines, totals
):
    for item, distance in enumerate(distances):
        line = lines.at[item * STRETCH : (item + 1) * STRETCH]
        lines_of(targets, distance, own, squares, other, gain, line, totals.at[item])
    for weight, out in ((weight_a, out_a), (weight_b, out_b)):
        for head in range(2):
            product = jnp.dot(lines[...], weight[head], preferred_element_type=F32)
            for item in range(len(distances)):
                part = product[item * STRETCH : (item + 1) * STRETCH]
                begin = head * STRETCH
                out[item, begin : begin + STRETCH] = part[:, :HEAD_DIM]
                begin += 2 * STRETCH
                out[item, begin : begin + STRETCH] = part[:, HEAD_DIM:]
        for item in range(len(distances)):
            out[item, 4 * STRETCH :] = totals[item]


def project(distances, targets, own, squares, other, gain, weights):
    shape = jax.ShapeDtypeStruct((len(distances), 4 * STRETCH + 8, HEAD_DIM), F32)
    line, total = line_specs(distances, own)
    return pl.pallas_call(
        functools.partial(project_kernel, distances),
        in_specs=[SMEM] + [VMEM] * 6,
        out_specs=[VMEM] * 2,
        out_shape=[shape, shape],
        scratch_shapes=[pltpu.VMEM(line.shape, BF16), pltpu.VMEM(total.shape, F32)],
        compiler_params=pltpu.CompilerParams(vmem_limit_bytes=24 * MIB),
        cost_estimate=project_cost(distances, weights[0]),
        name="project",
    )(targets, own, squares, other, gain, *weights)


def send_kernel(half, first, terms, right, left, to_right, to_left):
    rows = 4 * STRETCH
    middle = 2 * STRETCH
    if first:
        to_right[:middle] = (terms[0, :middle] + right[:middle].astype(F32)).astype(BF16)
        to_right[middle:rows] = terms[0, middle:rows].astype(BF16)
        to_left[:middle] = terms[1, :middle].astype(BF16)
        to_left[middle:rows] = (terms[1, middle:rows] + left[...].astype(F32)).astype(BF16)
    else:
        to_right[:rows] = (terms[0, :rows] + right[:rows].astype(F32)).astype(BF16)
        to_left[:rows] = (terms[1, :rows] + left[:rows].astype(F32)).astype(BF16)
    if half == 0:
        right_sum, left_sum = terms[0, rows:], terms[1, rows:]
        right_sum += one_piece(right[middle if first else rows :])
        if not first:
            left_sum += one_piece(left[rows:])
        to_right[rows:] = two_pieces(right_sum)
        to_left[rows:] = two_pieces(left_sum)


def sends(half, first, terms, right, left):
    rows = 4 * STRETCH + (TAIL if half == 0 else 0)
    shape = jax.ShapeDtypeStruct((rows, HEAD_DIM), BF16)
    return pl.pallas_call(
        functools.partial(send_kernel, half, first),
        in_specs=[VMEM] * 3,
        out_specs=[VMEM] * 2,
        out_shape=[shape, shape],
        compiler_params=pltpu.CompilerParams(vmem_limit_bytes=16 * MIB),
        name="sends",
    )(terms, right, left)


def prepare_kernel(targets, queries, starts, turns, grouped, rotary):
    for head in range(KV_HEADS):
        for member in range(GROUP):
            begin = (head * GROUP + member) * HEAD_DIM
            rows = slice(member * STEPS, (member + 1) * STEPS)
            grouped[head, rows] = queries[0, :, begin : begin + HEAD_DIM]
    row = pl.ds(jnp.maximum(prompt_of(targets, lax.axis_index("tp")), 0), 1)
    cosine, sine = starts[0, row, :], starts[1, row, :]
    lane = lax.broadcasted_iota(jnp.int32, turns.shape[1:], 1)
    rotary[0] = turns[0] * cosine - turns[1] * sine
    sine = turns[1] * cosine + turns[0] * sine
    rotary[1] = jnp.where(lane < HEAD_DIM // 2, -sine, sine)


def prepare(targets, queries, starts, turns):
    return pl.pallas_call(
        prepare_kernel,
        in_specs=[SMEM] + [VMEM] * 3,
        out_specs=[VMEM] * 2,
        out_shape=[
            jax.ShapeDtypeStruct((KV_HEADS, ROWS, HEAD_DIM), BF16),
            jax.ShapeDtypeStruct(turns.shape, F32),
        ],
        compiler_params=pltpu.CompilerParams(vmem_limit_bytes=16 * MIB),
        name="prepare",
    )(targets, queries, starts, turns)


def cache_kernel(part, targets, lengths, stored, q, cache, new, out):
    scaling = HEAD_DIM ** (-0.5)
    dims = (((1,), (1,)), ((), ()))
    here = lax.axis_index("tp")
    rep = lax.axis_index("rep")
    length = cache.shape[1]
    prompt = prompt_of(targets, here)
    handed = lengths[jnp.maximum(prompt, 0)] - STRETCH
    span = jnp.where(prompt >= 0, handed, stored[0]) - rep * length
    allowed = lax.broadcasted_iota(jnp.int32, (ROWS, length), 1) < span
    second_step = lax.broadcasted_iota(jnp.int32, (ROWS, 1), 0) % STEPS == 1
    for at in range(CORE_HEADS):
        head = part * CORE_HEADS + at
        key_lanes = slice(head * HEAD_DIM, (head + 1) * HEAD_DIM)
        value_lanes = slice((KV_HEADS + head) * HEAD_DIM, (KV_HEADS + head + 1) * HEAD_DIM)
        query = q[head]
        wide = query.astype(F32)
        scores = lax.dot_general(query, cache[0, :, key_lanes], dims, preferred_element_type=F32)
        scores = jnp.where(allowed, scores * scaling, NEGATIVE)
        highest = jnp.max(scores, axis=1, keepdims=True)
        fresh = []
        for step in range(STEPS):
            key = new[0, step : step + 1, key_lanes].astype(F32)
            score = jnp.sum(wide * key, axis=1, keepdims=True) * scaling
            shown = rep == 0 if step == 0 else second_step & (rep == 0)
            score = jnp.where(shown, score, NEGATIVE)
            highest = jnp.maximum(highest, score)
            fresh.append(score)
        some = highest > 0.5 * NEGATIVE
        highest = jnp.where(some, highest, 0.0)
        weight = jnp.exp(scores - highest)
        totals = jnp.sum(weight, axis=1, keepdims=True)
        sums = jnp.dot(weight.astype(BF16), cache[0, :, value_lanes], preferred_element_type=F32)
        for step in range(STEPS):
            share = jnp.exp(fresh[step] - highest)
            totals += share
            value = new[0, step : step + 1, value_lanes].astype(F32)
            sums += share.astype(BF16).astype(F32) * value
        totals = jnp.where(some, totals, 1.0)
        out[at, :ROWS] = (sums / totals).astype(BF16)
        out[at, ROWS:] = pieces_tail(jnp.where(some, highest + jnp.log(totals), NEGATIVE))


def cache_attention(part, targets, lengths, stored, grouped, kv_cache, new_kv):
    return pl.pallas_call(
        functools.partial(cache_kernel, part),
        in_specs=[SMEM] * 3 + [VMEM] * 3,
        out_specs=VMEM,
        out_shape=jax.ShapeDtypeStruct((CORE_HEADS, PART, HEAD_DIM), BF16),
        compiler_params=pltpu.CompilerParams(vmem_limit_bytes=16 * MIB),
        cost_estimate=pl.CostEstimate(
            flops=2 * grouped.size * kv_cache.shape[1],
            bytes_accessed=kv_cache.size,
            transcendentals=CORE_HEADS * ROWS * kv_cache.shape[1],
        ),
        name="cache_attention",
    )(targets, lengths, stored, grouped, kv_cache, new_kv)


def final_kernel(
    targets, rotary, own_a, own_b, right_a, left_a, right_b, left_b, grouped, *refs
):
    cached, out = refs
    scaling = HEAD_DIM ** (-0.5)
    dims = (((1,), (1,)), ((), ()))
    mine = own_a.shape[0] - 1
    rep = lax.axis_index("rep")
    first = rep * CORE_HEADS
    prompt = prompt_of(targets, lax.axis_index("tp"))
    cosine, sine = rotary[0], rotary[1]
    rows = 4 * STRETCH
    squares = own_a[mine, rows:] + one_piece(right_a[rows:]) + one_piece(left_a[rows:])
    scale = token_column(lax.rsqrt(squares / D + EPSILON))
    for head in range(CORE_HEADS):
        own, right, left = ((own_a, right_a, left_a), (own_b, right_b, left_b))[head // 2]
        at = slice(head % 2 * STRETCH, (head % 2 + 1) * STRETCH)
        keys = own[mine, at] + right[at].astype(F32) + left[at].astype(F32)
        at = slice((2 + head % 2) * STRETCH, (3 + head % 2) * STRETCH)
        values = own[mine, at] + right[at].astype(F32) + left[at].astype(F32)
        keys = (keys * scale).astype(BF16).astype(F32)
        values = (values * scale).astype(BF16)
        keys = keys * cosine + pltpu.roll(keys, HEAD_DIM // 2, 1) * sine
        scores = lax.dot_general(
            grouped[first + head], keys.astype(BF16), dims, preferred_element_type=F32
        )
        scores = scores * scaling
        highest = jnp.max(scores, axis=1, keepdims=True)
        weight = jnp.exp(scores - highest)
        totals = jnp.sum(weight, axis=1, keepdims=True)
        sums = jnp.dot(weight.astype(BF16), values, preferred_element_type=F32) / totals
        logs = jnp.where(prompt >= 0, highest + jnp.log(totals), NEGATIVE)
        parts = [cached[0, first + head], cached[1, first + head]]
        logs = [tail_pieces(part[ROWS:]) for part in parts] + [logs]
        sums = [part[:ROWS].astype(F32) for part in parts] + [sums]
        highest = functools.reduce(jnp.maximum, logs)
        shares = [jnp.exp(log - highest) for log in logs]
        total = functools.reduce(jnp.add, shares)
        joined = functools.reduce(jnp.add, [share * part for share, part in zip(shares, sums)])
        result = (joined / total).astype(BF16)
        for member in range(GROUP):
            begin = (head * GROUP + member) * HEAD_DIM
            out[0, :, begin : begin + HEAD_DIM] = result[member * STEPS : (member + 1) * STEPS]


def finish(targets, rotary, own, arrived, grouped, cached):
    width = CORE_HEADS * GROUP * HEAD_DIM
    return pl.pallas_call(
        final_kernel,
        in_specs=[SMEM] + [VMEM] * 9,
        out_specs=VMEM,
        out_shape=jax.ShapeDtypeStruct((1, STEPS, width), BF16),
        compiler_params=pltpu.CompilerParams(vmem_limit_bytes=16 * MIB),
        name="finish",
    )(targets, rotary, *own, *arrived, grouped, cached)


def rotary_turns():
    half = np.arange(HEAD_DIM // 2, dtype=np.float64) / (HEAD_DIM // 2)
    frequency = ROTARY_BASE ** (-np.concatenate([half, half]))
    angles = np.arange(STRETCH, dtype=np.float64)[:, None] * frequency
    return frequency.astype(np.float32), np.stack([np.cos(angles), np.sin(angles)]).astype(np.float32)


def per_device(
    stretch,
    norm_gain,
    kv_codes,
    scale_codes,
    outer_scales,
    prompt_lengths,
    target_rows,
    cache_lengths,
    kv_cache,
    queries,
    new_kv,
):
    count = lax.axis_size("tp")
    half = count // 2
    lines = stretch.transpose(1, 0, 2)
    gain = norm_gain.reshape(1, -1)
    ring = [ring_device(at, count) for at in range(count)]
    to_right = [(ring[at], ring[(at + 1) % count]) for at in range(count)]
    to_left = [(ring[at], ring[at - 1]) for at in range(count)]

    def pass_on(right, left):
        return lax.ppermute(right, "tp", to_right), lax.ppermute(left, "tp", to_left)

    other = lax.ppermute(lines, "rep", [(0, 1), (1, 0)])
    first_half, second_half, own, squares = dequantize(
        lines, kv_codes, scale_codes, outer_scales.T, gain
    )
    frequency, turns = rotary_turns()
    start = (prompt_lengths - STRETCH).astype(F32)[:, None] * jnp.asarray(frequency)
    starts = jnp.stack([jnp.cos(start), jnp.sin(start)])
    targets, second_half = lax.optimization_barrier((target_rows, second_half))
    grouped, rotary = prepare(targets, queries, starts, jnp.asarray(turns))

    gain, second_half, grouped, rotary = lax.optimization_barrier(
        (gain, second_half, grouped, rotary)
    )
    distances = [half, half - 1, 1 - half]
    right, left, terms_a, lines_here, totals = project_first(
        distances, target_rows, own, squares, other, gain, first_half
    )
    arrived = [pass_on(right, left), None]
    right, left, terms_b = project_second(distances, lines_here, totals, second_half)
    arrived[1] = pass_on(right, left)
    terms = [terms_a, terms_b]

    targets = target_rows
    cached = []
    for distance in range(half - 1, 0, -1):
        if distance < half - 1:
            distances = [distance, -distance] + ([0] if distance == 1 else [])
            terms = list(
                project(distances, targets, own, squares, other, gain, [first_half, second_half])
            )
        for part in range(2):
            right, left = sends(part, distance == half - 1, terms[part], *arrived[part])
            if part == 0:
                right, cached, terms[1] = lax.optimization_barrier((right, cached, terms[1]))
            targets, _ = lax.optimization_barrier((target_rows, right))
            arrived[part] = pass_on(right, left)
        if distance in (2, 3):
            cached.append(
                cache_attention(
                    3 - distance, targets, prompt_lengths, cache_lengths, grouped, kv_cache, new_kv
                )
            )

    cached, _ = lax.optimization_barrier((cached, right))
    cached = lax.all_gather(jnp.concatenate(cached), "rep")
    out = finish(target_rows, rotary, terms, [*arrived[0], *arrived[1]], grouped, cached)
    return lax.all_gather(out, "rep", axis=2, tiled=True)


def solution(mesh):
    in_specs = (
        P(None, ("grp", "rep"), "tp"),
        P("tp"),
        P("tp", None),
        P("tp", None),
        P("tp", None),
        P("grp"),
        P("grp"),
        P(("grp", "tp")),
        P(("grp", "tp"), "rep", None),
        P(("grp", "tp"), None, None),
        P(("grp", "tp"), None, None),
    )
    out_specs = P(("grp", "tp"), None, None)
    return jax.shard_map(
        per_device, mesh=mesh, in_specs=in_specs, out_specs=out_specs, check_vma=False
    )
```

```python
import functools
import math

import jax
import jax.numpy as jnp
import numpy as np
from jax import lax
from jax.experimental import pallas as pl
from jax.experimental.pallas import tpu as pltpu
from jax.sharding import PartitionSpec as P

D = 16384
HEADS = 128
KV_HEADS = 8
HEAD_DIM = 128
STRETCH = 192
STEPS = 2
QBLOCK = 64
GROUP = HEADS // KV_HEADS
ROWS = GROUP * STEPS
TAIL = 16
PART = ROWS + TAIL
CORE_HEADS = KV_HEADS // 2
NORMAL_FLOAT_LEVELS = [
    -1.0,
    -0.6961928009986877,
    -0.5250730514526367,
    -0.39491748809814453,
    -0.28444138169288635,
    -0.18477343022823334,
    -0.09105003625154495,
    0.0,
    0.07958029955625534,
    0.16093020141124725,
    0.24611230194568634,
    0.33791524171829224,
    0.44070982933044434,
    0.5626170039176941,
    0.7229568362236023,
    1.0,
]
ROTARY_BASE = 500000.0
EPSILON = 1e-05
NEGATIVE = -1e30
BF16 = jnp.bfloat16
F32 = jnp.float32
MIB = 1024 * 1024
VMEM = pl.BlockSpec(memory_space=pltpu.VMEM)
SMEM = pl.BlockSpec(memory_space=pltpu.SMEM)


def in_hbm(*arrays):
    return [pltpu.with_memory_space_constraint(array, pltpu.HBM) for array in arrays]


def ring_device(place, count):
    half = count // 2
    if isinstance(place, int):
        return 2 * place if place < half else 2 * (count - 1 - place) + 1
    return jnp.where(place < half, 2 * place, 2 * (count - 1 - place) + 1)


def owner_at(distance):
    count = lax.axis_size("tp")
    here = lax.axis_index("tp")
    place = jnp.where(here % 2 == 0, here // 2, count - 1 - here // 2)
    return ring_device((place + distance + count) % count, count)


def turned(column):
    rows = lax.broadcasted_iota(jnp.int32, (column.shape[0], 128), 0)
    lanes = lax.broadcasted_iota(jnp.int32, (column.shape[0], 128), 1)
    return jnp.sum(jnp.where(rows == lanes, column, 0.0), axis=0, keepdims=True)


def stood(row, count):
    rows = lax.broadcasted_iota(jnp.int32, (count, 128), 0)
    lanes = lax.broadcasted_iota(jnp.int32, (count, 128), 1)
    return jnp.sum(jnp.where(rows == lanes, row, 0.0), axis=1, keepdims=True)


def token_rows(column):
    at = lax.broadcasted_iota(jnp.int32, (8, 128), 0)
    ends = turned(column[128:])
    return jnp.where(at == 0, turned(column[:128]), jnp.where(at == 1, ends, 0.0))


def token_column(rows):
    return jnp.concatenate([stood(rows[0:1], 128), stood(rows[1:2], STRETCH - 128)], axis=0)


def two_pieces(rows):
    high = rows.astype(BF16).astype(F32)
    return jnp.concatenate([high, rows - high], axis=0).astype(BF16)


def one_piece(rows):
    rows = rows.astype(F32)
    return rows[:8] + rows[8:]


def pieces_tail(logs):
    row = turned(logs)
    high = row.astype(BF16).astype(F32)
    middle = (row - high).astype(BF16).astype(F32)
    low = row - high - middle
    at = lax.broadcasted_iota(jnp.int32, (TAIL, 128), 0)
    tail = jnp.where(at == 0, high, jnp.where(at == 1, middle, jnp.where(at == 2, low, 0.0)))
    return tail.astype(BF16)


def tail_pieces(tail):
    tail = tail.astype(F32)
    return stood(tail[0:1, :] + tail[1:2, :] + tail[2:3, :], ROWS)


def gathered_levels(table, codes):
    numbers = lax.GatherDimensionNumbers(
        offset_dims=(),
        collapsed_slice_dims=(1,),
        start_index_map=(1,),
        operand_batching_dims=(0,),
        start_indices_batching_dims=(0,),
    )
    return lax.gather(
        table, codes[..., None], numbers, (1, 1), mode=lax.GatherScatterMode.PROMISE_IN_BOUNDS
    )


def selected_levels(codes):
    masks = [(codes & 1) != 0, (codes & 2) != 0, (codes & 4) != 0, codes >= 8]

    def node(bit, base):
        if bit < 0:
            return jnp.float32(NORMAL_FLOAT_LEVELS[base])
        low = node(bit - 1, base)
        return jnp.where(masks[bit], node(bit - 1, base + (1 << bit)), low)

    return node(3, 0)


def block_scales(scales, outer, column):
    count = scales.shape[0]
    line = lax.broadcasted_iota(jnp.int32, outer.shape, 0)
    line = jnp.sum(jnp.where(line == column, outer, 0.0), axis=0, keepdims=True)
    rows = lax.broadcasted_iota(jnp.int32, (count, count), 0)
    lanes = lax.broadcasted_iota(jnp.int32, (count, count), 1)
    second = jnp.sum(jnp.where(rows == lanes, line, 0.0), axis=1, keepdims=True)
    return (scales.astype(F32) + 1.0) / 256.0 * second


def code_tiles(table, key_codes, value_codes, scales, out_a, out_b, step):
    begin = pl.multiple_of(step * QBLOCK, QBLOCK)
    row = pl.ds(step, 1)
    for at in range(CORE_HEADS):
        lanes = slice(at * HEAD_DIM, (at + 1) * HEAD_DIM)
        out = (out_a, out_b)[at // 2]
        key_scale, value_scale = scales[2 * at, row, :], scales[2 * at + 1, row, :]
        for tile in range(QBLOCK // 16):
            rows = pl.ds(pl.multiple_of(begin + 16 * tile, 16), 16)
            key, value = key_codes[rows, lanes], value_codes[rows, lanes]
            keys = [gathered_levels(table, key[half : half + 8]) for half in (0, 8)]
            values = [selected_levels(value[half : half + 8]) for half in (0, 8)]
            keys = jnp.concatenate([level * key_scale for level in keys], axis=0)
            values = jnp.concatenate([level * value_scale for level in values], axis=0)
            out[at % 2, rows, :HEAD_DIM] = keys.astype(BF16)
            out[at % 2, rows, HEAD_DIM:] = values.astype(BF16)


def scale_prompt(x, gain, scaled, column, squares, prompt):
    def body(step, _):
        rows = pl.ds(pl.multiple_of(step * 16, 16), 16)
        wide = x[prompt, rows, :].astype(F32)
        scaled[prompt, rows, :] = (wide * gain[...]).astype(BF16)
        total = jnp.sum(wide * wide, axis=1, keepdims=True)
        column[rows, :] = jnp.broadcast_to(total, (16, 128))
        return 0

    lax.fori_loop(0, STRETCH // 16, body, 0)
    squares[prompt] = token_rows(column[:, :1])


def weights_kernel(
    x, codes, key_scales, value_scales, outer, gain,
    out_a, out_b, scaled, squares, key_codes, value_codes, lines, column, scales, arrivals,
):
    per_rep = x.shape[0]
    features, width = key_codes.shape
    depth = min(256, features)
    blocks = features // depth
    columns = outer.shape[0] // 2
    rep = lax.axis_index("rep")

    def code_copies(block):
        rows = pl.ds(block * depth, depth)
        return [
            pltpu.make_async_copy(
                codes.at[rows, pl.ds(pl.multiple_of((2 * kind + rep) * width, width), width)],
                buffer.at[rows],
                arrivals.at[2 * block + kind],
            )
            for kind, buffer in enumerate((key_codes, value_codes))
        ]

    def line_copy(prompt):
        return pltpu.make_async_copy(
            x.at[prompt], lines.at[prompt], arrivals.at[2 * blocks + prompt]
        )

    shares = [range(per_rep * at // blocks, per_rep * (at + 1) // blocks) for at in range(blocks)]
    for block in range(blocks):
        for copy in code_copies(block):
            copy.start()
        for prompt in shares[block]:
            line_copy(prompt).start()

    for at in range(CORE_HEADS):
        column_at = (rep * CORE_HEADS + at) // (KV_HEADS // columns)
        lanes = slice(at * HEAD_DIM, (at + 1) * HEAD_DIM)
        scales[2 * at] = block_scales(key_scales[:, lanes], outer[...], column_at)
        scales[2 * at + 1] = block_scales(value_scales[:, lanes], outer[...], columns + column_at)
    lane = lax.broadcasted_iota(jnp.int32, (8, 128), 1)
    table = jnp.zeros((8, 128), F32)
    for code, level in enumerate(NORMAL_FLOAT_LEVELS):
        table = jnp.where(lane == code, level, table)

    def body(step, _):
        code_tiles(table, key_codes, value_codes, scales, out_a, out_b, step)
        return 0

    steps = depth // QBLOCK
    for block in range(blocks):
        for copy in code_copies(block):
            copy.wait()
        lax.fori_loop(block * steps, (block + 1) * steps, body, 0)
        for prompt in shares[block]:
            line_copy(prompt).wait()
            scale_prompt(lines, gain, scaled, column, squares, prompt)


def dequantize(x, codes, scales, outer, gain):
    per_rep, _, features = x.shape
    width = CORE_HEADS * HEAD_DIM
    blocks = features // min(256, features)
    rep = lambda: lax.axis_index("rep")
    x, codes, scales, outer, gain = in_hbm(x, codes, scales, outer, gain)
    weight = jax.ShapeDtypeStruct((2, features, 2 * HEAD_DIM), BF16)
    return pl.pallas_call(
        weights_kernel,
        grid=(1,),
        in_specs=[
            pl.BlockSpec(memory_space=pltpu.HBM),
            pl.BlockSpec(memory_space=pltpu.HBM),
            pl.BlockSpec((scales.shape[0], width), lambda k: (0, rep())),
            pl.BlockSpec((scales.shape[0], width), lambda k: (0, 2 + rep())),
            pl.BlockSpec(outer.shape, lambda k: (0, 0)),
            pl.BlockSpec(gain.shape, lambda k: (0, 0)),
        ],
        out_specs=[VMEM] * 4,
        out_shape=[
            weight,
            weight,
            jax.ShapeDtypeStruct(x.shape, BF16),
            jax.ShapeDtypeStruct((per_rep, 8, 128), F32),
        ],
        scratch_shapes=[
            pltpu.VMEM((features, width), jnp.int32),
            pltpu.VMEM((features, width), jnp.int32),
            pltpu.VMEM(x.shape, BF16),
            pltpu.VMEM((STRETCH, 128), F32),
            pltpu.VMEM((2 * CORE_HEADS, scales.shape[0], HEAD_DIM), F32),
            pltpu.SemaphoreType.DMA((2 * blocks + per_rep,)),
        ],
        compiler_params=pltpu.CompilerParams(vmem_limit_bytes=36 * MIB),
        cost_estimate=pl.CostEstimate(
            flops=32 * codes.size, bytes_accessed=codes.size * 2, transcendentals=0
        ),
        name="dequantize",
    )(x, codes, scales, scales, outer, gain)


def prompt_of(targets, owner):
    prompt = jnp.int32(-1)
    for at in range(targets.shape[0]):
        prompt = jnp.where(targets[at] == owner, at, prompt)
    return prompt


def lines_of(targets, distance, own, squares, other, gain, line, total):
    per_rep = own.shape[0]
    prompt = prompt_of(targets, owner_at(distance))
    at = lax.rem(jnp.maximum(prompt, 0), per_rep)
    is_own = prompt // per_rep == lax.axis_index("rep")

    @pl.when((prompt >= 0) & is_own)
    def _():
        line[...] = own[at]
        total[...] = squares[at]

    @pl.when((prompt >= 0) & jnp.logical_not(is_own))
    def _():
        wide = other[at].astype(F32)
        line[...] = (wide * gain[...]).astype(BF16)
        total[...] = token_rows(jnp.sum(wide * wide, axis=1, keepdims=True))

    @pl.when(prompt < 0)
    def _():
        line[...] = jnp.zeros(line.shape, BF16)
        total[...] = jnp.zeros(total.shape, F32)


def line_specs(distances, x):
    return [
        jax.ShapeDtypeStruct((len(distances) * STRETCH, x.shape[2]), BF16),
        jax.ShapeDtypeStruct((len(distances), 8, 128), F32),
    ]


def first_kernel(distances, targets, own, squares, other, gain, weight, *refs):
    right, left, terms, lines, totals = refs
    for item, distance in enumerate(distances):
        line = lines.at[item * STRETCH : (item + 1) * STRETCH]
        lines_of(targets, distance, own, squares, other, gain, line, totals.at[item])
    products(distances, lines, totals, weight, right, left, terms)


def second_kernel(distances, lines, totals, weight, *refs):
    products(distances, lines, totals, weight, *refs)


def products(distances, lines, totals, weight, right, left, terms):
    for head in range(2):
        product = jnp.dot(lines[...], weight[head], preferred_element_type=F32)
        rows = slice(head * STRETCH, (head + 1) * STRETCH)
        right[rows] = product[:STRETCH, :HEAD_DIM].astype(BF16)
        left[rows] = product[:STRETCH, HEAD_DIM:].astype(BF16)
        for item in range(1, len(distances)):
            part = product[item * STRETCH : (item + 1) * STRETCH]
            begin = head * STRETCH
            terms[item - 1, begin : begin + STRETCH] = part[:, :HEAD_DIM]
            begin += 2 * STRETCH
            terms[item - 1, begin : begin + STRETCH] = part[:, HEAD_DIM:]
    for item in range(1, len(distances)):
        terms[item - 1, 4 * STRETCH :] = totals[item]
    right[2 * STRETCH :] = two_pieces(totals[0])


def first_shapes(distances):
    rows = 2 * STRETCH
    return [
        jax.ShapeDtypeStruct((rows + TAIL, HEAD_DIM), BF16),
        jax.ShapeDtypeStruct((rows, HEAD_DIM), BF16),
        jax.ShapeDtypeStruct((len(distances) - 1, 2 * rows + 8, HEAD_DIM), F32),
    ]


def project_cost(distances, weight):
    return pl.CostEstimate(
        flops=len(distances) * STRETCH * weight.size * 2,
        bytes_accessed=weight.size,
        transcendentals=0,
    )


def project_first(distances, targets, own, squares, other, gain, weight):
    return pl.pallas_call(
        functools.partial(first_kernel, distances),
        in_specs=[SMEM] + [VMEM] * 5,
        out_specs=[VMEM] * 5,
        out_shape=first_shapes(distances) + line_specs(distances, own),
        compiler_params=pltpu.CompilerParams(vmem_limit_bytes=24 * MIB),
        cost_estimate=project_cost(distances, weight),
        name="project_first",
    )(targets, own, squares, other, gain, weight)


def project_second(distances, lines, totals, weight):
    return pl.pallas_call(
        functools.partial(second_kernel, distances),
        in_specs=[VMEM] * 3,
        out_specs=[VMEM] * 3,
        out_shape=first_shapes(distances),
        compiler_params=pltpu.CompilerParams(vmem_limit_bytes=24 * MIB),
        cost_estimate=project_cost(distances, weight),
        name="project_second",
    )(lines, totals, weight)


def project_kernel(
    distances, targets, own, squares, other, gain, weight_a, weight_b, out_a, out_b, lines, totals
):
    for item, distance in enumerate(distances):
        line = lines.at[item * STRETCH : (item + 1) * STRETCH]
        lines_of(targets, distance, own, squares, other, gain, line, totals.at[item])
    for weight, out in ((weight_a, out_a), (weight_b, out_b)):
        for head in range(2):
            product = jnp.dot(lines[...], weight[head], preferred_element_type=F32)
            for item in range(len(distances)):
                part = product[item * STRETCH : (item + 1) * STRETCH]
                begin = head * STRETCH
                out[item, begin : begin + STRETCH] = part[:, :HEAD_DIM]
                begin += 2 * STRETCH
                out[item, begin : begin + STRETCH] = part[:, HEAD_DIM:]
        for item in range(len(distances)):
            out[item, 4 * STRETCH :] = totals[item]


def project(distances, targets, own, squares, other, gain, weights):
    shape = jax.ShapeDtypeStruct((len(distances), 4 * STRETCH + 8, HEAD_DIM), F32)
    line, total = line_specs(distances, own)
    return pl.pallas_call(
        functools.partial(project_kernel, distances),
        in_specs=[SMEM] + [VMEM] * 6,
        out_specs=[VMEM] * 2,
        out_shape=[shape, shape],
        scratch_shapes=[pltpu.VMEM(line.shape, BF16), pltpu.VMEM(total.shape, F32)],
        compiler_params=pltpu.CompilerParams(vmem_limit_bytes=24 * MIB),
        cost_estimate=project_cost(distances, weights[0]),
        name="project",
    )(targets, own, squares, other, gain, *weights)


def send_kernel(half, first, terms, right, left, to_right, to_left):
    rows = 4 * STRETCH
    middle = 2 * STRETCH
    if first:
        to_right[:middle] = (terms[0, :middle] + right[:middle].astype(F32)).astype(BF16)
        to_right[middle:rows] = terms[0, middle:rows].astype(BF16)
        to_left[:middle] = terms[1, :middle].astype(BF16)
        to_left[middle:rows] = (terms[1, middle:rows] + left[...].astype(F32)).astype(BF16)
    else:
        to_right[:rows] = (terms[0, :rows] + right[:rows].astype(F32)).astype(BF16)
        to_left[:rows] = (terms[1, :rows] + left[:rows].astype(F32)).astype(BF16)
    if half == 0:
        right_sum, left_sum = terms[0, rows:], terms[1, rows:]
        right_sum += one_piece(right[middle if first else rows :])
        if not first:
            left_sum += one_piece(left[rows:])
        to_right[rows:] = two_pieces(right_sum)
        to_left[rows:] = two_pieces(left_sum)


def sends(half, first, terms, right, left):
    rows = 4 * STRETCH + (TAIL if half == 0 else 0)
    shape = jax.ShapeDtypeStruct((rows, HEAD_DIM), BF16)
    return pl.pallas_call(
        functools.partial(send_kernel, half, first),
        in_specs=[VMEM] * 3,
        out_specs=[VMEM] * 2,
        out_shape=[shape, shape],
        compiler_params=pltpu.CompilerParams(vmem_limit_bytes=16 * MIB),
        name="sends",
    )(terms, right, left)


def prepare_kernel(targets, queries, starts, turns, grouped, rotary):
    for head in range(KV_HEADS):
        for member in range(GROUP):
            begin = (head * GROUP + member) * HEAD_DIM
            rows = slice(member * STEPS, (member + 1) * STEPS)
            grouped[head, rows] = queries[0, :, begin : begin + HEAD_DIM]
    row = pl.ds(jnp.maximum(prompt_of(targets, lax.axis_index("tp")), 0), 1)
    cosine, sine = starts[0, row, :], starts[1, row, :]
    lane = lax.broadcasted_iota(jnp.int32, turns.shape[1:], 1)
    rotary[0] = turns[0] * cosine - turns[1] * sine
    sine = turns[1] * cosine + turns[0] * sine
    rotary[1] = jnp.where(lane < HEAD_DIM // 2, -sine, sine)


def prepare(targets, queries, starts, turns):
    return pl.pallas_call(
        prepare_kernel,
        in_specs=[SMEM] + [VMEM] * 3,
        out_specs=[VMEM] * 2,
        out_shape=[
            jax.ShapeDtypeStruct((KV_HEADS, ROWS, HEAD_DIM), BF16),
            jax.ShapeDtypeStruct(turns.shape, F32),
        ],
        compiler_params=pltpu.CompilerParams(vmem_limit_bytes=16 * MIB),
        name="prepare",
    )(targets, queries, starts, turns)


def cache_kernel(part, targets, lengths, stored, q, cache, new, out):
    scaling = HEAD_DIM ** (-0.5)
    dims = (((1,), (1,)), ((), ()))
    here = lax.axis_index("tp")
    rep = lax.axis_index("rep")
    length = cache.shape[1]
    prompt = prompt_of(targets, here)
    handed = lengths[jnp.maximum(prompt, 0)] - STRETCH
    span = jnp.where(prompt >= 0, handed, stored[0]) - rep * length
    allowed = lax.broadcasted_iota(jnp.int32, (ROWS, length), 1) < span
    second_step = lax.broadcasted_iota(jnp.int32, (ROWS, 1), 0) % STEPS == 1
    for at in range(CORE_HEADS):
        head = part * CORE_HEADS + at
        key_lanes = slice(head * HEAD_DIM, (head + 1) * HEAD_DIM)
        value_lanes = slice((KV_HEADS + head) * HEAD_DIM, (KV_HEADS + head + 1) * HEAD_DIM)
        query = q[head]
        wide = query.astype(F32)
        scores = lax.dot_general(query, cache[0, :, key_lanes], dims, preferred_element_type=F32)
        scores = jnp.where(allowed, scores * scaling, NEGATIVE)
        highest = jnp.max(scores, axis=1, keepdims=True)
        fresh = []
        for step in range(STEPS):
            key = new[0, step : step + 1, key_lanes].astype(F32)
            score = jnp.sum(wide * key, axis=1, keepdims=True) * scaling
            shown = rep == 0 if step == 0 else second_step & (rep == 0)
            score = jnp.where(shown, score, NEGATIVE)
            highest = jnp.maximum(highest, score)
            fresh.append(score)
        some = highest > 0.5 * NEGATIVE
        highest = jnp.where(some, highest, 0.0)
        weight = jnp.exp(scores - highest)
        totals = jnp.sum(weight, axis=1, keepdims=True)
        sums = jnp.dot(weight.astype(BF16), cache[0, :, value_lanes], preferred_element_type=F32)
        for step in range(STEPS):
            share = jnp.exp(fresh[step] - highest)
            totals += share
            value = new[0, step : step + 1, value_lanes].astype(F32)
            sums += share.astype(BF16).astype(F32) * value
        totals = jnp.where(some, totals, 1.0)
        out[at, :ROWS] = (sums / totals).astype(BF16)
        out[at, ROWS:] = pieces_tail(jnp.where(some, highest + jnp.log(totals), NEGATIVE))


def cache_attention(part, targets, lengths, stored, grouped, kv_cache, new_kv):
    return pl.pallas_call(
        functools.partial(cache_kernel, part),
        in_specs=[SMEM] * 3 + [VMEM] * 3,
        out_specs=VMEM,
        out_shape=jax.ShapeDtypeStruct((CORE_HEADS, PART, HEAD_DIM), BF16),
        compiler_params=pltpu.CompilerParams(vmem_limit_bytes=16 * MIB),
        cost_estimate=pl.CostEstimate(
            flops=2 * grouped.size * kv_cache.shape[1],
            bytes_accessed=kv_cache.size,
            transcendentals=CORE_HEADS * ROWS * kv_cache.shape[1],
        ),
        name="cache_attention",
    )(targets, lengths, stored, grouped, kv_cache, new_kv)


def final_kernel(
    targets, rotary, own_a, own_b, right_a, left_a, right_b, left_b, grouped, *refs
):
    cached, out = refs
    scaling = HEAD_DIM ** (-0.5)
    dims = (((1,), (1,)), ((), ()))
    mine = own_a.shape[0] - 1
    rep = lax.axis_index("rep")
    first = rep * CORE_HEADS
    prompt = prompt_of(targets, lax.axis_index("tp"))
    cosine, sine = rotary[0], rotary[1]
    rows = 4 * STRETCH
    squares = own_a[mine, rows:] + one_piece(right_a[rows:]) + one_piece(left_a[rows:])
    scale = token_column(lax.rsqrt(squares / D + EPSILON))
    for head in range(CORE_HEADS):
        own, right, left = ((own_a, right_a, left_a), (own_b, right_b, left_b))[head // 2]
        at = slice(head % 2 * STRETCH, (head % 2 + 1) * STRETCH)
        keys = own[mine, at] + right[at].astype(F32) + left[at].astype(F32)
        at = slice((2 + head % 2) * STRETCH, (3 + head % 2) * STRETCH)
        values = own[mine, at] + right[at].astype(F32) + left[at].astype(F32)
        keys = (keys * scale).astype(BF16).astype(F32)
        values = (values * scale).astype(BF16)
        keys = keys * cosine + pltpu.roll(keys, HEAD_DIM // 2, 1) * sine
        scores = lax.dot_general(
            grouped[first + head], keys.astype(BF16), dims, preferred_element_type=F32
        )
        scores = scores * scaling
        highest = jnp.max(scores, axis=1, keepdims=True)
        weight = jnp.exp(scores - highest)
        totals = jnp.sum(weight, axis=1, keepdims=True)
        sums = jnp.dot(weight.astype(BF16), values, preferred_element_type=F32) / totals
        logs = jnp.where(prompt >= 0, highest + jnp.log(totals), NEGATIVE)
        parts = [cached[0, first + head], cached[1, first + head]]
        logs = [tail_pieces(part[ROWS:]) for part in parts] + [logs]
        sums = [part[:ROWS].astype(F32) for part in parts] + [sums]
        highest = functools.reduce(jnp.maximum, logs)
        shares = [jnp.exp(log - highest) for log in logs]
        total = functools.reduce(jnp.add, shares)
        joined = functools.reduce(jnp.add, [share * part for share, part in zip(shares, sums)])
        result = (joined / total).astype(BF16)
        for member in range(GROUP):
            begin = (head * GROUP + member) * HEAD_DIM
            out[0, :, begin : begin + HEAD_DIM] = result[member * STEPS : (member + 1) * STEPS]


def finish(targets, rotary, own, arrived, grouped, cached):
    width = CORE_HEADS * GROUP * HEAD_DIM
    return pl.pallas_call(
        final_kernel,
        in_specs=[SMEM] + [VMEM] * 9,
        out_specs=VMEM,
        out_shape=jax.ShapeDtypeStruct((1, STEPS, width), BF16),
        compiler_params=pltpu.CompilerParams(vmem_limit_bytes=16 * MIB),
        name="finish",
    )(targets, rotary, *own, *arrived, grouped, cached)


def rotary_turns():
    half = np.arange(HEAD_DIM // 2, dtype=np.float64) / (HEAD_DIM // 2)
    frequency = ROTARY_BASE ** (-np.concatenate([half, half]))
    angles = np.arange(STRETCH, dtype=np.float64)[:, None] * frequency
    return frequency.astype(np.float32), np.stack([np.cos(angles), np.sin(angles)]).astype(np.float32)


def per_device(
    stretch,
    norm_gain,
    kv_codes,
    scale_codes,
    outer_scales,
    prompt_lengths,
    target_rows,
    cache_lengths,
    kv_cache,
    queries,
    new_kv,
):
    count = lax.axis_size("tp")
    half = count // 2
    lines = stretch.transpose(1, 0, 2)
    gain = norm_gain.reshape(1, -1)
    ring = [ring_device(at, count) for at in range(count)]
    to_right = [(ring[at], ring[(at + 1) % count]) for at in range(count)]
    to_left = [(ring[at], ring[at - 1]) for at in range(count)]

    def pass_on(right, left):
        return lax.ppermute(right, "tp", to_right), lax.ppermute(left, "tp", to_left)

    other = lax.ppermute(lines, "rep", [(0, 1), (1, 0)])
    first_half, second_half, own, squares = dequantize(
        lines, kv_codes, scale_codes, outer_scales.T, gain
    )
    frequency, turns = rotary_turns()
    start = (prompt_lengths - STRETCH).astype(F32)[:, None] * jnp.asarray(frequency)
    starts = jnp.stack([jnp.cos(start), jnp.sin(start)])
    targets, second_half = lax.optimization_barrier((target_rows, second_half))
    grouped, rotary = prepare(targets, queries, starts, jnp.asarray(turns))

    gain, second_half, grouped, rotary = lax.optimization_barrier(
        (gain, second_half, grouped, rotary)
    )
    distances = [half, half - 1, 1 - half]
    right, left, terms_a, lines_here, totals = project_first(
        distances, target_rows, own, squares, other, gain, first_half
    )
    arrived = [pass_on(right, left), None]
    right, left, terms_b = project_second(distances, lines_here, totals, second_half)
    arrived[1] = pass_on(right, left)
    terms = [terms_a, terms_b]

    targets = target_rows
    cached = []
    for distance in range(half - 1, 0, -1):
        if distance < half - 1:
            distances = [distance, -distance] + ([0] if distance == 1 else [])
            terms = list(
                project(distances, targets, own, squares, other, gain, [first_half, second_half])
            )
        for part in range(2):
            right, left = sends(part, distance == half - 1, terms[part], *arrived[part])
            if part == 0:
                right, cached, terms[1] = lax.optimization_barrier((right, cached, terms[1]))
            targets, _ = lax.optimization_barrier((target_rows, right))
            arrived[part] = pass_on(right, left)
        if distance in (2, 3):
            cached.append(
                cache_attention(
                    3 - distance, targets, prompt_lengths, cache_lengths, grouped, kv_cache, new_kv
                )
            )

    cached, _ = lax.optimization_barrier((cached, right))
    cached = lax.all_gather(jnp.concatenate(cached), "rep")
    out = finish(target_rows, rotary, terms, [*arrived[0], *arrived[1]], grouped, cached)
    return lax.all_gather(out, "rep", axis=2, tiled=True)


def solution(mesh):
    in_specs = (
        P(None, ("grp", "rep"), "tp"),
        P("tp"),
        P("tp", None),
        P("tp", None),
        P("tp", None),
        P("grp"),
        P("grp"),
        P(("grp", "tp")),
        P(("grp", "tp"), "rep", None),
        P(("grp", "tp"), None, None),
        P(("grp", "tp"), None, None),
    )
    out_specs = P(("grp", "tp"), None, None)
    return jax.shard_map(
        per_device, mesh=mesh, in_specs=in_specs, out_specs=out_specs, check_vma=False
    )
```

```python
import functools
import math

import jax
import jax.numpy as jnp
import numpy as np
from jax import lax
from jax.experimental import pallas as pl
from jax.experimental.pallas import tpu as pltpu
from jax.sharding import PartitionSpec as P

D = 16384
HEADS = 128
KV_HEADS = 8
HEAD_DIM = 128
STRETCH = 192
STEPS = 2
QBLOCK = 64
GROUP = HEADS // KV_HEADS
ROWS = GROUP * STEPS
TAIL = 16
PART = ROWS + TAIL
CORE_HEADS = KV_HEADS // 2
NORMAL_FLOAT_LEVELS = [
    -1.0,
    -0.6961928009986877,
    -0.5250730514526367,
    -0.39491748809814453,
    -0.28444138169288635,
    -0.18477343022823334,
    -0.09105003625154495,
    0.0,
    0.07958029955625534,
    0.16093020141124725,
    0.24611230194568634,
    0.33791524171829224,
    0.44070982933044434,
    0.5626170039176941,
    0.7229568362236023,
    1.0,
]
ROTARY_BASE = 500000.0
EPSILON = 1e-05
NEGATIVE = -1e30
BF16 = jnp.bfloat16
F32 = jnp.float32
MIB = 1024 * 1024
VMEM = pl.BlockSpec(memory_space=pltpu.VMEM)
SMEM = pl.BlockSpec(memory_space=pltpu.SMEM)


def in_hbm(*arrays):
    return [pltpu.with_memory_space_constraint(array, pltpu.HBM) for array in arrays]


def turned(column):
    rows = lax.broadcasted_iota(jnp.int32, (column.shape[0], 128), 0)
    lanes = lax.broadcasted_iota(jnp.int32, (column.shape[0], 128), 1)
    return jnp.sum(jnp.where(rows == lanes, column, 0.0), axis=0, keepdims=True)


def stood(row, count):
    rows = lax.broadcasted_iota(jnp.int32, (count, 128), 0)
    lanes = lax.broadcasted_iota(jnp.int32, (count, 128), 1)
    return jnp.sum(jnp.where(rows == lanes, row, 0.0), axis=1, keepdims=True)


def token_rows(column):
    at = lax.broadcasted_iota(jnp.int32, (8, 128), 0)
    ends = turned(column[128:])
    return jnp.where(at == 0, turned(column[:128]), jnp.where(at == 1, ends, 0.0))


def token_column(rows):
    return jnp.concatenate([stood(rows[0:1], 128), stood(rows[1:2], STRETCH - 128)], axis=0)


def pieces_tail(logs):
    row = turned(logs)
    high = row.astype(BF16).astype(F32)
    middle = (row - high).astype(BF16).astype(F32)
    low = row - high - middle
    at = lax.broadcasted_iota(jnp.int32, (TAIL, 128), 0)
    tail = jnp.where(at == 0, high, jnp.where(at == 1, middle, jnp.where(at == 2, low, 0.0)))
    return tail.astype(BF16)


def two_pieces(rows):
    high = rows.astype(BF16).astype(F32)
    return jnp.concatenate([high, rows - high], axis=0).astype(BF16)


def one_piece(rows):
    rows = rows.astype(F32)
    return rows[:8] + rows[8:]


def tail_pieces(tail):
    tail = tail.astype(F32)
    return stood(tail[0:1, :] + tail[1:2, :] + tail[2:3, :], ROWS)


def gathered_levels(table, codes):
    numbers = lax.GatherDimensionNumbers(
        offset_dims=(),
        collapsed_slice_dims=(1,),
        start_index_map=(1,),
        operand_batching_dims=(0,),
        start_indices_batching_dims=(0,),
    )
    return lax.gather(
        table, codes[..., None], numbers, (1, 1), mode=lax.GatherScatterMode.PROMISE_IN_BOUNDS
    )


def selected_levels(codes):
    masks = [(codes & 1) != 0, (codes & 2) != 0, (codes & 4) != 0, codes >= 8]

    def node(bit, base):
        if bit < 0:
            return jnp.float32(NORMAL_FLOAT_LEVELS[base])
        low = node(bit - 1, base)
        return jnp.where(masks[bit], node(bit - 1, base + (1 << bit)), low)

    return node(3, 0)


def block_scales(scales, outer, column):
    count = scales.shape[0]
    line = lax.broadcasted_iota(jnp.int32, outer.shape, 0)
    line = jnp.sum(jnp.where(line == column, outer, 0.0), axis=0, keepdims=True)
    rows = lax.broadcasted_iota(jnp.int32, (count, count), 0)
    lanes = lax.broadcasted_iota(jnp.int32, (count, count), 1)
    second = jnp.sum(jnp.where(rows == lanes, line, 0.0), axis=1, keepdims=True)
    return (scales.astype(F32) + 1.0) / 256.0 * second


def weights_kernel(
    x, key_codes, value_codes, key_scales, value_scales, outer, gain,
    out_a, out_b, scaled, squares, scales,
):
    block = pl.program_id(0)
    depth = key_codes.shape[0]
    columns = outer.shape[0] // 2

    @pl.when(block == 0)
    def _():
        squares[...] = jnp.zeros(squares.shape, F32)
        for at in range(CORE_HEADS):
            head = lax.axis_index("rep") * CORE_HEADS + at
            column = head // (KV_HEADS // columns)
            lanes = slice(at * HEAD_DIM, (at + 1) * HEAD_DIM)
            scales[2 * at] = block_scales(key_scales[:, lanes], outer[...], column)
            scales[2 * at + 1] = block_scales(value_scales[:, lanes], outer[...], columns + column)

    lane = lax.broadcasted_iota(jnp.int32, (8, 128), 1)
    table = jnp.zeros((8, 128), F32)
    for code, level in enumerate(NORMAL_FLOAT_LEVELS):
        table = jnp.where(lane == code, level, table)

    def body(step, _):
        begin = pl.multiple_of(step * QBLOCK, QBLOCK)
        row = pl.ds(block * (depth // QBLOCK) + step, 1)
        for at in range(CORE_HEADS):
            lanes = slice(at * HEAD_DIM, (at + 1) * HEAD_DIM)
            out = (out_a, out_b)[at // 2]
            key_scale, value_scale = scales[2 * at, row, :], scales[2 * at + 1, row, :]
            for tile in range(QBLOCK // 16):
                rows = pl.ds(pl.multiple_of(begin + 16 * tile, 16), 16)
                key, value = key_codes[rows, lanes], value_codes[rows, lanes]
                keys = [gathered_levels(table, key[half : half + 8]) for half in (0, 8)]
                values = [selected_levels(value[half : half + 8]) for half in (0, 8)]
                rows = pl.ds(pl.multiple_of(block * depth + begin + 16 * tile, 16), 16)
                keys = jnp.concatenate([level * key_scale for level in keys], axis=0)
                values = jnp.concatenate([level * value_scale for level in values], axis=0)
                out[at % 2, rows, :HEAD_DIM] = keys.astype(BF16)
                out[at % 2, rows, HEAD_DIM:] = values.astype(BF16)
        return 0

    lax.fori_loop(0, depth // QBLOCK, body, 0)

    width = x.shape[2]
    begin = pl.multiple_of(block * width, 128)
    for prompt in range(x.shape[0]):
        wide = x[prompt].astype(F32)
        scaled[prompt, :, pl.ds(begin, width)] = (wide * gain[...]).astype(BF16)
        squares[prompt] += token_rows(jnp.sum(wide * wide, axis=1, keepdims=True))


def dequantize(x, codes, scales, outer, gain):
    per_rep, _, features = x.shape
    depth = min(256, features)
    width = CORE_HEADS * HEAD_DIM
    rep = lambda: lax.axis_index("rep")
    x, codes, scales, outer, gain = in_hbm(x, codes, scales, outer, gain)
    weight = jax.ShapeDtypeStruct((2, features, 2 * HEAD_DIM), BF16)
    return pl.pallas_call(
        weights_kernel,
        grid=(features // depth,),
        in_specs=[
            pl.BlockSpec((per_rep, STRETCH, depth), lambda k: (0, 0, k)),
            pl.BlockSpec((depth, width), lambda k: (k, rep())),
            pl.BlockSpec((depth, width), lambda k: (k, 2 + rep())),
            pl.BlockSpec((scales.shape[0], width), lambda k: (0, rep())),
            pl.BlockSpec((scales.shape[0], width), lambda k: (0, 2 + rep())),
            pl.BlockSpec(outer.shape, lambda k: (0, 0)),
            pl.BlockSpec((1, depth), lambda k: (0, k)),
        ],
        out_specs=[VMEM] * 4,
        out_shape=[
            weight,
            weight,
            jax.ShapeDtypeStruct(x.shape, BF16),
            jax.ShapeDtypeStruct((per_rep, 8, 128), F32),
        ],
        scratch_shapes=[pltpu.VMEM((2 * CORE_HEADS, scales.shape[0], HEAD_DIM), F32)],
        compiler_params=pltpu.CompilerParams(vmem_limit_bytes=32 * MIB),
        cost_estimate=pl.CostEstimate(
            flops=32 * codes.size, bytes_accessed=codes.size * 2, transcendentals=0
        ),
        name="dequantize",
    )(x, codes, codes, scales, scales, outer, gain)


def prompt_of(targets, owner):
    prompt = jnp.int32(-1)
    for at in range(targets.shape[0]):
        prompt = jnp.where(targets[at] == owner, at, prompt)
    return prompt


def lines_of(targets, owner, own, squares, other, gain, line, total):
    per_rep = own.shape[0]
    prompt = prompt_of(targets, owner)
    at = lax.rem(jnp.maximum(prompt, 0), per_rep)
    is_own = prompt // per_rep == lax.axis_index("rep")

    @pl.when((prompt >= 0) & is_own)
    def _():
        line[...] = own[at]
        total[...] = squares[at]

    @pl.when((prompt >= 0) & jnp.logical_not(is_own))
    def _():
        wide = other[at].astype(F32)
        line[...] = (wide * gain[...]).astype(BF16)
        total[...] = token_rows(jnp.sum(wide * wide, axis=1, keepdims=True))

    @pl.when(prompt < 0)
    def _():
        line[...] = jnp.zeros(line.shape, BF16)
        total[...] = jnp.zeros(total.shape, F32)


def line_specs(distances, x):
    return [
        jax.ShapeDtypeStruct((len(distances) * STRETCH, x.shape[2]), BF16),
        jax.ShapeDtypeStruct((len(distances), 8, 128), F32),
    ]


def owners_kernel(targets, own, squares, other, gain, weight, out, lines, totals):
    together = out.shape[0]
    for item in range(together):
        line = lines.at[item * STRETCH : (item + 1) * STRETCH]
        owner = pl.program_id(0) * together + item
        lines_of(targets, owner, own, squares, other, gain, line, totals.at[item])
    products(lines, weight, out)


def again_kernel(lines, weight, out):
    products(lines, weight, out)


def products(lines, weight, out):
    for head in range(2):
        product = jnp.dot(lines[...], weight[head], preferred_element_type=F32).astype(BF16)
        for item in range(out.shape[0]):
            part = product[item * STRETCH : (item + 1) * STRETCH]
            begin = head * STRETCH
            out[item, begin : begin + STRETCH] = part[:, :HEAD_DIM]
            begin += 2 * STRETCH
            out[item, begin : begin + STRETCH] = part[:, HEAD_DIM:]


TOGETHER = 4


def project_owners(count, targets, own, squares, other, gain, weight):
    features = own.shape[2]
    return pl.pallas_call(
        owners_kernel,
        grid=(count // TOGETHER,),
        in_specs=[SMEM] + [VMEM] * 5,
        out_specs=[
            pl.BlockSpec((TOGETHER, 4 * STRETCH, HEAD_DIM), lambda i: (i, 0, 0)),
            pl.BlockSpec((TOGETHER * STRETCH, features), lambda i: (i, 0)),
            pl.BlockSpec((TOGETHER, 8, 128), lambda i: (i, 0, 0)),
        ],
        out_shape=[
            jax.ShapeDtypeStruct((count, 4 * STRETCH, HEAD_DIM), BF16),
            jax.ShapeDtypeStruct((count * STRETCH, features), BF16),
            jax.ShapeDtypeStruct((count, 8, 128), F32),
        ],
        compiler_params=pltpu.CompilerParams(vmem_limit_bytes=32 * MIB),
        name="project_owners",
    )(targets, own, squares, other, gain, weight)


def project_again(count, lines, weight):
    features = lines.shape[1]
    return pl.pallas_call(
        again_kernel,
        grid=(count // TOGETHER,),
        in_specs=[pl.BlockSpec((TOGETHER * STRETCH, features), lambda i: (i, 0)), VMEM],
        out_specs=pl.BlockSpec((TOGETHER, 4 * STRETCH, HEAD_DIM), lambda i: (i, 0, 0)),
        out_shape=jax.ShapeDtypeStruct((count, 4 * STRETCH, HEAD_DIM), BF16),
        compiler_params=pltpu.CompilerParams(vmem_limit_bytes=32 * MIB),
        name="project_again",
    )(lines, weight)


def prepare_kernel(targets, queries, starts, turns, grouped, rotary):
    for head in range(KV_HEADS):
        for member in range(GROUP):
            begin = (head * GROUP + member) * HEAD_DIM
            rows = slice(member * STEPS, (member + 1) * STEPS)
            grouped[head, rows] = queries[0, :, begin : begin + HEAD_DIM]
    row = pl.ds(jnp.maximum(prompt_of(targets, lax.axis_index("tp")), 0), 1)
    cosine, sine = starts[0, row, :], starts[1, row, :]
    lane = lax.broadcasted_iota(jnp.int32, turns.shape[1:], 1)
    rotary[0] = turns[0] * cosine - turns[1] * sine
    sine = turns[1] * cosine + turns[0] * sine
    rotary[1] = jnp.where(lane < HEAD_DIM // 2, -sine, sine)


def prepare(targets, queries, starts, turns):
    return pl.pallas_call(
        prepare_kernel,
        in_specs=[SMEM] + [VMEM] * 3,
        out_specs=[VMEM] * 2,
        out_shape=[
            jax.ShapeDtypeStruct((KV_HEADS, ROWS, HEAD_DIM), BF16),
            jax.ShapeDtypeStruct(turns.shape, F32),
        ],
        compiler_params=pltpu.CompilerParams(vmem_limit_bytes=16 * MIB),
        name="prepare",
    )(targets, queries, starts, turns)


def cache_kernel(part, targets, lengths, stored, q, cache, new, out):
    scaling = HEAD_DIM ** (-0.5)
    dims = (((1,), (1,)), ((), ()))
    here = lax.axis_index("tp")
    rep = lax.axis_index("rep")
    length = cache.shape[1]
    prompt = prompt_of(targets, here)
    handed = lengths[jnp.maximum(prompt, 0)] - STRETCH
    span = jnp.where(prompt >= 0, handed, stored[0]) - rep * length
    allowed = lax.broadcasted_iota(jnp.int32, (ROWS, length), 1) < span
    second_step = lax.broadcasted_iota(jnp.int32, (ROWS, 1), 0) % STEPS == 1
    for at in range(CORE_HEADS):
        head = part * CORE_HEADS + at
        key_lanes = slice(head * HEAD_DIM, (head + 1) * HEAD_DIM)
        value_lanes = slice((KV_HEADS + head) * HEAD_DIM, (KV_HEADS + head + 1) * HEAD_DIM)
        query = q[head]
        wide = query.astype(F32)
        scores = lax.dot_general(query, cache[0, :, key_lanes], dims, preferred_element_type=F32)
        scores = jnp.where(allowed, scores * scaling, NEGATIVE)
        highest = jnp.max(scores, axis=1, keepdims=True)
        fresh = []
        for step in range(STEPS):
            key = new[0, step : step + 1, key_lanes].astype(F32)
            score = jnp.sum(wide * key, axis=1, keepdims=True) * scaling
            shown = rep == 0 if step == 0 else second_step & (rep == 0)
            score = jnp.where(shown, score, NEGATIVE)
            highest = jnp.maximum(highest, score)
            fresh.append(score)
        some = highest > 0.5 * NEGATIVE
        highest = jnp.where(some, highest, 0.0)
        weight = jnp.exp(scores - highest)
        totals = jnp.sum(weight, axis=1, keepdims=True)
        sums = jnp.dot(weight.astype(BF16), cache[0, :, value_lanes], preferred_element_type=F32)
        for step in range(STEPS):
            share = jnp.exp(fresh[step] - highest)
            totals += share
            value = new[0, step : step + 1, value_lanes].astype(F32)
            sums += share.astype(BF16).astype(F32) * value
        totals = jnp.where(some, totals, 1.0)
        out[at, :ROWS] = (sums / totals).astype(BF16)
        out[at, ROWS:] = pieces_tail(jnp.where(some, highest + jnp.log(totals), NEGATIVE))


def cache_attention(part, targets, lengths, stored, grouped, kv_cache, new_kv):
    return pl.pallas_call(
        functools.partial(cache_kernel, part),
        in_specs=[SMEM] * 3 + [VMEM] * 3,
        out_specs=VMEM,
        out_shape=jax.ShapeDtypeStruct((CORE_HEADS, PART, HEAD_DIM), BF16),
        compiler_params=pltpu.CompilerParams(vmem_limit_bytes=16 * MIB),
        cost_estimate=pl.CostEstimate(
            flops=2 * grouped.size * kv_cache.shape[1],
            bytes_accessed=kv_cache.size,
            transcendentals=CORE_HEADS * ROWS * kv_cache.shape[1],
        ),
        name="cache_attention",
    )(targets, lengths, stored, grouped, kv_cache, new_kv)


def final_kernel(targets, rotary, squares, summed_a, summed_b, grouped, cached, out):
    scaling = HEAD_DIM ** (-0.5)
    dims = (((1,), (1,)), ((), ()))
    first = lax.axis_index("rep") * CORE_HEADS
    prompt = prompt_of(targets, lax.axis_index("tp"))
    cosine, sine = rotary[0], rotary[1]
    squares = squares[lax.axis_index("tp")]
    scale = token_column(lax.rsqrt(squares / D + EPSILON))
    for head in range(CORE_HEADS):
        summed = (summed_a, summed_b)[head // 2]
        keys = summed[head % 2 * STRETCH : (head % 2 + 1) * STRETCH].astype(F32)
        values = summed[(2 + head % 2) * STRETCH : (3 + head % 2) * STRETCH].astype(F32)
        keys = (keys * scale).astype(BF16).astype(F32)
        values = (values * scale).astype(BF16)
        keys = keys * cosine + pltpu.roll(keys, HEAD_DIM // 2, 1) * sine
        scores = lax.dot_general(
            grouped[first + head], keys.astype(BF16), dims, preferred_element_type=F32
        )
        scores = scores * scaling
        highest = jnp.max(scores, axis=1, keepdims=True)
        weight = jnp.exp(scores - highest)
        totals = jnp.sum(weight, axis=1, keepdims=True)
        sums = jnp.dot(weight.astype(BF16), values, preferred_element_type=F32) / totals
        logs = jnp.where(prompt >= 0, highest + jnp.log(totals), NEGATIVE)
        parts = [cached[0, first + head], cached[1, first + head]]
        logs = [tail_pieces(part[ROWS:]) for part in parts] + [logs]
        sums = [part[:ROWS].astype(F32) for part in parts] + [sums]
        highest = functools.reduce(jnp.maximum, logs)
        shares = [jnp.exp(log - highest) for log in logs]
        total = functools.reduce(jnp.add, shares)
        joined = functools.reduce(jnp.add, [share * part for share, part in zip(shares, sums)])
        result = (joined / total).astype(BF16)
        for member in range(GROUP):
            begin = (head * GROUP + member) * HEAD_DIM
            out[0, :, begin : begin + HEAD_DIM] = result[member * STEPS : (member + 1) * STEPS]


def finish(targets, rotary, squares, summed, grouped, cached):
    width = CORE_HEADS * GROUP * HEAD_DIM
    return pl.pallas_call(
        final_kernel,
        in_specs=[SMEM] + [VMEM] * 6,
        out_specs=VMEM,
        out_shape=jax.ShapeDtypeStruct((1, STEPS, width), BF16),
        compiler_params=pltpu.CompilerParams(vmem_limit_bytes=16 * MIB),
        name="finish",
    )(targets, rotary, squares, *summed, grouped, cached)


def rotary_turns():
    half = np.arange(HEAD_DIM // 2, dtype=np.float64) / (HEAD_DIM // 2)
    frequency = ROTARY_BASE ** (-np.concatenate([half, half]))
    angles = np.arange(STRETCH, dtype=np.float64)[:, None] * frequency
    return frequency.astype(np.float32), np.stack([np.cos(angles), np.sin(angles)]).astype(np.float32)


def per_device(
    stretch,
    norm_gain,
    kv_codes,
    scale_codes,
    outer_scales,
    prompt_lengths,
    target_rows,
    cache_lengths,
    kv_cache,
    queries,
    new_kv,
):
    count = lax.axis_size("tp")
    lines = stretch.transpose(1, 0, 2)
    gain = norm_gain.reshape(1, -1)

    def scatter(array):
        flat = array.reshape(-1, array.shape[2])
        return lax.psum_scatter(flat, "tp", scatter_dimension=0, tiled=True)

    other = lax.ppermute(lines, "rep", [(0, 1), (1, 0)])
    first_half, second_half, own, squares = dequantize(
        lines, kv_codes, scale_codes, outer_scales.T, gain
    )
    frequency, turns = rotary_turns()
    start = (prompt_lengths - STRETCH).astype(F32)[:, None] * jnp.asarray(frequency)
    starts = jnp.stack([jnp.cos(start), jnp.sin(start)])
    targets, second_half = lax.optimization_barrier((target_rows, second_half))
    grouped, rotary = prepare(targets, queries, starts, jnp.asarray(turns))

    gain, grouped, rotary = lax.optimization_barrier((gain, grouped, rotary))
    sums, lines, squares = project_owners(
        count, target_rows, own, squares, other, gain, first_half
    )
    summed = [scatter(sums)]
    sums = project_again(count, lines, second_half)
    sums, squares, targets = lax.optimization_barrier((sums, squares, target_rows))
    summed.append(scatter(sums))
    cached = [
        cache_attention(
            part, targets, prompt_lengths, cache_lengths, grouped, kv_cache, new_kv
        )
        for part in range(2)
    ]
    step = 1
    while step < count:
        squares += lax.ppermute(squares, "tp", [(at, at ^ step) for at in range(count)])
        step *= 2
    cached = lax.all_gather(jnp.concatenate(cached), "rep")
    out = finish(target_rows, rotary, squares, summed, grouped, cached)
    return lax.all_gather(out, "rep", axis=2, tiled=True)


def solution(mesh):
    in_specs = (
        P(None, ("grp", "rep"), "tp"),
        P("tp"),
        P("tp", None),
        P("tp", None),
        P("tp", None),
        P("grp"),
        P("grp"),
        P(("grp", "tp")),
        P(("grp", "tp"), "rep", None),
        P(("grp", "tp"), None, None),
        P(("grp", "tp"), None, None),
    )
    out_specs = P(("grp", "tp"), None, None)
    return jax.shard_map(
        per_device, mesh=mesh, in_specs=in_specs, out_specs=out_specs, check_vma=False
    )
```

```python
import functools
import math

import jax
import jax.numpy as jnp
import numpy as np
from jax import lax
from jax.experimental import pallas as pl
from jax.experimental.pallas import tpu as pltpu
from jax.sharding import PartitionSpec as P

D = 16384
HEADS = 128
KV_HEADS = 8
HEAD_DIM = 128
STRETCH = 192
STEPS = 2
QBLOCK = 64
GROUP = HEADS // KV_HEADS
ROWS = GROUP * STEPS
TAIL = 16
PART = ROWS + TAIL
CORE_HEADS = KV_HEADS // 2
NORMAL_FLOAT_LEVELS = [
    -1.0,
    -0.6961928009986877,
    -0.5250730514526367,
    -0.39491748809814453,
    -0.28444138169288635,
    -0.18477343022823334,
    -0.09105003625154495,
    0.0,
    0.07958029955625534,
    0.16093020141124725,
    0.24611230194568634,
    0.33791524171829224,
    0.44070982933044434,
    0.5626170039176941,
    0.7229568362236023,
    1.0,
]
ROTARY_BASE = 500000.0
EPSILON = 1e-05
NEGATIVE = -1e30
BF16 = jnp.bfloat16
F32 = jnp.float32
MIB = 1024 * 1024
VMEM = pl.BlockSpec(memory_space=pltpu.VMEM)
SMEM = pl.BlockSpec(memory_space=pltpu.SMEM)


def in_hbm(*arrays):
    return [pltpu.with_memory_space_constraint(array, pltpu.HBM) for array in arrays]


def ring_device(place, count):
    half = count // 2
    if isinstance(place, int):
        return 2 * place if place < half else 2 * (count - 1 - place) + 1
    return jnp.where(place < half, 2 * place, 2 * (count - 1 - place) + 1)


def owner_at(distance):
    count = lax.axis_size("tp")
    here = lax.axis_index("tp")
    place = jnp.where(here % 2 == 0, here // 2, count - 1 - here // 2)
    return ring_device((place + distance + count) % count, count)


def turned(column):
    rows = lax.broadcasted_iota(jnp.int32, (column.shape[0], 128), 0)
    lanes = lax.broadcasted_iota(jnp.int32, (column.shape[0], 128), 1)
    return jnp.sum(jnp.where(rows == lanes, column, 0.0), axis=0, keepdims=True)


def stood(row, count):
    rows = lax.broadcasted_iota(jnp.int32, (count, 128), 0)
    lanes = lax.broadcasted_iota(jnp.int32, (count, 128), 1)
    return jnp.sum(jnp.where(rows == lanes, row, 0.0), axis=1, keepdims=True)


def token_rows(column):
    at = lax.broadcasted_iota(jnp.int32, (8, 128), 0)
    ends = turned(column[128:])
    return jnp.where(at == 0, turned(column[:128]), jnp.where(at == 1, ends, 0.0))


def token_column(rows):
    return jnp.concatenate([stood(rows[0:1], 128), stood(rows[1:2], STRETCH - 128)], axis=0)


def two_pieces(rows):
    high = rows.astype(BF16).astype(F32)
    return jnp.concatenate([high, rows - high], axis=0).astype(BF16)


def one_piece(rows):
    rows = rows.astype(F32)
    return rows[:8] + rows[8:]


def pieces_tail(logs):
    row = turned(logs)
    high = row.astype(BF16).astype(F32)
    middle = (row - high).astype(BF16).astype(F32)
    low = row - high - middle
    at = lax.broadcasted_iota(jnp.int32, (TAIL, 128), 0)
    tail = jnp.where(at == 0, high, jnp.where(at == 1, middle, jnp.where(at == 2, low, 0.0)))
    return tail.astype(BF16)


def tail_pieces(tail):
    tail = tail.astype(F32)
    return stood(tail[0:1, :] + tail[1:2, :] + tail[2:3, :], ROWS)


def gathered_levels(table, codes):
    numbers = lax.GatherDimensionNumbers(
        offset_dims=(),
        collapsed_slice_dims=(1,),
        start_index_map=(1,),
        operand_batching_dims=(0,),
        start_indices_batching_dims=(0,),
    )
    return lax.gather(
        table, codes[..., None], numbers, (1, 1), mode=lax.GatherScatterMode.PROMISE_IN_BOUNDS
    )


def block_scales(scales, outer, column):
    count = scales.shape[0]
    line = lax.broadcasted_iota(jnp.int32, outer.shape, 0)
    line = jnp.sum(jnp.where(line == column, outer, 0.0), axis=0, keepdims=True)
    rows = lax.broadcasted_iota(jnp.int32, (count, count), 0)
    lanes = lax.broadcasted_iota(jnp.int32, (count, count), 1)
    second = jnp.sum(jnp.where(rows == lanes, line, 0.0), axis=1, keepdims=True)
    return (scales.astype(F32) + 1.0) / 256.0 * second


def weights_kernel(key_codes, value_codes, key_scales, value_scales, outer, out, scales):
    block = pl.program_id(0)
    depth = key_codes.shape[0]
    columns = outer.shape[0] // 2

    @pl.when(block == 0)
    def _():
        for at in range(CORE_HEADS):
            head = lax.axis_index("rep") * CORE_HEADS + at
            column = head // (KV_HEADS // columns)
            lanes = slice(at * HEAD_DIM, (at + 1) * HEAD_DIM)
            scales[2 * at] = block_scales(key_scales[:, lanes], outer[...], column)
            scales[2 * at + 1] = block_scales(value_scales[:, lanes], outer[...], columns + column)

    lane = lax.broadcasted_iota(jnp.int32, (8, 128), 1)
    table = jnp.zeros((8, 128), F32)
    for code, level in enumerate(NORMAL_FLOAT_LEVELS):
        table = jnp.where(lane == code, level, table)

    def body(step, _):
        begin = pl.multiple_of(step * QBLOCK, QBLOCK)
        row = pl.ds(block * (depth // QBLOCK) + step, 1)
        for at in range(CORE_HEADS):
            lanes = slice(at * HEAD_DIM, (at + 1) * HEAD_DIM)
            key_scale, value_scale = scales[2 * at, row, :], scales[2 * at + 1, row, :]
            for tile in range(QBLOCK // 16):
                rows = pl.ds(pl.multiple_of(begin + 16 * tile, 16), 16)
                key, value = key_codes[rows, lanes], value_codes[rows, lanes]
                keys = [gathered_levels(table, key[half : half + 8]) for half in (0, 8)]
                values = [gathered_levels(table, value[half : half + 8]) for half in (0, 8)]
                rows = pl.ds(pl.multiple_of(block * depth + begin + 16 * tile, 16), 16)
                keys = jnp.concatenate([level * key_scale for level in keys], axis=0)
                values = jnp.concatenate([level * value_scale for level in values], axis=0)
                out[at, rows, :HEAD_DIM] = keys.astype(BF16)
                out[at, rows, HEAD_DIM:] = values.astype(BF16)
        return 0

    lax.fori_loop(0, depth // QBLOCK, body, 0)


def dequantize(codes, scales, outer):
    features = codes.shape[0]
    depth = min(256, features)
    width = CORE_HEADS * HEAD_DIM
    rep = lambda: lax.axis_index("rep")
    codes, scales, outer = in_hbm(codes, scales, outer)
    return pl.pallas_call(
        weights_kernel,
        grid=(features // depth,),
        in_specs=[
            pl.BlockSpec((depth, width), lambda k: (k, rep())),
            pl.BlockSpec((depth, width), lambda k: (k, 2 + rep())),
            pl.BlockSpec((scales.shape[0], width), lambda k: (0, rep())),
            pl.BlockSpec((scales.shape[0], width), lambda k: (0, 2 + rep())),
            pl.BlockSpec(outer.shape, lambda k: (0, 0)),
        ],
        out_specs=VMEM,
        out_shape=jax.ShapeDtypeStruct((CORE_HEADS, features, 2 * HEAD_DIM), BF16),
        scratch_shapes=[pltpu.VMEM((2 * CORE_HEADS, scales.shape[0], HEAD_DIM), F32)],
        compiler_params=pltpu.CompilerParams(vmem_limit_bytes=32 * MIB),
        cost_estimate=pl.CostEstimate(
            flops=32 * codes.size, bytes_accessed=codes.size * 2, transcendentals=0
        ),
        name="dequantize",
    )(codes, codes, scales, scales, outer)


def scale_kernel(x, gain, scaled, squares):
    item = pl.program_id(0)

    @pl.when(item == 0)
    def _():
        squares[...] = jnp.zeros(squares.shape, F32)

    width = x.shape[2]
    begin = pl.multiple_of(item * width, 128)
    for prompt in range(x.shape[0]):
        wide = x[prompt].astype(F32)
        scaled[prompt, :, pl.ds(begin, width)] = (wide * gain[...]).astype(BF16)
        squares[prompt] += token_rows(jnp.sum(wide * wide, axis=1, keepdims=True))


def scale_features(x, gain):
    per_rep, _, features = x.shape
    width = max(128, features // 4)
    x, gain = in_hbm(x, gain)
    return pl.pallas_call(
        scale_kernel,
        grid=(features // width,),
        in_specs=[
            pl.BlockSpec((per_rep, STRETCH, width), lambda i: (0, 0, i)),
            pl.BlockSpec((1, width), lambda i: (0, i)),
        ],
        out_specs=[VMEM] * 2,
        out_shape=[
            jax.ShapeDtypeStruct(x.shape, BF16),
            jax.ShapeDtypeStruct((per_rep, 8, 128), F32),
        ],
        compiler_params=pltpu.CompilerParams(vmem_limit_bytes=24 * MIB),
        name="scale_features",
    )(x, gain)


def prompt_of(targets, owner):
    prompt = jnp.int32(-1)
    for at in range(targets.shape[0]):
        prompt = jnp.where(targets[at] == owner, at, prompt)
    return prompt


def with_lines(targets, distance, own, squares, other, other_squares, some, none):
    per_rep = own.shape[0]
    prompt = prompt_of(targets, owner_at(distance))
    at = lax.rem(jnp.maximum(prompt, 0), per_rep)
    is_own = prompt // per_rep == lax.axis_index("rep")
    pl.when((prompt >= 0) & is_own)(lambda: some(own.at[at], squares.at[at]))
    pl.when((prompt >= 0) & jnp.logical_not(is_own))(
        lambda: some(other.at[at], other_squares.at[at])
    )
    pl.when(prompt < 0)(none)


def first_kernel(distance, targets, own, squares, other, other_squares, weight, right, left):
    def some(lines, sums):
        for head in range(CORE_HEADS):
            product = jnp.dot(lines[...], weight[head], preferred_element_type=F32)
            rows = slice(head * STRETCH, (head + 1) * STRETCH)
            right[rows] = product[:, :HEAD_DIM].astype(BF16)
            left[rows] = product[:, HEAD_DIM:].astype(BF16)
        right[CORE_HEADS * STRETCH :] = two_pieces(sums[...])

    def none():
        right[...] = jnp.zeros(right.shape, BF16)
        left[...] = jnp.zeros(left.shape, BF16)

    with_lines(targets, distance, own, squares, other, other_squares, some, none)


def project_first(distance, targets, own, squares, other, other_squares, weight):
    rows = CORE_HEADS * STRETCH
    return pl.pallas_call(
        functools.partial(first_kernel, distance),
        in_specs=[SMEM] + [VMEM] * 5,
        out_specs=[VMEM] * 2,
        out_shape=[
            jax.ShapeDtypeStruct((rows + TAIL, HEAD_DIM), BF16),
            jax.ShapeDtypeStruct((rows, HEAD_DIM), BF16),
        ],
        compiler_params=pltpu.CompilerParams(vmem_limit_bytes=24 * MIB),
        cost_estimate=pl.CostEstimate(
            flops=STRETCH * weight.size * 2, bytes_accessed=weight.size, transcendentals=0
        ),
        name="project_first",
    )(targets, own, squares, other, other_squares, weight)


def project_kernel(distances, targets, own, squares, other, other_squares, weight, out):
    for item, distance in enumerate(distances):

        def some(lines, sums, item=item):
            for head in range(CORE_HEADS):
                product = jnp.dot(lines[...], weight[head], preferred_element_type=F32)
                begin = head % 2 * STRETCH
                out[item, head // 2, begin : begin + STRETCH] = product[:, :HEAD_DIM]
                begin += 2 * STRETCH
                out[item, head // 2, begin : begin + STRETCH] = product[:, HEAD_DIM:]
            for half in range(2):
                out[item, half, 4 * STRETCH :] = sums[...]

        def none(item=item):
            out[item] = jnp.zeros(out.shape[1:], F32)

        with_lines(targets, distance, own, squares, other, other_squares, some, none)


def project(distances, targets, own, squares, other, other_squares, weight):
    return pl.pallas_call(
        functools.partial(project_kernel, distances),
        in_specs=[SMEM] + [VMEM] * 5,
        out_specs=VMEM,
        out_shape=jax.ShapeDtypeStruct((len(distances), 2, 4 * STRETCH + 8, HEAD_DIM), F32),
        compiler_params=pltpu.CompilerParams(vmem_limit_bytes=24 * MIB),
        cost_estimate=pl.CostEstimate(
            flops=len(distances) * STRETCH * weight.size * 2 // 2,
            bytes_accessed=weight.size,
            transcendentals=0,
        ),
        name="project",
    )(targets, own, squares, other, other_squares, weight)


def send_kernel(half, first, terms, right, left, to_right, to_left):
    rows = 4 * STRETCH
    middle = 2 * STRETCH
    if first:
        from_right = right[half * middle : (half + 1) * middle].astype(F32)
        from_left = left[half * middle : (half + 1) * middle].astype(F32)
        to_right[:middle] = (terms[0, half, :middle] + from_right).astype(BF16)
        to_right[middle:rows] = terms[0, half, middle:rows].astype(BF16)
        to_left[:middle] = terms[1, half, :middle].astype(BF16)
        to_left[middle:rows] = (terms[1, half, middle:rows] + from_left).astype(BF16)
    else:
        to_right[:rows] = (terms[0, half, :rows] + right[:rows].astype(F32)).astype(BF16)
        to_left[:rows] = (terms[1, half, :rows] + left[:rows].astype(F32)).astype(BF16)
    if half == 0:
        right_sum = terms[0, 0, rows:] + one_piece(right[rows:])
        left_sum = terms[1, 0, rows:]
        if not first:
            left_sum += one_piece(left[rows:])
        to_right[rows:] = two_pieces(right_sum)
        to_left[rows:] = two_pieces(left_sum)


def sends(half, first, terms, right, left):
    rows = 4 * STRETCH + (TAIL if half == 0 else 0)
    shape = jax.ShapeDtypeStruct((rows, HEAD_DIM), BF16)
    return pl.pallas_call(
        functools.partial(send_kernel, half, first),
        in_specs=[VMEM] * 3,
        out_specs=[VMEM] * 2,
        out_shape=[shape, shape],
        compiler_params=pltpu.CompilerParams(vmem_limit_bytes=16 * MIB),
        name="sends",
    )(terms, right, left)


def prepare_kernel(targets, queries, starts, turns, grouped, rotary):
    for head in range(KV_HEADS):
        for member in range(GROUP):
            begin = (head * GROUP + member) * HEAD_DIM
            rows = slice(member * STEPS, (member + 1) * STEPS)
            grouped[head, rows] = queries[0, :, begin : begin + HEAD_DIM]
    row = pl.ds(jnp.maximum(prompt_of(targets, lax.axis_index("tp")), 0), 1)
    cosine, sine = starts[0, row, :], starts[1, row, :]
    lane = lax.broadcasted_iota(jnp.int32, turns.shape[1:], 1)
    rotary[0] = turns[0] * cosine - turns[1] * sine
    sine = turns[1] * cosine + turns[0] * sine
    rotary[1] = jnp.where(lane < HEAD_DIM // 2, -sine, sine)


def prepare(targets, queries, starts, turns):
    return pl.pallas_call(
        prepare_kernel,
        in_specs=[SMEM] + [VMEM] * 3,
        out_specs=[VMEM] * 2,
        out_shape=[
            jax.ShapeDtypeStruct((KV_HEADS, ROWS, HEAD_DIM), BF16),
            jax.ShapeDtypeStruct(turns.shape, F32),
        ],
        compiler_params=pltpu.CompilerParams(vmem_limit_bytes=16 * MIB),
        name="prepare",
    )(targets, queries, starts, turns)


def cache_kernel(part, targets, lengths, stored, q, cache, new, out):
    scaling = HEAD_DIM ** (-0.5)
    dims = (((1,), (1,)), ((), ()))
    here = lax.axis_index("tp")
    rep = lax.axis_index("rep")
    length = cache.shape[1]
    prompt = prompt_of(targets, here)
    handed = lengths[jnp.maximum(prompt, 0)] - STRETCH
    span = jnp.where(prompt >= 0, handed, stored[0]) - rep * length
    allowed = lax.broadcasted_iota(jnp.int32, (ROWS, length), 1) < span
    second_step = lax.broadcasted_iota(jnp.int32, (ROWS, 1), 0) % STEPS == 1
    for at in range(CORE_HEADS):
        head = (rep if part == 1 else 1 - rep) * CORE_HEADS + at
        key_lanes = pl.ds(pl.multiple_of(head * HEAD_DIM, HEAD_DIM), HEAD_DIM)
        value_lanes = pl.ds(pl.multiple_of((KV_HEADS + head) * HEAD_DIM, HEAD_DIM), HEAD_DIM)
        query = q[head]
        wide = query.astype(F32)
        scores = lax.dot_general(query, cache[0, :, key_lanes], dims, preferred_element_type=F32)
        scores = jnp.where(allowed, scores * scaling, NEGATIVE)
        highest = jnp.max(scores, axis=1, keepdims=True)
        fresh = []
        for step in range(STEPS):
            key = new[0, step : step + 1, key_lanes].astype(F32)
            score = jnp.sum(wide * key, axis=1, keepdims=True) * scaling
            shown = rep == 0 if step == 0 else second_step & (rep == 0)
            score = jnp.where(shown, score, NEGATIVE)
            highest = jnp.maximum(highest, score)
            fresh.append(score)
        some = highest > 0.5 * NEGATIVE
        highest = jnp.where(some, highest, 0.0)
        weight = jnp.exp(scores - highest)
        totals = jnp.sum(weight, axis=1, keepdims=True)
        sums = jnp.dot(weight.astype(BF16), cache[0, :, value_lanes], preferred_element_type=F32)
        for step in range(STEPS):
            share = jnp.exp(fresh[step] - highest)
            totals += share
            value = new[0, step : step + 1, value_lanes].astype(F32)
            sums += share.astype(BF16).astype(F32) * value
        totals = jnp.where(some, totals, 1.0)
        out[at, :ROWS] = (sums / totals).astype(BF16)
        out[at, ROWS:] = pieces_tail(jnp.where(some, highest + jnp.log(totals), NEGATIVE))


def cache_attention(part, targets, lengths, stored, grouped, kv_cache, new_kv):
    return pl.pallas_call(
        functools.partial(cache_kernel, part),
        in_specs=[SMEM] * 3 + [VMEM] * 3,
        out_specs=VMEM,
        out_shape=jax.ShapeDtypeStruct((CORE_HEADS, PART, HEAD_DIM), BF16),
        compiler_params=pltpu.CompilerParams(vmem_limit_bytes=16 * MIB),
        cost_estimate=pl.CostEstimate(
            flops=2 * grouped.size * kv_cache.shape[1],
            bytes_accessed=kv_cache.size,
            transcendentals=CORE_HEADS * ROWS * kv_cache.shape[1],
        ),
        name="cache_attention",
    )(targets, lengths, stored, grouped, kv_cache, new_kv)


def final_kernel(
    targets, rotary, own, right_a, left_a, right_b, left_b, grouped, cached_there, cached_here, out
):
    scaling = HEAD_DIM ** (-0.5)
    dims = (((1,), (1,)), ((), ()))
    mine = own.shape[0] - 1
    rep = lax.axis_index("rep")
    first = rep * CORE_HEADS
    prompt = prompt_of(targets, lax.axis_index("tp"))
    cosine, sine = rotary[0], rotary[1]
    rows = 4 * STRETCH
    squares = own[mine, 0, rows:] + one_piece(right_a[rows:]) + one_piece(left_a[rows:])
    scale = token_column(lax.rsqrt(squares / D + EPSILON))
    for head in range(CORE_HEADS):
        right, left = ((right_a, left_a), (right_b, left_b))[head // 2]
        at = slice(head % 2 * STRETCH, (head % 2 + 1) * STRETCH)
        keys = own[mine, head // 2, at] + right[at].astype(F32) + left[at].astype(F32)
        at = slice((2 + head % 2) * STRETCH, (3 + head % 2) * STRETCH)
        values = own[mine, head // 2, at] + right[at].astype(F32) + left[at].astype(F32)
        keys = (keys * scale).astype(BF16).astype(F32)
        values = (values * scale).astype(BF16)
        keys = keys * cosine + pltpu.roll(keys, HEAD_DIM // 2, 1) * sine
        scores = lax.dot_general(
            grouped[first + head], keys.astype(BF16), dims, preferred_element_type=F32
        )
        scores = scores * scaling
        highest = jnp.max(scores, axis=1, keepdims=True)
        weight = jnp.exp(scores - highest)
        totals = jnp.sum(weight, axis=1, keepdims=True)
        sums = jnp.dot(weight.astype(BF16), values, preferred_element_type=F32) / totals
        logs = jnp.where(prompt >= 0, highest + jnp.log(totals), NEGATIVE)
        parts = [cached_there[head], cached_here[head]]
        logs = [tail_pieces(part[ROWS:]) for part in parts] + [logs]
        sums = [part[:ROWS].astype(F32) for part in parts] + [sums]
        highest = functools.reduce(jnp.maximum, logs)
        shares = [jnp.exp(log - highest) for log in logs]
        total = functools.reduce(jnp.add, shares)
        joined = functools.reduce(jnp.add, [share * part for share, part in zip(shares, sums)])
        result = (joined / total).astype(BF16)
        for member in range(GROUP):
            begin = (head * GROUP + member) * HEAD_DIM
            out[0, :, begin : begin + HEAD_DIM] = result[member * STEPS : (member + 1) * STEPS]


def finish(targets, rotary, own, arrived, grouped, cached):
    width = CORE_HEADS * GROUP * HEAD_DIM
    return pl.pallas_call(
        final_kernel,
        in_specs=[SMEM] + [VMEM] * 9,
        out_specs=VMEM,
        out_shape=jax.ShapeDtypeStruct((1, STEPS, width), BF16),
        compiler_params=pltpu.CompilerParams(vmem_limit_bytes=16 * MIB),
        name="finish",
    )(targets, rotary, own, *arrived, grouped, *cached)


def rotary_turns():
    half = np.arange(HEAD_DIM // 2, dtype=np.float64) / (HEAD_DIM // 2)
    frequency = ROTARY_BASE ** (-np.concatenate([half, half]))
    angles = np.arange(STRETCH, dtype=np.float64)[:, None] * frequency
    return frequency.astype(np.float32), np.stack([np.cos(angles), np.sin(angles)]).astype(np.float32)


def per_device(
    stretch,
    norm_gain,
    kv_codes,
    scale_codes,
    outer_scales,
    prompt_lengths,
    target_rows,
    cache_lengths,
    kv_cache,
    queries,
    new_kv,
):
    count = lax.axis_size("tp")
    half = count // 2
    lines = stretch.transpose(1, 0, 2)
    gain = norm_gain.reshape(1, -1)
    ring = [ring_device(at, count) for at in range(count)]
    to_right = [(ring[at], ring[(at + 1) % count]) for at in range(count)]
    to_left = [(ring[at], ring[at - 1]) for at in range(count)]

    def pass_on(right, left):
        return lax.ppermute(right, "tp", to_right), lax.ppermute(left, "tp", to_left)

    own, squares = scale_features(lines, gain)
    swap = lambda array: lax.ppermute(array, "rep", [(0, 1), (1, 0)])
    other, other_squares = swap(own), swap(squares)
    weight = dequantize(kv_codes, scale_codes, outer_scales.T)
    frequency, turns = rotary_turns()
    start = (prompt_lengths - STRETCH).astype(F32)[:, None] * jnp.asarray(frequency)
    starts = jnp.stack([jnp.cos(start), jnp.sin(start)])
    targets, weight = lax.optimization_barrier((target_rows, weight))
    grouped, rotary = prepare(targets, queries, starts, jnp.asarray(turns))

    weight, grouped, rotary = lax.optimization_barrier((weight, grouped, rotary))
    features = [own, squares, other, other_squares]
    right, left = project_first(half, target_rows, *features, weight)
    targets, _ = lax.optimization_barrier((target_rows, left))
    arrived = [pass_on(right, left)] * 2

    cached = []
    for distance in range(half - 1, 0, -1):
        distances = [distance, -distance] + ([0] if distance == 1 else [])
        if len(cached) < 2:
            cached.append(
                cache_attention(
                    len(cached), targets, prompt_lengths, cache_lengths, grouped, kv_cache, new_kv
                )
            )
        if len(cached) == 1:
            cached = [swap(cached[0])]
        terms = project(distances, targets, *features, weight)
        later = terms
        for part in range(2):
            right, left = sends(part, distance == half - 1, (terms, later)[part], *arrived[part])
            if part == 0:
                right, cached, later = lax.optimization_barrier((right, cached, terms))
            targets, _ = lax.optimization_barrier((target_rows, right))
            arrived[part] = pass_on(right, left)

    out = finish(target_rows, rotary, terms, [*arrived[0], *arrived[1]], grouped, cached)
    return lax.all_gather(out, "rep", axis=2, tiled=True)


def solution(mesh):
    in_specs = (
        P(None, ("grp", "rep"), "tp"),
        P("tp"),
        P("tp", None),
        P("tp", None),
        P("tp", None),
        P("grp"),
        P("grp"),
        P(("grp", "tp")),
        P(("grp", "tp"), "rep", None),
        P(("grp", "tp"), None, None),
        P(("grp", "tp"), None, None),
    )
    out_specs = P(("grp", "tp"), None, None)
    return jax.shard_map(
        per_device, mesh=mesh, in_specs=in_specs, out_specs=out_specs, check_vma=False
    )
```

```python
import functools
import math

import jax
import jax.numpy as jnp
import numpy as np
from jax import lax
from jax.experimental import pallas as pl
from jax.experimental.pallas import tpu as pltpu
from jax.sharding import PartitionSpec as P

D = 16384
HEADS = 128
KV_HEADS = 8
HEAD_DIM = 128
STRETCH = 192
STEPS = 2
QBLOCK = 64
GROUP = HEADS // KV_HEADS
ROWS = GROUP * STEPS
TAIL = 16
PART = ROWS + TAIL
CORE_HEADS = KV_HEADS // 2
NORMAL_FLOAT_LEVELS = [
    -1.0,
    -0.6961928009986877,
    -0.5250730514526367,
    -0.39491748809814453,
    -0.28444138169288635,
    -0.18477343022823334,
    -0.09105003625154495,
    0.0,
    0.07958029955625534,
    0.16093020141124725,
    0.24611230194568634,
    0.33791524171829224,
    0.44070982933044434,
    0.5626170039176941,
    0.7229568362236023,
    1.0,
]
ROTARY_BASE = 500000.0
EPSILON = 1e-05
NEGATIVE = -1e30
BF16 = jnp.bfloat16
F32 = jnp.float32
MIB = 1024 * 1024
VMEM = pl.BlockSpec(memory_space=pltpu.VMEM)
SMEM = pl.BlockSpec(memory_space=pltpu.SMEM)


def in_hbm(*arrays):
    return [pltpu.with_memory_space_constraint(array, pltpu.HBM) for array in arrays]


def ring_device(place, count):
    half = count // 2
    if isinstance(place, int):
        return 2 * place if place < half else 2 * (count - 1 - place) + 1
    return jnp.where(place < half, 2 * place, 2 * (count - 1 - place) + 1)


def owner_at(distance):
    count = lax.axis_size("tp")
    here = lax.axis_index("tp")
    place = jnp.where(here % 2 == 0, here // 2, count - 1 - here // 2)
    return ring_device((place + distance + count) % count, count)


def turned(column):
    rows = lax.broadcasted_iota(jnp.int32, (column.shape[0], 128), 0)
    lanes = lax.broadcasted_iota(jnp.int32, (column.shape[0], 128), 1)
    return jnp.sum(jnp.where(rows == lanes, column, 0.0), axis=0, keepdims=True)


def stood(row, count):
    rows = lax.broadcasted_iota(jnp.int32, (count, 128), 0)
    lanes = lax.broadcasted_iota(jnp.int32, (count, 128), 1)
    return jnp.sum(jnp.where(rows == lanes, row, 0.0), axis=1, keepdims=True)


def token_rows(column):
    at = lax.broadcasted_iota(jnp.int32, (8, 128), 0)
    ends = turned(column[128:])
    return jnp.where(at == 0, turned(column[:128]), jnp.where(at == 1, ends, 0.0))


def token_column(rows):
    return jnp.concatenate([stood(rows[0:1], 128), stood(rows[1:2], STRETCH - 128)], axis=0)


def two_pieces(rows):
    high = rows.astype(BF16).astype(F32)
    return jnp.concatenate([high, rows - high], axis=0).astype(BF16)


def one_piece(rows):
    rows = rows.astype(F32)
    return rows[:8] + rows[8:]


def pieces_tail(logs):
    row = turned(logs)
    high = row.astype(BF16).astype(F32)
    middle = (row - high).astype(BF16).astype(F32)
    low = row - high - middle
    at = lax.broadcasted_iota(jnp.int32, (TAIL, 128), 0)
    tail = jnp.where(at == 0, high, jnp.where(at == 1, middle, jnp.where(at == 2, low, 0.0)))
    return tail.astype(BF16)


def tail_pieces(tail):
    tail = tail.astype(F32)
    return stood(tail[0:1, :] + tail[1:2, :] + tail[2:3, :], ROWS)


def block_leaves(scale):
    wide = jnp.broadcast_to(scale, (16, HEAD_DIM))
    return [(wide * jnp.float32(level)).astype(BF16) for level in NORMAL_FLOAT_LEVELS]


def selected(codes, leaves):
    codes = codes.astype(jnp.int16)
    masks = [(codes & (1 << bit)) != 0 for bit in range(4)]

    def node(bit, base):
        if bit < 0:
            return leaves[base]
        low = node(bit - 1, base)
        return jnp.where(masks[bit], node(bit - 1, base + (1 << bit)), low)

    return node(3, 0)


def block_scales(scales, outer, column):
    count = scales.shape[0]
    line = lax.broadcasted_iota(jnp.int32, outer.shape, 0)
    line = jnp.sum(jnp.where(line == column, outer, 0.0), axis=0, keepdims=True)
    rows = lax.broadcasted_iota(jnp.int32, (count, count), 0)
    lanes = lax.broadcasted_iota(jnp.int32, (count, count), 1)
    second = jnp.sum(jnp.where(rows == lanes, line, 0.0), axis=1, keepdims=True)
    return (scales.astype(F32) + 1.0) / 256.0 * second


def weights_kernel(key_codes, value_codes, key_scales, value_scales, outer, out, scales):
    block = pl.program_id(0)
    depth = key_codes.shape[0]
    columns = outer.shape[0] // 2

    @pl.when(block == 0)
    def _():
        for at in range(CORE_HEADS):
            head = lax.axis_index("rep") * CORE_HEADS + at
            column = head // (KV_HEADS // columns)
            lanes = slice(at * HEAD_DIM, (at + 1) * HEAD_DIM)
            scales[2 * at] = block_scales(key_scales[:, lanes], outer[...], column)
            scales[2 * at + 1] = block_scales(value_scales[:, lanes], outer[...], columns + column)

    def body(step, _):
        begin = pl.multiple_of(step * QBLOCK, QBLOCK)
        row = pl.ds(block * (depth // QBLOCK) + step, 1)
        for at in range(CORE_HEADS):
            lanes = slice(at * HEAD_DIM, (at + 1) * HEAD_DIM)
            for kind, codes in enumerate((key_codes, value_codes)):
                leaves = block_leaves(scales[2 * at + kind, row, :])
                columns = slice(kind * HEAD_DIM, (kind + 1) * HEAD_DIM)
                for tile in range(QBLOCK // 16):
                    rows = pl.ds(pl.multiple_of(begin + 16 * tile, 16), 16)
                    weight = selected(codes[rows, lanes], leaves)
                    rows = pl.ds(pl.multiple_of(block * depth + begin + 16 * tile, 16), 16)
                    out[at, rows, columns] = weight
        return 0

    lax.fori_loop(0, depth // QBLOCK, body, 0)


def dequantize(codes, scales, outer):
    features = codes.shape[0]
    depth = min(256, features)
    width = CORE_HEADS * HEAD_DIM
    rep = lambda: lax.axis_index("rep")
    codes, scales, outer = in_hbm(codes, scales, outer)
    return pl.pallas_call(
        weights_kernel,
        grid=(features // depth,),
        in_specs=[
            pl.BlockSpec((depth, width), lambda k: (k, rep())),
            pl.BlockSpec((depth, width), lambda k: (k, 2 + rep())),
            pl.BlockSpec((scales.shape[0], width), lambda k: (0, rep())),
            pl.BlockSpec((scales.shape[0], width), lambda k: (0, 2 + rep())),
            pl.BlockSpec(outer.shape, lambda k: (0, 0)),
        ],
        out_specs=VMEM,
        out_shape=jax.ShapeDtypeStruct((CORE_HEADS, features, 2 * HEAD_DIM), BF16),
        scratch_shapes=[pltpu.VMEM((2 * CORE_HEADS, scales.shape[0], HEAD_DIM), F32)],
        compiler_params=pltpu.CompilerParams(vmem_limit_bytes=32 * MIB),
        cost_estimate=pl.CostEstimate(
            flops=32 * codes.size, bytes_accessed=codes.size * 2, transcendentals=0
        ),
        name="dequantize",
    )(codes, codes, scales, scales, outer)


def scale_kernel(x, gain, scaled, squares, lines, factors, column, arrivals):
    half = STRETCH // 2
    pieces = [(prompt, slice(at, at + half)) for prompt in range(x.shape[0]) for at in (0, half)]

    def copy(item):
        prompt, rows = pieces[item]
        return pltpu.make_async_copy(
            x.at[prompt, rows], lines.at[prompt, rows], arrivals.at[item]
        )

    gain_copy = pltpu.make_async_copy(gain, factors, arrivals.at[len(pieces)])
    gain_copy.start()
    for item in range(len(pieces)):
        copy(item).start()
    gain_copy.wait()
    for item, (prompt, rows) in enumerate(pieces):
        copy(item).wait()
        begin = rows.start

        def body(step, _, prompt=prompt, begin=begin):
            rows = pl.ds(pl.multiple_of(begin + step * 16, 16), 16)
            wide = lines[prompt, rows, :].astype(F32)
            scaled[prompt, rows, :] = (wide * factors[...]).astype(BF16)
            total = jnp.sum(wide * wide, axis=1, keepdims=True)
            column[rows, :] = jnp.broadcast_to(total, (16, 128))
            return 0

        lax.fori_loop(0, half // 16, body, 0)
        if begin > 0:
            squares[prompt] = token_rows(column[:, :1])


def scale_features(x, gain):
    x, gain = in_hbm(x, gain)
    return pl.pallas_call(
        scale_kernel,
        in_specs=[pl.BlockSpec(memory_space=pltpu.HBM)] * 2,
        out_specs=[VMEM] * 2,
        out_shape=[
            jax.ShapeDtypeStruct(x.shape, BF16),
            jax.ShapeDtypeStruct((x.shape[0], 8, 128), F32),
        ],
        scratch_shapes=[
            pltpu.VMEM(x.shape, BF16),
            pltpu.VMEM(gain.shape, F32),
            pltpu.VMEM((STRETCH, 128), F32),
            pltpu.SemaphoreType.DMA((2 * x.shape[0] + 1,)),
        ],
        compiler_params=pltpu.CompilerParams(vmem_limit_bytes=24 * MIB),
        name="scale_features",
    )(x, gain)


def prompt_of(targets, owner):
    prompt = jnp.int32(-1)
    for at in range(targets.shape[0]):
        prompt = jnp.where(targets[at] == owner, at, prompt)
    return prompt


def with_lines(targets, distance, own, squares, other, other_squares, some, none):
    per_rep = own.shape[0]
    prompt = prompt_of(targets, owner_at(distance))
    at = lax.rem(jnp.maximum(prompt, 0), per_rep)
    is_own = prompt // per_rep == lax.axis_index("rep")
    pl.when((prompt >= 0) & is_own)(lambda: some(own.at[at], squares.at[at]))
    pl.when((prompt >= 0) & jnp.logical_not(is_own))(
        lambda: some(other.at[at], other_squares.at[at])
    )
    pl.when(prompt < 0)(none)


def first_kernel(distance, targets, own, squares, other, other_squares, weight, right, left):
    def some(lines, sums):
        for head in range(CORE_HEADS):
            product = jnp.dot(lines[...], weight[head], preferred_element_type=F32)
            rows = slice(head * STRETCH, (head + 1) * STRETCH)
            right[rows] = product[:, :HEAD_DIM].astype(BF16)
            left[rows] = product[:, HEAD_DIM:].astype(BF16)
        right[CORE_HEADS * STRETCH :] = two_pieces(sums[...])

    def none():
        right[...] = jnp.zeros(right.shape, BF16)
        left[...] = jnp.zeros(left.shape, BF16)

    with_lines(targets, distance, own, squares, other, other_squares, some, none)


def project_first(distance, targets, own, squares, other, other_squares, weight):
    rows = CORE_HEADS * STRETCH
    return pl.pallas_call(
        functools.partial(first_kernel, distance),
        in_specs=[SMEM] + [VMEM] * 5,
        out_specs=[VMEM] * 2,
        out_shape=[
            jax.ShapeDtypeStruct((rows + TAIL, HEAD_DIM), BF16),
            jax.ShapeDtypeStruct((rows, HEAD_DIM), BF16),
        ],
        compiler_params=pltpu.CompilerParams(vmem_limit_bytes=24 * MIB),
        cost_estimate=pl.CostEstimate(
            flops=STRETCH * weight.size * 2, bytes_accessed=weight.size, transcendentals=0
        ),
        name="project_first",
    )(targets, own, squares, other, other_squares, weight)


def project_kernel(distances, targets, own, squares, other, other_squares, weight, out):
    for item, distance in enumerate(distances):

        def some(lines, sums, item=item):
            for head in range(CORE_HEADS):
                product = jnp.dot(lines[...], weight[head], preferred_element_type=F32)
                begin = head % 2 * STRETCH
                out[item, head // 2, begin : begin + STRETCH] = product[:, :HEAD_DIM]
                begin += 2 * STRETCH
                out[item, head // 2, begin : begin + STRETCH] = product[:, HEAD_DIM:]
            for half in range(2):
                out[item, half, 4 * STRETCH :] = sums[...]

        def none(item=item):
            out[item] = jnp.zeros(out.shape[1:], F32)

        with_lines(targets, distance, own, squares, other, other_squares, some, none)


def project(distances, targets, own, squares, other, other_squares, weight):
    return pl.pallas_call(
        functools.partial(project_kernel, distances),
        in_specs=[SMEM] + [VMEM] * 5,
        out_specs=VMEM,
        out_shape=jax.ShapeDtypeStruct((len(distances), 2, 4 * STRETCH + 8, HEAD_DIM), F32),
        compiler_params=pltpu.CompilerParams(vmem_limit_bytes=24 * MIB),
        cost_estimate=pl.CostEstimate(
            flops=len(distances) * STRETCH * weight.size * 2 // 2,
            bytes_accessed=weight.size,
            transcendentals=0,
        ),
        name="project",
    )(targets, own, squares, other, other_squares, weight)


def send_kernel(half, first, terms, right, left, to_right, to_left):
    rows = 4 * STRETCH
    middle = 2 * STRETCH
    if first:
        from_right = right[half * middle : (half + 1) * middle].astype(F32)
        from_left = left[half * middle : (half + 1) * middle].astype(F32)
        to_right[:middle] = (terms[0, half, :middle] + from_right).astype(BF16)
        to_right[middle:rows] = terms[0, half, middle:rows].astype(BF16)
        to_left[:middle] = terms[1, half, :middle].astype(BF16)
        to_left[middle:rows] = (terms[1, half, middle:rows] + from_left).astype(BF16)
    else:
        to_right[:rows] = (terms[0, half, :rows] + right[:rows].astype(F32)).astype(BF16)
        to_left[:rows] = (terms[1, half, :rows] + left[:rows].astype(F32)).astype(BF16)
    if half == 0:
        right_sum = terms[0, 0, rows:] + one_piece(right[rows:])
        left_sum = terms[1, 0, rows:]
        if not first:
            left_sum += one_piece(left[rows:])
        to_right[rows:] = two_pieces(right_sum)
        to_left[rows:] = two_pieces(left_sum)


def sends(half, first, terms, right, left):
    rows = 4 * STRETCH + (TAIL if half == 0 else 0)
    shape = jax.ShapeDtypeStruct((rows, HEAD_DIM), BF16)
    return pl.pallas_call(
        functools.partial(send_kernel, half, first),
        in_specs=[VMEM] * 3,
        out_specs=[VMEM] * 2,
        out_shape=[shape, shape],
        compiler_params=pltpu.CompilerParams(vmem_limit_bytes=16 * MIB),
        name="sends",
    )(terms, right, left)


def prepare_kernel(targets, queries, starts, turns, grouped, rotary):
    for head in range(KV_HEADS):
        for member in range(GROUP):
            begin = (head * GROUP + member) * HEAD_DIM
            rows = slice(member * STEPS, (member + 1) * STEPS)
            grouped[head, rows] = queries[0, :, begin : begin + HEAD_DIM]
    row = pl.ds(jnp.maximum(prompt_of(targets, lax.axis_index("tp")), 0), 1)
    cosine, sine = starts[0, row, :], starts[1, row, :]
    lane = lax.broadcasted_iota(jnp.int32, turns.shape[1:], 1)
    rotary[0] = turns[0] * cosine - turns[1] * sine
    sine = turns[1] * cosine + turns[0] * sine
    rotary[1] = jnp.where(lane < HEAD_DIM // 2, -sine, sine)


def prepare(targets, queries, starts, turns):
    return pl.pallas_call(
        prepare_kernel,
        in_specs=[SMEM] + [VMEM] * 3,
        out_specs=[VMEM] * 2,
        out_shape=[
            jax.ShapeDtypeStruct((KV_HEADS, ROWS, HEAD_DIM), BF16),
            jax.ShapeDtypeStruct(turns.shape, F32),
        ],
        compiler_params=pltpu.CompilerParams(vmem_limit_bytes=16 * MIB),
        name="prepare",
    )(targets, queries, starts, turns)


def cache_kernel(part, targets, lengths, stored, q, cache, new, out):
    scaling = HEAD_DIM ** (-0.5)
    dims = (((1,), (1,)), ((), ()))
    here = lax.axis_index("tp")
    rep = lax.axis_index("rep")
    length = cache.shape[1]
    prompt = prompt_of(targets, here)
    handed = lengths[jnp.maximum(prompt, 0)] - STRETCH
    span = jnp.where(prompt >= 0, handed, stored[0]) - rep * length
    allowed = lax.broadcasted_iota(jnp.int32, (ROWS, length), 1) < span
    second_step = lax.broadcasted_iota(jnp.int32, (ROWS, 1), 0) % STEPS == 1
    for at in range(CORE_HEADS):
        head = (rep if part == 1 else 1 - rep) * CORE_HEADS + at
        key_lanes = pl.ds(pl.multiple_of(head * HEAD_DIM, HEAD_DIM), HEAD_DIM)
        value_lanes = pl.ds(pl.multiple_of((KV_HEADS + head) * HEAD_DIM, HEAD_DIM), HEAD_DIM)
        query = q[head]
        wide = query.astype(F32)
        scores = lax.dot_general(query, cache[0, :, key_lanes], dims, preferred_element_type=F32)
        scores = jnp.where(allowed, scores * scaling, NEGATIVE)
        highest = jnp.max(scores, axis=1, keepdims=True)
        fresh = []
        for step in range(STEPS):
            key = new[0, step : step + 1, key_lanes].astype(F32)
            score = jnp.sum(wide * key, axis=1, keepdims=True) * scaling
            shown = rep == 0 if step == 0 else second_step & (rep == 0)
            score = jnp.where(shown, score, NEGATIVE)
            highest = jnp.maximum(highest, score)
            fresh.append(score)
        some = highest > 0.5 * NEGATIVE
        highest = jnp.where(some, highest, 0.0)
        weight = jnp.exp(scores - highest)
        totals = jnp.sum(weight, axis=1, keepdims=True)
        sums = jnp.dot(weight.astype(BF16), cache[0, :, value_lanes], preferred_element_type=F32)
        for step in range(STEPS):
            share = jnp.exp(fresh[step] - highest)
            totals += share
            value = new[0, step : step + 1, value_lanes].astype(F32)
            sums += share.astype(BF16).astype(F32) * value
        totals = jnp.where(some, totals, 1.0)
        out[at, :ROWS] = (sums / totals).astype(BF16)
        out[at, ROWS:] = pieces_tail(jnp.where(some, highest + jnp.log(totals), NEGATIVE))


def cache_attention(part, targets, lengths, stored, grouped, kv_cache, new_kv):
    return pl.pallas_call(
        functools.partial(cache_kernel, part),
        in_specs=[SMEM] * 3 + [VMEM] * 3,
        out_specs=VMEM,
        out_shape=jax.ShapeDtypeStruct((CORE_HEADS, PART, HEAD_DIM), BF16),
        compiler_params=pltpu.CompilerParams(vmem_limit_bytes=16 * MIB),
        cost_estimate=pl.CostEstimate(
            flops=2 * grouped.size * kv_cache.shape[1],
            bytes_accessed=kv_cache.size,
            transcendentals=CORE_HEADS * ROWS * kv_cache.shape[1],
        ),
        name="cache_attention",
    )(targets, lengths, stored, grouped, kv_cache, new_kv)


def final_kernel(
    targets, rotary, own, right_a, left_a, right_b, left_b, grouped, cached_there, cached_here, out
):
    scaling = HEAD_DIM ** (-0.5)
    dims = (((1,), (1,)), ((), ()))
    mine = own.shape[0] - 1
    rep = lax.axis_index("rep")
    first = rep * CORE_HEADS
    prompt = prompt_of(targets, lax.axis_index("tp"))
    cosine, sine = rotary[0], rotary[1]
    rows = 4 * STRETCH
    squares = own[mine, 0, rows:] + one_piece(right_a[rows:]) + one_piece(left_a[rows:])
    scale = token_column(lax.rsqrt(squares / D + EPSILON))
    for head in range(CORE_HEADS):
        right, left = ((right_a, left_a), (right_b, left_b))[head // 2]
        at = slice(head % 2 * STRETCH, (head % 2 + 1) * STRETCH)
        keys = own[mine, head // 2, at] + right[at].astype(F32) + left[at].astype(F32)
        at = slice((2 + head % 2) * STRETCH, (3 + head % 2) * STRETCH)
        values = own[mine, head // 2, at] + right[at].astype(F32) + left[at].astype(F32)
        keys = (keys * scale).astype(BF16).astype(F32)
        values = (values * scale).astype(BF16)
        keys = keys * cosine + pltpu.roll(keys, HEAD_DIM // 2, 1) * sine
        scores = lax.dot_general(
            grouped[first + head], keys.astype(BF16), dims, preferred_element_type=F32
        )
        scores = scores * scaling
        highest = jnp.max(scores, axis=1, keepdims=True)
        weight = jnp.exp(scores - highest)
        totals = jnp.sum(weight, axis=1, keepdims=True)
        sums = jnp.dot(weight.astype(BF16), values, preferred_element_type=F32) / totals
        logs = jnp.where(prompt >= 0, highest + jnp.log(totals), NEGATIVE)
        parts = [cached_there[head], cached_here[head]]
        logs = [tail_pieces(part[ROWS:]) for part in parts] + [logs]
        sums = [part[:ROWS].astype(F32) for part in parts] + [sums]
        highest = functools.reduce(jnp.maximum, logs)
        shares = [jnp.exp(log - highest) for log in logs]
        total = functools.reduce(jnp.add, shares)
        joined = functools.reduce(jnp.add, [share * part for share, part in zip(shares, sums)])
        result = (joined / total).astype(BF16)
        for member in range(GROUP):
            begin = (head * GROUP + member) * HEAD_DIM
            out[0, :, begin : begin + HEAD_DIM] = result[member * STEPS : (member + 1) * STEPS]


def finish(targets, rotary, own, arrived, grouped, cached):
    width = CORE_HEADS * GROUP * HEAD_DIM
    return pl.pallas_call(
        final_kernel,
        in_specs=[SMEM] + [VMEM] * 9,
        out_specs=VMEM,
        out_shape=jax.ShapeDtypeStruct((1, STEPS, width), BF16),
        compiler_params=pltpu.CompilerParams(vmem_limit_bytes=16 * MIB),
        name="finish",
    )(targets, rotary, own, *arrived, grouped, *cached)


def rotary_turns():
    half = np.arange(HEAD_DIM // 2, dtype=np.float64) / (HEAD_DIM // 2)
    frequency = ROTARY_BASE ** (-np.concatenate([half, half]))
    angles = np.arange(STRETCH, dtype=np.float64)[:, None] * frequency
    return frequency.astype(np.float32), np.stack([np.cos(angles), np.sin(angles)]).astype(np.float32)


def per_device(
    stretch,
    norm_gain,
    kv_codes,
    scale_codes,
    outer_scales,
    prompt_lengths,
    target_rows,
    cache_lengths,
    kv_cache,
    queries,
    new_kv,
):
    count = lax.axis_size("tp")
    half = count // 2
    lines = stretch.transpose(1, 0, 2)
    gain = norm_gain.reshape(1, -1)
    ring = [ring_device(at, count) for at in range(count)]
    to_right = [(ring[at], ring[(at + 1) % count]) for at in range(count)]
    to_left = [(ring[at], ring[at - 1]) for at in range(count)]

    def pass_on(right, left):
        return lax.ppermute(right, "tp", to_right), lax.ppermute(left, "tp", to_left)

    own, squares = scale_features(lines, gain)
    swap = lambda array: lax.ppermute(array, "rep", [(0, 1), (1, 0)])
    other, other_squares = swap(own), swap(squares)
    weight = dequantize(kv_codes, scale_codes, outer_scales.T)
    frequency, turns = rotary_turns()
    start = (prompt_lengths - STRETCH).astype(F32)[:, None] * jnp.asarray(frequency)
    starts = jnp.stack([jnp.cos(start), jnp.sin(start)])

    features = [own, squares, other, other_squares]
    right, left = project_first(half, target_rows, *features, weight)
    targets, _ = lax.optimization_barrier((target_rows, left))
    arrived = [pass_on(right, left)] * 2
    grouped, rotary = prepare(targets, queries, starts, jnp.asarray(turns))

    cached = []
    for distance in range(half - 1, 0, -1):
        distances = [distance, -distance] + ([0] if distance == 1 else [])
        if len(cached) < 2:
            cached.append(
                cache_attention(
                    len(cached), targets, prompt_lengths, cache_lengths, grouped, kv_cache, new_kv
                )
            )
        if len(cached) == 1:
            cached = [swap(cached[0])]
        terms = project(distances, targets, *features, weight)
        later = terms
        for part in range(2):
            right, left = sends(part, distance == half - 1, (terms, later)[part], *arrived[part])
            if part == 0:
                right, cached, later = lax.optimization_barrier((right, cached, terms))
            targets, _ = lax.optimization_barrier((target_rows, right))
            arrived[part] = pass_on(right, left)

    out = finish(target_rows, rotary, terms, [*arrived[0], *arrived[1]], grouped, cached)
    return lax.all_gather(out, "rep", axis=2, tiled=True)


def solution(mesh):
    in_specs = (
        P(None, ("grp", "rep"), "tp"),
        P("tp"),
        P("tp", None),
        P("tp", None),
        P("tp", None),
        P("grp"),
        P("grp"),
        P(("grp", "tp")),
        P(("grp", "tp"), "rep", None),
        P(("grp", "tp"), None, None),
        P(("grp", "tp"), None, None),
    )
    out_specs = P(("grp", "tp"), None, None)
    return jax.shard_map(
        per_device, mesh=mesh, in_specs=in_specs, out_specs=out_specs, check_vma=False
    )
```

```python
import functools
import math

import jax
import jax.numpy as jnp
import numpy as np
from jax import lax
from jax.experimental import pallas as pl
from jax.experimental.pallas import tpu as pltpu
from jax.sharding import PartitionSpec as P

D = 16384
HEADS = 128
KV_HEADS = 8
HEAD_DIM = 128
STRETCH = 192
STEPS = 2
QBLOCK = 64
GROUP = HEADS // KV_HEADS
ROWS = GROUP * STEPS
TAIL = 16
PART = ROWS + TAIL
CORE_HEADS = KV_HEADS // 2
NORMAL_FLOAT_LEVELS = [
    -1.0,
    -0.6961928009986877,
    -0.5250730514526367,
    -0.39491748809814453,
    -0.28444138169288635,
    -0.18477343022823334,
    -0.09105003625154495,
    0.0,
    0.07958029955625534,
    0.16093020141124725,
    0.24611230194568634,
    0.33791524171829224,
    0.44070982933044434,
    0.5626170039176941,
    0.7229568362236023,
    1.0,
]
ROTARY_BASE = 500000.0
EPSILON = 1e-05
NEGATIVE = -1e30
BF16 = jnp.bfloat16
F32 = jnp.float32
MIB = 1024 * 1024
VMEM = pl.BlockSpec(memory_space=pltpu.VMEM)
SMEM = pl.BlockSpec(memory_space=pltpu.SMEM)


def in_hbm(*arrays):
    return [pltpu.with_memory_space_constraint(array, pltpu.HBM) for array in arrays]


def ring_device(place, count):
    half = count // 2
    if isinstance(place, int):
        return 2 * place if place < half else 2 * (count - 1 - place) + 1
    return jnp.where(place < half, 2 * place, 2 * (count - 1 - place) + 1)


def owner_at(distance):
    count = lax.axis_size("tp")
    here = lax.axis_index("tp")
    place = jnp.where(here % 2 == 0, here // 2, count - 1 - here // 2)
    return ring_device((place + distance + count) % count, count)


def turned(column):
    rows = lax.broadcasted_iota(jnp.int32, (column.shape[0], 128), 0)
    lanes = lax.broadcasted_iota(jnp.int32, (column.shape[0], 128), 1)
    return jnp.sum(jnp.where(rows == lanes, column, 0.0), axis=0, keepdims=True)


def stood(row, count):
    rows = lax.broadcasted_iota(jnp.int32, (count, 128), 0)
    lanes = lax.broadcasted_iota(jnp.int32, (count, 128), 1)
    return jnp.sum(jnp.where(rows == lanes, row, 0.0), axis=1, keepdims=True)


def token_rows(column):
    at = lax.broadcasted_iota(jnp.int32, (8, 128), 0)
    ends = turned(column[128:])
    return jnp.where(at == 0, turned(column[:128]), jnp.where(at == 1, ends, 0.0))


def token_column(rows):
    return jnp.concatenate([stood(rows[0:1], 128), stood(rows[1:2], STRETCH - 128)], axis=0)


def two_pieces(rows):
    high = rows.astype(BF16).astype(F32)
    return jnp.concatenate([high, rows - high], axis=0).astype(BF16)


def one_piece(rows):
    rows = rows.astype(F32)
    return rows[:8] + rows[8:]


def pieces_tail(logs):
    row = turned(logs)
    high = row.astype(BF16).astype(F32)
    middle = (row - high).astype(BF16).astype(F32)
    low = row - high - middle
    at = lax.broadcasted_iota(jnp.int32, (TAIL, 128), 0)
    tail = jnp.where(at == 0, high, jnp.where(at == 1, middle, jnp.where(at == 2, low, 0.0)))
    return tail.astype(BF16)


def tail_pieces(tail):
    tail = tail.astype(F32)
    return stood(tail[0:1, :] + tail[1:2, :] + tail[2:3, :], ROWS)


def block_leaves(scale):
    wide = jnp.broadcast_to(scale, (8, HEAD_DIM))
    leaves = [wide * jnp.float32(level) for level in NORMAL_FLOAT_LEVELS]
    return [jnp.concatenate([leaf, leaf], axis=0).astype(BF16) for leaf in leaves]


def selected(codes, leaves):
    codes = codes.astype(jnp.int16)
    masks = [(codes & (1 << bit)) != 0 for bit in range(4)]

    def node(bit, base):
        if bit < 0:
            return leaves[base]
        low = node(bit - 1, base)
        return jnp.where(masks[bit], node(bit - 1, base + (1 << bit)), low)

    return node(3, 0)


def block_scales(scales, outer, column):
    count = scales.shape[0]
    line = lax.broadcasted_iota(jnp.int32, outer.shape, 0)
    line = jnp.sum(jnp.where(line == column, outer, 0.0), axis=0, keepdims=True)
    rows = lax.broadcasted_iota(jnp.int32, (count, count), 0)
    lanes = lax.broadcasted_iota(jnp.int32, (count, count), 1)
    second = jnp.sum(jnp.where(rows == lanes, line, 0.0), axis=1, keepdims=True)
    return (scales.astype(F32) + 1.0) / 256.0 * second


def weights_kernel(
    x, codes, key_scales, value_scales, outer, gain,
    out, scaled, squares, key_codes, value_codes, lines, scales, arrivals,
):
    per_rep = x.shape[0]
    features, width = key_codes.shape
    depth = min(256, features)
    blocks = features // depth
    columns = outer.shape[0] // 2
    rep = lax.axis_index("rep")

    def code_copies(block):
        rows = pl.ds(block * depth, depth)
        return [
            pltpu.make_async_copy(
                codes.at[rows, pl.ds(pl.multiple_of((2 * kind + rep) * width, width), width)],
                buffer.at[rows],
                arrivals.at[2 * block + kind],
            )
            for kind, buffer in enumerate((key_codes, value_codes))
        ]

    def line_copy(prompt):
        return pltpu.make_async_copy(
            x.at[prompt], lines.at[prompt], arrivals.at[2 * blocks + prompt]
        )

    for block in range(blocks):
        if block == blocks // 2:
            for prompt in range(per_rep):
                line_copy(prompt).start()
        for copy in code_copies(block):
            copy.start()
    for at in range(CORE_HEADS):
        column = (rep * CORE_HEADS + at) // (KV_HEADS // columns)
        lanes = slice(at * HEAD_DIM, (at + 1) * HEAD_DIM)
        scales[2 * at] = block_scales(key_scales[:, lanes], outer[...], column)
        scales[2 * at + 1] = block_scales(value_scales[:, lanes], outer[...], columns + column)
    squares[...] = jnp.zeros(squares.shape, F32)

    def body(step, _):
        row = pl.ds(step, 1)
        for at in range(CORE_HEADS):
            lanes = slice(at * HEAD_DIM, (at + 1) * HEAD_DIM)
            for kind, buffer in enumerate((key_codes, value_codes)):
                leaves = block_leaves(scales[2 * at + kind, row, :])
                for tile in range(QBLOCK // 16):
                    rows = pl.ds(pl.multiple_of(step * QBLOCK + 16 * tile, 16), 16)
                    out[at, rows, kind * HEAD_DIM : (kind + 1) * HEAD_DIM] = selected(
                        buffer[rows, lanes], leaves
                    )
        return 0

    steps = depth // QBLOCK
    late = blocks - blocks // 2
    for block in range(blocks):
        for copy in code_copies(block):
            copy.wait()
        lax.fori_loop(block * steps, (block + 1) * steps, body, 0)
        if block == blocks // 2:
            for prompt in range(per_rep):
                line_copy(prompt).wait()
        for chunk in range(blocks):
            if blocks // 2 + chunk * late // blocks != block:
                continue
            lanes = slice(chunk * depth, (chunk + 1) * depth)
            for prompt in range(per_rep):
                wide = lines[prompt, :, lanes].astype(F32)
                scaled[prompt, :, lanes] = (wide * gain[:, lanes]).astype(BF16)
                squares[prompt] += token_rows(jnp.sum(wide * wide, axis=1, keepdims=True))


def dequantize(x, codes, scales, outer, gain):
    per_rep, _, features = x.shape
    width = CORE_HEADS * HEAD_DIM
    blocks = features // min(256, features)
    rep = lambda: lax.axis_index("rep")
    x, codes, scales, outer, gain = in_hbm(x, codes, scales, outer, gain)
    return pl.pallas_call(
        weights_kernel,
        grid=(1,),
        in_specs=[
            pl.BlockSpec(memory_space=pltpu.HBM),
            pl.BlockSpec(memory_space=pltpu.HBM),
            pl.BlockSpec((scales.shape[0], width), lambda k: (0, rep())),
            pl.BlockSpec((scales.shape[0], width), lambda k: (0, 2 + rep())),
            pl.BlockSpec(outer.shape, lambda k: (0, 0)),
            pl.BlockSpec(gain.shape, lambda k: (0, 0)),
        ],
        out_specs=[VMEM] * 3,
        out_shape=[
            jax.ShapeDtypeStruct((CORE_HEADS, features, 2 * HEAD_DIM), BF16),
            jax.ShapeDtypeStruct(x.shape, BF16),
            jax.ShapeDtypeStruct((per_rep, 8, 128), F32),
        ],
        scratch_shapes=[
            pltpu.VMEM((features, width), jnp.int32),
            pltpu.VMEM((features, width), jnp.int32),
            pltpu.VMEM(x.shape, BF16),
            pltpu.VMEM((2 * CORE_HEADS, scales.shape[0], HEAD_DIM), F32),
            pltpu.SemaphoreType.DMA((2 * blocks + per_rep,)),
        ],
        compiler_params=pltpu.CompilerParams(vmem_limit_bytes=36 * MIB),
        cost_estimate=pl.CostEstimate(
            flops=32 * codes.size, bytes_accessed=codes.size * 2, transcendentals=0
        ),
        name="dequantize",
    )(x, codes, scales, scales, outer, gain)


def prompt_of(targets, owner):
    prompt = jnp.int32(-1)
    for at in range(targets.shape[0]):
        prompt = jnp.where(targets[at] == owner, at, prompt)
    return prompt


def with_lines(targets, distance, own, squares, other, gain, line, total, some, none):
    per_rep = own.shape[0]
    prompt = prompt_of(targets, owner_at(distance))
    at = lax.rem(jnp.maximum(prompt, 0), per_rep)
    is_own = prompt // per_rep == lax.axis_index("rep")

    @pl.when((prompt >= 0) & is_own)
    def _():
        some(own.at[at], squares.at[at])

    @pl.when((prompt >= 0) & jnp.logical_not(is_own))
    def _():
        width = min(512, line.shape[1])
        total[...] = jnp.zeros(total.shape, F32)
        for begin in range(0, line.shape[1], width):
            lanes = slice(begin, begin + width)
            wide = other[at, :, lanes].astype(F32)
            line[:, lanes] = (wide * gain[:, lanes]).astype(BF16)
            total[...] += token_rows(jnp.sum(wide * wide, axis=1, keepdims=True))
        some(line, total)

    pl.when(prompt < 0)(none)


def line_scratch(x):
    return [pltpu.VMEM(x.shape[1:], BF16), pltpu.VMEM((8, 128), F32)]


def first_kernel(distance, targets, own, squares, other, gain, weight, right, left, line, total):
    def some(lines, sums):
        for head in range(CORE_HEADS):
            product = jnp.dot(lines[...], weight[head], preferred_element_type=F32)
            rows = slice(head * STRETCH, (head + 1) * STRETCH)
            right[rows] = product[:, :HEAD_DIM].astype(BF16)
            left[rows] = product[:, HEAD_DIM:].astype(BF16)
        right[CORE_HEADS * STRETCH :] = two_pieces(sums[...])

    def none():
        right[...] = jnp.zeros(right.shape, BF16)
        left[...] = jnp.zeros(left.shape, BF16)

    with_lines(targets, distance, own, squares, other, gain, line, total, some, none)


def project_first(distance, targets, own, squares, other, gain, weight):
    rows = CORE_HEADS * STRETCH
    return pl.pallas_call(
        functools.partial(first_kernel, distance),
        in_specs=[SMEM] + [VMEM] * 5,
        out_specs=[VMEM] * 2,
        out_shape=[
            jax.ShapeDtypeStruct((rows + TAIL, HEAD_DIM), BF16),
            jax.ShapeDtypeStruct((rows, HEAD_DIM), BF16),
        ],
        scratch_shapes=line_scratch(own),
        compiler_params=pltpu.CompilerParams(vmem_limit_bytes=24 * MIB),
        cost_estimate=pl.CostEstimate(
            flops=STRETCH * weight.size * 2, bytes_accessed=weight.size, transcendentals=0
        ),
        name="project_first",
    )(targets, own, squares, other, gain, weight)


def project_kernel(distances, targets, own, squares, other, gain, weight, out, line, total):
    for item, distance in enumerate(distances):

        def some(lines, sums, item=item):
            for head in range(CORE_HEADS):
                product = jnp.dot(lines[...], weight[head], preferred_element_type=F32)
                begin = head % 2 * STRETCH
                out[item, head // 2, begin : begin + STRETCH] = product[:, :HEAD_DIM]
                begin += 2 * STRETCH
                out[item, head // 2, begin : begin + STRETCH] = product[:, HEAD_DIM:]
            for half in range(2):
                out[item, half, 4 * STRETCH :] = sums[...]

        def none(item=item):
            out[item] = jnp.zeros(out.shape[1:], F32)

        with_lines(targets, distance, own, squares, other, gain, line, total, some, none)


def project(distances, targets, own, squares, other, gain, weight):
    return pl.pallas_call(
        functools.partial(project_kernel, distances),
        in_specs=[SMEM] + [VMEM] * 5,
        out_specs=VMEM,
        out_shape=jax.ShapeDtypeStruct((len(distances), 2, 4 * STRETCH + 8, HEAD_DIM), F32),
        scratch_shapes=line_scratch(own),
        compiler_params=pltpu.CompilerParams(vmem_limit_bytes=24 * MIB),
        cost_estimate=pl.CostEstimate(
            flops=len(distances) * STRETCH * weight.size,
            bytes_accessed=weight.size,
            transcendentals=0,
        ),
        name="project",
    )(targets, own, squares, other, gain, weight)


def send_kernel(half, first, terms, right, left, to_right, to_left):
    rows = 4 * STRETCH
    middle = 2 * STRETCH
    if first:
        from_right = right[half * middle : (half + 1) * middle].astype(F32)
        from_left = left[half * middle : (half + 1) * middle].astype(F32)
        to_right[:middle] = (terms[0, half, :middle] + from_right).astype(BF16)
        to_right[middle:rows] = terms[0, half, middle:rows].astype(BF16)
        to_left[:middle] = terms[1, half, :middle].astype(BF16)
        to_left[middle:rows] = (terms[1, half, middle:rows] + from_left).astype(BF16)
    else:
        to_right[:rows] = (terms[0, half, :rows] + right[:rows].astype(F32)).astype(BF16)
        to_left[:rows] = (terms[1, half, :rows] + left[:rows].astype(F32)).astype(BF16)
    if half == 0:
        right_sum = terms[0, 0, rows:] + one_piece(right[rows:])
        left_sum = terms[1, 0, rows:]
        if not first:
            left_sum += one_piece(left[rows:])
        to_right[rows:] = two_pieces(right_sum)
        to_left[rows:] = two_pieces(left_sum)


def sends(half, first, terms, right, left):
    rows = 4 * STRETCH + (TAIL if half == 0 else 0)
    shape = jax.ShapeDtypeStruct((rows, HEAD_DIM), BF16)
    return pl.pallas_call(
        functools.partial(send_kernel, half, first),
        in_specs=[VMEM] * 3,
        out_specs=[VMEM] * 2,
        out_shape=[shape, shape],
        compiler_params=pltpu.CompilerParams(vmem_limit_bytes=16 * MIB),
        name="sends",
    )(terms, right, left)


def prepare_kernel(targets, queries, starts, turns, grouped, rotary):
    for head in range(KV_HEADS):
        for member in range(GROUP):
            begin = (head * GROUP + member) * HEAD_DIM
            rows = slice(member * STEPS, (member + 1) * STEPS)
            grouped[head, rows] = queries[0, :, begin : begin + HEAD_DIM]
    row = pl.ds(jnp.maximum(prompt_of(targets, lax.axis_index("tp")), 0), 1)
    cosine, sine = starts[0, row, :], starts[1, row, :]
    lane = lax.broadcasted_iota(jnp.int32, turns.shape[1:], 1)
    rotary[0] = turns[0] * cosine - turns[1] * sine
    sine = turns[1] * cosine + turns[0] * sine
    rotary[1] = jnp.where(lane < HEAD_DIM // 2, -sine, sine)


def prepare(targets, queries, starts, turns):
    return pl.pallas_call(
        prepare_kernel,
        in_specs=[SMEM] + [VMEM] * 3,
        out_specs=[VMEM] * 2,
        out_shape=[
            jax.ShapeDtypeStruct((KV_HEADS, ROWS, HEAD_DIM), BF16),
            jax.ShapeDtypeStruct(turns.shape, F32),
        ],
        compiler_params=pltpu.CompilerParams(vmem_limit_bytes=16 * MIB),
        name="prepare",
    )(targets, queries, starts, turns)


def cache_kernel(part, targets, lengths, stored, q, cache, new, out):
    scaling = HEAD_DIM ** (-0.5)
    dims = (((1,), (1,)), ((), ()))
    here = lax.axis_index("tp")
    rep = lax.axis_index("rep")
    length = cache.shape[1]
    prompt = prompt_of(targets, here)
    handed = lengths[jnp.maximum(prompt, 0)] - STRETCH
    span = jnp.where(prompt >= 0, handed, stored[0]) - rep * length
    allowed = lax.broadcasted_iota(jnp.int32, (ROWS, length), 1) < span
    second_step = lax.broadcasted_iota(jnp.int32, (ROWS, 1), 0) % STEPS == 1
    for at in range(CORE_HEADS):
        head = (rep if part == 1 else 1 - rep) * CORE_HEADS + at
        key_lanes = pl.ds(pl.multiple_of(head * HEAD_DIM, HEAD_DIM), HEAD_DIM)
        value_lanes = pl.ds(pl.multiple_of((KV_HEADS + head) * HEAD_DIM, HEAD_DIM), HEAD_DIM)
        query = q[head]
        wide = query.astype(F32)
        scores = lax.dot_general(query, cache[0, :, key_lanes], dims, preferred_element_type=F32)
        scores = jnp.where(allowed, scores * scaling, NEGATIVE)
        highest = jnp.max(scores, axis=1, keepdims=True)
        fresh = []
        for step in range(STEPS):
            key = new[0, step : step + 1, key_lanes].astype(F32)
            score = jnp.sum(wide * key, axis=1, keepdims=True) * scaling
            shown = rep == 0 if step == 0 else second_step & (rep == 0)
            score = jnp.where(shown, score, NEGATIVE)
            highest = jnp.maximum(highest, score)
            fresh.append(score)
        some = highest > 0.5 * NEGATIVE
        highest = jnp.where(some, highest, 0.0)
        weight = jnp.exp(scores - highest)
        totals = jnp.sum(weight, axis=1, keepdims=True)
        sums = jnp.dot(weight.astype(BF16), cache[0, :, value_lanes], preferred_element_type=F32)
        for step in range(STEPS):
            share = jnp.exp(fresh[step] - highest)
            totals += share
            value = new[0, step : step + 1, value_lanes].astype(F32)
            sums += share.astype(BF16).astype(F32) * value
        totals = jnp.where(some, totals, 1.0)
        out[at, :ROWS] = (sums / totals).astype(BF16)
        out[at, ROWS:] = pieces_tail(jnp.where(some, highest + jnp.log(totals), NEGATIVE))


def cache_attention(part, targets, lengths, stored, grouped, kv_cache, new_kv):
    return pl.pallas_call(
        functools.partial(cache_kernel, part),
        in_specs=[SMEM] * 3 + [VMEM] * 3,
        out_specs=VMEM,
        out_shape=jax.ShapeDtypeStruct((CORE_HEADS, PART, HEAD_DIM), BF16),
        compiler_params=pltpu.CompilerParams(vmem_limit_bytes=16 * MIB),
        cost_estimate=pl.CostEstimate(
            flops=2 * grouped.size * kv_cache.shape[1],
            bytes_accessed=kv_cache.size,
            transcendentals=CORE_HEADS * ROWS * kv_cache.shape[1],
        ),
        name="cache_attention",
    )(targets, lengths, stored, grouped, kv_cache, new_kv)


def final_kernel(
    targets, rotary, own, right_a, left_a, right_b, left_b, grouped, cached_there, cached_here, out
):
    scaling = HEAD_DIM ** (-0.5)
    dims = (((1,), (1,)), ((), ()))
    mine = own.shape[0] - 1
    rep = lax.axis_index("rep")
    first = rep * CORE_HEADS
    prompt = prompt_of(targets, lax.axis_index("tp"))
    cosine, sine = rotary[0], rotary[1]
    rows = 4 * STRETCH
    squares = own[mine, 0, rows:] + one_piece(right_a[rows:]) + one_piece(left_a[rows:])
    scale = token_column(lax.rsqrt(squares / D + EPSILON))
    for head in range(CORE_HEADS):
        right, left = ((right_a, left_a), (right_b, left_b))[head // 2]
        at = slice(head % 2 * STRETCH, (head % 2 + 1) * STRETCH)
        keys = own[mine, head // 2, at] + right[at].astype(F32) + left[at].astype(F32)
        at = slice((2 + head % 2) * STRETCH, (3 + head % 2) * STRETCH)
        values = own[mine, head // 2, at] + right[at].astype(F32) + left[at].astype(F32)
        keys = (keys * scale).astype(BF16).astype(F32)
        values = (values * scale).astype(BF16)
        keys = keys * cosine + pltpu.roll(keys, HEAD_DIM // 2, 1) * sine
        scores = lax.dot_general(
            grouped[first + head], keys.astype(BF16), dims, preferred_element_type=F32
        )
        scores = scores * scaling
        highest = jnp.max(scores, axis=1, keepdims=True)
        weight = jnp.exp(scores - highest)
        totals = jnp.sum(weight, axis=1, keepdims=True)
        sums = jnp.dot(weight.astype(BF16), values, preferred_element_type=F32) / totals
        logs = jnp.where(prompt >= 0, highest + jnp.log(totals), NEGATIVE)
        parts = [cached_there[head], cached_here[head]]
        logs = [tail_pieces(part[ROWS:]) for part in parts] + [logs]
        sums = [part[:ROWS].astype(F32) for part in parts] + [sums]
        highest = functools.reduce(jnp.maximum, logs)
        shares = [jnp.exp(log - highest) for log in logs]
        total = functools.reduce(jnp.add, shares)
        joined = functools.reduce(jnp.add, [share * part for share, part in zip(shares, sums)])
        result = (joined / total).astype(BF16)
        for member in range(GROUP):
            begin = (head * GROUP + member) * HEAD_DIM
            out[0, :, begin : begin + HEAD_DIM] = result[member * STEPS : (member + 1) * STEPS]


def finish(targets, rotary, own, arrived, grouped, cached):
    width = CORE_HEADS * GROUP * HEAD_DIM
    return pl.pallas_call(
        final_kernel,
        in_specs=[SMEM] + [VMEM] * 9,
        out_specs=VMEM,
        out_shape=jax.ShapeDtypeStruct((1, STEPS, width), BF16),
        compiler_params=pltpu.CompilerParams(vmem_limit_bytes=16 * MIB),
        name="finish",
    )(targets, rotary, own, *arrived, grouped, *cached)


def rotary_turns():
    half = np.arange(HEAD_DIM // 2, dtype=np.float64) / (HEAD_DIM // 2)
    frequency = ROTARY_BASE ** (-np.concatenate([half, half]))
    angles = np.arange(STRETCH, dtype=np.float64)[:, None] * frequency
    return frequency.astype(np.float32), np.stack([np.cos(angles), np.sin(angles)]).astype(np.float32)


def per_device(
    stretch,
    norm_gain,
    kv_codes,
    scale_codes,
    outer_scales,
    prompt_lengths,
    target_rows,
    cache_lengths,
    kv_cache,
    queries,
    new_kv,
):
    count = lax.axis_size("tp")
    half = count // 2
    lines = stretch.transpose(1, 0, 2)
    gain = norm_gain.reshape(1, -1)
    ring = [ring_device(at, count) for at in range(count)]
    to_right = [(ring[at], ring[(at + 1) % count]) for at in range(count)]
    to_left = [(ring[at], ring[at - 1]) for at in range(count)]

    def pass_on(right, left):
        return lax.ppermute(right, "tp", to_right), lax.ppermute(left, "tp", to_left)

    swap = lambda array: lax.ppermute(array, "rep", [(0, 1), (1, 0)])
    other = swap(lines)
    weight, own, squares = dequantize(lines, kv_codes, scale_codes, outer_scales.T, gain)
    frequency, turns = rotary_turns()
    start = (prompt_lengths - STRETCH).astype(F32)[:, None] * jnp.asarray(frequency)
    starts = jnp.stack([jnp.cos(start), jnp.sin(start)])

    features = [own, squares, other, gain]
    right, left = project_first(half, target_rows, *features, weight)
    targets, _ = lax.optimization_barrier((target_rows, left))
    arrived = [pass_on(right, left)] * 2
    grouped, rotary = prepare(targets, queries, starts, jnp.asarray(turns))

    cached = []
    for distance in range(half - 1, 0, -1):
        distances = [distance, -distance] + ([0] if distance == 1 else [])
        if len(cached) < 2:
            cached.append(
                cache_attention(
                    len(cached), targets, prompt_lengths, cache_lengths, grouped, kv_cache, new_kv
                )
            )
        if len(cached) == 1:
            cached = [swap(cached[0])]
        terms = project(distances, targets, *features, weight)
        later = terms
        for part in range(2):
            right, left = sends(part, distance == half - 1, (terms, later)[part], *arrived[part])
            if part == 0:
                right, cached, later = lax.optimization_barrier((right, cached, terms))
            targets, _ = lax.optimization_barrier((target_rows, right))
            arrived[part] = pass_on(right, left)

    out = finish(target_rows, rotary, terms, [*arrived[0], *arrived[1]], grouped, cached)
    return lax.all_gather(out, "rep", axis=2, tiled=True)


def solution(mesh):
    in_specs = (
        P(None, ("grp", "rep"), "tp"),
        P("tp"),
        P("tp", None),
        P("tp", None),
        P("tp", None),
        P("grp"),
        P("grp"),
        P(("grp", "tp")),
        P(("grp", "tp"), "rep", None),
        P(("grp", "tp"), None, None),
        P(("grp", "tp"), None, None),
    )
    out_specs = P(("grp", "tp"), None, None)
    return jax.shard_map(
        per_device, mesh=mesh, in_specs=in_specs, out_specs=out_specs, check_vma=False
    )
```

```python
import functools
import math

import jax
import jax.numpy as jnp
import numpy as np
from jax import lax
from jax.experimental import pallas as pl
from jax.experimental.pallas import tpu as pltpu
from jax.sharding import PartitionSpec as P

D = 16384
HEADS = 128
KV_HEADS = 8
HEAD_DIM = 128
STRETCH = 192
STEPS = 2
QBLOCK = 64
GROUP = HEADS // KV_HEADS
ROWS = GROUP * STEPS
TAIL = 16
PART = ROWS + TAIL
CORE_HEADS = KV_HEADS // 2
NORMAL_FLOAT_LEVELS = [
    -1.0,
    -0.6961928009986877,
    -0.5250730514526367,
    -0.39491748809814453,
    -0.28444138169288635,
    -0.18477343022823334,
    -0.09105003625154495,
    0.0,
    0.07958029955625534,
    0.16093020141124725,
    0.24611230194568634,
    0.33791524171829224,
    0.44070982933044434,
    0.5626170039176941,
    0.7229568362236023,
    1.0,
]
ROTARY_BASE = 500000.0
EPSILON = 1e-05
NEGATIVE = -1e30
BF16 = jnp.bfloat16
F32 = jnp.float32
MIB = 1024 * 1024
VMEM = pl.BlockSpec(memory_space=pltpu.VMEM)
SMEM = pl.BlockSpec(memory_space=pltpu.SMEM)


def in_hbm(*arrays):
    return [pltpu.with_memory_space_constraint(array, pltpu.HBM) for array in arrays]


def ring_device(place, count):
    half = count // 2
    if isinstance(place, int):
        return 2 * place if place < half else 2 * (count - 1 - place) + 1
    return jnp.where(place < half, 2 * place, 2 * (count - 1 - place) + 1)


def owner_at(distance):
    count = lax.axis_size("tp")
    here = lax.axis_index("tp")
    place = jnp.where(here % 2 == 0, here // 2, count - 1 - here // 2)
    return ring_device((place + distance + count) % count, count)


def turned(column):
    rows = lax.broadcasted_iota(jnp.int32, (column.shape[0], 128), 0)
    lanes = lax.broadcasted_iota(jnp.int32, (column.shape[0], 128), 1)
    return jnp.sum(jnp.where(rows == lanes, column, 0.0), axis=0, keepdims=True)


def stood(row, count):
    rows = lax.broadcasted_iota(jnp.int32, (count, 128), 0)
    lanes = lax.broadcasted_iota(jnp.int32, (count, 128), 1)
    return jnp.sum(jnp.where(rows == lanes, row, 0.0), axis=1, keepdims=True)


def token_rows(column):
    at = lax.broadcasted_iota(jnp.int32, (8, 128), 0)
    ends = turned(column[128:])
    return jnp.where(at == 0, turned(column[:128]), jnp.where(at == 1, ends, 0.0))


def token_column(rows):
    return jnp.concatenate([stood(rows[0:1], 128), stood(rows[1:2], STRETCH - 128)], axis=0)


def two_pieces(rows):
    high = rows.astype(BF16).astype(F32)
    return jnp.concatenate([high, rows - high], axis=0).astype(BF16)


def one_piece(rows):
    rows = rows.astype(F32)
    return rows[:8] + rows[8:]


def pieces_tail(logs):
    row = turned(logs)
    high = row.astype(BF16).astype(F32)
    middle = (row - high).astype(BF16).astype(F32)
    low = row - high - middle
    at = lax.broadcasted_iota(jnp.int32, (TAIL, 128), 0)
    tail = jnp.where(at == 0, high, jnp.where(at == 1, middle, jnp.where(at == 2, low, 0.0)))
    return tail.astype(BF16)


def tail_pieces(tail):
    tail = tail.astype(F32)
    return stood(tail[0:1, :] + tail[1:2, :] + tail[2:3, :], ROWS)


def block_leaves(scale):
    wide = jnp.broadcast_to(scale, (8, HEAD_DIM))
    leaves = [wide * jnp.float32(level) for level in NORMAL_FLOAT_LEVELS]
    return [jnp.concatenate([leaf, leaf], axis=0).astype(BF16) for leaf in leaves]


def selected(codes, leaves):
    codes = codes.astype(jnp.int16)
    masks = [(codes & (1 << bit)) != 0 for bit in range(4)]

    def node(bit, base):
        if bit < 0:
            return leaves[base]
        low = node(bit - 1, base)
        return jnp.where(masks[bit], node(bit - 1, base + (1 << bit)), low)

    return node(3, 0)


def block_scales(scales, outer, column):
    count = scales.shape[0]
    line = lax.broadcasted_iota(jnp.int32, outer.shape, 0)
    line = jnp.sum(jnp.where(line == column, outer, 0.0), axis=0, keepdims=True)
    rows = lax.broadcasted_iota(jnp.int32, (count, count), 0)
    lanes = lax.broadcasted_iota(jnp.int32, (count, count), 1)
    second = jnp.sum(jnp.where(rows == lanes, line, 0.0), axis=1, keepdims=True)
    return (scales.astype(F32) + 1.0) / 256.0 * second


def weights_kernel(
    x, codes, key_scales, value_scales, outer, gain,
    out, scaled, squares, key_codes, value_codes, lines, scales, arrivals,
):
    per_rep = x.shape[0]
    features, width = key_codes.shape
    depth = min(256, features)
    blocks = features // depth
    columns = outer.shape[0] // 2
    rep = lax.axis_index("rep")

    def code_copies(block):
        rows = pl.ds(block * depth, depth)
        return [
            pltpu.make_async_copy(
                codes.at[rows, pl.ds(pl.multiple_of((2 * kind + rep) * width, width), width)],
                buffer.at[rows],
                arrivals.at[2 * block + kind],
            )
            for kind, buffer in enumerate((key_codes, value_codes))
        ]

    def line_copy(prompt):
        return pltpu.make_async_copy(
            x.at[prompt], lines.at[prompt], arrivals.at[2 * blocks + prompt]
        )

    for block in range(blocks):
        if block == blocks // 2:
            for prompt in range(per_rep):
                line_copy(prompt).start()
        for copy in code_copies(block):
            copy.start()
    for at in range(CORE_HEADS):
        column = (rep * CORE_HEADS + at) // (KV_HEADS // columns)
        lanes = slice(at * HEAD_DIM, (at + 1) * HEAD_DIM)
        scales[2 * at] = block_scales(key_scales[:, lanes], outer[...], column)
        scales[2 * at + 1] = block_scales(value_scales[:, lanes], outer[...], columns + column)
    squares[...] = jnp.zeros(squares.shape, F32)

    def body(step, _):
        row = pl.ds(step, 1)
        for at in range(CORE_HEADS):
            lanes = slice(at * HEAD_DIM, (at + 1) * HEAD_DIM)
            for kind, buffer in enumerate((key_codes, value_codes)):
                leaves = block_leaves(scales[2 * at + kind, row, :])
                for tile in range(QBLOCK // 16):
                    rows = pl.ds(pl.multiple_of(step * QBLOCK + 16 * tile, 16), 16)
                    out[at, rows, kind * HEAD_DIM : (kind + 1) * HEAD_DIM] = selected(
                        buffer[rows, lanes], leaves
                    )
        return 0

    steps = depth // QBLOCK
    late = blocks - blocks // 2
    for block in range(blocks):
        for copy in code_copies(block):
            copy.wait()
        lax.fori_loop(block * steps, (block + 1) * steps, body, 0)
        if block == blocks // 2:
            for prompt in range(per_rep):
                line_copy(prompt).wait()
        for chunk in range(blocks):
            if blocks // 2 + chunk * late // blocks != block:
                continue
            lanes = slice(chunk * depth, (chunk + 1) * depth)
            for prompt in range(per_rep):
                wide = lines[prompt, :, lanes].astype(F32)
                scaled[prompt, :, lanes] = (wide * gain[:, lanes]).astype(BF16)
                squares[prompt] += token_rows(jnp.sum(wide * wide, axis=1, keepdims=True))


def dequantize(x, codes, scales, outer, gain):
    per_rep, _, features = x.shape
    width = CORE_HEADS * HEAD_DIM
    blocks = features // min(256, features)
    rep = lambda: lax.axis_index("rep")
    x, codes, scales, outer, gain = in_hbm(x, codes, scales, outer, gain)
    return pl.pallas_call(
        weights_kernel,
        grid=(1,),
        in_specs=[
            pl.BlockSpec(memory_space=pltpu.HBM),
            pl.BlockSpec(memory_space=pltpu.HBM),
            pl.BlockSpec((scales.shape[0], width), lambda k: (0, rep())),
            pl.BlockSpec((scales.shape[0], width), lambda k: (0, 2 + rep())),
            pl.BlockSpec(outer.shape, lambda k: (0, 0)),
            pl.BlockSpec(gain.shape, lambda k: (0, 0)),
        ],
        out_specs=[VMEM] * 3,
        out_shape=[
            jax.ShapeDtypeStruct((CORE_HEADS, features, 2 * HEAD_DIM), BF16),
            jax.ShapeDtypeStruct(x.shape, BF16),
            jax.ShapeDtypeStruct((per_rep, 8, 128), F32),
        ],
        scratch_shapes=[
            pltpu.VMEM((features, width), jnp.int32),
            pltpu.VMEM((features, width), jnp.int32),
            pltpu.VMEM(x.shape, BF16),
            pltpu.VMEM((2 * CORE_HEADS, scales.shape[0], HEAD_DIM), F32),
            pltpu.SemaphoreType.DMA((2 * blocks + per_rep,)),
        ],
        compiler_params=pltpu.CompilerParams(vmem_limit_bytes=36 * MIB),
        cost_estimate=pl.CostEstimate(
            flops=32 * codes.size, bytes_accessed=codes.size * 2, transcendentals=0
        ),
        name="dequantize",
    )(x, codes, scales, scales, outer, gain)


def prompt_of(targets, owner):
    prompt = jnp.int32(-1)
    for at in range(targets.shape[0]):
        prompt = jnp.where(targets[at] == owner, at, prompt)
    return prompt


def with_lines(targets, distance, own, squares, other, gain, line, total, some, none):
    per_rep = own.shape[0]
    prompt = prompt_of(targets, owner_at(distance))
    at = lax.rem(jnp.maximum(prompt, 0), per_rep)
    is_own = prompt // per_rep == lax.axis_index("rep")

    @pl.when((prompt >= 0) & is_own)
    def _():
        some(own.at[at], squares.at[at])

    @pl.when((prompt >= 0) & jnp.logical_not(is_own))
    def _():
        width = min(512, line.shape[1])
        total[...] = jnp.zeros(total.shape, F32)
        for begin in range(0, line.shape[1], width):
            lanes = slice(begin, begin + width)
            wide = other[at, :, lanes].astype(F32)
            line[:, lanes] = (wide * gain[:, lanes]).astype(BF16)
            total[...] += token_rows(jnp.sum(wide * wide, axis=1, keepdims=True))
        some(line, total)

    pl.when(prompt < 0)(none)


def line_scratch(x):
    return [pltpu.VMEM(x.shape[1:], BF16), pltpu.VMEM((8, 128), F32)]


def first_kernel(distance, targets, own, squares, other, gain, weight, right, left, line, total):
    def some(lines, sums):
        for head in range(CORE_HEADS):
            product = jnp.dot(lines[...], weight[head], preferred_element_type=F32)
            rows = slice(head * STRETCH, (head + 1) * STRETCH)
            right[rows] = product[:, :HEAD_DIM].astype(BF16)
            left[rows] = product[:, HEAD_DIM:].astype(BF16)
        right[CORE_HEADS * STRETCH :] = two_pieces(sums[...])

    def none():
        right[...] = jnp.zeros(right.shape, BF16)
        left[...] = jnp.zeros(left.shape, BF16)

    with_lines(targets, distance, own, squares, other, gain, line, total, some, none)


def project_first(distance, targets, own, squares, other, gain, weight):
    rows = CORE_HEADS * STRETCH
    return pl.pallas_call(
        functools.partial(first_kernel, distance),
        in_specs=[SMEM] + [VMEM] * 5,
        out_specs=[VMEM] * 2,
        out_shape=[
            jax.ShapeDtypeStruct((rows + TAIL, HEAD_DIM), BF16),
            jax.ShapeDtypeStruct((rows, HEAD_DIM), BF16),
        ],
        scratch_shapes=line_scratch(own),
        compiler_params=pltpu.CompilerParams(vmem_limit_bytes=24 * MIB),
        cost_estimate=pl.CostEstimate(
            flops=STRETCH * weight.size * 2, bytes_accessed=weight.size, transcendentals=0
        ),
        name="project_first",
    )(targets, own, squares, other, gain, weight)


def project_kernel(distances, targets, own, squares, other, gain, weight, out, line, total):
    for item, distance in enumerate(distances):

        def some(lines, sums, item=item):
            for head in range(CORE_HEADS):
                product = jnp.dot(lines[...], weight[head], preferred_element_type=F32)
                rows = slice(head * STRETCH, (head + 1) * STRETCH)
                out[item, 0, rows] = product[:, :HEAD_DIM]
                out[item, 1, rows] = product[:, HEAD_DIM:]
            out[item, 0, CORE_HEADS * STRETCH :] = sums[...]

        def none(item=item):
            out[item] = jnp.zeros(out.shape[1:], F32)

        with_lines(targets, distance, own, squares, other, gain, line, total, some, none)


def project(distances, targets, own, squares, other, gain, weight):
    return pl.pallas_call(
        functools.partial(project_kernel, distances),
        in_specs=[SMEM] + [VMEM] * 5,
        out_specs=VMEM,
        out_shape=jax.ShapeDtypeStruct((len(distances), 2, 4 * STRETCH + 8, HEAD_DIM), F32),
        scratch_shapes=line_scratch(own),
        compiler_params=pltpu.CompilerParams(vmem_limit_bytes=24 * MIB),
        cost_estimate=pl.CostEstimate(
            flops=len(distances) * STRETCH * weight.size,
            bytes_accessed=weight.size,
            transcendentals=0,
        ),
        name="project",
    )(targets, own, squares, other, gain, weight)


def send_kernel(half, terms, *refs):
    *arrived, to_right, to_left = refs
    rows = CORE_HEADS * STRETCH
    for item, out in enumerate((to_right, to_left)):
        kind = (half + item) % 2
        total = terms[item, kind, :rows]
        if arrived:
            total += arrived[item][:rows].astype(F32)
        out[:rows] = total.astype(BF16)
        if kind == 0:
            squares = terms[item, 0, rows:]
            if arrived:
                squares += one_piece(arrived[item][rows : rows + TAIL])
            out[rows : rows + TAIL] = two_pieces(squares)
        spare = rows + (TAIL if kind == 0 else 0)
        if spare < out.shape[0]:
            out[spare:] = jnp.zeros((out.shape[0] - spare, HEAD_DIM), BF16)


def sends(half, terms, arrived):
    rows = CORE_HEADS * STRETCH
    shapes = [jax.ShapeDtypeStruct((rows + TAIL, HEAD_DIM), BF16)] * 2
    return pl.pallas_call(
        functools.partial(send_kernel, half),
        in_specs=[VMEM] * (1 + len(arrived)),
        out_specs=[VMEM] * 2,
        out_shape=shapes,
        compiler_params=pltpu.CompilerParams(vmem_limit_bytes=16 * MIB),
        name="sends",
    )(terms, *arrived)


def prepare_kernel(targets, queries, starts, turns, grouped, rotary):
    for head in range(KV_HEADS):
        for member in range(GROUP):
            begin = (head * GROUP + member) * HEAD_DIM
            rows = slice(member * STEPS, (member + 1) * STEPS)
            grouped[head, rows] = queries[0, :, begin : begin + HEAD_DIM]
    row = pl.ds(jnp.maximum(prompt_of(targets, lax.axis_index("tp")), 0), 1)
    cosine, sine = starts[0, row, :], starts[1, row, :]
    lane = lax.broadcasted_iota(jnp.int32, turns.shape[1:], 1)
    rotary[0] = turns[0] * cosine - turns[1] * sine
    sine = turns[1] * cosine + turns[0] * sine
    rotary[1] = jnp.where(lane < HEAD_DIM // 2, -sine, sine)


def prepare(targets, queries, starts, turns):
    return pl.pallas_call(
        prepare_kernel,
        in_specs=[SMEM] + [VMEM] * 3,
        out_specs=[VMEM] * 2,
        out_shape=[
            jax.ShapeDtypeStruct((KV_HEADS, ROWS, HEAD_DIM), BF16),
            jax.ShapeDtypeStruct(turns.shape, F32),
        ],
        compiler_params=pltpu.CompilerParams(vmem_limit_bytes=16 * MIB),
        name="prepare",
    )(targets, queries, starts, turns)


def cache_kernel(part, targets, lengths, stored, q, cache, new, out):
    scaling = HEAD_DIM ** (-0.5)
    dims = (((1,), (1,)), ((), ()))
    here = lax.axis_index("tp")
    rep = lax.axis_index("rep")
    length = cache.shape[1]
    prompt = prompt_of(targets, here)
    handed = lengths[jnp.maximum(prompt, 0)] - STRETCH
    span = jnp.where(prompt >= 0, handed, stored[0]) - rep * length
    allowed = lax.broadcasted_iota(jnp.int32, (ROWS, length), 1) < span
    second_step = lax.broadcasted_iota(jnp.int32, (ROWS, 1), 0) % STEPS == 1
    for at in range(CORE_HEADS):
        head = (rep if part == 1 else 1 - rep) * CORE_HEADS + at
        key_lanes = pl.ds(pl.multiple_of(head * HEAD_DIM, HEAD_DIM), HEAD_DIM)
        value_lanes = pl.ds(pl.multiple_of((KV_HEADS + head) * HEAD_DIM, HEAD_DIM), HEAD_DIM)
        query = q[head]
        wide = query.astype(F32)
        scores = lax.dot_general(query, cache[0, :, key_lanes], dims, preferred_element_type=F32)
        scores = jnp.where(allowed, scores * scaling, NEGATIVE)
        highest = jnp.max(scores, axis=1, keepdims=True)
        fresh = []
        for step in range(STEPS):
            key = new[0, step : step + 1, key_lanes].astype(F32)
            score = jnp.sum(wide * key, axis=1, keepdims=True) * scaling
            shown = rep == 0 if step == 0 else second_step & (rep == 0)
            score = jnp.where(shown, score, NEGATIVE)
            highest = jnp.maximum(highest, score)
            fresh.append(score)
        some = highest > 0.5 * NEGATIVE
        highest = jnp.where(some, highest, 0.0)
        weight = jnp.exp(scores - highest)
        totals = jnp.sum(weight, axis=1, keepdims=True)
        sums = jnp.dot(weight.astype(BF16), cache[0, :, value_lanes], preferred_element_type=F32)
        for step in range(STEPS):
            share = jnp.exp(fresh[step] - highest)
            totals += share
            value = new[0, step : step + 1, value_lanes].astype(F32)
            sums += share.astype(BF16).astype(F32) * value
        totals = jnp.where(some, totals, 1.0)
        out[at, :ROWS] = (sums / totals).astype(BF16)
        out[at, ROWS:] = pieces_tail(jnp.where(some, highest + jnp.log(totals), NEGATIVE))


def cache_attention(part, targets, lengths, stored, grouped, kv_cache, new_kv):
    return pl.pallas_call(
        functools.partial(cache_kernel, part),
        in_specs=[SMEM] * 3 + [VMEM] * 3,
        out_specs=VMEM,
        out_shape=jax.ShapeDtypeStruct((CORE_HEADS, PART, HEAD_DIM), BF16),
        compiler_params=pltpu.CompilerParams(vmem_limit_bytes=16 * MIB),
        cost_estimate=pl.CostEstimate(
            flops=2 * grouped.size * kv_cache.shape[1],
            bytes_accessed=kv_cache.size,
            transcendentals=CORE_HEADS * ROWS * kv_cache.shape[1],
        ),
        name="cache_attention",
    )(targets, lengths, stored, grouped, kv_cache, new_kv)


def final_kernel(
    targets, rotary, own, right_keys, left_values, right_values, left_keys, grouped,
    cached_there, cached_here, out,
):
    scaling = HEAD_DIM ** (-0.5)
    dims = (((1,), (1,)), ((), ()))
    mine = own.shape[0] - 1
    first = lax.axis_index("rep") * CORE_HEADS
    prompt = prompt_of(targets, lax.axis_index("tp"))
    cosine, sine = rotary[0], rotary[1]
    rows = CORE_HEADS * STRETCH
    squares = own[mine, 0, rows:] + one_piece(right_keys[rows : rows + TAIL]) + one_piece(left_keys[rows : rows + TAIL])
    scale = token_column(lax.rsqrt(squares / D + EPSILON))
    for head in range(CORE_HEADS):
        at = slice(head * STRETCH, (head + 1) * STRETCH)
        keys = own[mine, 0, at] + right_keys[at].astype(F32) + left_keys[at].astype(F32)
        values = own[mine, 1, at] + right_values[at].astype(F32) + left_values[at].astype(F32)
        keys = (keys * scale).astype(BF16).astype(F32)
        values = (values * scale).astype(BF16)
        keys = keys * cosine + pltpu.roll(keys, HEAD_DIM // 2, 1) * sine
        scores = lax.dot_general(
            grouped[first + head], keys.astype(BF16), dims, preferred_element_type=F32
        )
        scores = scores * scaling
        highest = jnp.max(scores, axis=1, keepdims=True)
        weight = jnp.exp(scores - highest)
        totals = jnp.sum(weight, axis=1, keepdims=True)
        sums = jnp.dot(weight.astype(BF16), values, preferred_element_type=F32) / totals
        logs = jnp.where(prompt >= 0, highest + jnp.log(totals), NEGATIVE)
        parts = [cached_there[head], cached_here[head]]
        logs = [tail_pieces(part[ROWS:]) for part in parts] + [logs]
        sums = [part[:ROWS].astype(F32) for part in parts] + [sums]
        highest = functools.reduce(jnp.maximum, logs)
        shares = [jnp.exp(log - highest) for log in logs]
        total = functools.reduce(jnp.add, shares)
        joined = functools.reduce(jnp.add, [share * part for share, part in zip(shares, sums)])
        result = (joined / total).astype(BF16)
        for member in range(GROUP):
            begin = (head * GROUP + member) * HEAD_DIM
            out[0, :, begin : begin + HEAD_DIM] = result[member * STEPS : (member + 1) * STEPS]


def finish(targets, rotary, own, arrived, grouped, cached):
    width = CORE_HEADS * GROUP * HEAD_DIM
    return pl.pallas_call(
        final_kernel,
        in_specs=[SMEM] + [VMEM] * 9,
        out_specs=VMEM,
        out_shape=jax.ShapeDtypeStruct((1, STEPS, width), BF16),
        compiler_params=pltpu.CompilerParams(vmem_limit_bytes=16 * MIB),
        name="finish",
    )(targets, rotary, own, *arrived, grouped, *cached)


def rotary_turns():
    half = np.arange(HEAD_DIM // 2, dtype=np.float64) / (HEAD_DIM // 2)
    frequency = ROTARY_BASE ** (-np.concatenate([half, half]))
    angles = np.arange(STRETCH, dtype=np.float64)[:, None] * frequency
    return frequency.astype(np.float32), np.stack([np.cos(angles), np.sin(angles)]).astype(np.float32)


def per_device(
    stretch,
    norm_gain,
    kv_codes,
    scale_codes,
    outer_scales,
    prompt_lengths,
    target_rows,
    cache_lengths,
    kv_cache,
    queries,
    new_kv,
):
    count = lax.axis_size("tp")
    half = count // 2
    lines = stretch.transpose(1, 0, 2)
    gain = norm_gain.reshape(1, -1)
    ring = [ring_device(at, count) for at in range(count)]
    to_right = [(ring[at], ring[(at + 1) % count]) for at in range(count)]
    to_left = [(ring[at], ring[at - 1]) for at in range(count)]

    def pass_on(right, left):
        return lax.ppermute(right, "tp", to_right), lax.ppermute(left, "tp", to_left)

    swap = lambda array: lax.ppermute(array, "rep", [(0, 1), (1, 0)])
    other = swap(lines)
    weight, own, squares = dequantize(lines, kv_codes, scale_codes, outer_scales.T, gain)
    frequency, turns = rotary_turns()
    start = (prompt_lengths - STRETCH).astype(F32)[:, None] * jnp.asarray(frequency)
    starts = jnp.stack([jnp.cos(start), jnp.sin(start)])

    features = [own, squares, other, gain]
    right, left = project_first(half, target_rows, *features, weight)
    targets, _ = lax.optimization_barrier((target_rows, left))
    arrived = [pass_on(right, left), []]

    cached = []
    for distance in range(half - 1, 0, -1):
        distances = [distance, -distance] + ([0] if distance == 1 else [])
        terms = project(distances, targets, *features, weight)
        right, left = sends(1, terms, arrived[1])
        if distance == half - 1:
            targets, _ = lax.optimization_barrier((target_rows, right))
        terms, right = lax.optimization_barrier((terms, right))
        arrived[1] = pass_on(right, left)
        if distance == half - 1:
            grouped, rotary = prepare(targets, queries, starts, jnp.asarray(turns))
            cached = [
                swap(
                    cache_attention(
                        0, targets, prompt_lengths, cache_lengths, grouped, kv_cache, new_kv
                    )
                )
            ]
        right, left = sends(0, terms, arrived[0])
        if distance == half - 2 or half == 2:
            cached, right = lax.optimization_barrier((cached, right))
        targets, _ = lax.optimization_barrier((target_rows, right))
        arrived[0] = pass_on(right, left)

    cached.append(
        cache_attention(1, targets, prompt_lengths, cache_lengths, grouped, kv_cache, new_kv)
    )
    out = finish(target_rows, rotary, terms, [*arrived[0], *arrived[1]], grouped, cached)
    return lax.all_gather(out, "rep", axis=2, tiled=True)


def solution(mesh):
    in_specs = (
        P(None, ("grp", "rep"), "tp"),
        P("tp"),
        P("tp", None),
        P("tp", None),
        P("tp", None),
        P("grp"),
        P("grp"),
        P(("grp", "tp")),
        P(("grp", "tp"), "rep", None),
        P(("grp", "tp"), None, None),
        P(("grp", "tp"), None, None),
    )
    out_specs = P(("grp", "tp"), None, None)
    return jax.shard_map(
        per_device, mesh=mesh, in_specs=in_specs, out_specs=out_specs, check_vma=False
    )
```

```python
import functools
import math

import jax
import jax.numpy as jnp
import numpy as np
from jax import lax
from jax.experimental import pallas as pl
from jax.experimental.pallas import tpu as pltpu
from jax.sharding import PartitionSpec as P

D = 16384
HEADS = 128
KV_HEADS = 8
HEAD_DIM = 128
STRETCH = 192
STEPS = 2
QBLOCK = 64
GROUP = HEADS // KV_HEADS
ROWS = GROUP * STEPS
TAIL = 16
PART = ROWS + TAIL
CORE_HEADS = KV_HEADS // 2
NORMAL_FLOAT_LEVELS = [
    -1.0,
    -0.6961928009986877,
    -0.5250730514526367,
    -0.39491748809814453,
    -0.28444138169288635,
    -0.18477343022823334,
    -0.09105003625154495,
    0.0,
    0.07958029955625534,
    0.16093020141124725,
    0.24611230194568634,
    0.33791524171829224,
    0.44070982933044434,
    0.5626170039176941,
    0.7229568362236023,
    1.0,
]
ROTARY_BASE = 500000.0
EPSILON = 1e-05
NEGATIVE = -1e30
BF16 = jnp.bfloat16
F32 = jnp.float32
MIB = 1024 * 1024
VMEM = pl.BlockSpec(memory_space=pltpu.VMEM)
SMEM = pl.BlockSpec(memory_space=pltpu.SMEM)


def in_hbm(*arrays):
    return [pltpu.with_memory_space_constraint(array, pltpu.HBM) for array in arrays]


def ring_device(place, count):
    half = count // 2
    if isinstance(place, int):
        return 2 * place if place < half else 2 * (count - 1 - place) + 1
    return jnp.where(place < half, 2 * place, 2 * (count - 1 - place) + 1)


def owner_at(distance):
    count = lax.axis_size("tp")
    here = lax.axis_index("tp")
    place = jnp.where(here % 2 == 0, here // 2, count - 1 - here // 2)
    return ring_device((place + distance + count) % count, count)


def turned(column):
    rows = lax.broadcasted_iota(jnp.int32, (column.shape[0], 128), 0)
    lanes = lax.broadcasted_iota(jnp.int32, (column.shape[0], 128), 1)
    return jnp.sum(jnp.where(rows == lanes, column, 0.0), axis=0, keepdims=True)


def stood(row, count):
    rows = lax.broadcasted_iota(jnp.int32, (count, 128), 0)
    lanes = lax.broadcasted_iota(jnp.int32, (count, 128), 1)
    return jnp.sum(jnp.where(rows == lanes, row, 0.0), axis=1, keepdims=True)


def token_rows(column):
    at = lax.broadcasted_iota(jnp.int32, (8, 128), 0)
    ends = turned(column[128:])
    return jnp.where(at == 0, turned(column[:128]), jnp.where(at == 1, ends, 0.0))


def token_column(rows):
    return jnp.concatenate([stood(rows[0:1], 128), stood(rows[1:2], STRETCH - 128)], axis=0)


def two_pieces(rows):
    high = rows.astype(BF16).astype(F32)
    return jnp.concatenate([high, rows - high], axis=0).astype(BF16)


def one_piece(rows):
    rows = rows.astype(F32)
    return rows[:8] + rows[8:]


def pieces_tail(logs):
    row = turned(logs)
    high = row.astype(BF16).astype(F32)
    middle = (row - high).astype(BF16).astype(F32)
    low = row - high - middle
    at = lax.broadcasted_iota(jnp.int32, (TAIL, 128), 0)
    tail = jnp.where(at == 0, high, jnp.where(at == 1, middle, jnp.where(at == 2, low, 0.0)))
    return tail.astype(BF16)


def tail_pieces(tail):
    tail = tail.astype(F32)
    return stood(tail[0:1, :] + tail[1:2, :] + tail[2:3, :], ROWS)


def block_leaves(scale):
    wide = jnp.broadcast_to(scale, (8, HEAD_DIM))
    leaves = [wide * jnp.float32(level) for level in NORMAL_FLOAT_LEVELS]
    return [jnp.concatenate([leaf, leaf], axis=0).astype(BF16) for leaf in leaves]


def selected(codes, leaves):
    codes = codes.astype(jnp.int16)
    masks = [(codes & (1 << bit)) != 0 for bit in range(4)]

    def node(bit, base):
        if bit < 0:
            return leaves[base]
        low = node(bit - 1, base)
        return jnp.where(masks[bit], node(bit - 1, base + (1 << bit)), low)

    return node(3, 0)


def block_scales(scales, outer, column):
    count = scales.shape[0]
    line = lax.broadcasted_iota(jnp.int32, outer.shape, 0)
    line = jnp.sum(jnp.where(line == column, outer, 0.0), axis=0, keepdims=True)
    rows = lax.broadcasted_iota(jnp.int32, (count, count), 0)
    lanes = lax.broadcasted_iota(jnp.int32, (count, count), 1)
    second = jnp.sum(jnp.where(rows == lanes, line, 0.0), axis=1, keepdims=True)
    return (scales.astype(F32) + 1.0) / 256.0 * second


def weights_kernel(
    x, codes, key_scales, value_scales, outer, gain,
    out, scaled, squares, key_codes, value_codes, lines, scales, arrivals,
):
    per_rep = x.shape[0]
    features, width = key_codes.shape
    depth = min(256, features)
    blocks = features // depth
    columns = outer.shape[0] // 2
    rep = lax.axis_index("rep")

    def code_copies(block):
        rows = pl.ds(block * depth, depth)
        return [
            pltpu.make_async_copy(
                codes.at[rows, pl.ds(pl.multiple_of((2 * kind + rep) * width, width), width)],
                buffer.at[rows],
                arrivals.at[2 * block + kind],
            )
            for kind, buffer in enumerate((key_codes, value_codes))
        ]

    def line_copy(prompt):
        return pltpu.make_async_copy(
            x.at[prompt], lines.at[prompt], arrivals.at[2 * blocks + prompt]
        )

    for block in range(blocks):
        if block == blocks // 2:
            for prompt in range(per_rep):
                line_copy(prompt).start()
        for copy in code_copies(block):
            copy.start()
    for at in range(CORE_HEADS):
        column = (rep * CORE_HEADS + at) // (KV_HEADS // columns)
        lanes = slice(at * HEAD_DIM, (at + 1) * HEAD_DIM)
        scales[2 * at] = block_scales(key_scales[:, lanes], outer[...], column)
        scales[2 * at + 1] = block_scales(value_scales[:, lanes], outer[...], columns + column)
    squares[...] = jnp.zeros(squares.shape, F32)

    def body(step, _):
        row = pl.ds(step, 1)
        for at in range(CORE_HEADS):
            lanes = slice(at * HEAD_DIM, (at + 1) * HEAD_DIM)
            for kind, buffer in enumerate((key_codes, value_codes)):
                leaves = block_leaves(scales[2 * at + kind, row, :])
                for tile in range(QBLOCK // 16):
                    rows = pl.ds(pl.multiple_of(step * QBLOCK + 16 * tile, 16), 16)
                    out[at, rows, kind * HEAD_DIM : (kind + 1) * HEAD_DIM] = selected(
                        buffer[rows, lanes], leaves
                    )
        return 0

    steps = depth // QBLOCK
    late = blocks - blocks // 2
    for block in range(blocks):
        for copy in code_copies(block):
            copy.wait()
        lax.fori_loop(block * steps, (block + 1) * steps, body, 0)
        if block == blocks // 2:
            for prompt in range(per_rep):
                line_copy(prompt).wait()
        for chunk in range(blocks):
            if blocks // 2 + chunk * late // blocks != block:
                continue
            lanes = slice(chunk * depth, (chunk + 1) * depth)
            for prompt in range(per_rep):
                wide = lines[prompt, :, lanes].astype(F32)
                scaled[prompt, :, lanes] = (wide * gain[:, lanes]).astype(BF16)
                squares[prompt] += token_rows(jnp.sum(wide * wide, axis=1, keepdims=True))


def dequantize(x, codes, scales, outer, gain):
    per_rep, _, features = x.shape
    width = CORE_HEADS * HEAD_DIM
    blocks = features // min(256, features)
    rep = lambda: lax.axis_index("rep")
    x, codes, scales, outer, gain = in_hbm(x, codes, scales, outer, gain)
    return pl.pallas_call(
        weights_kernel,
        grid=(1,),
        in_specs=[
            pl.BlockSpec(memory_space=pltpu.HBM),
            pl.BlockSpec(memory_space=pltpu.HBM),
            pl.BlockSpec((scales.shape[0], width), lambda k: (0, rep())),
            pl.BlockSpec((scales.shape[0], width), lambda k: (0, 2 + rep())),
            pl.BlockSpec(outer.shape, lambda k: (0, 0)),
            pl.BlockSpec(gain.shape, lambda k: (0, 0)),
        ],
        out_specs=[VMEM] * 3,
        out_shape=[
            jax.ShapeDtypeStruct((CORE_HEADS, features, 2 * HEAD_DIM), BF16),
            jax.ShapeDtypeStruct(x.shape, BF16),
            jax.ShapeDtypeStruct((per_rep, 8, 128), F32),
        ],
        scratch_shapes=[
            pltpu.VMEM((features, width), jnp.int32),
            pltpu.VMEM((features, width), jnp.int32),
            pltpu.VMEM(x.shape, BF16),
            pltpu.VMEM((2 * CORE_HEADS, scales.shape[0], HEAD_DIM), F32),
            pltpu.SemaphoreType.DMA((2 * blocks + per_rep,)),
        ],
        compiler_params=pltpu.CompilerParams(vmem_limit_bytes=36 * MIB),
        cost_estimate=pl.CostEstimate(
            flops=32 * codes.size, bytes_accessed=codes.size * 2, transcendentals=0
        ),
        name="dequantize",
    )(x, codes, scales, scales, outer, gain)


def prompt_of(targets, owner):
    prompt = jnp.int32(-1)
    for at in range(targets.shape[0]):
        prompt = jnp.where(targets[at] == owner, at, prompt)
    return prompt


def with_lines(targets, distance, own, squares, other, gain, line, total, some, none):
    per_rep = own.shape[0]
    prompt = prompt_of(targets, owner_at(distance))
    at = lax.rem(jnp.maximum(prompt, 0), per_rep)
    is_own = prompt // per_rep == lax.axis_index("rep")

    @pl.when((prompt >= 0) & is_own)
    def _():
        some(own.at[at], squares.at[at])

    @pl.when((prompt >= 0) & jnp.logical_not(is_own))
    def _():
        width = min(512, line.shape[1])
        total[...] = jnp.zeros(total.shape, F32)
        for begin in range(0, line.shape[1], width):
            lanes = slice(begin, begin + width)
            wide = other[at, :, lanes].astype(F32)
            line[:, lanes] = (wide * gain[:, lanes]).astype(BF16)
            total[...] += token_rows(jnp.sum(wide * wide, axis=1, keepdims=True))
        some(line, total)

    pl.when(prompt < 0)(none)


def line_scratch(x):
    return [pltpu.VMEM(x.shape[1:], BF16), pltpu.VMEM((8, 128), F32)]


def first_kernel(distance, targets, own, squares, other, gain, weight, right, left, line, total):
    def some(lines, sums):
        for head in range(CORE_HEADS):
            product = jnp.dot(lines[...], weight[head], preferred_element_type=F32)
            rows = slice(head * STRETCH, (head + 1) * STRETCH)
            right[rows] = product[:, :HEAD_DIM].astype(BF16)
            left[rows] = product[:, HEAD_DIM:].astype(BF16)
        right[CORE_HEADS * STRETCH :] = two_pieces(sums[...])

    def none():
        right[...] = jnp.zeros(right.shape, BF16)
        left[...] = jnp.zeros(left.shape, BF16)

    with_lines(targets, distance, own, squares, other, gain, line, total, some, none)


def project_first(distance, targets, own, squares, other, gain, weight):
    rows = CORE_HEADS * STRETCH
    return pl.pallas_call(
        functools.partial(first_kernel, distance),
        in_specs=[SMEM] + [VMEM] * 5,
        out_specs=[VMEM] * 2,
        out_shape=[
            jax.ShapeDtypeStruct((rows + TAIL, HEAD_DIM), BF16),
            jax.ShapeDtypeStruct((rows, HEAD_DIM), BF16),
        ],
        scratch_shapes=line_scratch(own),
        compiler_params=pltpu.CompilerParams(vmem_limit_bytes=24 * MIB),
        cost_estimate=pl.CostEstimate(
            flops=STRETCH * weight.size * 2, bytes_accessed=weight.size, transcendentals=0
        ),
        name="project_first",
    )(targets, own, squares, other, gain, weight)


def project_kernel(distances, targets, own, squares, other, gain, weight, out, line, total):
    for item, distance in enumerate(distances):

        def some(lines, sums, item=item):
            for head in range(CORE_HEADS):
                product = jnp.dot(lines[...], weight[head], preferred_element_type=F32)
                rows = slice(head * STRETCH, (head + 1) * STRETCH)
                out[item, 0, rows] = product[:, :HEAD_DIM]
                out[item, 1, rows] = product[:, HEAD_DIM:]
            out[item, 0, CORE_HEADS * STRETCH :] = sums[...]

        def none(item=item):
            out[item] = jnp.zeros(out.shape[1:], F32)

        with_lines(targets, distance, own, squares, other, gain, line, total, some, none)


def project(distances, targets, own, squares, other, gain, weight):
    return pl.pallas_call(
        functools.partial(project_kernel, distances),
        in_specs=[SMEM] + [VMEM] * 5,
        out_specs=VMEM,
        out_shape=jax.ShapeDtypeStruct((len(distances), 2, 4 * STRETCH + 8, HEAD_DIM), F32),
        scratch_shapes=line_scratch(own),
        compiler_params=pltpu.CompilerParams(vmem_limit_bytes=24 * MIB),
        cost_estimate=pl.CostEstimate(
            flops=len(distances) * STRETCH * weight.size,
            bytes_accessed=weight.size,
            transcendentals=0,
        ),
        name="project",
    )(targets, own, squares, other, gain, weight)


def send_kernel(half, terms, *refs):
    *arrived, to_right, to_left = refs
    rows = CORE_HEADS * STRETCH
    for item, out in enumerate((to_right, to_left)):
        kind = (half + item) % 2
        total = terms[item, kind, :rows]
        if arrived:
            total += arrived[item][:rows].astype(F32)
        out[:rows] = total.astype(BF16)
        if kind == 0:
            squares = terms[item, 0, rows:]
            if arrived:
                squares += one_piece(arrived[item][rows : rows + TAIL])
            out[rows : rows + TAIL] = two_pieces(squares)
        spare = rows + (TAIL if kind == 0 else 0)
        if spare < out.shape[0]:
            out[spare:] = jnp.zeros((out.shape[0] - spare, HEAD_DIM), BF16)


def sends(half, terms, arrived):
    rows = CORE_HEADS * STRETCH
    shapes = [jax.ShapeDtypeStruct((rows + TAIL, HEAD_DIM), BF16)] * 2
    return pl.pallas_call(
        functools.partial(send_kernel, half),
        in_specs=[VMEM] * (1 + len(arrived)),
        out_specs=[VMEM] * 2,
        out_shape=shapes,
        compiler_params=pltpu.CompilerParams(vmem_limit_bytes=16 * MIB),
        name="sends",
    )(terms, *arrived)


def prepare_kernel(targets, queries, starts, turns, grouped, rotary):
    for head in range(KV_HEADS):
        for member in range(GROUP):
            begin = (head * GROUP + member) * HEAD_DIM
            rows = slice(member * STEPS, (member + 1) * STEPS)
            grouped[head, rows] = queries[0, :, begin : begin + HEAD_DIM]
    row = pl.ds(jnp.maximum(prompt_of(targets, lax.axis_index("tp")), 0), 1)
    cosine, sine = starts[0, row, :], starts[1, row, :]
    lane = lax.broadcasted_iota(jnp.int32, turns.shape[1:], 1)
    rotary[0] = turns[0] * cosine - turns[1] * sine
    sine = turns[1] * cosine + turns[0] * sine
    rotary[1] = jnp.where(lane < HEAD_DIM // 2, -sine, sine)


def prepare(targets, queries, starts, turns):
    return pl.pallas_call(
        prepare_kernel,
        in_specs=[SMEM] + [VMEM] * 3,
        out_specs=[VMEM] * 2,
        out_shape=[
            jax.ShapeDtypeStruct((KV_HEADS, ROWS, HEAD_DIM), BF16),
            jax.ShapeDtypeStruct(turns.shape, F32),
        ],
        compiler_params=pltpu.CompilerParams(vmem_limit_bytes=16 * MIB),
        name="prepare",
    )(targets, queries, starts, turns)


def cache_kernel(part, targets, lengths, stored, q, cache, new, out):
    scaling = HEAD_DIM ** (-0.5)
    dims = (((1,), (1,)), ((), ()))
    here = lax.axis_index("tp")
    rep = lax.axis_index("rep")
    length = cache.shape[1]
    prompt = prompt_of(targets, here)
    handed = lengths[jnp.maximum(prompt, 0)] - STRETCH
    span = jnp.where(prompt >= 0, handed, stored[0]) - rep * length
    allowed = lax.broadcasted_iota(jnp.int32, (ROWS, length), 1) < span
    second_step = lax.broadcasted_iota(jnp.int32, (ROWS, 1), 0) % STEPS == 1
    for at in range(CORE_HEADS):
        head = (rep if part == 1 else 1 - rep) * CORE_HEADS + at
        key_lanes = pl.ds(pl.multiple_of(head * HEAD_DIM, HEAD_DIM), HEAD_DIM)
        value_lanes = pl.ds(pl.multiple_of((KV_HEADS + head) * HEAD_DIM, HEAD_DIM), HEAD_DIM)
        query = q[head]
        wide = query.astype(F32)
        scores = lax.dot_general(query, cache[0, :, key_lanes], dims, preferred_element_type=F32)
        scores = jnp.where(allowed, scores * scaling, NEGATIVE)
        highest = jnp.max(scores, axis=1, keepdims=True)
        fresh = []
        for step in range(STEPS):
            key = new[0, step : step + 1, key_lanes].astype(F32)
            score = jnp.sum(wide * key, axis=1, keepdims=True) * scaling
            shown = rep == 0 if step == 0 else second_step & (rep == 0)
            score = jnp.where(shown, score, NEGATIVE)
            highest = jnp.maximum(highest, score)
            fresh.append(score)
        some = highest > 0.5 * NEGATIVE
        highest = jnp.where(some, highest, 0.0)
        weight = jnp.exp(scores - highest)
        totals = jnp.sum(weight, axis=1, keepdims=True)
        sums = jnp.dot(weight.astype(BF16), cache[0, :, value_lanes], preferred_element_type=F32)
        for step in range(STEPS):
            share = jnp.exp(fresh[step] - highest)
            totals += share
            value = new[0, step : step + 1, value_lanes].astype(F32)
            sums += share.astype(BF16).astype(F32) * value
        totals = jnp.where(some, totals, 1.0)
        out[at, :ROWS] = (sums / totals).astype(BF16)
        out[at, ROWS:] = pieces_tail(jnp.where(some, highest + jnp.log(totals), NEGATIVE))


def cache_attention(part, targets, lengths, stored, grouped, kv_cache, new_kv):
    return pl.pallas_call(
        functools.partial(cache_kernel, part),
        in_specs=[SMEM] * 3 + [VMEM] * 3,
        out_specs=VMEM,
        out_shape=jax.ShapeDtypeStruct((CORE_HEADS, PART, HEAD_DIM), BF16),
        compiler_params=pltpu.CompilerParams(vmem_limit_bytes=16 * MIB),
        cost_estimate=pl.CostEstimate(
            flops=2 * grouped.size * kv_cache.shape[1],
            bytes_accessed=kv_cache.size,
            transcendentals=CORE_HEADS * ROWS * kv_cache.shape[1],
        ),
        name="cache_attention",
    )(targets, lengths, stored, grouped, kv_cache, new_kv)


def final_kernel(
    targets, rotary, own, right_keys, left_values, right_values, left_keys, grouped,
    cached_there, cached_here, out,
):
    scaling = HEAD_DIM ** (-0.5)
    dims = (((1,), (1,)), ((), ()))
    mine = own.shape[0] - 1
    first = lax.axis_index("rep") * CORE_HEADS
    prompt = prompt_of(targets, lax.axis_index("tp"))
    cosine, sine = rotary[0], rotary[1]
    rows = CORE_HEADS * STRETCH
    squares = own[mine, 0, rows:] + one_piece(right_keys[rows : rows + TAIL]) + one_piece(left_keys[rows : rows + TAIL])
    scale = token_column(lax.rsqrt(squares / D + EPSILON))
    for head in range(CORE_HEADS):
        at = slice(head * STRETCH, (head + 1) * STRETCH)
        keys = own[mine, 0, at] + right_keys[at].astype(F32) + left_keys[at].astype(F32)
        values = own[mine, 1, at] + right_values[at].astype(F32) + left_values[at].astype(F32)
        keys = (keys * scale).astype(BF16).astype(F32)
        values = (values * scale).astype(BF16)
        keys = keys * cosine + pltpu.roll(keys, HEAD_DIM // 2, 1) * sine
        scores = lax.dot_general(
            grouped[first + head], keys.astype(BF16), dims, preferred_element_type=F32
        )
        scores = scores * scaling
        highest = jnp.max(scores, axis=1, keepdims=True)
        weight = jnp.exp(scores - highest)
        totals = jnp.sum(weight, axis=1, keepdims=True)
        sums = jnp.dot(weight.astype(BF16), values, preferred_element_type=F32) / totals
        logs = jnp.where(prompt >= 0, highest + jnp.log(totals), NEGATIVE)
        parts = [cached_there[head], cached_here[head]]
        logs = [tail_pieces(part[ROWS:]) for part in parts] + [logs]
        sums = [part[:ROWS].astype(F32) for part in parts] + [sums]
        highest = functools.reduce(jnp.maximum, logs)
        shares = [jnp.exp(log - highest) for log in logs]
        total = functools.reduce(jnp.add, shares)
        joined = functools.reduce(jnp.add, [share * part for share, part in zip(shares, sums)])
        result = (joined / total).astype(BF16)
        for member in range(GROUP):
            begin = (head * GROUP + member) * HEAD_DIM
            out[0, :, begin : begin + HEAD_DIM] = result[member * STEPS : (member + 1) * STEPS]


def finish(targets, rotary, own, arrived, grouped, cached):
    width = CORE_HEADS * GROUP * HEAD_DIM
    return pl.pallas_call(
        final_kernel,
        in_specs=[SMEM] + [VMEM] * 9,
        out_specs=VMEM,
        out_shape=jax.ShapeDtypeStruct((1, STEPS, width), BF16),
        compiler_params=pltpu.CompilerParams(vmem_limit_bytes=16 * MIB),
        name="finish",
    )(targets, rotary, own, *arrived, grouped, *cached)


def rotary_turns():
    half = np.arange(HEAD_DIM // 2, dtype=np.float64) / (HEAD_DIM // 2)
    frequency = ROTARY_BASE ** (-np.concatenate([half, half]))
    angles = np.arange(STRETCH, dtype=np.float64)[:, None] * frequency
    return frequency.astype(np.float32), np.stack([np.cos(angles), np.sin(angles)]).astype(np.float32)


def per_device(
    stretch,
    norm_gain,
    kv_codes,
    scale_codes,
    outer_scales,
    prompt_lengths,
    target_rows,
    cache_lengths,
    kv_cache,
    queries,
    new_kv,
):
    count = lax.axis_size("tp")
    half = count // 2
    lines = stretch.transpose(1, 0, 2)
    gain = norm_gain.reshape(1, -1)
    ring = [ring_device(at, count) for at in range(count)]
    to_right = [(ring[at], ring[(at + 1) % count]) for at in range(count)]
    to_left = [(ring[at], ring[at - 1]) for at in range(count)]

    def pass_on(right, left):
        return lax.ppermute(right, "tp", to_right), lax.ppermute(left, "tp", to_left)

    swap = lambda array: lax.ppermute(array, "rep", [(0, 1), (1, 0)])
    other = swap(lines)
    weight, own, squares = dequantize(lines, kv_codes, scale_codes, outer_scales.T, gain)
    frequency, turns = rotary_turns()
    start = (prompt_lengths - STRETCH).astype(F32)[:, None] * jnp.asarray(frequency)
    starts = jnp.stack([jnp.cos(start), jnp.sin(start)])

    features = [own, squares, other, gain]
    right, left = project_first(half, target_rows, *features, weight)
    targets, _ = lax.optimization_barrier((target_rows, left))
    arrived = [pass_on(right, left), []]

    for distance in range(half - 1, 0, -1):
        distances = [distance, -distance] + ([0] if distance == 1 else [])
        terms = project(distances, targets, *features, weight)
        right, left = sends(1, terms, arrived[1])
        terms, right = lax.optimization_barrier((terms, right))
        if distance == 1:
            targets, _ = lax.optimization_barrier((target_rows, right))
        arrived[1] = pass_on(right, left)
        if distance == 1:
            grouped, rotary = prepare(targets, queries, starts, jnp.asarray(turns))
            cached = cache_attention(
                0, targets, prompt_lengths, cache_lengths, grouped, kv_cache, new_kv
            )
        right, left = sends(0, terms, arrived[0])
        if distance == 1:
            cached, right = lax.optimization_barrier((cached, right))
        targets, _ = lax.optimization_barrier((target_rows, right))
        arrived[0] = pass_on(right, left)

    cached = [swap(cached)]
    cached.append(
        cache_attention(1, targets, prompt_lengths, cache_lengths, grouped, kv_cache, new_kv)
    )
    out = finish(target_rows, rotary, terms, [*arrived[0], *arrived[1]], grouped, cached)
    return lax.all_gather(out, "rep", axis=2, tiled=True)


def solution(mesh):
    in_specs = (
        P(None, ("grp", "rep"), "tp"),
        P("tp"),
        P("tp", None),
        P("tp", None),
        P("tp", None),
        P("grp"),
        P("grp"),
        P(("grp", "tp")),
        P(("grp", "tp"), "rep", None),
        P(("grp", "tp"), None, None),
        P(("grp", "tp"), None, None),
    )
    out_specs = P(("grp", "tp"), None, None)
    return jax.shard_map(
        per_device, mesh=mesh, in_specs=in_specs, out_specs=out_specs, check_vma=False
    )
```

```python
import functools
import math

import jax
import jax.numpy as jnp
import numpy as np
from jax import lax
from jax.experimental import pallas as pl
from jax.experimental.pallas import tpu as pltpu
from jax.sharding import PartitionSpec as P

D = 16384
HEADS = 128
KV_HEADS = 8
HEAD_DIM = 128
STRETCH = 192
STEPS = 2
QBLOCK = 64
GROUP = HEADS // KV_HEADS
ROWS = GROUP * STEPS
TAIL = 16
PART = ROWS + TAIL
CORE_HEADS = KV_HEADS // 2
NORMAL_FLOAT_LEVELS = [
    -1.0,
    -0.6961928009986877,
    -0.5250730514526367,
    -0.39491748809814453,
    -0.28444138169288635,
    -0.18477343022823334,
    -0.09105003625154495,
    0.0,
    0.07958029955625534,
    0.16093020141124725,
    0.24611230194568634,
    0.33791524171829224,
    0.44070982933044434,
    0.5626170039176941,
    0.7229568362236023,
    1.0,
]
ROTARY_BASE = 500000.0
EPSILON = 1e-05
NEGATIVE = -1e30
BF16 = jnp.bfloat16
F32 = jnp.float32
MIB = 1024 * 1024
VMEM = pl.BlockSpec(memory_space=pltpu.VMEM)
SMEM = pl.BlockSpec(memory_space=pltpu.SMEM)


def in_hbm(*arrays):
    return [pltpu.with_memory_space_constraint(array, pltpu.HBM) for array in arrays]


def ring_device(place, count):
    half = count // 2
    if isinstance(place, int):
        return 2 * place if place < half else 2 * (count - 1 - place) + 1
    return jnp.where(place < half, 2 * place, 2 * (count - 1 - place) + 1)


def owner_at(distance):
    count = lax.axis_size("tp")
    here = lax.axis_index("tp")
    place = jnp.where(here % 2 == 0, here // 2, count - 1 - here // 2)
    return ring_device((place + distance + count) % count, count)


def turned(column):
    rows = lax.broadcasted_iota(jnp.int32, (column.shape[0], 128), 0)
    lanes = lax.broadcasted_iota(jnp.int32, (column.shape[0], 128), 1)
    return jnp.sum(jnp.where(rows == lanes, column, 0.0), axis=0, keepdims=True)


def stood(row, count):
    rows = lax.broadcasted_iota(jnp.int32, (count, 128), 0)
    lanes = lax.broadcasted_iota(jnp.int32, (count, 128), 1)
    return jnp.sum(jnp.where(rows == lanes, row, 0.0), axis=1, keepdims=True)


def token_rows(column):
    at = lax.broadcasted_iota(jnp.int32, (8, 128), 0)
    ends = turned(column[128:])
    return jnp.where(at == 0, turned(column[:128]), jnp.where(at == 1, ends, 0.0))


def token_column(rows):
    return jnp.concatenate([stood(rows[0:1], 128), stood(rows[1:2], STRETCH - 128)], axis=0)


def two_pieces(rows):
    high = rows.astype(BF16).astype(F32)
    return jnp.concatenate([high, rows - high], axis=0).astype(BF16)


def one_piece(rows):
    rows = rows.astype(F32)
    return rows[:8] + rows[8:]


def pieces_tail(logs):
    row = turned(logs)
    high = row.astype(BF16).astype(F32)
    middle = (row - high).astype(BF16).astype(F32)
    low = row - high - middle
    at = lax.broadcasted_iota(jnp.int32, (TAIL, 128), 0)
    tail = jnp.where(at == 0, high, jnp.where(at == 1, middle, jnp.where(at == 2, low, 0.0)))
    return tail.astype(BF16)


def tail_pieces(tail):
    tail = tail.astype(F32)
    return stood(tail[0:1, :] + tail[1:2, :] + tail[2:3, :], ROWS)


def block_leaves(scale):
    wide = jnp.broadcast_to(scale, (8, HEAD_DIM))
    leaves = [wide * jnp.float32(level) for level in NORMAL_FLOAT_LEVELS]
    return [jnp.concatenate([leaf, leaf], axis=0).astype(BF16) for leaf in leaves]


def selected(codes, leaves):
    codes = codes.astype(jnp.int16)
    masks = [(codes & (1 << bit)) != 0 for bit in range(4)]

    def node(bit, base):
        if bit < 0:
            return leaves[base]
        low = node(bit - 1, base)
        return jnp.where(masks[bit], node(bit - 1, base + (1 << bit)), low)

    return node(3, 0)


def block_scales(scales, outer, column):
    count = scales.shape[0]
    line = lax.broadcasted_iota(jnp.int32, outer.shape, 0)
    line = jnp.sum(jnp.where(line == column, outer, 0.0), axis=0, keepdims=True)
    rows = lax.broadcasted_iota(jnp.int32, (count, count), 0)
    lanes = lax.broadcasted_iota(jnp.int32, (count, count), 1)
    second = jnp.sum(jnp.where(rows == lanes, line, 0.0), axis=1, keepdims=True)
    return (scales.astype(F32) + 1.0) / 256.0 * second


def weights_kernel(
    x, codes, key_scales, value_scales, outer, gain,
    out, scaled, squares, key_codes, value_codes, lines, scales, arrivals,
):
    per_rep = x.shape[0]
    features, width = key_codes.shape
    depth = min(256, features)
    blocks = features // depth
    columns = outer.shape[0] // 2
    rep = lax.axis_index("rep")

    def code_copies(block):
        rows = pl.ds(block * depth, depth)
        return [
            pltpu.make_async_copy(
                codes.at[rows, pl.ds(pl.multiple_of((2 * kind + rep) * width, width), width)],
                buffer.at[rows],
                arrivals.at[2 * block + kind],
            )
            for kind, buffer in enumerate((key_codes, value_codes))
        ]

    def line_copy(prompt):
        return pltpu.make_async_copy(
            x.at[prompt], lines.at[prompt], arrivals.at[2 * blocks + prompt]
        )

    for block in range(blocks):
        if block == blocks // 2:
            for prompt in range(per_rep):
                line_copy(prompt).start()
        for copy in code_copies(block):
            copy.start()
    for at in range(CORE_HEADS):
        column = (rep * CORE_HEADS + at) // (KV_HEADS // columns)
        lanes = slice(at * HEAD_DIM, (at + 1) * HEAD_DIM)
        scales[2 * at] = block_scales(key_scales[:, lanes], outer[...], column)
        scales[2 * at + 1] = block_scales(value_scales[:, lanes], outer[...], columns + column)
    squares[...] = jnp.zeros(squares.shape, F32)

    def body(step, _):
        row = pl.ds(step, 1)
        for at in range(CORE_HEADS):
            lanes = slice(at * HEAD_DIM, (at + 1) * HEAD_DIM)
            for kind, buffer in enumerate((key_codes, value_codes)):
                leaves = block_leaves(scales[2 * at + kind, row, :])
                for tile in range(QBLOCK // 16):
                    rows = pl.ds(pl.multiple_of(step * QBLOCK + 16 * tile, 16), 16)
                    out[at, rows, kind * HEAD_DIM : (kind + 1) * HEAD_DIM] = selected(
                        buffer[rows, lanes], leaves
                    )
        return 0

    steps = depth // QBLOCK
    late = blocks - blocks // 2
    for block in range(blocks):
        for copy in code_copies(block):
            copy.wait()
        lax.fori_loop(block * steps, (block + 1) * steps, body, 0)
        if block == blocks // 2:
            for prompt in range(per_rep):
                line_copy(prompt).wait()
        for chunk in range(blocks):
            if blocks // 2 + chunk * late // blocks != block:
                continue
            lanes = slice(chunk * depth, (chunk + 1) * depth)
            for prompt in range(per_rep):
                wide = lines[prompt, :, lanes].astype(F32)
                scaled[prompt, :, lanes] = (wide * gain[:, lanes]).astype(BF16)
                squares[prompt] += token_rows(jnp.sum(wide * wide, axis=1, keepdims=True))


def dequantize(x, codes, scales, outer, gain):
    per_rep, _, features = x.shape
    width = CORE_HEADS * HEAD_DIM
    blocks = features // min(256, features)
    rep = lambda: lax.axis_index("rep")
    x, codes, scales, outer, gain = in_hbm(x, codes, scales, outer, gain)
    return pl.pallas_call(
        weights_kernel,
        grid=(1,),
        in_specs=[
            pl.BlockSpec(memory_space=pltpu.HBM),
            pl.BlockSpec(memory_space=pltpu.HBM),
            pl.BlockSpec((scales.shape[0], width), lambda k: (0, rep())),
            pl.BlockSpec((scales.shape[0], width), lambda k: (0, 2 + rep())),
            pl.BlockSpec(outer.shape, lambda k: (0, 0)),
            pl.BlockSpec(gain.shape, lambda k: (0, 0)),
        ],
        out_specs=[VMEM] * 3,
        out_shape=[
            jax.ShapeDtypeStruct((CORE_HEADS, features, 2 * HEAD_DIM), BF16),
            jax.ShapeDtypeStruct(x.shape, BF16),
            jax.ShapeDtypeStruct((per_rep, 8, 128), F32),
        ],
        scratch_shapes=[
            pltpu.VMEM((features, width), jnp.int32),
            pltpu.VMEM((features, width), jnp.int32),
            pltpu.VMEM(x.shape, BF16),
            pltpu.VMEM((2 * CORE_HEADS, scales.shape[0], HEAD_DIM), F32),
            pltpu.SemaphoreType.DMA((2 * blocks + per_rep,)),
        ],
        compiler_params=pltpu.CompilerParams(vmem_limit_bytes=36 * MIB),
        cost_estimate=pl.CostEstimate(
            flops=32 * codes.size, bytes_accessed=codes.size * 2, transcendentals=0
        ),
        name="dequantize",
    )(x, codes, scales, scales, outer, gain)


def prompt_of(targets, owner):
    prompt = jnp.int32(-1)
    for at in range(targets.shape[0]):
        prompt = jnp.where(targets[at] == owner, at, prompt)
    return prompt


def with_lines(targets, distance, own, squares, other, gain, line, total, some, none):
    per_rep = own.shape[0]
    prompt = prompt_of(targets, owner_at(distance))
    at = lax.rem(jnp.maximum(prompt, 0), per_rep)
    is_own = prompt // per_rep == lax.axis_index("rep")

    @pl.when((prompt >= 0) & is_own)
    def _():
        some(own.at[at], squares.at[at])

    @pl.when((prompt >= 0) & jnp.logical_not(is_own))
    def _():
        width = min(512, line.shape[1])
        total[...] = jnp.zeros(total.shape, F32)
        for begin in range(0, line.shape[1], width):
            lanes = slice(begin, begin + width)
            wide = other[at, :, lanes].astype(F32)
            line[:, lanes] = (wide * gain[:, lanes]).astype(BF16)
            total[...] += token_rows(jnp.sum(wide * wide, axis=1, keepdims=True))
        some(line, total)

    pl.when(prompt < 0)(none)


def line_scratch(x):
    return [pltpu.VMEM(x.shape[1:], BF16), pltpu.VMEM((8, 128), F32)]


def first_kernel(distance, targets, own, squares, other, gain, weight, right, left, line, total):
    def some(lines, sums):
        for head in range(CORE_HEADS):
            product = jnp.dot(lines[...], weight[head], preferred_element_type=F32)
            rows = slice(head * STRETCH, (head + 1) * STRETCH)
            right[rows] = product[:, :HEAD_DIM].astype(BF16)
            left[rows] = product[:, HEAD_DIM:].astype(BF16)
        right[CORE_HEADS * STRETCH :] = two_pieces(sums[...])

    def none():
        right[...] = jnp.zeros(right.shape, BF16)
        left[...] = jnp.zeros(left.shape, BF16)

    with_lines(targets, distance, own, squares, other, gain, line, total, some, none)


def project_first(distance, targets, own, squares, other, gain, weight):
    rows = CORE_HEADS * STRETCH
    return pl.pallas_call(
        functools.partial(first_kernel, distance),
        in_specs=[SMEM] + [VMEM] * 5,
        out_specs=[VMEM] * 2,
        out_shape=[
            jax.ShapeDtypeStruct((rows + TAIL, HEAD_DIM), BF16),
            jax.ShapeDtypeStruct((rows, HEAD_DIM), BF16),
        ],
        scratch_shapes=line_scratch(own),
        compiler_params=pltpu.CompilerParams(vmem_limit_bytes=24 * MIB),
        cost_estimate=pl.CostEstimate(
            flops=STRETCH * weight.size * 2, bytes_accessed=weight.size, transcendentals=0
        ),
        name="project_first",
    )(targets, own, squares, other, gain, weight)


def project_kernel(distances, targets, own, squares, other, gain, weight, out, line, total):
    for item, distance in enumerate(distances):

        def some(lines, sums, item=item):
            for head in range(CORE_HEADS):
                product = jnp.dot(lines[...], weight[head], preferred_element_type=F32)
                rows = slice(head * STRETCH, (head + 1) * STRETCH)
                out[item, 0, rows] = product[:, :HEAD_DIM]
                out[item, 1, rows] = product[:, HEAD_DIM:]
            out[item, 0, CORE_HEADS * STRETCH :] = sums[...]

        def none(item=item):
            out[item] = jnp.zeros(out.shape[1:], F32)

        with_lines(targets, distance, own, squares, other, gain, line, total, some, none)


def project(distances, targets, own, squares, other, gain, weight):
    return pl.pallas_call(
        functools.partial(project_kernel, distances),
        in_specs=[SMEM] + [VMEM] * 5,
        out_specs=VMEM,
        out_shape=jax.ShapeDtypeStruct((len(distances), 2, 4 * STRETCH + 8, HEAD_DIM), F32),
        scratch_shapes=line_scratch(own),
        compiler_params=pltpu.CompilerParams(vmem_limit_bytes=24 * MIB),
        cost_estimate=pl.CostEstimate(
            flops=len(distances) * STRETCH * weight.size,
            bytes_accessed=weight.size,
            transcendentals=0,
        ),
        name="project",
    )(targets, own, squares, other, gain, weight)


def send_kernel(half, terms, *refs):
    *arrived, to_right, to_left = refs
    rows = CORE_HEADS * STRETCH
    for item, out in enumerate((to_right, to_left)):
        kind = (half + item) % 2
        total = terms[item, kind, :rows]
        if arrived:
            total += arrived[item][:rows].astype(F32)
        out[:rows] = total.astype(BF16)
        if kind == 0:
            squares = terms[item, 0, rows:]
            if arrived:
                squares += one_piece(arrived[item][rows : rows + TAIL])
            out[rows : rows + TAIL] = two_pieces(squares)
        spare = rows + (TAIL if kind == 0 else 0)
        if spare < out.shape[0]:
            out[spare:] = jnp.zeros((out.shape[0] - spare, HEAD_DIM), BF16)


def sends(half, terms, arrived):
    rows = CORE_HEADS * STRETCH
    shapes = [jax.ShapeDtypeStruct((rows + TAIL, HEAD_DIM), BF16)] * 2
    return pl.pallas_call(
        functools.partial(send_kernel, half),
        in_specs=[VMEM] * (1 + len(arrived)),
        out_specs=[VMEM] * 2,
        out_shape=shapes,
        compiler_params=pltpu.CompilerParams(vmem_limit_bytes=16 * MIB),
        name="sends",
    )(terms, *arrived)


def prepare_kernel(targets, queries, starts, turns, grouped, rotary):
    for head in range(KV_HEADS):
        for member in range(GROUP):
            begin = (head * GROUP + member) * HEAD_DIM
            rows = slice(member * STEPS, (member + 1) * STEPS)
            grouped[head, rows] = queries[0, :, begin : begin + HEAD_DIM]
    row = pl.ds(jnp.maximum(prompt_of(targets, lax.axis_index("tp")), 0), 1)
    cosine, sine = starts[0, row, :], starts[1, row, :]
    lane = lax.broadcasted_iota(jnp.int32, turns.shape[1:], 1)
    rotary[0] = turns[0] * cosine - turns[1] * sine
    sine = turns[1] * cosine + turns[0] * sine
    rotary[1] = jnp.where(lane < HEAD_DIM // 2, -sine, sine)


def prepare(targets, queries, starts, turns):
    return pl.pallas_call(
        prepare_kernel,
        in_specs=[SMEM] + [VMEM] * 3,
        out_specs=[VMEM] * 2,
        out_shape=[
            jax.ShapeDtypeStruct((KV_HEADS, ROWS, HEAD_DIM), BF16),
            jax.ShapeDtypeStruct(turns.shape, F32),
        ],
        compiler_params=pltpu.CompilerParams(vmem_limit_bytes=16 * MIB),
        name="prepare",
    )(targets, queries, starts, turns)


def cache_kernel(part, targets, lengths, stored, q, cache, new, out):
    scaling = HEAD_DIM ** (-0.5)
    dims = (((1,), (1,)), ((), ()))
    here = lax.axis_index("tp")
    rep = lax.axis_index("rep")
    length = cache.shape[1]
    prompt = prompt_of(targets, here)
    handed = lengths[jnp.maximum(prompt, 0)] - STRETCH
    span = jnp.where(prompt >= 0, handed, stored[0]) - rep * length
    count = CORE_HEADS * ROWS
    allowed = lax.broadcasted_iota(jnp.int32, (count, length), 1) < span
    second_step = lax.broadcasted_iota(jnp.int32, (count, 1), 0) % STEPS == 1
    scores, fresh, key_lanes, value_lanes = [], [[], []], [], []
    for at in range(CORE_HEADS):
        head = (rep if part == 1 else 1 - rep) * CORE_HEADS + at
        key_lanes.append(pl.ds(pl.multiple_of(head * HEAD_DIM, HEAD_DIM), HEAD_DIM))
        begin = pl.multiple_of((KV_HEADS + head) * HEAD_DIM, HEAD_DIM)
        value_lanes.append(pl.ds(begin, HEAD_DIM))
        query = q[head]
        wide = query.astype(F32)
        keys = cache[0, :, key_lanes[at]]
        scores.append(lax.dot_general(query, keys, dims, preferred_element_type=F32))
        for step in range(STEPS):
            key = new[0, step : step + 1, key_lanes[at]].astype(F32)
            fresh[step].append(jnp.sum(wide * key, axis=1, keepdims=True))
    scores = jnp.where(allowed, jnp.concatenate(scores, axis=0) * scaling, NEGATIVE)
    highest = jnp.max(scores, axis=1, keepdims=True)
    for step in range(STEPS):
        shown = rep == 0 if step == 0 else second_step & (rep == 0)
        fresh[step] = jnp.where(shown, jnp.concatenate(fresh[step], axis=0) * scaling, NEGATIVE)
        highest = jnp.maximum(highest, fresh[step])
    some = highest > 0.5 * NEGATIVE
    highest = jnp.where(some, highest, 0.0)
    weight = jnp.exp(scores - highest)
    shares = [jnp.exp(score - highest) for score in fresh]
    totals = jnp.sum(weight, axis=1, keepdims=True) + shares[0] + shares[1]
    totals = jnp.where(some, totals, 1.0)
    logs = jnp.where(some, highest + jnp.log(totals), NEGATIVE)
    weight = weight.astype(BF16)
    for at in range(CORE_HEADS):
        rows = slice(at * ROWS, (at + 1) * ROWS)
        values = cache[0, :, value_lanes[at]]
        sums = jnp.dot(weight[rows], values, preferred_element_type=F32)
        for step in range(STEPS):
            value = new[0, step : step + 1, value_lanes[at]].astype(F32)
            sums += shares[step][rows].astype(BF16).astype(F32) * value
        out[at, :ROWS] = (sums / totals[rows]).astype(BF16)
        out[at, ROWS:] = pieces_tail(logs[rows])


def cache_attention(part, targets, lengths, stored, grouped, kv_cache, new_kv):
    return pl.pallas_call(
        functools.partial(cache_kernel, part),
        in_specs=[SMEM] * 3 + [VMEM] * 3,
        out_specs=VMEM,
        out_shape=jax.ShapeDtypeStruct((CORE_HEADS, PART, HEAD_DIM), BF16),
        compiler_params=pltpu.CompilerParams(vmem_limit_bytes=16 * MIB),
        cost_estimate=pl.CostEstimate(
            flops=1, bytes_accessed=1, transcendentals=0
        ),
        name="cache_attention",
    )(targets, lengths, stored, grouped, kv_cache, new_kv)


def final_kernel(
    targets, rotary, own, right_keys, left_values, right_values, left_keys, grouped,
    cached_there, cached_here, out,
):
    scaling = HEAD_DIM ** (-0.5)
    dims = (((1,), (1,)), ((), ()))
    mine = own.shape[0] - 1
    first = lax.axis_index("rep") * CORE_HEADS
    prompt = prompt_of(targets, lax.axis_index("tp"))
    cosine, sine = rotary[0], rotary[1]
    rows = CORE_HEADS * STRETCH
    squares = own[mine, 0, rows:] + one_piece(right_keys[rows : rows + TAIL]) + one_piece(left_keys[rows : rows + TAIL])
    scale = token_column(lax.rsqrt(squares / D + EPSILON))
    scores, handed = [], []
    for head in range(CORE_HEADS):
        at = slice(head * STRETCH, (head + 1) * STRETCH)
        keys = own[mine, 0, at] + right_keys[at].astype(F32) + left_keys[at].astype(F32)
        values = own[mine, 1, at] + right_values[at].astype(F32) + left_values[at].astype(F32)
        keys = (keys * scale).astype(BF16).astype(F32)
        handed.append((values * scale).astype(BF16))
        keys = keys * cosine + pltpu.roll(keys, HEAD_DIM // 2, 1) * sine
        scores.append(
            lax.dot_general(
                grouped[first + head], keys.astype(BF16), dims, preferred_element_type=F32
            )
        )
    scores = jnp.concatenate(scores, axis=0) * scaling
    highest = jnp.max(scores, axis=1, keepdims=True)
    weight = jnp.exp(scores - highest)
    totals = jnp.sum(weight, axis=1, keepdims=True)
    weight = weight.astype(BF16)
    sums = [
        jnp.dot(weight[head * ROWS : (head + 1) * ROWS], handed[head], preferred_element_type=F32)
        for head in range(CORE_HEADS)
    ]
    sums = [jnp.concatenate(sums, axis=0) / totals]
    logs = [jnp.where(prompt >= 0, highest + jnp.log(totals), NEGATIVE)]
    for cached in (cached_there, cached_here):
        parts = [cached[head] for head in range(CORE_HEADS)]
        sums.append(jnp.concatenate([part[:ROWS].astype(F32) for part in parts], axis=0))
        logs.append(jnp.concatenate([tail_pieces(part[ROWS:]) for part in parts], axis=0))
    highest = functools.reduce(jnp.maximum, logs)
    shares = [jnp.exp(log - highest) for log in logs]
    total = functools.reduce(jnp.add, shares)
    joined = functools.reduce(jnp.add, [share * part for share, part in zip(shares, sums)])
    result = (joined / total).astype(BF16)
    for member in range(CORE_HEADS * GROUP):
        lanes = slice(member * HEAD_DIM, (member + 1) * HEAD_DIM)
        out[0, :, lanes] = result[member * STEPS : (member + 1) * STEPS]


def finish(targets, rotary, own, arrived, grouped, cached):
    width = CORE_HEADS * GROUP * HEAD_DIM
    return pl.pallas_call(
        final_kernel,
        in_specs=[SMEM] + [VMEM] * 9,
        out_specs=VMEM,
        out_shape=jax.ShapeDtypeStruct((1, STEPS, width), BF16),
        compiler_params=pltpu.CompilerParams(vmem_limit_bytes=16 * MIB),
        name="finish",
    )(targets, rotary, own, *arrived, grouped, *cached)


def rotary_turns():
    half = np.arange(HEAD_DIM // 2, dtype=np.float64) / (HEAD_DIM // 2)
    frequency = ROTARY_BASE ** (-np.concatenate([half, half]))
    angles = np.arange(STRETCH, dtype=np.float64)[:, None] * frequency
    return frequency.astype(np.float32), np.stack([np.cos(angles), np.sin(angles)]).astype(np.float32)


def per_device(
    stretch,
    norm_gain,
    kv_codes,
    scale_codes,
    outer_scales,
    prompt_lengths,
    target_rows,
    cache_lengths,
    kv_cache,
    queries,
    new_kv,
):
    count = lax.axis_size("tp")
    half = count // 2
    lines = stretch.transpose(1, 0, 2)
    gain = norm_gain.reshape(1, -1)
    ring = [ring_device(at, count) for at in range(count)]
    to_right = [(ring[at], ring[(at + 1) % count]) for at in range(count)]
    to_left = [(ring[at], ring[at - 1]) for at in range(count)]

    def pass_on(right, left):
        return lax.ppermute(right, "tp", to_right), lax.ppermute(left, "tp", to_left)

    swap = lambda array: lax.ppermute(array, "rep", [(0, 1), (1, 0)])
    other = swap(lines)
    weight, own, squares = dequantize(lines, kv_codes, scale_codes, outer_scales.T, gain)
    frequency, turns = rotary_turns()
    start = (prompt_lengths - STRETCH).astype(F32)[:, None] * jnp.asarray(frequency)
    starts = jnp.stack([jnp.cos(start), jnp.sin(start)])

    features = [own, squares, other, gain]
    right, left = project_first(half, target_rows, *features, weight)
    targets, _ = lax.optimization_barrier((target_rows, left))
    arrived = [pass_on(right, left), []]

    for distance in range(half - 1, 0, -1):
        terms = project([distance, -distance], targets, *features, weight)
        right, left = sends(1, terms, arrived[1])
        terms, right, left = lax.optimization_barrier((terms, right, left))
        targets, _ = lax.optimization_barrier((target_rows, left))
        arrived[1] = pass_on(right, left)
        if distance == half - 1:
            prepared = prepare(targets, queries, starts, jnp.asarray(turns))
            terms, prepared = lax.optimization_barrier((terms, prepared))
            grouped, rotary = prepared
        if distance == max(1, half - 2):
            cached = cache_attention(
                0, targets, prompt_lengths, cache_lengths, grouped, kv_cache, new_kv
            )
            terms, cached = lax.optimization_barrier((terms, cached))
        right, left = sends(0, terms, arrived[0])
        targets, right = lax.optimization_barrier((target_rows, right))
        arrived[0] = pass_on(right, left)

    cached, _ = lax.optimization_barrier((cached, right))
    cached = [swap(cached)]
    terms = project([0], targets, *features, weight)
    cached.append(
        cache_attention(1, targets, prompt_lengths, cache_lengths, grouped, kv_cache, new_kv)
    )
    out = finish(target_rows, rotary, terms, [*arrived[0], *arrived[1]], grouped, cached)
    return lax.all_gather(out, "rep", axis=2, tiled=True)


def solution(mesh):
    in_specs = (
        P(None, ("grp", "rep"), "tp"),
        P("tp"),
        P("tp", None),
        P("tp", None),
        P("tp", None),
        P("grp"),
        P("grp"),
        P(("grp", "tp")),
        P(("grp", "tp"), "rep", None),
        P(("grp", "tp"), None, None),
        P(("grp", "tp"), None, None),
    )
    out_specs = P(("grp", "tp"), None, None)
    return jax.shard_map(
        per_device, mesh=mesh, in_specs=in_specs, out_specs=out_specs, check_vma=False
    )
```

```python
import functools
import math

import jax
import jax.numpy as jnp
import numpy as np
from jax import lax
from jax.experimental import pallas as pl
from jax.experimental.pallas import tpu as pltpu
from jax.sharding import PartitionSpec as P

D = 16384
HEADS = 128
KV_HEADS = 8
HEAD_DIM = 128
STRETCH = 192
STEPS = 2
QBLOCK = 64
GROUP = HEADS // KV_HEADS
ROWS = GROUP * STEPS
TAIL = 16
PART = ROWS + TAIL
CORE_HEADS = KV_HEADS // 2
NORMAL_FLOAT_LEVELS = [
    -1.0,
    -0.6961928009986877,
    -0.5250730514526367,
    -0.39491748809814453,
    -0.28444138169288635,
    -0.18477343022823334,
    -0.09105003625154495,
    0.0,
    0.07958029955625534,
    0.16093020141124725,
    0.24611230194568634,
    0.33791524171829224,
    0.44070982933044434,
    0.5626170039176941,
    0.7229568362236023,
    1.0,
]
ROTARY_BASE = 500000.0
EPSILON = 1e-05
NEGATIVE = -1e30
BF16 = jnp.bfloat16
F32 = jnp.float32
MIB = 1024 * 1024
VMEM = pl.BlockSpec(memory_space=pltpu.VMEM)
SMEM = pl.BlockSpec(memory_space=pltpu.SMEM)


def in_hbm(*arrays):
    return [pltpu.with_memory_space_constraint(array, pltpu.HBM) for array in arrays]


def ring_device(place, count):
    half = count // 2
    if isinstance(place, int):
        return 2 * place if place < half else 2 * (count - 1 - place) + 1
    return jnp.where(place < half, 2 * place, 2 * (count - 1 - place) + 1)


def owner_at(distance):
    count = lax.axis_size("tp")
    here = lax.axis_index("tp")
    place = jnp.where(here % 2 == 0, here // 2, count - 1 - here // 2)
    return ring_device((place + distance + count) % count, count)


def turned(column):
    rows = lax.broadcasted_iota(jnp.int32, (column.shape[0], 128), 0)
    lanes = lax.broadcasted_iota(jnp.int32, (column.shape[0], 128), 1)
    return jnp.sum(jnp.where(rows == lanes, column, 0.0), axis=0, keepdims=True)


def stood(row, count):
    rows = lax.broadcasted_iota(jnp.int32, (count, 128), 0)
    lanes = lax.broadcasted_iota(jnp.int32, (count, 128), 1)
    return jnp.sum(jnp.where(rows == lanes, row, 0.0), axis=1, keepdims=True)


def token_rows(column):
    at = lax.broadcasted_iota(jnp.int32, (8, 128), 0)
    ends = turned(column[128:])
    return jnp.where(at == 0, turned(column[:128]), jnp.where(at == 1, ends, 0.0))


def token_column(rows):
    return jnp.concatenate([stood(rows[0:1], 128), stood(rows[1:2], STRETCH - 128)], axis=0)


def two_pieces(rows):
    high = rows.astype(BF16).astype(F32)
    return jnp.concatenate([high, rows - high], axis=0).astype(BF16)


def one_piece(rows):
    rows = rows.astype(F32)
    return rows[:8] + rows[8:]


def pieces_tail(logs):
    row = turned(logs)
    high = row.astype(BF16).astype(F32)
    middle = (row - high).astype(BF16).astype(F32)
    low = row - high - middle
    at = lax.broadcasted_iota(jnp.int32, (TAIL, 128), 0)
    tail = jnp.where(at == 0, high, jnp.where(at == 1, middle, jnp.where(at == 2, low, 0.0)))
    return tail.astype(BF16)


def tail_pieces(tail):
    tail = tail.astype(F32)
    return stood(tail[0:1, :] + tail[1:2, :] + tail[2:3, :], ROWS)


CODE_ROWS = 128


def block_leaves(scale):
    wide = jnp.broadcast_to(scale, (8, HEAD_DIM))
    leaves = [wide * jnp.float32(level) for level in NORMAL_FLOAT_LEVELS]
    return [jnp.concatenate([leaf, leaf], axis=0).astype(BF16) for leaf in leaves]


def selected(codes, leaves):
    codes = codes.astype(jnp.int16)
    masks = [(codes & (1 << bit)) != 0 for bit in range(4)]

    def node(bit, base):
        if bit < 0:
            return leaves[base]
        low = node(bit - 1, base)
        return jnp.where(masks[bit], node(bit - 1, base + (1 << bit)), low)

    return node(3, 0)


def block_scales(scales, outer, column):
    count = scales.shape[0]
    line = lax.broadcasted_iota(jnp.int32, outer.shape, 0)
    line = jnp.sum(jnp.where(line == column, outer, 0.0), axis=0, keepdims=True)
    rows = lax.broadcasted_iota(jnp.int32, (count, count), 0)
    lanes = lax.broadcasted_iota(jnp.int32, (count, count), 1)
    second = jnp.sum(jnp.where(rows == lanes, line, 0.0), axis=1, keepdims=True)
    return (scales.astype(F32) + 1.0) / 256.0 * second


def weights_kernel(
    codes, key_scales, value_scales, outer, out, key_codes, value_codes, scales, arrivals
):
    features, width = key_codes.shape
    depth = min(CODE_ROWS, features)
    blocks = features // depth
    columns = outer.shape[0] // 2
    rep = lax.axis_index("rep")

    def code_copies(block):
        rows = pl.ds(block * depth, depth)
        return [
            pltpu.make_async_copy(
                codes.at[rows, pl.ds(pl.multiple_of((2 * kind + rep) * width, width), width)],
                buffer.at[rows],
                arrivals.at[2 * block + kind],
            )
            for kind, buffer in enumerate((key_codes, value_codes))
        ]

    for block in range(blocks):
        for copy in code_copies(block):
            copy.start()
    for at in range(CORE_HEADS):
        column = (rep * CORE_HEADS + at) // (KV_HEADS // columns)
        lanes = slice(at * HEAD_DIM, (at + 1) * HEAD_DIM)
        scales[2 * at] = block_scales(key_scales[:, lanes], outer[...], column)
        scales[2 * at + 1] = block_scales(value_scales[:, lanes], outer[...], columns + column)

    def body(step, _):
        row = pl.ds(step, 1)
        for at in range(CORE_HEADS):
            lanes = slice(at * HEAD_DIM, (at + 1) * HEAD_DIM)
            for kind, buffer in enumerate((key_codes, value_codes)):
                leaves = block_leaves(scales[2 * at + kind, row, :])
                for tile in range(QBLOCK // 16):
                    rows = pl.ds(pl.multiple_of(step * QBLOCK + 16 * tile, 16), 16)
                    out[at, rows, kind * HEAD_DIM : (kind + 1) * HEAD_DIM] = selected(
                        buffer[rows, lanes], leaves
                    )
        return 0

    steps = depth // QBLOCK
    for block in range(blocks):
        for copy in code_copies(block):
            copy.wait()
        lax.fori_loop(block * steps, (block + 1) * steps, body, 0)


def dequantize(codes, scales, outer):
    features = codes.shape[0]
    width = CORE_HEADS * HEAD_DIM
    blocks = features // min(CODE_ROWS, features)
    rep = lambda: lax.axis_index("rep")
    codes, scales, outer = in_hbm(codes, scales, outer)
    return pl.pallas_call(
        weights_kernel,
        grid=(1,),
        in_specs=[
            pl.BlockSpec(memory_space=pltpu.HBM),
            pl.BlockSpec((scales.shape[0], width), lambda k: (0, rep())),
            pl.BlockSpec((scales.shape[0], width), lambda k: (0, 2 + rep())),
            pl.BlockSpec(outer.shape, lambda k: (0, 0)),
        ],
        out_specs=VMEM,
        out_shape=jax.ShapeDtypeStruct((CORE_HEADS, features, 2 * HEAD_DIM), BF16),
        scratch_shapes=[
            pltpu.VMEM((features, width), jnp.int32),
            pltpu.VMEM((features, width), jnp.int32),
            pltpu.VMEM((2 * CORE_HEADS, scales.shape[0], HEAD_DIM), F32),
            pltpu.SemaphoreType.DMA((2 * blocks,)),
        ],
        compiler_params=pltpu.CompilerParams(vmem_limit_bytes=32 * MIB),
        cost_estimate=pl.CostEstimate(
            flops=32 * codes.size, bytes_accessed=codes.size * 2, transcendentals=0
        ),
        name="dequantize",
    )(codes, scales, scales, outer)


def prompt_of(targets, owner):
    prompt = jnp.int32(-1)
    for at in range(targets.shape[0]):
        prompt = jnp.where(targets[at] == owner, at, prompt)
    return prompt


def with_lines(targets, distance, own, other, gain, line, total, some, none):
    per_rep = own.shape[0]
    prompt = prompt_of(targets, owner_at(distance))
    at = lax.rem(jnp.maximum(prompt, 0), per_rep)
    is_own = prompt // per_rep == lax.axis_index("rep")
    width = min(512, line.shape[1])

    def scale(x):
        total[...] = jnp.zeros(total.shape, F32)
        for begin in range(0, line.shape[1], width):
            lanes = slice(begin, begin + width)
            wide = x[at, :, lanes].astype(F32)
            line[:, lanes] = (wide * gain[:, lanes]).astype(BF16)
            total[...] += token_rows(jnp.sum(wide * wide, axis=1, keepdims=True))

    pl.when((prompt >= 0) & is_own)(lambda: scale(own))
    pl.when((prompt >= 0) & jnp.logical_not(is_own))(lambda: scale(other))
    pl.when(prompt >= 0)(some)
    pl.when(prompt < 0)(none)


def line_scratch(x):
    return [pltpu.VMEM(x.shape[1:], BF16), pltpu.VMEM((8, 128), F32)]


def first_kernel(distance, targets, own, other, gain, weight, right, left, line, total):
    def some():
        for head in range(CORE_HEADS):
            product = jnp.dot(line[...], weight[head], preferred_element_type=F32)
            rows = slice(head * STRETCH, (head + 1) * STRETCH)
            right[rows] = product[:, :HEAD_DIM].astype(BF16)
            left[rows] = product[:, HEAD_DIM:].astype(BF16)
        right[CORE_HEADS * STRETCH :] = two_pieces(total[...])

    def none():
        right[...] = jnp.zeros(right.shape, BF16)
        left[...] = jnp.zeros(left.shape, BF16)

    with_lines(targets, distance, own, other, gain, line, total, some, none)


def project_first(distance, targets, own, other, gain, weight):
    rows = CORE_HEADS * STRETCH
    return pl.pallas_call(
        functools.partial(first_kernel, distance),
        in_specs=[SMEM] + [VMEM] * 4,
        out_specs=[VMEM] * 2,
        out_shape=[
            jax.ShapeDtypeStruct((rows + TAIL, HEAD_DIM), BF16),
            jax.ShapeDtypeStruct((rows, HEAD_DIM), BF16),
        ],
        scratch_shapes=line_scratch(own),
        compiler_params=pltpu.CompilerParams(vmem_limit_bytes=24 * MIB),
        cost_estimate=pl.CostEstimate(
            flops=STRETCH * weight.size * 2, bytes_accessed=weight.size, transcendentals=0
        ),
        name="project_first",
    )(targets, own, other, gain, weight)


def project_kernel(distances, targets, own, other, gain, weight, out, line, total):
    for item, distance in enumerate(distances):

        def some(item=item):
            for head in range(CORE_HEADS):
                product = jnp.dot(line[...], weight[head], preferred_element_type=F32)
                rows = slice(head * STRETCH, (head + 1) * STRETCH)
                out[item, 0, rows] = product[:, :HEAD_DIM]
                out[item, 1, rows] = product[:, HEAD_DIM:]
            out[item, 0, CORE_HEADS * STRETCH :] = total[...]

        def none(item=item):
            out[item] = jnp.zeros(out.shape[1:], F32)

        with_lines(targets, distance, own, other, gain, line, total, some, none)


def project(distances, targets, own, other, gain, weight):
    return pl.pallas_call(
        functools.partial(project_kernel, distances),
        in_specs=[SMEM] + [VMEM] * 4,
        out_specs=VMEM,
        out_shape=jax.ShapeDtypeStruct((len(distances), 2, 4 * STRETCH + 8, HEAD_DIM), F32),
        scratch_shapes=line_scratch(own),
        compiler_params=pltpu.CompilerParams(vmem_limit_bytes=24 * MIB),
        cost_estimate=pl.CostEstimate(
            flops=len(distances) * STRETCH * weight.size,
            bytes_accessed=weight.size,
            transcendentals=0,
        ),
        name="project",
    )(targets, own, other, gain, weight)


def send_kernel(half, terms, *refs):
    *arrived, to_right, to_left = refs
    rows = CORE_HEADS * STRETCH
    for item, out in enumerate((to_right, to_left)):
        kind = (half + item) % 2
        total = terms[item, kind, :rows]
        if arrived:
            total += arrived[item][:rows].astype(F32)
        out[:rows] = total.astype(BF16)
        if kind == 0:
            squares = terms[item, 0, rows:]
            if arrived:
                squares += one_piece(arrived[item][rows : rows + TAIL])
            out[rows : rows + TAIL] = two_pieces(squares)
        spare = rows + (TAIL if kind == 0 else 0)
        if spare < out.shape[0]:
            out[spare:] = jnp.zeros((out.shape[0] - spare, HEAD_DIM), BF16)


def sends(half, terms, arrived):
    rows = CORE_HEADS * STRETCH
    shapes = [jax.ShapeDtypeStruct((rows + TAIL, HEAD_DIM), BF16)] * 2
    return pl.pallas_call(
        functools.partial(send_kernel, half),
        in_specs=[VMEM] * (1 + len(arrived)),
        out_specs=[VMEM] * 2,
        out_shape=shapes,
        compiler_params=pltpu.CompilerParams(vmem_limit_bytes=16 * MIB),
        name="sends",
    )(terms, *arrived)


def prepare_kernel(targets, queries, starts, turns, grouped, rotary):
    for head in range(KV_HEADS):
        for member in range(GROUP):
            begin = (head * GROUP + member) * HEAD_DIM
            rows = slice(member * STEPS, (member + 1) * STEPS)
            grouped[head, rows] = queries[0, :, begin : begin + HEAD_DIM]
    row = pl.ds(jnp.maximum(prompt_of(targets, lax.axis_index("tp")), 0), 1)
    cosine, sine = starts[0, row, :], starts[1, row, :]
    lane = lax.broadcasted_iota(jnp.int32, turns.shape[1:], 1)
    rotary[0] = turns[0] * cosine - turns[1] * sine
    sine = turns[1] * cosine + turns[0] * sine
    rotary[1] = jnp.where(lane < HEAD_DIM // 2, -sine, sine)


def prepare(targets, queries, starts, turns):
    return pl.pallas_call(
        prepare_kernel,
        in_specs=[SMEM] + [VMEM] * 3,
        out_specs=[VMEM] * 2,
        out_shape=[
            jax.ShapeDtypeStruct((KV_HEADS, ROWS, HEAD_DIM), BF16),
            jax.ShapeDtypeStruct(turns.shape, F32),
        ],
        compiler_params=pltpu.CompilerParams(vmem_limit_bytes=16 * MIB),
        name="prepare",
    )(targets, queries, starts, turns)


def cache_kernel(part, targets, lengths, stored, q, cache, new, out):
    scaling = HEAD_DIM ** (-0.5)
    dims = (((1,), (1,)), ((), ()))
    here = lax.axis_index("tp")
    rep = lax.axis_index("rep")
    length = cache.shape[1]
    prompt = prompt_of(targets, here)
    handed = lengths[jnp.maximum(prompt, 0)] - STRETCH
    span = jnp.where(prompt >= 0, handed, stored[0]) - rep * length
    count = CORE_HEADS * ROWS
    allowed = lax.broadcasted_iota(jnp.int32, (count, length), 1) < span
    second_step = lax.broadcasted_iota(jnp.int32, (count, 1), 0) % STEPS == 1
    scores, fresh, key_lanes, value_lanes = [], [[], []], [], []
    for at in range(CORE_HEADS):
        head = (rep if part == 1 else 1 - rep) * CORE_HEADS + at
        key_lanes.append(pl.ds(pl.multiple_of(head * HEAD_DIM, HEAD_DIM), HEAD_DIM))
        begin = pl.multiple_of((KV_HEADS + head) * HEAD_DIM, HEAD_DIM)
        value_lanes.append(pl.ds(begin, HEAD_DIM))
        query = q[head]
        wide = query.astype(F32)
        keys = cache[0, :, key_lanes[at]]
        scores.append(lax.dot_general(query, keys, dims, preferred_element_type=F32))
        for step in range(STEPS):
            key = new[0, step : step + 1, key_lanes[at]].astype(F32)
            fresh[step].append(jnp.sum(wide * key, axis=1, keepdims=True))
    scores = jnp.where(allowed, jnp.concatenate(scores, axis=0) * scaling, NEGATIVE)
    highest = jnp.max(scores, axis=1, keepdims=True)
    for step in range(STEPS):
        shown = rep == 0 if step == 0 else second_step & (rep == 0)
        fresh[step] = jnp.where(shown, jnp.concatenate(fresh[step], axis=0) * scaling, NEGATIVE)
        highest = jnp.maximum(highest, fresh[step])
    some = highest > 0.5 * NEGATIVE
    highest = jnp.where(some, highest, 0.0)
    weight = jnp.exp(scores - highest)
    shares = [jnp.exp(score - highest) for score in fresh]
    totals = jnp.sum(weight, axis=1, keepdims=True) + shares[0] + shares[1]
    totals = jnp.where(some, totals, 1.0)
    logs = jnp.where(some, highest + jnp.log(totals), NEGATIVE)
    weight = weight.astype(BF16)
    for at in range(CORE_HEADS):
        rows = slice(at * ROWS, (at + 1) * ROWS)
        values = cache[0, :, value_lanes[at]]
        sums = jnp.dot(weight[rows], values, preferred_element_type=F32)
        for step in range(STEPS):
            value = new[0, step : step + 1, value_lanes[at]].astype(F32)
            sums += shares[step][rows].astype(BF16).astype(F32) * value
        out[at, :ROWS] = (sums / totals[rows]).astype(BF16)
        out[at, ROWS:] = pieces_tail(logs[rows])


def cache_attention(part, targets, lengths, stored, grouped, kv_cache, new_kv):
    return pl.pallas_call(
        functools.partial(cache_kernel, part),
        in_specs=[SMEM] * 3 + [VMEM] * 3,
        out_specs=VMEM,
        out_shape=jax.ShapeDtypeStruct((CORE_HEADS, PART, HEAD_DIM), BF16),
        compiler_params=pltpu.CompilerParams(vmem_limit_bytes=16 * MIB),
        cost_estimate=pl.CostEstimate(
            flops=1, bytes_accessed=1, transcendentals=0
        ),
        name="cache_attention",
    )(targets, lengths, stored, grouped, kv_cache, new_kv)


def final_kernel(
    targets, rotary, own, right_keys, left_values, right_values, left_keys, grouped,
    cached_there, cached_here, out,
):
    scaling = HEAD_DIM ** (-0.5)
    dims = (((1,), (1,)), ((), ()))
    mine = own.shape[0] - 1
    first = lax.axis_index("rep") * CORE_HEADS
    prompt = prompt_of(targets, lax.axis_index("tp"))
    cosine, sine = rotary[0], rotary[1]
    rows = CORE_HEADS * STRETCH
    squares = own[mine, 0, rows:] + one_piece(right_keys[rows : rows + TAIL]) + one_piece(left_keys[rows : rows + TAIL])
    scale = token_column(lax.rsqrt(squares / D + EPSILON))
    scores, handed = [], []
    for head in range(CORE_HEADS):
        at = slice(head * STRETCH, (head + 1) * STRETCH)
        keys = own[mine, 0, at] + right_keys[at].astype(F32) + left_keys[at].astype(F32)
        values = own[mine, 1, at] + right_values[at].astype(F32) + left_values[at].astype(F32)
        keys = (keys * scale).astype(BF16).astype(F32)
        handed.append((values * scale).astype(BF16))
        keys = keys * cosine + pltpu.roll(keys, HEAD_DIM // 2, 1) * sine
        scores.append(
            lax.dot_general(
                grouped[first + head], keys.astype(BF16), dims, preferred_element_type=F32
            )
        )
    scores = jnp.concatenate(scores, axis=0) * scaling
    highest = jnp.max(scores, axis=1, keepdims=True)
    weight = jnp.exp(scores - highest)
    totals = jnp.sum(weight, axis=1, keepdims=True)
    weight = weight.astype(BF16)
    sums = [
        jnp.dot(weight[head * ROWS : (head + 1) * ROWS], handed[head], preferred_element_type=F32)
        for head in range(CORE_HEADS)
    ]
    sums = [jnp.concatenate(sums, axis=0) / totals]
    logs = [jnp.where(prompt >= 0, highest + jnp.log(totals), NEGATIVE)]
    for cached in (cached_there, cached_here):
        parts = [cached[head] for head in range(CORE_HEADS)]
        sums.append(jnp.concatenate([part[:ROWS].astype(F32) for part in parts], axis=0))
        logs.append(jnp.concatenate([tail_pieces(part[ROWS:]) for part in parts], axis=0))
    highest = functools.reduce(jnp.maximum, logs)
    shares = [jnp.exp(log - highest) for log in logs]
    total = functools.reduce(jnp.add, shares)
    joined = functools.reduce(jnp.add, [share * part for share, part in zip(shares, sums)])
    result = (joined / total).astype(BF16)
    for member in range(CORE_HEADS * GROUP):
        lanes = slice(member * HEAD_DIM, (member + 1) * HEAD_DIM)
        out[0, :, lanes] = result[member * STEPS : (member + 1) * STEPS]


def finish(targets, rotary, own, arrived, grouped, cached):
    width = CORE_HEADS * GROUP * HEAD_DIM
    return pl.pallas_call(
        final_kernel,
        in_specs=[SMEM] + [VMEM] * 9,
        out_specs=VMEM,
        out_shape=jax.ShapeDtypeStruct((1, STEPS, width), BF16),
        compiler_params=pltpu.CompilerParams(vmem_limit_bytes=16 * MIB),
        name="finish",
    )(targets, rotary, own, *arrived, grouped, *cached)


def rotary_turns():
    half = np.arange(HEAD_DIM // 2, dtype=np.float64) / (HEAD_DIM // 2)
    frequency = ROTARY_BASE ** (-np.concatenate([half, half]))
    angles = np.arange(STRETCH, dtype=np.float64)[:, None] * frequency
    return frequency.astype(np.float32), np.stack([np.cos(angles), np.sin(angles)]).astype(np.float32)


def per_device(
    stretch,
    norm_gain,
    kv_codes,
    scale_codes,
    outer_scales,
    prompt_lengths,
    target_rows,
    cache_lengths,
    kv_cache,
    queries,
    new_kv,
):
    count = lax.axis_size("tp")
    half = count // 2
    lines = stretch.transpose(1, 0, 2)
    gain = norm_gain.reshape(1, -1)
    ring = [ring_device(at, count) for at in range(count)]
    to_right = [(ring[at], ring[(at + 1) % count]) for at in range(count)]
    to_left = [(ring[at], ring[at - 1]) for at in range(count)]

    def pass_on(right, left):
        return lax.ppermute(right, "tp", to_right), lax.ppermute(left, "tp", to_left)

    swap = lambda array: lax.ppermute(array, "rep", [(0, 1), (1, 0)])
    other = swap(lines)
    weight = dequantize(kv_codes, scale_codes, outer_scales.T)
    frequency, turns = rotary_turns()
    start = (prompt_lengths - STRETCH).astype(F32)[:, None] * jnp.asarray(frequency)
    starts = jnp.stack([jnp.cos(start), jnp.sin(start)])

    features = [lines, other, gain]
    right, left = project_first(half, target_rows, *features, weight)
    targets, _ = lax.optimization_barrier((target_rows, left))
    arrived = [pass_on(right, left), []]

    for distance in range(half - 1, 0, -1):
        terms = project([distance, -distance], targets, *features, weight)
        right, left = sends(1, terms, arrived[1])
        terms, right, left = lax.optimization_barrier((terms, right, left))
        targets, _ = lax.optimization_barrier((target_rows, left))
        arrived[1] = pass_on(right, left)
        if distance == half - 1:
            prepared = prepare(targets, queries, starts, jnp.asarray(turns))
            terms, prepared = lax.optimization_barrier((terms, prepared))
            grouped, rotary = prepared
        if distance == max(1, half - 2):
            cached = cache_attention(
                0, targets, prompt_lengths, cache_lengths, grouped, kv_cache, new_kv
            )
            terms, cached = lax.optimization_barrier((terms, cached))
        right, left = sends(0, terms, arrived[0])
        targets, right = lax.optimization_barrier((target_rows, right))
        arrived[0] = pass_on(right, left)

    cached, _ = lax.optimization_barrier((cached, right))
    cached = [swap(cached)]
    terms = project([0], targets, *features, weight)
    cached.append(
        cache_attention(1, targets, prompt_lengths, cache_lengths, grouped, kv_cache, new_kv)
    )
    out = finish(target_rows, rotary, terms, [*arrived[0], *arrived[1]], grouped, cached)
    return lax.all_gather(out, "rep", axis=2, tiled=True)


def solution(mesh):
    in_specs = (
        P(None, ("grp", "rep"), "tp"),
        P("tp"),
        P("tp", None),
        P("tp", None),
        P("tp", None),
        P("grp"),
        P("grp"),
        P(("grp", "tp")),
        P(("grp", "tp"), "rep", None),
        P(("grp", "tp"), None, None),
        P(("grp", "tp"), None, None),
    )
    out_specs = P(("grp", "tp"), None, None)
    return jax.shard_map(
        per_device, mesh=mesh, in_specs=in_specs, out_specs=out_specs, check_vma=False
    )
```

```python
import functools
import math

import jax
import jax.numpy as jnp
import numpy as np
from jax import lax
from jax.experimental import pallas as pl
from jax.experimental.pallas import tpu as pltpu
from jax.sharding import PartitionSpec as P

D = 16384
HEADS = 128
KV_HEADS = 8
HEAD_DIM = 128
STRETCH = 192
STEPS = 2
QBLOCK = 64
GROUP = HEADS // KV_HEADS
ROWS = GROUP * STEPS
TAIL = 16
PART = ROWS + TAIL
CORE_HEADS = KV_HEADS // 2
NORMAL_FLOAT_LEVELS = [
    -1.0,
    -0.6961928009986877,
    -0.5250730514526367,
    -0.39491748809814453,
    -0.28444138169288635,
    -0.18477343022823334,
    -0.09105003625154495,
    0.0,
    0.07958029955625534,
    0.16093020141124725,
    0.24611230194568634,
    0.33791524171829224,
    0.44070982933044434,
    0.5626170039176941,
    0.7229568362236023,
    1.0,
]
ROTARY_BASE = 500000.0
EPSILON = 1e-05
NEGATIVE = -1e30
BF16 = jnp.bfloat16
F32 = jnp.float32
MIB = 1024 * 1024
VMEM = pl.BlockSpec(memory_space=pltpu.VMEM)
SMEM = pl.BlockSpec(memory_space=pltpu.SMEM)


def in_hbm(*arrays):
    return [pltpu.with_memory_space_constraint(array, pltpu.HBM) for array in arrays]


def ring_device(place, count):
    half = count // 2
    if isinstance(place, int):
        return 2 * place if place < half else 2 * (count - 1 - place) + 1
    return jnp.where(place < half, 2 * place, 2 * (count - 1 - place) + 1)


def owner_at(distance):
    count = lax.axis_size("tp")
    here = lax.axis_index("tp")
    place = jnp.where(here % 2 == 0, here // 2, count - 1 - here // 2)
    return ring_device((place + distance + count) % count, count)


def turned(column):
    rows = lax.broadcasted_iota(jnp.int32, (column.shape[0], 128), 0)
    lanes = lax.broadcasted_iota(jnp.int32, (column.shape[0], 128), 1)
    return jnp.sum(jnp.where(rows == lanes, column, 0.0), axis=0, keepdims=True)


def stood(row, count):
    rows = lax.broadcasted_iota(jnp.int32, (count, 128), 0)
    lanes = lax.broadcasted_iota(jnp.int32, (count, 128), 1)
    return jnp.sum(jnp.where(rows == lanes, row, 0.0), axis=1, keepdims=True)


def token_rows(column):
    at = lax.broadcasted_iota(jnp.int32, (8, 128), 0)
    ends = turned(column[128:])
    return jnp.where(at == 0, turned(column[:128]), jnp.where(at == 1, ends, 0.0))


def token_column(rows):
    return jnp.concatenate([stood(rows[0:1], 128), stood(rows[1:2], STRETCH - 128)], axis=0)


def two_pieces(rows):
    high = rows.astype(BF16).astype(F32)
    return jnp.concatenate([high, rows - high], axis=0).astype(BF16)


def one_piece(rows):
    rows = rows.astype(F32)
    return rows[:8] + rows[8:]


def pieces_tail(logs):
    row = turned(logs)
    high = row.astype(BF16).astype(F32)
    middle = (row - high).astype(BF16).astype(F32)
    low = row - high - middle
    at = lax.broadcasted_iota(jnp.int32, (TAIL, 128), 0)
    tail = jnp.where(at == 0, high, jnp.where(at == 1, middle, jnp.where(at == 2, low, 0.0)))
    return tail.astype(BF16)


def tail_pieces(tail):
    tail = tail.astype(F32)
    return stood(tail[0:1, :] + tail[1:2, :] + tail[2:3, :], ROWS)


CODE_ROWS = 128


def block_leaves(scale):
    wide = jnp.broadcast_to(scale, (8, HEAD_DIM))
    leaves = [wide * jnp.float32(level) for level in NORMAL_FLOAT_LEVELS]
    return [jnp.concatenate([leaf, leaf], axis=0).astype(BF16) for leaf in leaves]


def selected(codes, leaves):
    codes = codes.astype(jnp.int16)
    masks = [(codes & (1 << bit)) != 0 for bit in range(4)]

    def node(bit, base):
        if bit < 0:
            return leaves[base]
        low = node(bit - 1, base)
        return jnp.where(masks[bit], node(bit - 1, base + (1 << bit)), low)

    return node(3, 0)


def block_scales(scales, outer, column):
    count = scales.shape[0]
    line = lax.broadcasted_iota(jnp.int32, outer.shape, 0)
    line = jnp.sum(jnp.where(line == column, outer, 0.0), axis=0, keepdims=True)
    rows = lax.broadcasted_iota(jnp.int32, (count, count), 0)
    lanes = lax.broadcasted_iota(jnp.int32, (count, count), 1)
    second = jnp.sum(jnp.where(rows == lanes, line, 0.0), axis=1, keepdims=True)
    return (scales.astype(F32) + 1.0) / 256.0 * second


def weights_kernel(
    codes, key_scales, value_scales, outer, out, key_codes, value_codes, scales, arrivals
):
    features, width = key_codes.shape
    depth = min(CODE_ROWS, features)
    blocks = features // depth
    columns = outer.shape[0] // 2
    rep = lax.axis_index("rep")

    def code_copies(block):
        rows = pl.ds(block * depth, depth)
        return [
            pltpu.make_async_copy(
                codes.at[rows, pl.ds(pl.multiple_of((2 * kind + rep) * width, width), width)],
                buffer.at[rows],
                arrivals.at[2 * block + kind],
            )
            for kind, buffer in enumerate((key_codes, value_codes))
        ]

    for block in range(blocks):
        for copy in code_copies(block):
            copy.start()
    for at in range(CORE_HEADS):
        column = (rep * CORE_HEADS + at) // (KV_HEADS // columns)
        lanes = slice(at * HEAD_DIM, (at + 1) * HEAD_DIM)
        scales[2 * at] = block_scales(key_scales[:, lanes], outer[...], column)
        scales[2 * at + 1] = block_scales(value_scales[:, lanes], outer[...], columns + column)

    def body(step, _):
        row = pl.ds(step, 1)
        for at in range(CORE_HEADS):
            lanes = slice(at * HEAD_DIM, (at + 1) * HEAD_DIM)
            for kind, buffer in enumerate((key_codes, value_codes)):
                leaves = block_leaves(scales[2 * at + kind, row, :])
                for tile in range(QBLOCK // 16):
                    rows = pl.ds(pl.multiple_of(step * QBLOCK + 16 * tile, 16), 16)
                    half = slice(at % 2 * HEAD_DIM, (at % 2 + 1) * HEAD_DIM)
                    out[2 * kind + at // 2, rows, half] = selected(buffer[rows, lanes], leaves)
        return 0

    steps = depth // QBLOCK
    for block in range(blocks):
        for copy in code_copies(block):
            copy.wait()
        lax.fori_loop(block * steps, (block + 1) * steps, body, 0)


def dequantize(codes, scales, outer):
    features = codes.shape[0]
    width = CORE_HEADS * HEAD_DIM
    blocks = features // min(CODE_ROWS, features)
    rep = lambda: lax.axis_index("rep")
    codes, scales, outer = in_hbm(codes, scales, outer)
    return pl.pallas_call(
        weights_kernel,
        grid=(1,),
        in_specs=[
            pl.BlockSpec(memory_space=pltpu.HBM),
            pl.BlockSpec((scales.shape[0], width), lambda k: (0, rep())),
            pl.BlockSpec((scales.shape[0], width), lambda k: (0, 2 + rep())),
            pl.BlockSpec(outer.shape, lambda k: (0, 0)),
        ],
        out_specs=VMEM,
        out_shape=jax.ShapeDtypeStruct((CORE_HEADS, features, 2 * HEAD_DIM), BF16),
        scratch_shapes=[
            pltpu.VMEM((features, width), jnp.int32),
            pltpu.VMEM((features, width), jnp.int32),
            pltpu.VMEM((2 * CORE_HEADS, scales.shape[0], HEAD_DIM), F32),
            pltpu.SemaphoreType.DMA((2 * blocks,)),
        ],
        compiler_params=pltpu.CompilerParams(vmem_limit_bytes=32 * MIB),
        cost_estimate=pl.CostEstimate(
            flops=32 * codes.size, bytes_accessed=codes.size * 2, transcendentals=0
        ),
        name="dequantize",
    )(codes, scales, scales, outer)


def prompt_of(targets, owner):
    prompt = jnp.int32(-1)
    for at in range(targets.shape[0]):
        prompt = jnp.where(targets[at] == owner, at, prompt)
    return prompt


def with_lines(targets, distance, own, other, gain, line, total, some, none):
    per_rep = own.shape[0]
    prompt = prompt_of(targets, owner_at(distance))
    at = lax.rem(jnp.maximum(prompt, 0), per_rep)
    is_own = prompt // per_rep == lax.axis_index("rep")
    width = min(512, line.shape[1])

    def scale(x):
        sums = jnp.zeros((STRETCH, 1), F32)
        for begin in range(0, line.shape[1], width):
            lanes = slice(begin, begin + width)
            wide = x[at, :, lanes].astype(F32)
            line[:, lanes] = (wide * gain[:, lanes]).astype(BF16)
            sums += jnp.sum(wide * wide, axis=1, keepdims=True)
        total[...] = token_rows(sums)

    pl.when((prompt >= 0) & is_own)(lambda: scale(own))
    pl.when((prompt >= 0) & jnp.logical_not(is_own))(lambda: scale(other))
    pl.when(prompt >= 0)(some)
    pl.when(prompt < 0)(none)


def products(line, weight, kind):
    for pair in range(2):
        product = jnp.dot(line[...], weight[2 * kind + pair], preferred_element_type=F32)
        for at in range(2):
            begin = (2 * pair + at) * STRETCH
            yield slice(begin, begin + STRETCH), product[:, at * HEAD_DIM : (at + 1) * HEAD_DIM]


def line_scratch(x):
    return [pltpu.VMEM(x.shape[1:], BF16), pltpu.VMEM((8, 128), F32)]


def first_kernel(distance, targets, own, other, gain, weight, right, left, line, total):
    def some():
        for kind, out in enumerate((right, left)):
            for rows, product in products(line, weight, kind):
                out[rows] = product.astype(BF16)
        right[CORE_HEADS * STRETCH :] = two_pieces(total[...])

    def none():
        right[...] = jnp.zeros(right.shape, BF16)
        left[...] = jnp.zeros(left.shape, BF16)

    with_lines(targets, distance, own, other, gain, line, total, some, none)


def project_first(distance, targets, own, other, gain, weight):
    rows = CORE_HEADS * STRETCH
    return pl.pallas_call(
        functools.partial(first_kernel, distance),
        in_specs=[SMEM] + [VMEM] * 4,
        out_specs=[VMEM] * 2,
        out_shape=[
            jax.ShapeDtypeStruct((rows + TAIL, HEAD_DIM), BF16),
            jax.ShapeDtypeStruct((rows, HEAD_DIM), BF16),
        ],
        scratch_shapes=line_scratch(own),
        compiler_params=pltpu.CompilerParams(vmem_limit_bytes=24 * MIB),
        cost_estimate=pl.CostEstimate(
            flops=STRETCH * weight.size * 2, bytes_accessed=weight.size, transcendentals=0
        ),
        name="project_first",
    )(targets, own, other, gain, weight)


def project_kernel(distances, targets, own, other, gain, weight, out, line, total):
    for item, distance in enumerate(distances):

        def some(item=item):
            for kind in range(2):
                for rows, product in products(line, weight, kind):
                    out[item, kind, rows] = product
            out[item, 0, CORE_HEADS * STRETCH :] = total[...]

        def none(item=item):
            out[item] = jnp.zeros(out.shape[1:], F32)

        with_lines(targets, distance, own, other, gain, line, total, some, none)


def project(distances, targets, own, other, gain, weight):
    return pl.pallas_call(
        functools.partial(project_kernel, distances),
        in_specs=[SMEM] + [VMEM] * 4,
        out_specs=VMEM,
        out_shape=jax.ShapeDtypeStruct((len(distances), 2, 4 * STRETCH + 8, HEAD_DIM), F32),
        scratch_shapes=line_scratch(own),
        compiler_params=pltpu.CompilerParams(vmem_limit_bytes=24 * MIB),
        cost_estimate=pl.CostEstimate(
            flops=len(distances) * STRETCH * weight.size,
            bytes_accessed=weight.size,
            transcendentals=0,
        ),
        name="project",
    )(targets, own, other, gain, weight)


def early_kernel(distance, targets, own, other, gain, weight, out, lines, totals):
    for item in range(2):
        line, total, kind = lines.at[item], totals.at[item], 1 - item

        def some(item=item, line=line, total=total, kind=kind):
            for rows, product in products(line, weight, kind):
                out[item, 0, rows] = product
            if kind == 0:
                out[item, 0, CORE_HEADS * STRETCH :] = total[...]

        def none(item=item, line=line, total=total):
            out[item] = jnp.zeros(out.shape[1:], F32)
            line[...] = jnp.zeros(line.shape, BF16)
            total[...] = jnp.zeros(total.shape, F32)

        towards = distance * (1 - 2 * item)
        with_lines(targets, towards, own, other, gain, line, total, some, none)


def late_kernel(lines, totals, weight, out):
    for item in range(2):
        for rows, product in products(lines.at[item], weight, item):
            out[item, 0, rows] = product
    out[0, 0, CORE_HEADS * STRETCH :] = totals[0]


def project_early(distance, targets, own, other, gain, weight):
    return pl.pallas_call(
        functools.partial(early_kernel, distance),
        in_specs=[SMEM] + [VMEM] * 4,
        out_specs=[VMEM] * 3,
        out_shape=[
            jax.ShapeDtypeStruct((2, 1, CORE_HEADS * STRETCH + 8, HEAD_DIM), F32),
            jax.ShapeDtypeStruct((2,) + own.shape[1:], BF16),
            jax.ShapeDtypeStruct((2, 8, 128), F32),
        ],
        compiler_params=pltpu.CompilerParams(vmem_limit_bytes=24 * MIB),
        cost_estimate=pl.CostEstimate(
            flops=STRETCH * weight.size, bytes_accessed=weight.size, transcendentals=0
        ),
        name="project_early",
    )(targets, own, other, gain, weight)


def project_late(lines, totals, weight):
    return pl.pallas_call(
        late_kernel,
        in_specs=[VMEM] * 3,
        out_specs=VMEM,
        out_shape=jax.ShapeDtypeStruct((2, 1, CORE_HEADS * STRETCH + 8, HEAD_DIM), F32),
        compiler_params=pltpu.CompilerParams(vmem_limit_bytes=24 * MIB),
        cost_estimate=pl.CostEstimate(
            flops=STRETCH * weight.size, bytes_accessed=weight.size, transcendentals=0
        ),
        name="project_late",
    )(lines, totals, weight)


def send_kernel(half, terms, *refs):
    *arrived, to_right, to_left = refs
    rows = CORE_HEADS * STRETCH
    for item, out in enumerate((to_right, to_left)):
        kind = (half + item) % 2
        total = terms[item, kind % terms.shape[1], :rows]
        if arrived:
            total += arrived[item][:rows].astype(F32)
        out[:rows] = total.astype(BF16)
        if kind == 0:
            squares = terms[item, 0, rows:]
            if arrived:
                squares += one_piece(arrived[item][rows : rows + TAIL])
            out[rows : rows + TAIL] = two_pieces(squares)
        spare = rows + (TAIL if kind == 0 else 0)
        if spare < out.shape[0]:
            out[spare:] = jnp.zeros((out.shape[0] - spare, HEAD_DIM), BF16)


def sends(half, terms, arrived):
    rows = CORE_HEADS * STRETCH
    shapes = [jax.ShapeDtypeStruct((rows + TAIL, HEAD_DIM), BF16)] * 2
    return pl.pallas_call(
        functools.partial(send_kernel, half),
        in_specs=[VMEM] * (1 + len(arrived)),
        out_specs=[VMEM] * 2,
        out_shape=shapes,
        compiler_params=pltpu.CompilerParams(vmem_limit_bytes=16 * MIB),
        name="sends",
    )(terms, *arrived)


def prepare_kernel(targets, queries, starts, turns, grouped, rotary):
    for head in range(KV_HEADS):
        for member in range(GROUP):
            begin = (head * GROUP + member) * HEAD_DIM
            rows = slice(member * STEPS, (member + 1) * STEPS)
            grouped[head, rows] = queries[0, :, begin : begin + HEAD_DIM]
    row = pl.ds(jnp.maximum(prompt_of(targets, lax.axis_index("tp")), 0), 1)
    cosine, sine = starts[0, row, :], starts[1, row, :]
    lane = lax.broadcasted_iota(jnp.int32, turns.shape[1:], 1)
    rotary[0] = turns[0] * cosine - turns[1] * sine
    sine = turns[1] * cosine + turns[0] * sine
    rotary[1] = jnp.where(lane < HEAD_DIM // 2, -sine, sine)


def prepare(targets, queries, starts, turns):
    return pl.pallas_call(
        prepare_kernel,
        in_specs=[SMEM] + [VMEM] * 3,
        out_specs=[VMEM] * 2,
        out_shape=[
            jax.ShapeDtypeStruct((KV_HEADS, ROWS, HEAD_DIM), BF16),
            jax.ShapeDtypeStruct(turns.shape, F32),
        ],
        compiler_params=pltpu.CompilerParams(vmem_limit_bytes=16 * MIB),
        name="prepare",
    )(targets, queries, starts, turns)


def cache_kernel(part, targets, lengths, stored, q, cache, new, out):
    scaling = HEAD_DIM ** (-0.5)
    dims = (((1,), (1,)), ((), ()))
    here = lax.axis_index("tp")
    rep = lax.axis_index("rep")
    length = cache.shape[1]
    prompt = prompt_of(targets, here)
    handed = lengths[jnp.maximum(prompt, 0)] - STRETCH
    span = jnp.where(prompt >= 0, handed, stored[0]) - rep * length
    count = CORE_HEADS * ROWS
    allowed = lax.broadcasted_iota(jnp.int32, (count, length), 1) < span
    second_step = lax.broadcasted_iota(jnp.int32, (count, 1), 0) % STEPS == 1
    scores, fresh, key_lanes, value_lanes = [], [[], []], [], []
    for at in range(CORE_HEADS):
        head = (rep if part == 1 else 1 - rep) * CORE_HEADS + at
        key_lanes.append(pl.ds(pl.multiple_of(head * HEAD_DIM, HEAD_DIM), HEAD_DIM))
        begin = pl.multiple_of((KV_HEADS + head) * HEAD_DIM, HEAD_DIM)
        value_lanes.append(pl.ds(begin, HEAD_DIM))
        query = q[head]
        wide = query.astype(F32)
        keys = cache[0, :, key_lanes[at]]
        scores.append(lax.dot_general(query, keys, dims, preferred_element_type=F32))
        for step in range(STEPS):
            key = new[0, step : step + 1, key_lanes[at]].astype(F32)
            fresh[step].append(jnp.sum(wide * key, axis=1, keepdims=True))
    scores = jnp.where(allowed, jnp.concatenate(scores, axis=0) * scaling, NEGATIVE)
    highest = jnp.max(scores, axis=1, keepdims=True)
    for step in range(STEPS):
        shown = rep == 0 if step == 0 else second_step & (rep == 0)
        fresh[step] = jnp.where(shown, jnp.concatenate(fresh[step], axis=0) * scaling, NEGATIVE)
        highest = jnp.maximum(highest, fresh[step])
    some = highest > 0.5 * NEGATIVE
    highest = jnp.where(some, highest, 0.0)
    weight = jnp.exp(scores - highest)
    shares = [jnp.exp(score - highest) for score in fresh]
    totals = jnp.sum(weight, axis=1, keepdims=True) + shares[0] + shares[1]
    totals = jnp.where(some, totals, 1.0)
    logs = jnp.where(some, highest + jnp.log(totals), NEGATIVE)
    weight = weight.astype(BF16)
    for at in range(CORE_HEADS):
        rows = slice(at * ROWS, (at + 1) * ROWS)
        values = cache[0, :, value_lanes[at]]
        sums = jnp.dot(weight[rows], values, preferred_element_type=F32)
        for step in range(STEPS):
            value = new[0, step : step + 1, value_lanes[at]].astype(F32)
            sums += shares[step][rows].astype(BF16).astype(F32) * value
        out[at, :ROWS] = (sums / totals[rows]).astype(BF16)
        out[at, ROWS:] = pieces_tail(logs[rows])


def cache_attention(part, targets, lengths, stored, grouped, kv_cache, new_kv):
    return pl.pallas_call(
        functools.partial(cache_kernel, part),
        in_specs=[SMEM] * 3 + [VMEM] * 3,
        out_specs=VMEM,
        out_shape=jax.ShapeDtypeStruct((CORE_HEADS, PART, HEAD_DIM), BF16),
        compiler_params=pltpu.CompilerParams(vmem_limit_bytes=16 * MIB),
        cost_estimate=pl.CostEstimate(
            flops=1, bytes_accessed=1, transcendentals=0
        ),
        name="cache_attention",
    )(targets, lengths, stored, grouped, kv_cache, new_kv)


def final_kernel(
    targets, rotary, own, right_keys, left_values, right_values, left_keys, grouped,
    cached_there, cached_here, out,
):
    scaling = HEAD_DIM ** (-0.5)
    dims = (((1,), (1,)), ((), ()))
    mine = own.shape[0] - 1
    first = lax.axis_index("rep") * CORE_HEADS
    prompt = prompt_of(targets, lax.axis_index("tp"))
    cosine, sine = rotary[0], rotary[1]
    rows = CORE_HEADS * STRETCH
    squares = own[mine, 0, rows:] + one_piece(right_keys[rows : rows + TAIL]) + one_piece(left_keys[rows : rows + TAIL])
    scale = token_column(lax.rsqrt(squares / D + EPSILON))
    scores, handed = [], []
    for head in range(CORE_HEADS):
        at = slice(head * STRETCH, (head + 1) * STRETCH)
        keys = own[mine, 0, at] + right_keys[at].astype(F32) + left_keys[at].astype(F32)
        values = own[mine, 1, at] + right_values[at].astype(F32) + left_values[at].astype(F32)
        keys = (keys * scale).astype(BF16).astype(F32)
        handed.append((values * scale).astype(BF16))
        keys = keys * cosine + pltpu.roll(keys, HEAD_DIM // 2, 1) * sine
        scores.append(
            lax.dot_general(
                grouped[first + head], keys.astype(BF16), dims, preferred_element_type=F32
            )
        )
    scores = jnp.concatenate(scores, axis=0) * scaling
    highest = jnp.max(scores, axis=1, keepdims=True)
    weight = jnp.exp(scores - highest)
    totals = jnp.sum(weight, axis=1, keepdims=True)
    weight = weight.astype(BF16)
    sums = [
        jnp.dot(weight[head * ROWS : (head + 1) * ROWS], handed[head], preferred_element_type=F32)
        for head in range(CORE_HEADS)
    ]
    sums = [jnp.concatenate(sums, axis=0) / totals]
    logs = [jnp.where(prompt >= 0, highest + jnp.log(totals), NEGATIVE)]
    for cached in (cached_there, cached_here):
        parts = [cached[head] for head in range(CORE_HEADS)]
        sums.append(jnp.concatenate([part[:ROWS].astype(F32) for part in parts], axis=0))
        logs.append(jnp.concatenate([tail_pieces(part[ROWS:]) for part in parts], axis=0))
    highest = functools.reduce(jnp.maximum, logs)
    shares = [jnp.exp(log - highest) for log in logs]
    total = functools.reduce(jnp.add, shares)
    joined = functools.reduce(jnp.add, [share * part for share, part in zip(shares, sums)])
    result = (joined / total).astype(BF16)
    for member in range(CORE_HEADS * GROUP):
        lanes = slice(member * HEAD_DIM, (member + 1) * HEAD_DIM)
        out[0, :, lanes] = result[member * STEPS : (member + 1) * STEPS]


def finish(targets, rotary, own, arrived, grouped, cached):
    width = CORE_HEADS * GROUP * HEAD_DIM
    return pl.pallas_call(
        final_kernel,
        in_specs=[SMEM] + [VMEM] * 9,
        out_specs=VMEM,
        out_shape=jax.ShapeDtypeStruct((1, STEPS, width), BF16),
        compiler_params=pltpu.CompilerParams(vmem_limit_bytes=16 * MIB),
        name="finish",
    )(targets, rotary, own, *arrived, grouped, *cached)


def rotary_turns():
    half = np.arange(HEAD_DIM // 2, dtype=np.float64) / (HEAD_DIM // 2)
    frequency = ROTARY_BASE ** (-np.concatenate([half, half]))
    angles = np.arange(STRETCH, dtype=np.float64)[:, None] * frequency
    return frequency.astype(np.float32), np.stack([np.cos(angles), np.sin(angles)]).astype(np.float32)


def per_device(
    stretch,
    norm_gain,
    kv_codes,
    scale_codes,
    outer_scales,
    prompt_lengths,
    target_rows,
    cache_lengths,
    kv_cache,
    queries,
    new_kv,
):
    count = lax.axis_size("tp")
    half = count // 2
    lines = stretch.transpose(1, 0, 2)
    gain = norm_gain.reshape(1, -1)
    ring = [ring_device(at, count) for at in range(count)]
    to_right = [(ring[at], ring[(at + 1) % count]) for at in range(count)]
    to_left = [(ring[at], ring[at - 1]) for at in range(count)]

    def pass_on(right, left):
        return lax.ppermute(right, "tp", to_right), lax.ppermute(left, "tp", to_left)

    swap = lambda array: lax.ppermute(array, "rep", [(0, 1), (1, 0)])
    other = swap(lines)
    weight = dequantize(kv_codes, scale_codes, outer_scales.T)
    frequency, turns = rotary_turns()
    start = (prompt_lengths - STRETCH).astype(F32)[:, None] * jnp.asarray(frequency)
    starts = jnp.stack([jnp.cos(start), jnp.sin(start)])

    features = [lines, other, gain]
    right, left = project_first(half, target_rows, *features, weight)
    targets, _ = lax.optimization_barrier((target_rows, left))
    arrived = [pass_on(right, left), []]

    for distance in range(half - 1, 0, -1):
        if distance == half - 1:
            terms, *kept = project_early(distance, targets, *features, weight)
        else:
            terms = project([distance, -distance], targets, *features, weight)
            kept = terms
        right, left = sends(1, terms, arrived[1])
        kept, right, left = lax.optimization_barrier((kept, right, left))
        targets, _ = lax.optimization_barrier((target_rows, left))
        arrived[1] = pass_on(right, left)
        terms = kept
        if distance == half - 1:
            prepared = prepare(targets, queries, starts, jnp.asarray(turns))
            terms = project_late(*kept, weight)
            terms, prepared = lax.optimization_barrier((terms, prepared))
            grouped, rotary = prepared
        if distance == max(1, half - 2):
            cached = cache_attention(
                0, targets, prompt_lengths, cache_lengths, grouped, kv_cache, new_kv
            )
            terms, cached = lax.optimization_barrier((terms, cached))
        right, left = sends(0, terms, arrived[0])
        targets, right = lax.optimization_barrier((target_rows, right))
        arrived[0] = pass_on(right, left)

    cached, _ = lax.optimization_barrier((cached, right))
    cached = [swap(cached)]
    terms = project([0], targets, *features, weight)
    cached.append(
        cache_attention(1, targets, prompt_lengths, cache_lengths, grouped, kv_cache, new_kv)
    )
    out = finish(target_rows, rotary, terms, [*arrived[0], *arrived[1]], grouped, cached)
    return lax.all_gather(out, "rep", axis=2, tiled=True)


def solution(mesh):
    in_specs = (
        P(None, ("grp", "rep"), "tp"),
        P("tp"),
        P("tp", None),
        P("tp", None),
        P("tp", None),
        P("grp"),
        P("grp"),
        P(("grp", "tp")),
        P(("grp", "tp"), "rep", None),
        P(("grp", "tp"), None, None),
        P(("grp", "tp"), None, None),
    )
    out_specs = P(("grp", "tp"), None, None)
    return jax.shard_map(
        per_device, mesh=mesh, in_specs=in_specs, out_specs=out_specs, check_vma=False
    )
```

```python
import functools
import math

import jax
import jax.numpy as jnp
import numpy as np
from jax import lax
from jax.experimental import pallas as pl
from jax.experimental.pallas import tpu as pltpu
from jax.sharding import PartitionSpec as P

D = 16384
HEADS = 128
KV_HEADS = 8
HEAD_DIM = 128
STRETCH = 192
STEPS = 2
QBLOCK = 64
GROUP = HEADS // KV_HEADS
ROWS = GROUP * STEPS
TAIL = 16
PART = ROWS + TAIL
CORE_HEADS = KV_HEADS // 2
NORMAL_FLOAT_LEVELS = [
    -1.0,
    -0.6961928009986877,
    -0.5250730514526367,
    -0.39491748809814453,
    -0.28444138169288635,
    -0.18477343022823334,
    -0.09105003625154495,
    0.0,
    0.07958029955625534,
    0.16093020141124725,
    0.24611230194568634,
    0.33791524171829224,
    0.44070982933044434,
    0.5626170039176941,
    0.7229568362236023,
    1.0,
]
ROTARY_BASE = 500000.0
EPSILON = 1e-05
NEGATIVE = -1e30
BF16 = jnp.bfloat16
F32 = jnp.float32
MIB = 1024 * 1024
VMEM = pl.BlockSpec(memory_space=pltpu.VMEM)
SMEM = pl.BlockSpec(memory_space=pltpu.SMEM)


def in_hbm(*arrays):
    return [pltpu.with_memory_space_constraint(array, pltpu.HBM) for array in arrays]


def ring_device(place, count):
    half = count // 2
    if isinstance(place, int):
        return 2 * place if place < half else 2 * (count - 1 - place) + 1
    return jnp.where(place < half, 2 * place, 2 * (count - 1 - place) + 1)


def owner_at(distance):
    count = lax.axis_size("tp")
    here = lax.axis_index("tp")
    place = jnp.where(here % 2 == 0, here // 2, count - 1 - here // 2)
    return ring_device((place + distance + count) % count, count)


def turned(column):
    rows = lax.broadcasted_iota(jnp.int32, (column.shape[0], 128), 0)
    lanes = lax.broadcasted_iota(jnp.int32, (column.shape[0], 128), 1)
    return jnp.sum(jnp.where(rows == lanes, column, 0.0), axis=0, keepdims=True)


def stood(row, count):
    rows = lax.broadcasted_iota(jnp.int32, (count, 128), 0)
    lanes = lax.broadcasted_iota(jnp.int32, (count, 128), 1)
    return jnp.sum(jnp.where(rows == lanes, row, 0.0), axis=1, keepdims=True)


def token_rows(column):
    at = lax.broadcasted_iota(jnp.int32, (8, 128), 0)
    ends = turned(column[128:])
    return jnp.where(at == 0, turned(column[:128]), jnp.where(at == 1, ends, 0.0))


def token_column(rows):
    return jnp.concatenate([stood(rows[0:1], 128), stood(rows[1:2], STRETCH - 128)], axis=0)


def two_pieces(rows):
    high = rows.astype(BF16).astype(F32)
    return jnp.concatenate([high, rows - high], axis=0).astype(BF16)


def one_piece(rows):
    rows = rows.astype(F32)
    return rows[:8] + rows[8:]


def pieces_tail(logs):
    row = turned(logs)
    high = row.astype(BF16).astype(F32)
    middle = (row - high).astype(BF16).astype(F32)
    low = row - high - middle
    at = lax.broadcasted_iota(jnp.int32, (TAIL, 128), 0)
    tail = jnp.where(at == 0, high, jnp.where(at == 1, middle, jnp.where(at == 2, low, 0.0)))
    return tail.astype(BF16)


def tail_pieces(tail):
    tail = tail.astype(F32)
    return stood(tail[0:1, :] + tail[1:2, :] + tail[2:3, :], ROWS)


CODE_ROWS = 128


def block_leaves(scale):
    wide = jnp.broadcast_to(scale, (8, HEAD_DIM))
    leaves = [wide * jnp.float32(level) for level in NORMAL_FLOAT_LEVELS]
    return [jnp.concatenate([leaf, leaf], axis=0).astype(BF16) for leaf in leaves]


def selected(codes, leaves):
    codes = codes.astype(jnp.int16)
    masks = [(codes & (1 << bit)) != 0 for bit in range(4)]

    def node(bit, base):
        if bit < 0:
            return leaves[base]
        low = node(bit - 1, base)
        return jnp.where(masks[bit], node(bit - 1, base + (1 << bit)), low)

    return node(3, 0)


def block_scales(scales, outer, column):
    count = scales.shape[0]
    line = lax.broadcasted_iota(jnp.int32, outer.shape, 0)
    line = jnp.sum(jnp.where(line == column, outer, 0.0), axis=0, keepdims=True)
    rows = lax.broadcasted_iota(jnp.int32, (count, count), 0)
    lanes = lax.broadcasted_iota(jnp.int32, (count, count), 1)
    second = jnp.sum(jnp.where(rows == lanes, line, 0.0), axis=1, keepdims=True)
    return (scales.astype(F32) + 1.0) / 256.0 * second


def weights_kernel(
    codes, key_scales, value_scales, outer, out, key_codes, value_codes, scales, arrivals
):
    features, width = key_codes.shape
    depth = min(CODE_ROWS, features)
    blocks = features // depth
    columns = outer.shape[0] // 2
    rep = lax.axis_index("rep")

    def code_copies(block):
        rows = pl.ds(block * depth, depth)
        return [
            pltpu.make_async_copy(
                codes.at[rows, pl.ds(pl.multiple_of((2 * kind + rep) * width, width), width)],
                buffer.at[rows],
                arrivals.at[2 * block + kind],
            )
            for kind, buffer in enumerate((key_codes, value_codes))
        ]

    for block in range(blocks):
        for copy in code_copies(block):
            copy.start()
    for at in range(CORE_HEADS):
        column = (rep * CORE_HEADS + at) // (KV_HEADS // columns)
        lanes = slice(at * HEAD_DIM, (at + 1) * HEAD_DIM)
        scales[2 * at] = block_scales(key_scales[:, lanes], outer[...], column)
        scales[2 * at + 1] = block_scales(value_scales[:, lanes], outer[...], columns + column)

    def body(step, _):
        row = pl.ds(step, 1)
        for at in range(CORE_HEADS):
            lanes = slice(at * HEAD_DIM, (at + 1) * HEAD_DIM)
            for kind, buffer in enumerate((key_codes, value_codes)):
                leaves = block_leaves(scales[2 * at + kind, row, :])
                for tile in range(QBLOCK // 16):
                    rows = pl.ds(pl.multiple_of(step * QBLOCK + 16 * tile, 16), 16)
                    half = slice(at % 2 * HEAD_DIM, (at % 2 + 1) * HEAD_DIM)
                    out[2 * kind + at // 2, rows, half] = selected(buffer[rows, lanes], leaves)
        return 0

    steps = depth // QBLOCK
    for block in range(blocks):
        for copy in code_copies(block):
            copy.wait()
        lax.fori_loop(block * steps, (block + 1) * steps, body, 0)


def dequantize(codes, scales, outer):
    features = codes.shape[0]
    width = CORE_HEADS * HEAD_DIM
    blocks = features // min(CODE_ROWS, features)
    rep = lambda: lax.axis_index("rep")
    codes, scales, outer = in_hbm(codes, scales, outer)
    return pl.pallas_call(
        weights_kernel,
        grid=(1,),
        in_specs=[
            pl.BlockSpec(memory_space=pltpu.HBM),
            pl.BlockSpec((scales.shape[0], width), lambda k: (0, rep())),
            pl.BlockSpec((scales.shape[0], width), lambda k: (0, 2 + rep())),
            pl.BlockSpec(outer.shape, lambda k: (0, 0)),
        ],
        out_specs=VMEM,
        out_shape=jax.ShapeDtypeStruct((CORE_HEADS, features, 2 * HEAD_DIM), BF16),
        scratch_shapes=[
            pltpu.VMEM((features, width), jnp.int32),
            pltpu.VMEM((features, width), jnp.int32),
            pltpu.VMEM((2 * CORE_HEADS, scales.shape[0], HEAD_DIM), F32),
            pltpu.SemaphoreType.DMA((2 * blocks,)),
        ],
        compiler_params=pltpu.CompilerParams(vmem_limit_bytes=32 * MIB),
        cost_estimate=pl.CostEstimate(
            flops=32 * codes.size, bytes_accessed=codes.size * 2, transcendentals=0
        ),
        name="dequantize",
    )(codes, scales, scales, outer)


def prompt_of(targets, owner):
    prompt = jnp.int32(-1)
    for at in range(targets.shape[0]):
        prompt = jnp.where(targets[at] == owner, at, prompt)
    return prompt


def with_lines(targets, distance, own, other, gain, line, total, some, none):
    per_rep = own.shape[0]
    prompt = prompt_of(targets, owner_at(distance))
    at = lax.rem(jnp.maximum(prompt, 0), per_rep)
    is_own = prompt // per_rep == lax.axis_index("rep")
    width = min(512, line.shape[1])

    def scale(x):
        sums = jnp.zeros((STRETCH, 1), F32)
        for begin in range(0, line.shape[1], width):
            lanes = slice(begin, begin + width)
            wide = x[at, :, lanes].astype(F32)
            line[:, lanes] = (wide * gain[:, lanes]).astype(BF16)
            sums += jnp.sum(wide * wide, axis=1, keepdims=True)
        total[...] = token_rows(sums)

    pl.when((prompt >= 0) & is_own)(lambda: scale(own))
    pl.when((prompt >= 0) & jnp.logical_not(is_own))(lambda: scale(other))
    pl.when(prompt >= 0)(some)
    pl.when(prompt < 0)(none)


def products(line, weight, kind):
    for pair in range(2):
        product = jnp.dot(line[...], weight[2 * kind + pair], preferred_element_type=F32)
        for at in range(2):
            begin = (2 * pair + at) * STRETCH
            yield slice(begin, begin + STRETCH), product[:, at * HEAD_DIM : (at + 1) * HEAD_DIM]


def line_scratch(x):
    return [pltpu.VMEM(x.shape[1:], BF16), pltpu.VMEM((8, 128), F32)]


def first_kernel(distance, targets, own, other, gain, weight, right, left, line, total):
    def some():
        for kind, out in enumerate((right, left)):
            for rows, product in products(line, weight, kind):
                out[rows] = product.astype(BF16)
        right[CORE_HEADS * STRETCH :] = two_pieces(total[...])

    def none():
        right[...] = jnp.zeros(right.shape, BF16)
        left[...] = jnp.zeros(left.shape, BF16)

    with_lines(targets, distance, own, other, gain, line, total, some, none)


def project_first(distance, targets, own, other, gain, weight):
    rows = CORE_HEADS * STRETCH
    return pl.pallas_call(
        functools.partial(first_kernel, distance),
        in_specs=[SMEM] + [VMEM] * 4,
        out_specs=[VMEM] * 2,
        out_shape=[
            jax.ShapeDtypeStruct((rows + TAIL, HEAD_DIM), BF16),
            jax.ShapeDtypeStruct((rows, HEAD_DIM), BF16),
        ],
        scratch_shapes=line_scratch(own),
        compiler_params=pltpu.CompilerParams(vmem_limit_bytes=24 * MIB),
        cost_estimate=pl.CostEstimate(
            flops=STRETCH * weight.size * 2, bytes_accessed=weight.size, transcendentals=0
        ),
        name="project_first",
    )(targets, own, other, gain, weight)


def project_kernel(distances, targets, own, other, gain, weight, out, line, total):
    for item, distance in enumerate(distances):

        def some(item=item):
            for kind in range(2):
                for rows, product in products(line, weight, kind):
                    out[item, kind, rows] = product
            out[item, 0, CORE_HEADS * STRETCH :] = total[...]

        def none(item=item):
            out[item] = jnp.zeros(out.shape[1:], F32)

        with_lines(targets, distance, own, other, gain, line, total, some, none)


def project(distances, targets, own, other, gain, weight):
    return pl.pallas_call(
        functools.partial(project_kernel, distances),
        in_specs=[SMEM] + [VMEM] * 4,
        out_specs=VMEM,
        out_shape=jax.ShapeDtypeStruct((len(distances), 2, 4 * STRETCH + 8, HEAD_DIM), F32),
        scratch_shapes=line_scratch(own),
        compiler_params=pltpu.CompilerParams(vmem_limit_bytes=24 * MIB),
        cost_estimate=pl.CostEstimate(
            flops=len(distances) * STRETCH * weight.size,
            bytes_accessed=weight.size,
            transcendentals=0,
        ),
        name="project",
    )(targets, own, other, gain, weight)


def early_kernel(distance, targets, own, other, gain, weight, out, lines, totals):
    for item in range(2):
        line, total, kind = lines.at[item], totals.at[item], 1 - item

        def some(item=item, line=line, total=total, kind=kind):
            for rows, product in products(line, weight, kind):
                out[item, 0, rows] = product
            if kind == 0:
                out[item, 0, CORE_HEADS * STRETCH :] = total[...]

        def none(item=item, line=line, total=total):
            out[item] = jnp.zeros(out.shape[1:], F32)
            line[...] = jnp.zeros(line.shape, BF16)
            total[...] = jnp.zeros(total.shape, F32)

        towards = distance * (1 - 2 * item)
        with_lines(targets, towards, own, other, gain, line, total, some, none)


def late_kernel(lines, totals, weight, out):
    for item in range(2):
        for rows, product in products(lines.at[item], weight, item):
            out[item, 0, rows] = product
    out[0, 0, CORE_HEADS * STRETCH :] = totals[0]


def project_early(distance, targets, own, other, gain, weight):
    return pl.pallas_call(
        functools.partial(early_kernel, distance),
        in_specs=[SMEM] + [VMEM] * 4,
        out_specs=[VMEM] * 3,
        out_shape=[
            jax.ShapeDtypeStruct((2, 1, CORE_HEADS * STRETCH + 8, HEAD_DIM), F32),
            jax.ShapeDtypeStruct((2,) + own.shape[1:], BF16),
            jax.ShapeDtypeStruct((2, 8, 128), F32),
        ],
        compiler_params=pltpu.CompilerParams(vmem_limit_bytes=24 * MIB),
        cost_estimate=pl.CostEstimate(
            flops=STRETCH * weight.size, bytes_accessed=weight.size, transcendentals=0
        ),
        name="project_early",
    )(targets, own, other, gain, weight)


def project_late(lines, totals, weight):
    return pl.pallas_call(
        late_kernel,
        in_specs=[VMEM] * 3,
        out_specs=VMEM,
        out_shape=jax.ShapeDtypeStruct((2, 1, CORE_HEADS * STRETCH + 8, HEAD_DIM), F32),
        compiler_params=pltpu.CompilerParams(vmem_limit_bytes=24 * MIB),
        cost_estimate=pl.CostEstimate(
            flops=STRETCH * weight.size, bytes_accessed=weight.size, transcendentals=0
        ),
        name="project_late",
    )(lines, totals, weight)


def send_kernel(half, terms, *refs):
    *arrived, to_right, to_left = refs
    rows = CORE_HEADS * STRETCH
    for item, out in enumerate((to_right, to_left)):
        kind = (half + item) % 2
        total = terms[item, kind % terms.shape[1], :rows]
        if arrived:
            total += arrived[item][:rows].astype(F32)
        out[:rows] = total.astype(BF16)
        if kind == 0:
            squares = terms[item, 0, rows:]
            if arrived:
                squares += one_piece(arrived[item][rows : rows + TAIL])
            out[rows : rows + TAIL] = two_pieces(squares)
        spare = rows + (TAIL if kind == 0 else 0)
        if spare < out.shape[0]:
            out[spare:] = jnp.zeros((out.shape[0] - spare, HEAD_DIM), BF16)


def sends(half, terms, arrived):
    rows = CORE_HEADS * STRETCH
    shapes = [jax.ShapeDtypeStruct((rows + TAIL, HEAD_DIM), BF16)] * 2
    return pl.pallas_call(
        functools.partial(send_kernel, half),
        in_specs=[VMEM] * (1 + len(arrived)),
        out_specs=[VMEM] * 2,
        out_shape=shapes,
        compiler_params=pltpu.CompilerParams(vmem_limit_bytes=16 * MIB),
        name="sends",
    )(terms, *arrived)


def prepare_kernel(targets, queries, starts, turns, grouped, rotary):
    for head in range(KV_HEADS):
        for member in range(GROUP):
            begin = (head * GROUP + member) * HEAD_DIM
            rows = slice(member * STEPS, (member + 1) * STEPS)
            grouped[head, rows] = queries[0, :, begin : begin + HEAD_DIM]
    row = pl.ds(jnp.maximum(prompt_of(targets, lax.axis_index("tp")), 0), 1)
    cosine, sine = starts[0, row, :], starts[1, row, :]
    lane = lax.broadcasted_iota(jnp.int32, turns.shape[1:], 1)
    rotary[0] = turns[0] * cosine - turns[1] * sine
    sine = turns[1] * cosine + turns[0] * sine
    rotary[1] = jnp.where(lane < HEAD_DIM // 2, -sine, sine)


def prepare(targets, queries, starts, turns):
    return pl.pallas_call(
        prepare_kernel,
        in_specs=[SMEM] + [VMEM] * 3,
        out_specs=[VMEM] * 2,
        out_shape=[
            jax.ShapeDtypeStruct((KV_HEADS, ROWS, HEAD_DIM), BF16),
            jax.ShapeDtypeStruct(turns.shape, F32),
        ],
        compiler_params=pltpu.CompilerParams(vmem_limit_bytes=16 * MIB),
        name="prepare",
    )(targets, queries, starts, turns)


def cache_kernel(part, targets, lengths, stored, q, cache, new, out):
    scaling = HEAD_DIM ** (-0.5)
    dims = (((1,), (1,)), ((), ()))
    here = lax.axis_index("tp")
    rep = lax.axis_index("rep")
    length = cache.shape[1]
    prompt = prompt_of(targets, here)
    handed = lengths[jnp.maximum(prompt, 0)] - STRETCH
    span = jnp.where(prompt >= 0, handed, stored[...]) - rep * length
    count = CORE_HEADS * ROWS
    allowed = lax.broadcasted_iota(jnp.int32, (count, length), 1) < span
    second_step = lax.broadcasted_iota(jnp.int32, (count, 1), 0) % STEPS == 1
    scores, fresh, key_lanes, value_lanes = [], [[], []], [], []
    for at in range(CORE_HEADS):
        head = (rep if part == 1 else 1 - rep) * CORE_HEADS + at
        key_lanes.append(pl.ds(pl.multiple_of(head * HEAD_DIM, HEAD_DIM), HEAD_DIM))
        begin = pl.multiple_of((KV_HEADS + head) * HEAD_DIM, HEAD_DIM)
        value_lanes.append(pl.ds(begin, HEAD_DIM))
        query = q[head]
        wide = query.astype(F32)
        keys = cache[0, :, key_lanes[at]]
        scores.append(lax.dot_general(query, keys, dims, preferred_element_type=F32))
        for step in range(STEPS):
            key = new[0, step : step + 1, key_lanes[at]].astype(F32)
            fresh[step].append(jnp.sum(wide * key, axis=1, keepdims=True))
    scores = jnp.where(allowed, jnp.concatenate(scores, axis=0) * scaling, NEGATIVE)
    highest = jnp.max(scores, axis=1, keepdims=True)
    for step in range(STEPS):
        shown = rep == 0 if step == 0 else second_step & (rep == 0)
        fresh[step] = jnp.where(shown, jnp.concatenate(fresh[step], axis=0) * scaling, NEGATIVE)
        highest = jnp.maximum(highest, fresh[step])
    some = highest > 0.5 * NEGATIVE
    highest = jnp.where(some, highest, 0.0)
    weight = jnp.exp(scores - highest)
    shares = [jnp.exp(score - highest) for score in fresh]
    totals = jnp.sum(weight, axis=1, keepdims=True) + shares[0] + shares[1]
    totals = jnp.where(some, totals, 1.0)
    logs = jnp.where(some, highest + jnp.log(totals), NEGATIVE)
    weight = weight.astype(BF16)
    for at in range(CORE_HEADS):
        rows = slice(at * ROWS, (at + 1) * ROWS)
        values = cache[0, :, value_lanes[at]]
        sums = jnp.dot(weight[rows], values, preferred_element_type=F32)
        for step in range(STEPS):
            value = new[0, step : step + 1, value_lanes[at]].astype(F32)
            sums += shares[step][rows].astype(BF16).astype(F32) * value
        out[at, :ROWS] = (sums / totals[rows]).astype(BF16)
        out[at, ROWS:] = pieces_tail(logs[rows])


def cache_attention(part, targets, lengths, stored, grouped, kv_cache, new_kv):
    return pl.pallas_call(
        functools.partial(cache_kernel, part),
        in_specs=[SMEM] * 2 + [VMEM] * 4,
        out_specs=VMEM,
        out_shape=jax.ShapeDtypeStruct((CORE_HEADS, PART, HEAD_DIM), BF16),
        compiler_params=pltpu.CompilerParams(vmem_limit_bytes=16 * MIB),
        cost_estimate=pl.CostEstimate(
            flops=1, bytes_accessed=1, transcendentals=0
        ),
        name="cache_attention",
    )(targets, lengths, stored.reshape(1, 1), grouped, kv_cache, new_kv)


def final_kernel(
    targets, rotary, own, right_keys, left_values, right_values, left_keys, grouped,
    cached_there, cached_here, out,
):
    scaling = HEAD_DIM ** (-0.5)
    dims = (((1,), (1,)), ((), ()))
    mine = own.shape[0] - 1
    first = lax.axis_index("rep") * CORE_HEADS
    prompt = prompt_of(targets, lax.axis_index("tp"))
    cosine, sine = rotary[0], rotary[1]
    rows = CORE_HEADS * STRETCH
    squares = own[mine, 0, rows:] + one_piece(right_keys[rows : rows + TAIL]) + one_piece(left_keys[rows : rows + TAIL])
    scale = token_column(lax.rsqrt(squares / D + EPSILON))
    scores, handed = [], []
    for head in range(CORE_HEADS):
        at = slice(head * STRETCH, (head + 1) * STRETCH)
        keys = own[mine, 0, at] + right_keys[at].astype(F32) + left_keys[at].astype(F32)
        values = own[mine, 1, at] + right_values[at].astype(F32) + left_values[at].astype(F32)
        keys = (keys * scale).astype(BF16).astype(F32)
        handed.append((values * scale).astype(BF16))
        keys = keys * cosine + pltpu.roll(keys, HEAD_DIM // 2, 1) * sine
        scores.append(
            lax.dot_general(
                grouped[first + head], keys.astype(BF16), dims, preferred_element_type=F32
            )
        )
    scores = jnp.concatenate(scores, axis=0) * scaling
    highest = jnp.max(scores, axis=1, keepdims=True)
    weight = jnp.exp(scores - highest)
    totals = jnp.sum(weight, axis=1, keepdims=True)
    weight = weight.astype(BF16)
    sums = [
        jnp.dot(weight[head * ROWS : (head + 1) * ROWS], handed[head], preferred_element_type=F32)
        for head in range(CORE_HEADS)
    ]
    sums = [jnp.concatenate(sums, axis=0) / totals]
    logs = [jnp.where(prompt >= 0, highest + jnp.log(totals), NEGATIVE)]
    for cached in (cached_there, cached_here):
        parts = [cached[head] for head in range(CORE_HEADS)]
        sums.append(jnp.concatenate([part[:ROWS].astype(F32) for part in parts], axis=0))
        logs.append(jnp.concatenate([tail_pieces(part[ROWS:]) for part in parts], axis=0))
    highest = functools.reduce(jnp.maximum, logs)
    shares = [jnp.exp(log - highest) for log in logs]
    total = functools.reduce(jnp.add, shares)
    joined = functools.reduce(jnp.add, [share * part for share, part in zip(shares, sums)])
    result = (joined / total).astype(BF16)
    for member in range(CORE_HEADS * GROUP):
        lanes = slice(member * HEAD_DIM, (member + 1) * HEAD_DIM)
        out[0, :, lanes] = result[member * STEPS : (member + 1) * STEPS]


def finish(targets, rotary, own, arrived, grouped, cached):
    width = CORE_HEADS * GROUP * HEAD_DIM
    return pl.pallas_call(
        final_kernel,
        in_specs=[SMEM] + [VMEM] * 9,
        out_specs=VMEM,
        out_shape=jax.ShapeDtypeStruct((1, STEPS, width), BF16),
        compiler_params=pltpu.CompilerParams(vmem_limit_bytes=16 * MIB),
        name="finish",
    )(targets, rotary, own, *arrived, grouped, *cached)


def rotary_turns():
    half = np.arange(HEAD_DIM // 2, dtype=np.float64) / (HEAD_DIM // 2)
    frequency = ROTARY_BASE ** (-np.concatenate([half, half]))
    angles = np.arange(STRETCH, dtype=np.float64)[:, None] * frequency
    return frequency.astype(np.float32), np.stack([np.cos(angles), np.sin(angles)]).astype(np.float32)


def per_device(
    stretch,
    norm_gain,
    kv_codes,
    scale_codes,
    outer_scales,
    prompt_lengths,
    target_rows,
    cache_lengths,
    kv_cache,
    queries,
    new_kv,
):
    count = lax.axis_size("tp")
    half = count // 2
    lines = stretch.transpose(1, 0, 2)
    gain = norm_gain.reshape(1, -1)
    ring = [ring_device(at, count) for at in range(count)]
    to_right = [(ring[at], ring[(at + 1) % count]) for at in range(count)]
    to_left = [(ring[at], ring[at - 1]) for at in range(count)]

    def pass_on(right, left):
        return lax.ppermute(right, "tp", to_right), lax.ppermute(left, "tp", to_left)

    swap = lambda array: lax.ppermute(array, "rep", [(0, 1), (1, 0)])
    other = swap(lines)
    weight = dequantize(kv_codes, scale_codes, outer_scales.T)
    frequency, turns = rotary_turns()
    start = (prompt_lengths - STRETCH).astype(F32)[:, None] * jnp.asarray(frequency)
    starts = jnp.stack([jnp.cos(start), jnp.sin(start)])

    features = [lines, other, gain]
    right, left = project_first(half, target_rows, *features, weight)
    targets, _ = lax.optimization_barrier((target_rows, left))
    arrived = [pass_on(right, left), []]

    for distance in range(half - 1, 0, -1):
        split = distance >= half - 2
        if split:
            terms, *kept = project_early(distance, targets, *features, weight)
        else:
            terms = project([distance, -distance], targets, *features, weight)
            kept = terms
        right, left = sends(1, terms, arrived[1])
        kept, right, left = lax.optimization_barrier((kept, right, left))
        targets, _, _ = lax.optimization_barrier((target_rows, right, left))
        arrived[1] = pass_on(right, left)
        terms = project_late(*kept, weight) if split else kept
        if distance == half - 1:
            prepared = prepare(targets, queries, starts, jnp.asarray(turns))
            terms, prepared = lax.optimization_barrier((terms, prepared))
            grouped, rotary = prepared
        if distance == 1:
            cached = cache_attention(
                0, targets, prompt_lengths, cache_lengths, grouped, kv_cache, new_kv
            )
            terms, cached = lax.optimization_barrier((terms, cached))
        right, left = sends(0, terms, arrived[0])
        targets, right = lax.optimization_barrier((target_rows, right))
        arrived[0] = pass_on(right, left)

    cached, _ = lax.optimization_barrier((cached, right))
    cached = [swap(cached)]
    terms = project([0], targets, *features, weight)
    cached.append(
        cache_attention(1, targets, prompt_lengths, cache_lengths, grouped, kv_cache, new_kv)
    )
    out = finish(target_rows, rotary, terms, [*arrived[0], *arrived[1]], grouped, cached)
    return lax.all_gather(out, "rep", axis=2, tiled=True)


def solution(mesh):
    in_specs = (
        P(None, ("grp", "rep"), "tp"),
        P("tp"),
        P("tp", None),
        P("tp", None),
        P("tp", None),
        P("grp"),
        P("grp"),
        P(("grp", "tp")),
        P(("grp", "tp"), "rep", None),
        P(("grp", "tp"), None, None),
        P(("grp", "tp"), None, None),
    )
    out_specs = P(("grp", "tp"), None, None)
    return jax.shard_map(
        per_device, mesh=mesh, in_specs=in_specs, out_specs=out_specs, check_vma=False
    )
```

```python
import functools
import math

import jax
import jax.numpy as jnp
import numpy as np
from jax import lax
from jax.experimental import pallas as pl
from jax.experimental.pallas import tpu as pltpu
from jax.sharding import PartitionSpec as P

D = 16384
HEADS = 128
KV_HEADS = 8
HEAD_DIM = 128
STRETCH = 192
STEPS = 2
QBLOCK = 64
GROUP = HEADS // KV_HEADS
ROWS = GROUP * STEPS
TAIL = 16
PART = ROWS + TAIL
CORE_HEADS = KV_HEADS // 2
NORMAL_FLOAT_LEVELS = [
    -1.0,
    -0.6961928009986877,
    -0.5250730514526367,
    -0.39491748809814453,
    -0.28444138169288635,
    -0.18477343022823334,
    -0.09105003625154495,
    0.0,
    0.07958029955625534,
    0.16093020141124725,
    0.24611230194568634,
    0.33791524171829224,
    0.44070982933044434,
    0.5626170039176941,
    0.7229568362236023,
    1.0,
]
ROTARY_BASE = 500000.0
EPSILON = 1e-05
NEGATIVE = -1e30
BF16 = jnp.bfloat16
F32 = jnp.float32
MIB = 1024 * 1024
VMEM = pl.BlockSpec(memory_space=pltpu.VMEM)
SMEM = pl.BlockSpec(memory_space=pltpu.SMEM)


def in_hbm(*arrays):
    return [pltpu.with_memory_space_constraint(array, pltpu.HBM) for array in arrays]


def ring_device(place, count):
    half = count // 2
    if isinstance(place, int):
        return 2 * place if place < half else 2 * (count - 1 - place) + 1
    return jnp.where(place < half, 2 * place, 2 * (count - 1 - place) + 1)


def owner_at(distance):
    count = lax.axis_size("tp")
    here = lax.axis_index("tp")
    place = jnp.where(here % 2 == 0, here // 2, count - 1 - here // 2)
    return ring_device((place + distance + count) % count, count)


def turned(column):
    rows = lax.broadcasted_iota(jnp.int32, (column.shape[0], 128), 0)
    lanes = lax.broadcasted_iota(jnp.int32, (column.shape[0], 128), 1)
    return jnp.sum(jnp.where(rows == lanes, column, 0.0), axis=0, keepdims=True)


def stood(row, count):
    rows = lax.broadcasted_iota(jnp.int32, (count, 128), 0)
    lanes = lax.broadcasted_iota(jnp.int32, (count, 128), 1)
    return jnp.sum(jnp.where(rows == lanes, row, 0.0), axis=1, keepdims=True)


def token_rows(column):
    at = lax.broadcasted_iota(jnp.int32, (8, 128), 0)
    ends = turned(column[128:])
    return jnp.where(at == 0, turned(column[:128]), jnp.where(at == 1, ends, 0.0))


def token_column(rows):
    return jnp.concatenate([stood(rows[0:1], 128), stood(rows[1:2], STRETCH - 128)], axis=0)


def two_pieces(rows):
    high = rows.astype(BF16).astype(F32)
    return jnp.concatenate([high, rows - high], axis=0).astype(BF16)


def one_piece(rows):
    rows = rows.astype(F32)
    return rows[:8] + rows[8:]


def pieces_tail(logs):
    row = turned(logs)
    high = row.astype(BF16).astype(F32)
    middle = (row - high).astype(BF16).astype(F32)
    low = row - high - middle
    at = lax.broadcasted_iota(jnp.int32, (TAIL, 128), 0)
    tail = jnp.where(at == 0, high, jnp.where(at == 1, middle, jnp.where(at == 2, low, 0.0)))
    return tail.astype(BF16)


def tail_pieces(tail):
    tail = tail.astype(F32)
    return stood(tail[0:1, :] + tail[1:2, :] + tail[2:3, :], ROWS)


CODE_ROWS = 128
AHEAD = 4


def block_leaves(scale):
    wide = jnp.broadcast_to(scale, (8, HEAD_DIM))
    leaves = [wide * jnp.float32(level) for level in NORMAL_FLOAT_LEVELS]
    return [jnp.concatenate([leaf, leaf], axis=0).astype(BF16) for leaf in leaves]


def selected(codes, leaves):
    codes = codes.astype(jnp.int16)
    masks = [(codes & (1 << bit)) != 0 for bit in range(4)]

    def node(bit, base):
        if bit < 0:
            return leaves[base]
        low = node(bit - 1, base)
        return jnp.where(masks[bit], node(bit - 1, base + (1 << bit)), low)

    return node(3, 0)


def block_scales(scales, outer, column):
    count = scales.shape[0]
    line = lax.broadcasted_iota(jnp.int32, outer.shape, 0)
    line = jnp.sum(jnp.where(line == column, outer, 0.0), axis=0, keepdims=True)
    rows = lax.broadcasted_iota(jnp.int32, (count, count), 0)
    lanes = lax.broadcasted_iota(jnp.int32, (count, count), 1)
    second = jnp.sum(jnp.where(rows == lanes, line, 0.0), axis=1, keepdims=True)
    return (scales.astype(F32) + 1.0) / 256.0 * second


def weights_kernel(
    codes, key_scales, value_scales, outer, out, key_codes, value_codes, scales, arrivals
):
    features, width = key_codes.shape
    depth = min(CODE_ROWS, features)
    blocks = features // depth
    columns = outer.shape[0] // 2
    rep = lax.axis_index("rep")

    def code_copies(block):
        rows = pl.ds(block * depth, depth)
        return [
            pltpu.make_async_copy(
                codes.at[rows, pl.ds(pl.multiple_of((2 * kind + rep) * width, width), width)],
                buffer.at[rows],
                arrivals.at[2 * block + kind],
            )
            for kind, buffer in enumerate((key_codes, value_codes))
        ]

    for block in range(min(AHEAD, blocks)):
        for copy in code_copies(block):
            copy.start()
    for at in range(CORE_HEADS):
        column = (rep * CORE_HEADS + at) // (KV_HEADS // columns)
        lanes = slice(at * HEAD_DIM, (at + 1) * HEAD_DIM)
        scales[2 * at] = block_scales(key_scales[:, lanes], outer[...], column)
        scales[2 * at + 1] = block_scales(value_scales[:, lanes], outer[...], columns + column)

    def body(step, _):
        row = pl.ds(step, 1)
        for at in range(CORE_HEADS):
            lanes = slice(at * HEAD_DIM, (at + 1) * HEAD_DIM)
            for kind, buffer in enumerate((key_codes, value_codes)):
                leaves = block_leaves(scales[2 * at + kind, row, :])
                for tile in range(QBLOCK // 16):
                    rows = pl.ds(pl.multiple_of(step * QBLOCK + 16 * tile, 16), 16)
                    half = slice(at % 2 * HEAD_DIM, (at % 2 + 1) * HEAD_DIM)
                    out[2 * kind + at // 2, rows, half] = selected(buffer[rows, lanes], leaves)
        return 0

    steps = depth // QBLOCK
    for block in range(blocks):
        for copy in code_copies(block):
            copy.wait()
        if block + AHEAD < blocks:
            for copy in code_copies(block + AHEAD):
                copy.start()
        lax.fori_loop(block * steps, (block + 1) * steps, body, 0)


def dequantize(codes, scales, outer):
    features = codes.shape[0]
    width = CORE_HEADS * HEAD_DIM
    blocks = features // min(CODE_ROWS, features)
    rep = lambda: lax.axis_index("rep")
    codes, scales, outer = in_hbm(codes, scales, outer)
    return pl.pallas_call(
        weights_kernel,
        grid=(1,),
        in_specs=[
            pl.BlockSpec(memory_space=pltpu.HBM),
            pl.BlockSpec((scales.shape[0], width), lambda k: (0, rep())),
            pl.BlockSpec((scales.shape[0], width), lambda k: (0, 2 + rep())),
            pl.BlockSpec(outer.shape, lambda k: (0, 0)),
        ],
        out_specs=VMEM,
        out_shape=jax.ShapeDtypeStruct((CORE_HEADS, features, 2 * HEAD_DIM), BF16),
        scratch_shapes=[
            pltpu.VMEM((features, width), jnp.int32),
            pltpu.VMEM((features, width), jnp.int32),
            pltpu.VMEM((2 * CORE_HEADS, scales.shape[0], HEAD_DIM), F32),
            pltpu.SemaphoreType.DMA((2 * blocks,)),
        ],
        compiler_params=pltpu.CompilerParams(vmem_limit_bytes=32 * MIB),
        cost_estimate=pl.CostEstimate(
            flops=32 * codes.size, bytes_accessed=codes.size * 2, transcendentals=0
        ),
        name="dequantize",
    )(codes, scales, scales, outer)


def prompt_of(targets, owner):
    prompt = jnp.int32(-1)
    for at in range(targets.shape[0]):
        prompt = jnp.where(targets[at] == owner, at, prompt)
    return prompt


def with_lines(targets, distance, own, other, gain, line, total, some, none):
    per_rep = own.shape[0]
    prompt = prompt_of(targets, owner_at(distance))
    at = lax.rem(jnp.maximum(prompt, 0), per_rep)
    is_own = prompt // per_rep == lax.axis_index("rep")
    width = min(512, line.shape[1])

    def scale(x):
        sums = jnp.zeros((STRETCH, 1), F32)
        for begin in range(0, line.shape[1], width):
            lanes = slice(begin, begin + width)
            wide = x[at, :, lanes].astype(F32)
            line[:, lanes] = (wide * gain[:, lanes]).astype(BF16)
            sums += jnp.sum(wide * wide, axis=1, keepdims=True)
        total[...] = token_rows(sums)

    pl.when((prompt >= 0) & is_own)(lambda: scale(own))
    pl.when((prompt >= 0) & jnp.logical_not(is_own))(lambda: scale(other))
    pl.when(prompt >= 0)(some)
    pl.when(prompt < 0)(none)


def products(line, weight, kind):
    for pair in range(2):
        product = jnp.dot(line[...], weight[2 * kind + pair], preferred_element_type=F32)
        for at in range(2):
            begin = (2 * pair + at) * STRETCH
            yield slice(begin, begin + STRETCH), product[:, at * HEAD_DIM : (at + 1) * HEAD_DIM]


def line_scratch(x):
    return [pltpu.VMEM(x.shape[1:], BF16), pltpu.VMEM((8, 128), F32)]


def first_kernel(distance, targets, own, other, gain, weight, right, left, line, total):
    def some():
        for kind, out in enumerate((right, left)):
            for rows, product in products(line, weight, kind):
                out[rows] = product.astype(BF16)
        right[CORE_HEADS * STRETCH :] = two_pieces(total[...])

    def none():
        right[...] = jnp.zeros(right.shape, BF16)
        left[...] = jnp.zeros(left.shape, BF16)

    with_lines(targets, distance, own, other, gain, line, total, some, none)


def project_first(distance, targets, own, other, gain, weight):
    rows = CORE_HEADS * STRETCH
    return pl.pallas_call(
        functools.partial(first_kernel, distance),
        in_specs=[SMEM] + [VMEM] * 4,
        out_specs=[VMEM] * 2,
        out_shape=[
            jax.ShapeDtypeStruct((rows + TAIL, HEAD_DIM), BF16),
            jax.ShapeDtypeStruct((rows, HEAD_DIM), BF16),
        ],
        scratch_shapes=line_scratch(own),
        compiler_params=pltpu.CompilerParams(vmem_limit_bytes=24 * MIB),
        cost_estimate=pl.CostEstimate(
            flops=STRETCH * weight.size * 2, bytes_accessed=weight.size, transcendentals=0
        ),
        name="project_first",
    )(targets, own, other, gain, weight)


def project_kernel(distances, targets, own, other, gain, weight, out, line, total):
    for item, distance in enumerate(distances):

        def some(item=item):
            for kind in range(2):
                for rows, product in products(line, weight, kind):
                    out[item, kind, rows] = product
            out[item, 0, CORE_HEADS * STRETCH :] = total[...]

        def none(item=item):
            out[item] = jnp.zeros(out.shape[1:], F32)

        with_lines(targets, distance, own, other, gain, line, total, some, none)


def project(distances, targets, own, other, gain, weight):
    return pl.pallas_call(
        functools.partial(project_kernel, distances),
        in_specs=[SMEM] + [VMEM] * 4,
        out_specs=VMEM,
        out_shape=jax.ShapeDtypeStruct((len(distances), 2, 4 * STRETCH + 8, HEAD_DIM), F32),
        scratch_shapes=line_scratch(own),
        compiler_params=pltpu.CompilerParams(vmem_limit_bytes=24 * MIB),
        cost_estimate=pl.CostEstimate(
            flops=len(distances) * STRETCH * weight.size,
            bytes_accessed=weight.size,
            transcendentals=0,
        ),
        name="project",
    )(targets, own, other, gain, weight)


def early_kernel(distance, targets, own, other, gain, weight, out, lines, totals):
    for item in range(2):
        line, total, kind = lines.at[item], totals.at[item], 1 - item

        def some(item=item, line=line, total=total, kind=kind):
            for rows, product in products(line, weight, kind):
                out[item, 0, rows] = product
            if kind == 0:
                out[item, 0, CORE_HEADS * STRETCH :] = total[...]

        def none(item=item, line=line, total=total):
            out[item] = jnp.zeros(out.shape[1:], F32)
            line[...] = jnp.zeros(line.shape, BF16)
            total[...] = jnp.zeros(total.shape, F32)

        towards = distance * (1 - 2 * item)
        with_lines(targets, towards, own, other, gain, line, total, some, none)


def late_kernel(lines, totals, weight, out):
    for item in range(2):
        for rows, product in products(lines.at[item], weight, item):
            out[item, 0, rows] = product
    out[0, 0, CORE_HEADS * STRETCH :] = totals[0]


def project_early(distance, targets, own, other, gain, weight):
    return pl.pallas_call(
        functools.partial(early_kernel, distance),
        in_specs=[SMEM] + [VMEM] * 4,
        out_specs=[VMEM] * 3,
        out_shape=[
            jax.ShapeDtypeStruct((2, 1, CORE_HEADS * STRETCH + 8, HEAD_DIM), F32),
            jax.ShapeDtypeStruct((2,) + own.shape[1:], BF16),
            jax.ShapeDtypeStruct((2, 8, 128), F32),
        ],
        compiler_params=pltpu.CompilerParams(vmem_limit_bytes=24 * MIB),
        cost_estimate=pl.CostEstimate(
            flops=STRETCH * weight.size, bytes_accessed=weight.size, transcendentals=0
        ),
        name="project_early",
    )(targets, own, other, gain, weight)


def project_late(lines, totals, weight):
    return pl.pallas_call(
        late_kernel,
        in_specs=[VMEM] * 3,
        out_specs=VMEM,
        out_shape=jax.ShapeDtypeStruct((2, 1, CORE_HEADS * STRETCH + 8, HEAD_DIM), F32),
        compiler_params=pltpu.CompilerParams(vmem_limit_bytes=24 * MIB),
        cost_estimate=pl.CostEstimate(
            flops=STRETCH * weight.size, bytes_accessed=weight.size, transcendentals=0
        ),
        name="project_late",
    )(lines, totals, weight)


def send_kernel(half, terms, *refs):
    *arrived, to_right, to_left = refs
    rows = CORE_HEADS * STRETCH
    for item, out in enumerate((to_right, to_left)):
        kind = (half + item) % 2
        total = terms[item, kind % terms.shape[1], :rows]
        if arrived:
            total += arrived[item][:rows].astype(F32)
        out[:rows] = total.astype(BF16)
        if kind == 0:
            squares = terms[item, 0, rows:]
            if arrived:
                squares += one_piece(arrived[item][rows : rows + TAIL])
            out[rows : rows + TAIL] = two_pieces(squares)
        spare = rows + (TAIL if kind == 0 else 0)
        if spare < out.shape[0]:
            out[spare:] = jnp.zeros((out.shape[0] - spare, HEAD_DIM), BF16)


def sends(half, terms, arrived):
    rows = CORE_HEADS * STRETCH
    shapes = [jax.ShapeDtypeStruct((rows + TAIL, HEAD_DIM), BF16)] * 2
    return pl.pallas_call(
        functools.partial(send_kernel, half),
        in_specs=[VMEM] * (1 + len(arrived)),
        out_specs=[VMEM] * 2,
        out_shape=shapes,
        compiler_params=pltpu.CompilerParams(vmem_limit_bytes=16 * MIB),
        name="sends",
    )(terms, *arrived)


def prepare_kernel(targets, queries, starts, turns, grouped, rotary):
    for head in range(KV_HEADS):
        for member in range(GROUP):
            begin = (head * GROUP + member) * HEAD_DIM
            rows = slice(member * STEPS, (member + 1) * STEPS)
            grouped[head, rows] = queries[0, :, begin : begin + HEAD_DIM]
    row = pl.ds(jnp.maximum(prompt_of(targets, lax.axis_index("tp")), 0), 1)
    cosine, sine = starts[0, row, :], starts[1, row, :]
    lane = lax.broadcasted_iota(jnp.int32, turns.shape[1:], 1)
    rotary[0] = turns[0] * cosine - turns[1] * sine
    sine = turns[1] * cosine + turns[0] * sine
    rotary[1] = jnp.where(lane < HEAD_DIM // 2, -sine, sine)


def prepare(targets, queries, starts, turns):
    return pl.pallas_call(
        prepare_kernel,
        in_specs=[SMEM] + [VMEM] * 3,
        out_specs=[VMEM] * 2,
        out_shape=[
            jax.ShapeDtypeStruct((KV_HEADS, ROWS, HEAD_DIM), BF16),
            jax.ShapeDtypeStruct(turns.shape, F32),
        ],
        compiler_params=pltpu.CompilerParams(vmem_limit_bytes=16 * MIB),
        name="prepare",
    )(targets, queries, starts, turns)


def cache_kernel(part, targets, lengths, stored, q, cache, new, out):
    scaling = HEAD_DIM ** (-0.5)
    dims = (((1,), (1,)), ((), ()))
    here = lax.axis_index("tp")
    rep = lax.axis_index("rep")
    length = cache.shape[1]
    prompt = prompt_of(targets, here)
    handed = lengths[jnp.maximum(prompt, 0)] - STRETCH
    span = jnp.where(prompt >= 0, handed, stored[0]) - rep * length
    count = CORE_HEADS * ROWS
    allowed = lax.broadcasted_iota(jnp.int32, (count, length), 1) < span
    second_step = lax.broadcasted_iota(jnp.int32, (count, 1), 0) % STEPS == 1
    scores, fresh, key_lanes, value_lanes = [], [[], []], [], []
    for at in range(CORE_HEADS):
        head = (rep if part == 1 else 1 - rep) * CORE_HEADS + at
        key_lanes.append(pl.ds(pl.multiple_of(head * HEAD_DIM, HEAD_DIM), HEAD_DIM))
        begin = pl.multiple_of((KV_HEADS + head) * HEAD_DIM, HEAD_DIM)
        value_lanes.append(pl.ds(begin, HEAD_DIM))
        query = q[head]
        wide = query.astype(F32)
        keys = cache[0, :, key_lanes[at]]
        scores.append(lax.dot_general(query, keys, dims, preferred_element_type=F32))
        for step in range(STEPS):
            key = new[0, step : step + 1, key_lanes[at]].astype(F32)
            fresh[step].append(jnp.sum(wide * key, axis=1, keepdims=True))
    scores = jnp.where(allowed, jnp.concatenate(scores, axis=0) * scaling, NEGATIVE)
    highest = jnp.max(scores, axis=1, keepdims=True)
    for step in range(STEPS):
        shown = rep == 0 if step == 0 else second_step & (rep == 0)
        fresh[step] = jnp.where(shown, jnp.concatenate(fresh[step], axis=0) * scaling, NEGATIVE)
        highest = jnp.maximum(highest, fresh[step])
    some = highest > 0.5 * NEGATIVE
    highest = jnp.where(some, highest, 0.0)
    weight = jnp.exp(scores - highest)
    shares = [jnp.exp(score - highest) for score in fresh]
    totals = jnp.sum(weight, axis=1, keepdims=True) + shares[0] + shares[1]
    totals = jnp.where(some, totals, 1.0)
    logs = jnp.where(some, highest + jnp.log(totals), NEGATIVE)
    weight = weight.astype(BF16)
    for at in range(CORE_HEADS):
        rows = slice(at * ROWS, (at + 1) * ROWS)
        values = cache[0, :, value_lanes[at]]
        sums = jnp.dot(weight[rows], values, preferred_element_type=F32)
        for step in range(STEPS):
            value = new[0, step : step + 1, value_lanes[at]].astype(F32)
            sums += shares[step][rows].astype(BF16).astype(F32) * value
        out[at, :ROWS] = (sums / totals[rows]).astype(BF16)
        out[at, ROWS:] = pieces_tail(logs[rows])


def cache_attention(part, targets, lengths, stored, grouped, kv_cache, new_kv):
    return pl.pallas_call(
        functools.partial(cache_kernel, part),
        in_specs=[SMEM] * 3 + [VMEM] * 3,
        out_specs=VMEM,
        out_shape=jax.ShapeDtypeStruct((CORE_HEADS, PART, HEAD_DIM), BF16),
        compiler_params=pltpu.CompilerParams(vmem_limit_bytes=16 * MIB),
        cost_estimate=pl.CostEstimate(
            flops=1, bytes_accessed=1, transcendentals=0
        ),
        name="cache_attention",
    )(targets, lengths, stored, grouped, kv_cache, new_kv)


def final_kernel(
    targets, rotary, own, right_keys, left_values, right_values, left_keys, grouped,
    cached_there, cached_here, out,
):
    scaling = HEAD_DIM ** (-0.5)
    dims = (((1,), (1,)), ((), ()))
    mine = own.shape[0] - 1
    first = lax.axis_index("rep") * CORE_HEADS
    prompt = prompt_of(targets, lax.axis_index("tp"))
    cosine, sine = rotary[0], rotary[1]
    rows = CORE_HEADS * STRETCH
    squares = own[mine, 0, rows:] + one_piece(right_keys[rows : rows + TAIL]) + one_piece(left_keys[rows : rows + TAIL])
    scale = token_column(lax.rsqrt(squares / D + EPSILON))
    scores, handed = [], []
    for head in range(CORE_HEADS):
        at = slice(head * STRETCH, (head + 1) * STRETCH)
        keys = own[mine, 0, at] + right_keys[at].astype(F32) + left_keys[at].astype(F32)
        values = own[mine, 1, at] + right_values[at].astype(F32) + left_values[at].astype(F32)
        keys = (keys * scale).astype(BF16).astype(F32)
        handed.append((values * scale).astype(BF16))
        keys = keys * cosine + pltpu.roll(keys, HEAD_DIM // 2, 1) * sine
        scores.append(
            lax.dot_general(
                grouped[first + head], keys.astype(BF16), dims, preferred_element_type=F32
            )
        )
    scores = jnp.concatenate(scores, axis=0) * scaling
    highest = jnp.max(scores, axis=1, keepdims=True)
    weight = jnp.exp(scores - highest)
    totals = jnp.sum(weight, axis=1, keepdims=True)
    weight = weight.astype(BF16)
    sums = [
        jnp.dot(weight[head * ROWS : (head + 1) * ROWS], handed[head], preferred_element_type=F32)
        for head in range(CORE_HEADS)
    ]
    sums = [jnp.concatenate(sums, axis=0) / totals]
    logs = [jnp.where(prompt >= 0, highest + jnp.log(totals), NEGATIVE)]
    for cached in (cached_there, cached_here):
        parts = [cached[head] for head in range(CORE_HEADS)]
        sums.append(jnp.concatenate([part[:ROWS].astype(F32) for part in parts], axis=0))
        logs.append(jnp.concatenate([tail_pieces(part[ROWS:]) for part in parts], axis=0))
    highest = functools.reduce(jnp.maximum, logs)
    shares = [jnp.exp(log - highest) for log in logs]
    total = functools.reduce(jnp.add, shares)
    joined = functools.reduce(jnp.add, [share * part for share, part in zip(shares, sums)])
    result = (joined / total).astype(BF16)
    for member in range(CORE_HEADS * GROUP):
        lanes = slice(member * HEAD_DIM, (member + 1) * HEAD_DIM)
        out[0, :, lanes] = result[member * STEPS : (member + 1) * STEPS]


def finish(targets, rotary, own, arrived, grouped, cached):
    width = CORE_HEADS * GROUP * HEAD_DIM
    return pl.pallas_call(
        final_kernel,
        in_specs=[SMEM] + [VMEM] * 9,
        out_specs=VMEM,
        out_shape=jax.ShapeDtypeStruct((1, STEPS, width), BF16),
        compiler_params=pltpu.CompilerParams(vmem_limit_bytes=16 * MIB),
        name="finish",
    )(targets, rotary, own, *arrived, grouped, *cached)


def rotary_turns():
    half = np.arange(HEAD_DIM // 2, dtype=np.float64) / (HEAD_DIM // 2)
    frequency = ROTARY_BASE ** (-np.concatenate([half, half]))
    angles = np.arange(STRETCH, dtype=np.float64)[:, None] * frequency
    return frequency.astype(np.float32), np.stack([np.cos(angles), np.sin(angles)]).astype(np.float32)


def per_device(
    stretch,
    norm_gain,
    kv_codes,
    scale_codes,
    outer_scales,
    prompt_lengths,
    target_rows,
    cache_lengths,
    kv_cache,
    queries,
    new_kv,
):
    count = lax.axis_size("tp")
    half = count // 2
    lines = stretch.transpose(1, 0, 2)
    gain = norm_gain.reshape(1, -1)
    ring = [ring_device(at, count) for at in range(count)]
    to_right = [(ring[at], ring[(at + 1) % count]) for at in range(count)]
    to_left = [(ring[at], ring[at - 1]) for at in range(count)]

    def pass_on(right, left):
        return lax.ppermute(right, "tp", to_right), lax.ppermute(left, "tp", to_left)

    swap = lambda array: lax.ppermute(array, "rep", [(0, 1), (1, 0)])
    other = swap(lines)
    weight = dequantize(kv_codes, scale_codes, outer_scales.T)
    frequency, turns = rotary_turns()
    start = (prompt_lengths - STRETCH).astype(F32)[:, None] * jnp.asarray(frequency)
    starts = jnp.stack([jnp.cos(start), jnp.sin(start)])

    features = [lines, other, gain]
    right, left = project_first(half, target_rows, *features, weight)
    targets, _ = lax.optimization_barrier((target_rows, left))
    arrived = [pass_on(right, left), []]

    for distance in range(half - 1, 0, -1):
        if distance == half - 1:
            terms, *kept = project_early(distance, targets, *features, weight)
        else:
            terms = project([distance, -distance], targets, *features, weight)
            kept = terms
        right, left = sends(1, terms, arrived[1])
        kept, right, left = lax.optimization_barrier((kept, right, left))
        targets, _ = lax.optimization_barrier((target_rows, left))
        arrived[1] = pass_on(right, left)
        terms = kept
        if distance == half - 1:
            prepared = prepare(targets, queries, starts, jnp.asarray(turns))
            terms = project_late(*kept, weight)
            terms, prepared = lax.optimization_barrier((terms, prepared))
            grouped, rotary = prepared
        if distance == max(1, half - 2):
            cached = cache_attention(
                0, targets, prompt_lengths, cache_lengths, grouped, kv_cache, new_kv
            )
            terms, cached = lax.optimization_barrier((terms, cached))
        right, left = sends(0, terms, arrived[0])
        targets, right = lax.optimization_barrier((target_rows, right))
        arrived[0] = pass_on(right, left)

    cached, _ = lax.optimization_barrier((cached, right))
    cached = [swap(cached)]
    terms = project([0], targets, *features, weight)
    cached.append(
        cache_attention(1, targets, prompt_lengths, cache_lengths, grouped, kv_cache, new_kv)
    )
    out = finish(target_rows, rotary, terms, [*arrived[0], *arrived[1]], grouped, cached)
    return lax.all_gather(out, "rep", axis=2, tiled=True)


def solution(mesh):
    in_specs = (
        P(None, ("grp", "rep"), "tp"),
        P("tp"),
        P("tp", None),
        P("tp", None),
        P("tp", None),
        P("grp"),
        P("grp"),
        P(("grp", "tp")),
        P(("grp", "tp"), "rep", None),
        P(("grp", "tp"), None, None),
        P(("grp", "tp"), None, None),
    )
    out_specs = P(("grp", "tp"), None, None)
    return jax.shard_map(
        per_device, mesh=mesh, in_specs=in_specs, out_specs=out_specs, check_vma=False
    )
```

```python
import functools
import math

import jax
import jax.numpy as jnp
import numpy as np
from jax import lax
from jax.experimental import pallas as pl
from jax.experimental.pallas import tpu as pltpu
from jax.sharding import PartitionSpec as P

D = 16384
HEADS = 128
KV_HEADS = 8
HEAD_DIM = 128
STRETCH = 192
STEPS = 2
QBLOCK = 64
GROUP = HEADS // KV_HEADS
ROWS = GROUP * STEPS
TAIL = 16
PART = ROWS + TAIL
CORE_HEADS = KV_HEADS // 2
NORMAL_FLOAT_LEVELS = [
    -1.0,
    -0.6961928009986877,
    -0.5250730514526367,
    -0.39491748809814453,
    -0.28444138169288635,
    -0.18477343022823334,
    -0.09105003625154495,
    0.0,
    0.07958029955625534,
    0.16093020141124725,
    0.24611230194568634,
    0.33791524171829224,
    0.44070982933044434,
    0.5626170039176941,
    0.7229568362236023,
    1.0,
]
ROTARY_BASE = 500000.0
EPSILON = 1e-05
NEGATIVE = -1e30
BF16 = jnp.bfloat16
F32 = jnp.float32
MIB = 1024 * 1024
VMEM = pl.BlockSpec(memory_space=pltpu.VMEM)
SMEM = pl.BlockSpec(memory_space=pltpu.SMEM)


def in_hbm(*arrays):
    return [pltpu.with_memory_space_constraint(array, pltpu.HBM) for array in arrays]


def ring_device(place, count):
    half = count // 2
    if isinstance(place, int):
        return 2 * place if place < half else 2 * (count - 1 - place) + 1
    return jnp.where(place < half, 2 * place, 2 * (count - 1 - place) + 1)


def owner_at(distance):
    count = lax.axis_size("tp")
    here = lax.axis_index("tp")
    place = jnp.where(here % 2 == 0, here // 2, count - 1 - here // 2)
    return ring_device((place + distance + count) % count, count)


def turned(column):
    rows = lax.broadcasted_iota(jnp.int32, (column.shape[0], 128), 0)
    lanes = lax.broadcasted_iota(jnp.int32, (column.shape[0], 128), 1)
    return jnp.sum(jnp.where(rows == lanes, column, 0.0), axis=0, keepdims=True)


def stood(row, count):
    rows = lax.broadcasted_iota(jnp.int32, (count, 128), 0)
    lanes = lax.broadcasted_iota(jnp.int32, (count, 128), 1)
    return jnp.sum(jnp.where(rows == lanes, row, 0.0), axis=1, keepdims=True)


def token_rows(column):
    at = lax.broadcasted_iota(jnp.int32, (8, 128), 0)
    ends = turned(column[128:])
    return jnp.where(at == 0, turned(column[:128]), jnp.where(at == 1, ends, 0.0))


def token_column(rows):
    return jnp.concatenate([stood(rows[0:1], 128), stood(rows[1:2], STRETCH - 128)], axis=0)


def two_pieces(rows):
    high = rows.astype(BF16).astype(F32)
    return jnp.concatenate([high, rows - high], axis=0).astype(BF16)


def one_piece(rows):
    rows = rows.astype(F32)
    return rows[:8] + rows[8:]


def pieces_tail(logs):
    row = turned(logs)
    high = row.astype(BF16).astype(F32)
    middle = (row - high).astype(BF16).astype(F32)
    low = row - high - middle
    at = lax.broadcasted_iota(jnp.int32, (TAIL, 128), 0)
    tail = jnp.where(at == 0, high, jnp.where(at == 1, middle, jnp.where(at == 2, low, 0.0)))
    return tail.astype(BF16)


def tail_pieces(tail):
    tail = tail.astype(F32)
    return stood(tail[0:1, :] + tail[1:2, :] + tail[2:3, :], ROWS)


CODE_ROWS = 128


def block_leaves(scale):
    wide = jnp.broadcast_to(scale, (8, HEAD_DIM))
    leaves = [wide * jnp.float32(level) for level in NORMAL_FLOAT_LEVELS]
    return [jnp.concatenate([leaf, leaf], axis=0).astype(BF16) for leaf in leaves]


def selected(codes, leaves):
    codes = codes.astype(jnp.int16)
    masks = [(codes & (1 << bit)) != 0 for bit in range(3)] + [codes > 7]

    def node(bit, base):
        if bit < 0:
            return leaves[base]
        low = node(bit - 1, base)
        return jnp.where(masks[bit], node(bit - 1, base + (1 << bit)), low)

    return node(3, 0)


def block_scales(scales, outer, column):
    count = scales.shape[0]
    line = lax.broadcasted_iota(jnp.int32, outer.shape, 0)
    line = jnp.sum(jnp.where(line == column, outer, 0.0), axis=0, keepdims=True)
    rows = lax.broadcasted_iota(jnp.int32, (count, count), 0)
    lanes = lax.broadcasted_iota(jnp.int32, (count, count), 1)
    second = jnp.sum(jnp.where(rows == lanes, line, 0.0), axis=1, keepdims=True)
    return (scales.astype(F32) + 1.0) / 256.0 * second


def weights_kernel(
    codes, key_scales, value_scales, outer, out, key_codes, value_codes, scales, arrivals
):
    features, width = key_codes.shape
    depth = min(CODE_ROWS, features)
    blocks = features // depth
    columns = outer.shape[0] // 2
    rep = lax.axis_index("rep")

    def code_copies(block):
        rows = pl.ds(block * depth, depth)
        return [
            pltpu.make_async_copy(
                codes.at[rows, pl.ds(pl.multiple_of((2 * kind + rep) * width, width), width)],
                buffer.at[rows],
                arrivals.at[2 * block + kind],
            )
            for kind, buffer in enumerate((key_codes, value_codes))
        ]

    for block in range(blocks):
        for copy in code_copies(block):
            copy.start()
    for at in range(CORE_HEADS):
        column = (rep * CORE_HEADS + at) // (KV_HEADS // columns)
        lanes = slice(at * HEAD_DIM, (at + 1) * HEAD_DIM)
        scales[2 * at] = block_scales(key_scales[:, lanes], outer[...], column)
        scales[2 * at + 1] = block_scales(value_scales[:, lanes], outer[...], columns + column)

    def body(step, _):
        row = pl.ds(step, 1)
        for at in range(CORE_HEADS):
            lanes = slice(at * HEAD_DIM, (at + 1) * HEAD_DIM)
            for kind, buffer in enumerate((key_codes, value_codes)):
                leaves = block_leaves(scales[2 * at + kind, row, :])
                for tile in range(QBLOCK // 16):
                    rows = pl.ds(pl.multiple_of(step * QBLOCK + 16 * tile, 16), 16)
                    half = slice(at % 2 * HEAD_DIM, (at % 2 + 1) * HEAD_DIM)
                    out[2 * kind + at // 2, rows, half] = selected(buffer[rows, lanes], leaves)
        return 0

    steps = depth // QBLOCK
    for block in range(blocks):
        for copy in code_copies(block):
            copy.wait()
        lax.fori_loop(block * steps, (block + 1) * steps, body, 0, unroll=2)


def dequantize(codes, scales, outer):
    features = codes.shape[0]
    width = CORE_HEADS * HEAD_DIM
    blocks = features // min(CODE_ROWS, features)
    rep = lambda: lax.axis_index("rep")
    codes, scales, outer = in_hbm(codes, scales, outer)
    return pl.pallas_call(
        weights_kernel,
        grid=(1,),
        in_specs=[
            pl.BlockSpec(memory_space=pltpu.HBM),
            pl.BlockSpec((scales.shape[0], width), lambda k: (0, rep())),
            pl.BlockSpec((scales.shape[0], width), lambda k: (0, 2 + rep())),
            pl.BlockSpec(outer.shape, lambda k: (0, 0)),
        ],
        out_specs=VMEM,
        out_shape=jax.ShapeDtypeStruct((CORE_HEADS, features, 2 * HEAD_DIM), BF16),
        scratch_shapes=[
            pltpu.VMEM((features, width), jnp.int32),
            pltpu.VMEM((features, width), jnp.int32),
            pltpu.VMEM((2 * CORE_HEADS, scales.shape[0], HEAD_DIM), F32),
            pltpu.SemaphoreType.DMA((2 * blocks,)),
        ],
        compiler_params=pltpu.CompilerParams(vmem_limit_bytes=32 * MIB),
        cost_estimate=pl.CostEstimate(
            flops=32 * codes.size, bytes_accessed=codes.size * 2, transcendentals=0
        ),
        name="dequantize",
    )(codes, scales, scales, outer)


def prompt_of(targets, owner):
    prompt = jnp.int32(-1)
    for at in range(targets.shape[0]):
        prompt = jnp.where(targets[at] == owner, at, prompt)
    return prompt


def with_lines(targets, distance, own, other, gain, line, total, some, none):
    per_rep = own.shape[0]
    prompt = prompt_of(targets, owner_at(distance))
    at = lax.rem(jnp.maximum(prompt, 0), per_rep)
    is_own = prompt // per_rep == lax.axis_index("rep")
    width = min(512, line.shape[1])

    def scale(x):
        sums = jnp.zeros((STRETCH, 1), F32)
        for begin in range(0, line.shape[1], width):
            lanes = slice(begin, begin + width)
            wide = x[at, :, lanes].astype(F32)
            line[:, lanes] = (wide * gain[:, lanes]).astype(BF16)
            sums += jnp.sum(wide * wide, axis=1, keepdims=True)
        total[...] = token_rows(sums)

    pl.when((prompt >= 0) & is_own)(lambda: scale(own))
    pl.when((prompt >= 0) & jnp.logical_not(is_own))(lambda: scale(other))
    pl.when(prompt >= 0)(some)
    pl.when(prompt < 0)(none)


def products(line, weight, kind):
    for pair in range(2):
        product = jnp.dot(line[...], weight[2 * kind + pair], preferred_element_type=F32)
        for at in range(2):
            begin = (2 * pair + at) * STRETCH
            yield slice(begin, begin + STRETCH), product[:, at * HEAD_DIM : (at + 1) * HEAD_DIM]


def line_scratch(x):
    return [pltpu.VMEM(x.shape[1:], BF16), pltpu.VMEM((8, 128), F32)]


def first_kernel(distance, targets, own, other, gain, weight, right, left, line, total):
    def some():
        for kind, out in enumerate((right, left)):
            for rows, product in products(line, weight, kind):
                out[rows] = product.astype(BF16)
        right[CORE_HEADS * STRETCH :] = two_pieces(total[...])

    def none():
        right[...] = jnp.zeros(right.shape, BF16)
        left[...] = jnp.zeros(left.shape, BF16)

    with_lines(targets, distance, own, other, gain, line, total, some, none)


def project_first(distance, targets, own, other, gain, weight):
    rows = CORE_HEADS * STRETCH
    return pl.pallas_call(
        functools.partial(first_kernel, distance),
        in_specs=[SMEM] + [VMEM] * 4,
        out_specs=[VMEM] * 2,
        out_shape=[
            jax.ShapeDtypeStruct((rows + TAIL, HEAD_DIM), BF16),
            jax.ShapeDtypeStruct((rows, HEAD_DIM), BF16),
        ],
        scratch_shapes=line_scratch(own),
        compiler_params=pltpu.CompilerParams(vmem_limit_bytes=24 * MIB),
        cost_estimate=pl.CostEstimate(
            flops=STRETCH * weight.size * 2, bytes_accessed=weight.size, transcendentals=0
        ),
        name="project_first",
    )(targets, own, other, gain, weight)


def project_kernel(distances, targets, own, other, gain, weight, out, line, total):
    for item, distance in enumerate(distances):

        def some(item=item):
            for kind in range(2):
                for rows, product in products(line, weight, kind):
                    out[item, kind, rows] = product
            out[item, 0, CORE_HEADS * STRETCH :] = total[...]

        def none(item=item):
            out[item] = jnp.zeros(out.shape[1:], F32)

        with_lines(targets, distance, own, other, gain, line, total, some, none)


def project(distances, targets, own, other, gain, weight):
    return pl.pallas_call(
        functools.partial(project_kernel, distances),
        in_specs=[SMEM] + [VMEM] * 4,
        out_specs=VMEM,
        out_shape=jax.ShapeDtypeStruct((len(distances), 2, 4 * STRETCH + 8, HEAD_DIM), F32),
        scratch_shapes=line_scratch(own),
        compiler_params=pltpu.CompilerParams(vmem_limit_bytes=24 * MIB),
        cost_estimate=pl.CostEstimate(
            flops=len(distances) * STRETCH * weight.size,
            bytes_accessed=weight.size,
            transcendentals=0,
        ),
        name="project",
    )(targets, own, other, gain, weight)


def early_kernel(distance, targets, own, other, gain, weight, out, lines, totals):
    for item in range(2):
        line, total, kind = lines.at[item], totals.at[item], 1 - item

        def some(item=item, line=line, total=total, kind=kind):
            for rows, product in products(line, weight, kind):
                out[item, 0, rows] = product
            if kind == 0:
                out[item, 0, CORE_HEADS * STRETCH :] = total[...]

        def none(item=item, line=line, total=total):
            out[item] = jnp.zeros(out.shape[1:], F32)
            line[...] = jnp.zeros(line.shape, BF16)
            total[...] = jnp.zeros(total.shape, F32)

        towards = distance * (1 - 2 * item)
        with_lines(targets, towards, own, other, gain, line, total, some, none)


def late_kernel(lines, totals, weight, out):
    for item in range(2):
        for rows, product in products(lines.at[item], weight, item):
            out[item, 0, rows] = product
    out[0, 0, CORE_HEADS * STRETCH :] = totals[0]


def project_early(distance, targets, own, other, gain, weight):
    return pl.pallas_call(
        functools.partial(early_kernel, distance),
        in_specs=[SMEM] + [VMEM] * 4,
        out_specs=[VMEM] * 3,
        out_shape=[
            jax.ShapeDtypeStruct((2, 1, CORE_HEADS * STRETCH + 8, HEAD_DIM), F32),
            jax.ShapeDtypeStruct((2,) + own.shape[1:], BF16),
            jax.ShapeDtypeStruct((2, 8, 128), F32),
        ],
        compiler_params=pltpu.CompilerParams(vmem_limit_bytes=24 * MIB),
        cost_estimate=pl.CostEstimate(
            flops=STRETCH * weight.size, bytes_accessed=weight.size, transcendentals=0
        ),
        name="project_early",
    )(targets, own, other, gain, weight)


def project_late(lines, totals, weight):
    return pl.pallas_call(
        late_kernel,
        in_specs=[VMEM] * 3,
        out_specs=VMEM,
        out_shape=jax.ShapeDtypeStruct((2, 1, CORE_HEADS * STRETCH + 8, HEAD_DIM), F32),
        compiler_params=pltpu.CompilerParams(vmem_limit_bytes=24 * MIB),
        cost_estimate=pl.CostEstimate(
            flops=STRETCH * weight.size, bytes_accessed=weight.size, transcendentals=0
        ),
        name="project_late",
    )(lines, totals, weight)


def send_kernel(half, terms, *refs):
    *arrived, to_right, to_left = refs
    rows = CORE_HEADS * STRETCH
    for item, out in enumerate((to_right, to_left)):
        kind = (half + item) % 2
        total = terms[item, kind % terms.shape[1], :rows]
        if arrived:
            total += arrived[item][:rows].astype(F32)
        out[:rows] = total.astype(BF16)
        if kind == 0:
            squares = terms[item, 0, rows:]
            if arrived:
                squares += one_piece(arrived[item][rows : rows + TAIL])
            out[rows : rows + TAIL] = two_pieces(squares)
        spare = rows + (TAIL if kind == 0 else 0)
        if spare < out.shape[0]:
            out[spare:] = jnp.zeros((out.shape[0] - spare, HEAD_DIM), BF16)


def sends(half, terms, arrived):
    rows = CORE_HEADS * STRETCH
    shapes = [jax.ShapeDtypeStruct((rows + TAIL, HEAD_DIM), BF16)] * 2
    return pl.pallas_call(
        functools.partial(send_kernel, half),
        in_specs=[VMEM] * (1 + len(arrived)),
        out_specs=[VMEM] * 2,
        out_shape=shapes,
        compiler_params=pltpu.CompilerParams(vmem_limit_bytes=16 * MIB),
        name="sends",
    )(terms, *arrived)


def prepare_kernel(targets, queries, starts, turns, grouped, rotary):
    for head in range(KV_HEADS):
        for member in range(GROUP):
            begin = (head * GROUP + member) * HEAD_DIM
            rows = slice(member * STEPS, (member + 1) * STEPS)
            grouped[head, rows] = queries[0, :, begin : begin + HEAD_DIM]
    row = pl.ds(jnp.maximum(prompt_of(targets, lax.axis_index("tp")), 0), 1)
    cosine, sine = starts[0, row, :], starts[1, row, :]
    lane = lax.broadcasted_iota(jnp.int32, turns.shape[1:], 1)
    rotary[0] = turns[0] * cosine - turns[1] * sine
    sine = turns[1] * cosine + turns[0] * sine
    rotary[1] = jnp.where(lane < HEAD_DIM // 2, -sine, sine)


def prepare(targets, queries, starts, turns):
    return pl.pallas_call(
        prepare_kernel,
        in_specs=[SMEM] + [VMEM] * 3,
        out_specs=[VMEM] * 2,
        out_shape=[
            jax.ShapeDtypeStruct((KV_HEADS, ROWS, HEAD_DIM), BF16),
            jax.ShapeDtypeStruct(turns.shape, F32),
        ],
        compiler_params=pltpu.CompilerParams(vmem_limit_bytes=16 * MIB),
        name="prepare",
    )(targets, queries, starts, turns)


def cache_kernel(part, targets, lengths, stored, q, cache, new, out):
    scaling = HEAD_DIM ** (-0.5)
    dims = (((1,), (1,)), ((), ()))
    here = lax.axis_index("tp")
    rep = lax.axis_index("rep")
    length = cache.shape[1]
    prompt = prompt_of(targets, here)
    handed = lengths[jnp.maximum(prompt, 0)] - STRETCH
    span = jnp.where(prompt >= 0, handed, stored[0]) - rep * length
    count = CORE_HEADS * ROWS
    allowed = lax.broadcasted_iota(jnp.int32, (count, length), 1) < span
    second_step = lax.broadcasted_iota(jnp.int32, (count, 1), 0) % STEPS == 1
    scores, fresh, key_lanes, value_lanes = [], [[], []], [], []
    for at in range(CORE_HEADS):
        head = (rep if part == 1 else 1 - rep) * CORE_HEADS + at
        key_lanes.append(pl.ds(pl.multiple_of(head * HEAD_DIM, HEAD_DIM), HEAD_DIM))
        begin = pl.multiple_of((KV_HEADS + head) * HEAD_DIM, HEAD_DIM)
        value_lanes.append(pl.ds(begin, HEAD_DIM))
        query = q[head]
        wide = query.astype(F32)
        keys = cache[0, :, key_lanes[at]]
        scores.append(lax.dot_general(query, keys, dims, preferred_element_type=F32))
        for step in range(STEPS):
            key = new[0, step : step + 1, key_lanes[at]].astype(F32)
            fresh[step].append(jnp.sum(wide * key, axis=1, keepdims=True))
    scores = jnp.where(allowed, jnp.concatenate(scores, axis=0) * scaling, NEGATIVE)
    highest = jnp.max(scores, axis=1, keepdims=True)
    for step in range(STEPS):
        shown = rep == 0 if step == 0 else second_step & (rep == 0)
        fresh[step] = jnp.where(shown, jnp.concatenate(fresh[step], axis=0) * scaling, NEGATIVE)
        highest = jnp.maximum(highest, fresh[step])
    some = highest > 0.5 * NEGATIVE
    highest = jnp.where(some, highest, 0.0)
    weight = jnp.exp(scores - highest)
    shares = [jnp.exp(score - highest) for score in fresh]
    totals = jnp.sum(weight, axis=1, keepdims=True) + shares[0] + shares[1]
    totals = jnp.where(some, totals, 1.0)
    logs = jnp.where(some, highest + jnp.log(totals), NEGATIVE)
    weight = weight.astype(BF16)
    for at in range(CORE_HEADS):
        rows = slice(at * ROWS, (at + 1) * ROWS)
        values = cache[0, :, value_lanes[at]]
        sums = jnp.dot(weight[rows], values, preferred_element_type=F32)
        for step in range(STEPS):
            value = new[0, step : step + 1, value_lanes[at]].astype(F32)
            sums += shares[step][rows].astype(BF16).astype(F32) * value
        out[at, :ROWS] = (sums / totals[rows]).astype(BF16)
        out[at, ROWS:] = pieces_tail(logs[rows])


def cache_attention(part, targets, lengths, stored, grouped, kv_cache, new_kv):
    return pl.pallas_call(
        functools.partial(cache_kernel, part),
        in_specs=[SMEM] * 3 + [VMEM] * 3,
        out_specs=VMEM,
        out_shape=jax.ShapeDtypeStruct((CORE_HEADS, PART, HEAD_DIM), BF16),
        compiler_params=pltpu.CompilerParams(vmem_limit_bytes=16 * MIB),
        cost_estimate=pl.CostEstimate(
            flops=1, bytes_accessed=1, transcendentals=0
        ),
        name="cache_attention",
    )(targets, lengths, stored, grouped, kv_cache, new_kv)


def final_kernel(
    targets, rotary, own, right_keys, left_values, right_values, left_keys, grouped,
    cached_there, cached_here, out,
):
    scaling = HEAD_DIM ** (-0.5)
    dims = (((1,), (1,)), ((), ()))
    mine = own.shape[0] - 1
    first = lax.axis_index("rep") * CORE_HEADS
    prompt = prompt_of(targets, lax.axis_index("tp"))
    cosine, sine = rotary[0], rotary[1]
    rows = CORE_HEADS * STRETCH
    squares = own[mine, 0, rows:] + one_piece(right_keys[rows : rows + TAIL]) + one_piece(left_keys[rows : rows + TAIL])
    scale = token_column(lax.rsqrt(squares / D + EPSILON))
    scores, handed = [], []
    for head in range(CORE_HEADS):
        at = slice(head * STRETCH, (head + 1) * STRETCH)
        keys = own[mine, 0, at] + right_keys[at].astype(F32) + left_keys[at].astype(F32)
        values = own[mine, 1, at] + right_values[at].astype(F32) + left_values[at].astype(F32)
        keys = (keys * scale).astype(BF16).astype(F32)
        handed.append((values * scale).astype(BF16))
        keys = keys * cosine + pltpu.roll(keys, HEAD_DIM // 2, 1) * sine
        scores.append(
            lax.dot_general(
                grouped[first + head], keys.astype(BF16), dims, preferred_element_type=F32
            )
        )
    scores = jnp.concatenate(scores, axis=0) * scaling
    highest = jnp.max(scores, axis=1, keepdims=True)
    weight = jnp.exp(scores - highest)
    totals = jnp.sum(weight, axis=1, keepdims=True)
    weight = weight.astype(BF16)
    sums = [
        jnp.dot(weight[head * ROWS : (head + 1) * ROWS], handed[head], preferred_element_type=F32)
        for head in range(CORE_HEADS)
    ]
    sums = [jnp.concatenate(sums, axis=0) / totals]
    logs = [jnp.where(prompt >= 0, highest + jnp.log(totals), NEGATIVE)]
    for cached in (cached_there, cached_here):
        parts = [cached[head] for head in range(CORE_HEADS)]
        sums.append(jnp.concatenate([part[:ROWS].astype(F32) for part in parts], axis=0))
        logs.append(jnp.concatenate([tail_pieces(part[ROWS:]) for part in parts], axis=0))
    highest = functools.reduce(jnp.maximum, logs)
    shares = [jnp.exp(log - highest) for log in logs]
    total = functools.reduce(jnp.add, shares)
    joined = functools.reduce(jnp.add, [share * part for share, part in zip(shares, sums)])
    result = (joined / total).astype(BF16)
    for member in range(CORE_HEADS * GROUP):
        lanes = slice(member * HEAD_DIM, (member + 1) * HEAD_DIM)
        out[0, :, lanes] = result[member * STEPS : (member + 1) * STEPS]


def finish(targets, rotary, own, arrived, grouped, cached):
    width = CORE_HEADS * GROUP * HEAD_DIM
    return pl.pallas_call(
        final_kernel,
        in_specs=[SMEM] + [VMEM] * 9,
        out_specs=VMEM,
        out_shape=jax.ShapeDtypeStruct((1, STEPS, width), BF16),
        compiler_params=pltpu.CompilerParams(vmem_limit_bytes=16 * MIB),
        name="finish",
    )(targets, rotary, own, *arrived, grouped, *cached)


def rotary_turns():
    half = np.arange(HEAD_DIM // 2, dtype=np.float64) / (HEAD_DIM // 2)
    frequency = ROTARY_BASE ** (-np.concatenate([half, half]))
    angles = np.arange(STRETCH, dtype=np.float64)[:, None] * frequency
    return frequency.astype(np.float32), np.stack([np.cos(angles), np.sin(angles)]).astype(np.float32)


def per_device(
    stretch,
    norm_gain,
    kv_codes,
    scale_codes,
    outer_scales,
    prompt_lengths,
    target_rows,
    cache_lengths,
    kv_cache,
    queries,
    new_kv,
):
    count = lax.axis_size("tp")
    half = count // 2
    lines = stretch.transpose(1, 0, 2)
    gain = norm_gain.reshape(1, -1)
    ring = [ring_device(at, count) for at in range(count)]
    to_right = [(ring[at], ring[(at + 1) % count]) for at in range(count)]
    to_left = [(ring[at], ring[at - 1]) for at in range(count)]

    def pass_on(right, left):
        return lax.ppermute(right, "tp", to_right), lax.ppermute(left, "tp", to_left)

    swap = lambda array: lax.ppermute(array, "rep", [(0, 1), (1, 0)])
    other = swap(lines)
    weight = dequantize(kv_codes, scale_codes, outer_scales.T)
    frequency, turns = rotary_turns()
    start = (prompt_lengths - STRETCH).astype(F32)[:, None] * jnp.asarray(frequency)
    starts = jnp.stack([jnp.cos(start), jnp.sin(start)])

    features = [lines, other, gain]
    right, left = project_first(half, target_rows, *features, weight)
    targets, _ = lax.optimization_barrier((target_rows, left))
    arrived = [pass_on(right, left), []]

    for distance in range(half - 1, 0, -1):
        if distance == half - 1:
            terms, *kept = project_early(distance, targets, *features, weight)
        else:
            terms = project([distance, -distance], targets, *features, weight)
            kept = terms
        right, left = sends(1, terms, arrived[1])
        kept, right, left = lax.optimization_barrier((kept, right, left))
        targets, _ = lax.optimization_barrier((target_rows, left))
        arrived[1] = pass_on(right, left)
        terms = kept
        if distance == half - 1:
            prepared = prepare(targets, queries, starts, jnp.asarray(turns))
            terms = project_late(*kept, weight)
            terms, prepared = lax.optimization_barrier((terms, prepared))
            grouped, rotary = prepared
        if distance == max(1, half - 2):
            cached = cache_attention(
                0, targets, prompt_lengths, cache_lengths, grouped, kv_cache, new_kv
            )
            terms, cached = lax.optimization_barrier((terms, cached))
        right, left = sends(0, terms, arrived[0])
        targets, right = lax.optimization_barrier((target_rows, right))
        arrived[0] = pass_on(right, left)

    cached, _ = lax.optimization_barrier((cached, right))
    cached = [swap(cached)]
    terms = project([0], targets, *features, weight)
    cached.append(
        cache_attention(1, targets, prompt_lengths, cache_lengths, grouped, kv_cache, new_kv)
    )
    out = finish(target_rows, rotary, terms, [*arrived[0], *arrived[1]], grouped, cached)
    return lax.all_gather(out, "rep", axis=2, tiled=True)


def solution(mesh):
    in_specs = (
        P(None, ("grp", "rep"), "tp"),
        P("tp"),
        P("tp", None),
        P("tp", None),
        P("tp", None),
        P("grp"),
        P("grp"),
        P(("grp", "tp")),
        P(("grp", "tp"), "rep", None),
        P(("grp", "tp"), None, None),
        P(("grp", "tp"), None, None),
    )
    out_specs = P(("grp", "tp"), None, None)
    return jax.shard_map(
        per_device, mesh=mesh, in_specs=in_specs, out_specs=out_specs, check_vma=False
    )
```
